32 devices in a mesh: tm: 4 (over z), height: 4 (over x, core), heads: 2 (over y).
Axes of the slice: x: 2, y: 2, z: 4, core: 2. Of those that a mesh axis runs over, the one named last changes fastest.
Arguments:
- queries: bfloat16 [24, 32, 8, 768], P('tm', 'height', None, 'heads'), may hold values from -18 to 18
- key_tokens: bfloat16 [24, 32, 8, 768], P('tm', 'height', None, 'heads'), may hold values from -4 to 4
- value_tokens: bfloat16 [24, 32, 8, 768], P('tm', 'height', None, 'heads'), may hold values from -5 to 5
- cotangent: bfloat16 [24, 32, 8, 768], P('tm', 'height', None, 'heads'), may hold values from -5 to 5
- window_mask: int32 [4, 4, 9], replicated, may hold values 0 or 1
Outputs:
- attended: bfloat16 [24, 32, 8, 768], P('tm', 'height', None, 'heads')
- query_grad: bfloat16 [24, 32, 8, 768], P('tm', 'height', None, 'heads')
- key_grad: bfloat16 [24, 32, 8, 768], P('tm', 'height', None, 'heads')
- value_grad: bfloat16 [24, 32, 8, 768], P('tm', 'height', None, 'heads')
The draws below stay inside these ranges and needn't reach their ends.
All inputs are finite; a program needn't handle non-finite values.
Results may differ from the reference program's by a relative error of at most 0.012.
Values may be sent and summed in bfloat16 or wider, within the bound.
No kernel may reach another device: no remote copies, remote signals or barrier semaphores. Data moves between devices by JAX's collectives and lax.ppermute only.
A program may use at most 128 MiB of HBM per device.

```python
import jax
import jax.numpy as jnp
from jax import lax

HEADS = 12
HEAD_DIM = 64
TILE_T = 6
TILE_H = 8
TILE_W = 8
TILE = 384
FEAT = 768
TTILES = 4
HTILES = 4
FRAMES = 24
ROWS = 32


def draw_queries(key, part):
    key = jax.random.fold_in(key, 1)
    drawn = jax.random.truncated_normal(key, -4.0, 4.0, (FRAMES, ROWS, TILE_W, FEAT), jnp.float32)
    return drawn.astype(jnp.bfloat16)


def draw_key_tokens(key, part):
    key = jax.random.fold_in(key, 2)
    drawn = jax.random.truncated_normal(key, -4.0, 4.0, (FRAMES, ROWS, TILE_W, FEAT), jnp.float32)
    return drawn.astype(jnp.bfloat16)


def place_ends(result, rng, smallest, high):
    spot = [jax.random.randint(jax.random.fold_in(rng, axis), (), 0, length) for axis, length in enumerate(result.shape)]
    widest = result.shape.index(max(result.shape))
    beside = spot[:widest] + [(spot[widest] + 1) % result.shape[widest]] + spot[widest + 1:]
    return result.at[tuple(spot)].set(smallest).at[tuple(beside)].set(high)


def levels(rng, dims, shards, smallest, top_value):
    def one(dim, shards_of):
        heights = jax.random.uniform(jax.random.fold_in(jax.random.fold_in(rng, 6), dim), (shards_of,), jnp.float32, smallest / len(shards), top_value / len(shards))
        return jnp.repeat(jnp.exp(heights), dims[dim] // shards_of).reshape((-1,) + (1,) * (len(dims) - dim - 1))

    gain = one(*shards[0])
    for cut in shards[1:]:
        gain = gain * one(*cut)
    return gain


def bell_draw(stream_key, shape, deviation, most, cuts=(), held_as=jnp.bfloat16):
    gain = levels(stream_key, shape, cuts, -0.22, 0.18) if cuts else 1.0
    drawn = jax.random.normal(stream_key, shape, jnp.float32) * deviation * gain
    return jnp.minimum(jnp.maximum(drawn, -most), most).astype(held_as)


def setup_inputs(seed: int = 0) -> dict:
    splits = jax.random.split(jax.random.key(seed), 6)
    return {
        "queries": draw_queries(jax.random.fold_in(splits[5], 71), 0),
        "key_tokens": draw_key_tokens(jax.random.fold_in(splits[5], 71), 0),
        "value_tokens": bell_draw(splits[2], (FRAMES, ROWS, TILE_W, FEAT), 1.0, 5.0, ((0, 4), (1, 4), (3, 2))),
        "cotangent": bell_draw(splits[3], (FRAMES, ROWS, TILE_W, FEAT), 1.0, 5.0, ((0, 4), (1, 4), (3, 2))),
        "window_mask": place_ends((jax.random.randint(splits[4], (TTILES, HTILES, 9), 0, 3) < 2).astype(jnp.int32), jax.random.fold_in(splits[4], 1), 0, 1),
    }


masked_score = -1e30


def to_tiles(grid):
    shaped = grid.reshape(TTILES, TILE_T, HTILES, TILE_H, TILE_W, FEAT)
    return shaped.transpose(0, 2, 1, 3, 4, 5).reshape(TTILES, HTILES, TILE, FEAT)


def to_grid(tiles):
    shaped = tiles.reshape(TTILES, HTILES, TILE_T, TILE_H, TILE_W, FEAT)
    return shaped.transpose(0, 2, 1, 3, 4, 5).reshape(FRAMES, ROWS, TILE_W, FEAT)


def border(tiles):
    widths = [(1, 1), (1, 1)] + [(0, 0)] * (tiles.ndim - 2)
    return jnp.pad(tiles, widths)


def block_of(padded, row_tile, column_tile):
    starts = (row_tile, column_tile) + (jnp.int32(0),) * (padded.ndim - 2)
    return lax.dynamic_slice(padded, starts, (3, 3) + padded.shape[2:])


def rounded(values):
    return lax.optimization_barrier(values.astype(jnp.bfloat16)).astype(jnp.float32)


def validity(window_mask):
    tile_time = jnp.arange(TTILES, dtype=jnp.int32)[:, None, None]
    tile_height = jnp.arange(HTILES, dtype=jnp.int32)[None, :, None]
    offset = jnp.arange(9, dtype=jnp.int32)[None, None, :]
    time_index = tile_time + offset // 3 - 1
    height_index = tile_height + offset % 3 - 1
    inside = (time_index >= 0) & (time_index < TTILES) & (height_index >= 0) & (height_index < HTILES)
    return inside & ((offset == 4) | (window_mask == 1))


def reference(queries, key_tokens, value_tokens, cotangent, window_mask):
    scale = HEAD_DIM ** -0.5
    query_tiles = to_tiles(queries)
    key_tiles = to_tiles(key_tokens)
    value_tiles = to_tiles(value_tokens)
    grad_tiles = to_tiles(cotangent)
    allowed = validity(window_mask)
    key_pad = border(key_tiles)
    value_pad = border(value_tiles)
    indices = jnp.arange(TTILES * HTILES, dtype=jnp.int32)

    def query_side(index):
        row_tile = index // HTILES
        column_tile = index % HTILES
        query = query_tiles[row_tile, column_tile].reshape(TILE, HEADS, HEAD_DIM).astype(jnp.float32)
        grads = grad_tiles[row_tile, column_tile].reshape(TILE, HEADS, HEAD_DIM).astype(jnp.float32)
        keys_near = block_of(key_pad, row_tile, column_tile).reshape(9 * TILE, HEADS, HEAD_DIM).astype(jnp.float32)
        values_near = block_of(value_pad, row_tile, column_tile).reshape(9 * TILE, HEADS, HEAD_DIM).astype(jnp.float32)
        usable = jnp.repeat(allowed[row_tile, column_tile], TILE)
        scores = jnp.einsum("qhd,khd->hqk", query, keys_near) * scale
        scores = jnp.where(usable[None, None, :], scores, masked_score)
        highest = jnp.max(scores, axis=-1, keepdims=True)
        logsum = highest + jnp.log(jnp.sum(jnp.exp(scores - highest), axis=-1, keepdims=True))
        weights = jnp.exp(scores - logsum)
        output = jnp.einsum("hqk,khd->qhd", rounded(weights), values_near).astype(jnp.bfloat16)
        carried = jnp.sum(grads * output.astype(jnp.float32), axis=-1).T
        product = jnp.einsum("qhd,khd->hqk", grads, values_near)
        slopes = rounded(weights * (product - carried[:, :, None]) * scale)
        query_grad = jnp.einsum("hqk,khd->qhd", slopes, keys_near).astype(jnp.bfloat16)
        return output.reshape(TILE, FEAT), query_grad.reshape(TILE, FEAT), logsum[:, :, 0], carried

    attended, query_grad, logsum, carried = lax.map(query_side, indices)
    logsum = logsum.reshape(TTILES, HTILES, HEADS, TILE)
    carried = carried.reshape(TTILES, HTILES, HEADS, TILE)
    query_pad = border(query_tiles)
    grad_pad = border(grad_tiles)
    logsum_pad = border(logsum)
    carried_pad = border(carried)
    allowed_pad = border(allowed)

    def key_side(index):
        row_tile = index // HTILES
        column_tile = index % HTILES
        own_keys = key_tiles[row_tile, column_tile].reshape(TILE, HEADS, HEAD_DIM).astype(jnp.float32)
        own_values = value_tiles[row_tile, column_tile].reshape(TILE, HEADS, HEAD_DIM).astype(jnp.float32)
        sources = block_of(query_pad, row_tile, column_tile)[::-1, ::-1].reshape(9 * TILE, HEADS, HEAD_DIM).astype(jnp.float32)
        grads = block_of(grad_pad, row_tile, column_tile)[::-1, ::-1].reshape(9 * TILE, HEADS, HEAD_DIM).astype(jnp.float32)
        logsums = block_of(logsum_pad, row_tile, column_tile)[::-1, ::-1].transpose(2, 0, 1, 3).reshape(HEADS, 9 * TILE)
        carries = block_of(carried_pad, row_tile, column_tile)[::-1, ::-1].transpose(2, 0, 1, 3).reshape(HEADS, 9 * TILE)
        flags = block_of(allowed_pad, row_tile, column_tile)[::-1, ::-1].reshape(9, 9)
        usable = jnp.repeat(jnp.diagonal(flags), TILE)
        scores = jnp.einsum("qhd,khd->hqk", sources, own_keys) * scale
        scores = jnp.where(usable[None, :, None], scores, masked_score)
        weights = jnp.exp(scores - logsums[:, :, None])
        value_grad = jnp.einsum("hqk,qhd->khd", rounded(weights), grads).astype(jnp.bfloat16)
        product = jnp.einsum("qhd,khd->hqk", grads, own_values)
        slopes = rounded(weights * (product - carries[:, :, None]) * scale)
        key_grad = jnp.einsum("hqk,qhd->khd", slopes, sources).astype(jnp.bfloat16)
        return key_grad.reshape(TILE, FEAT), value_grad.reshape(TILE, FEAT)

    key_grad, value_grad = lax.map(key_side, indices)
    shape = (TTILES, HTILES, TILE, FEAT)
    return (to_grid(attended.reshape(shape)), to_grid(query_grad.reshape(shape)), to_grid(key_grad.reshape(shape)), to_grid(value_grad.reshape(shape)))
```

```python
import functools

import jax
import jax.numpy as jnp
from jax import lax
from jax.experimental import pallas as pl
from jax.experimental.pallas import tpu as pltpu
from jax.sharding import PartitionSpec as P

HEAD_DIM = 64
TILE_T = 6
PAIR = 2 * HEAD_DIM
LOG2E = 1.4426950408889634


def shifted(array, axis, by):
    peers = lax.axis_size(axis)
    return lax.ppermute(array, axis, [(i, i + by) for i in range(peers) if 0 <= i + by < peers])


def near(array):
    peers = lax.axis_size("height")
    return lax.ppermute(array, "height", [(i, i ^ 1) for i in range(peers) if (i ^ 1) < peers])


def far(array):
    peers = lax.axis_size("height")
    pairs = [(i, i + 1) for i in range(1, peers - 1, 2)]
    return lax.ppermute(array, "height", pairs + [(b, a) for a, b in pairs])


def allowed(mask_ref, slot, tiles_t, tiles_h):
    time = lax.axis_index("tm")
    height = lax.axis_index("height")
    side = 1 - 2 * lax.rem(height, 2)
    column = slot // 3
    place = lax.rem(slot, 3)
    dt = jnp.where(place == 0, 0, jnp.where(place == 1, -1, 1))
    dh = jnp.where(column == 0, 0, jnp.where(column == 1, -side, side))
    inside = (
        (time + dt >= 0) & (time + dt < tiles_t) & (height + dh >= 0) & (height + dh < tiles_h)
    )
    flag = mask_ref[time, height, 3 * (dt + 1) + dh + 1]
    return inside & ((slot == 0) | (flag == 1))


def attention_kernel(
    tiles_t, tiles_h, mask_ref, q_ref, do_ref, *refs
):
    kv_hbm = refs[:9]
    o_ref, dq_ref = refs[9:11]
    g_hbm = refs[11:20]
    (kv, p_ref, qt, qm, dt_, dm, m_all, m_run, l_run, delta, acc, dq_acc, stage, in_sem, out_sem) = refs[20:]
    pairs, _, wide = qt.shape
    tokens = wide // 2

    def load(slot):
        return pltpu.make_async_copy(kv_hbm[slot], kv.at[slot], in_sem.at[slot])

    for slot in range(9):
        load(slot).start()

    def put_blocks(p, x, x_t, x_wide, x_tall):
        zero_t = jnp.zeros((HEAD_DIM, tokens), jnp.bfloat16)
        x_wide[p, :HEAD_DIM, :tokens] = x_t[:HEAD_DIM]
        x_wide[p, :HEAD_DIM, tokens:] = zero_t
        x_wide[p, HEAD_DIM:, :tokens] = zero_t
        x_wide[p, HEAD_DIM:, tokens:] = x_t[HEAD_DIM:]
        low = lax.broadcasted_iota(jnp.int32, x.shape, 1) < HEAD_DIM
        zero = jnp.zeros_like(x)
        x_tall[p, :tokens] = jnp.where(low, x, zero)
        x_tall[p, tokens:] = jnp.where(low, zero, x)

    for p in range(pairs):
        lanes = slice(p * PAIR, (p + 1) * PAIR)
        q = (q_ref[:, lanes].astype(jnp.float32) * HEAD_DIM ** -0.5).astype(jnp.bfloat16)
        put_blocks(p, q, q.T, qt, qm)
        d = do_ref[:, lanes]
        put_blocks(p, d, d.T, dt_, dm)

    m_run[...] = jnp.full_like(m_run, -1e30)
    l_run[...] = jnp.zeros_like(l_run)
    acc[...] = jnp.zeros_like(acc)
    dq_acc[...] = jnp.zeros_like(dq_acc)

    def forward(slot, carry):
        for s in range(9):
            @pl.when(slot == s)
            def _():
                load(s).wait()

        @pl.when(allowed(mask_ref, slot, tiles_t, tiles_h))
        def _():
            for p in range(pairs):
                lanes = slice(p * PAIR, (p + 1) * PAIR)
                s = jnp.dot(kv[slot, 0, :, lanes], qt[p], preferred_element_type=jnp.float32)
                m_old = m_run[p]
                m_new = jnp.maximum(m_old, jnp.max(s, axis=0, keepdims=True))
                e = jnp.exp2((s - m_new) * LOG2E)
                alpha = jnp.exp2((m_old - m_new) * LOG2E)
                l_run[p] = l_run[p] * alpha + jnp.sum(e, axis=0, keepdims=True)
                m_run[p] = m_new
                m_all[slot, p] = m_new
                low = e.astype(jnp.bfloat16)
                p_ref[slot, p] = low
                v_t = kv[slot, 1, :, lanes].T
                acc[p] = acc[p] * alpha + jnp.dot(v_t, low, preferred_element_type=jnp.float32)

        return carry

    lax.fori_loop(0, 9, forward, 0)

    def diagonal(x):
        return jnp.concatenate([x[:HEAD_DIM, :tokens], x[HEAD_DIM:, tokens:]], axis=0)

    for p in range(pairs):
        inverse = 1.0 / l_run[p]
        l_run[p] = inverse
        out_t = diagonal(acc[p] * inverse).astype(jnp.bfloat16)
        o_ref[:, p * PAIR : (p + 1) * PAIR] = out_t.T
        d_t = diagonal(dt_[p]).astype(jnp.float32)
        both = d_t * out_t.astype(jnp.float32)
        delta[p, :, :tokens] = jnp.sum(both[:HEAD_DIM], axis=0, keepdims=True)
        delta[p, :, tokens:] = jnp.sum(both[HEAD_DIM:], axis=0, keepdims=True)

    def store(slot, place):
        return pltpu.make_async_copy(stage.at[place], g_hbm[slot], out_sem.at[place])

    def backward(step, carry):
        slot = 8 - step
        place = lax.rem(step, 2)

        for s in range(9):
            @pl.when((slot == s - 2) & (s >= 2))
            def _():
                store(s, (8 - s) % 2).wait()

        ok = allowed(mask_ref, slot, tiles_t, tiles_h)

        @pl.when(jnp.logical_not(ok))
        def _():
            stage[place] = jnp.zeros(stage.shape[1:], stage.dtype)

        @pl.when(ok)
        def _():
            for p in range(pairs):
                lanes = slice(p * PAIR, (p + 1) * PAIR)
                beta = jnp.exp2((m_all[slot, p] - m_run[p]) * LOG2E) * l_run[p]
                w = p_ref[slot, p] * beta.astype(jnp.bfloat16)
                dp = jnp.dot(kv[slot, 1, :, lanes], dt_[p], preferred_element_type=jnp.float32)
                ds = w * (dp - delta[p]).astype(jnp.bfloat16)
                dv = jnp.dot(w, dm[p], preferred_element_type=jnp.float32)
                dk = jnp.dot(ds, qm[p], preferred_element_type=jnp.float32)
                stage[place, 0, :, lanes] = dk.astype(stage.dtype)
                stage[place, 1, :, lanes] = dv.astype(stage.dtype)
                k_t = kv[slot, 0, :, lanes].T
                dq_acc[p] += jnp.dot(k_t, ds, preferred_element_type=jnp.float32)

        for s in range(9):
            @pl.when(slot == s)
            def _():
                store(s, (8 - s) % 2).start()

        return carry

    lax.fori_loop(0, 9, backward, 0)
    for p in range(pairs):
        dq_t = (diagonal(dq_acc[p]) * HEAD_DIM ** -0.5).astype(jnp.bfloat16)
        dq_ref[:, p * PAIR : (p + 1) * PAIR] = dq_t.T
    store(1, 1).wait()
    store(0, 0).wait()


def attention(mask, q, d, kvs, tiles_t, tiles_h):
    tokens, features = q.shape
    pairs = features // PAIR
    wide = 2 * tokens
    f32, bf16 = jnp.float32, jnp.bfloat16
    whole = pl.BlockSpec(memory_space=pltpu.VMEM)
    anywhere = pl.BlockSpec(memory_space=pl.ANY)
    tile = jax.ShapeDtypeStruct(q.shape, bf16)
    grads = jax.ShapeDtypeStruct((2,) + q.shape, bf16)
    flops = 9 * 6 * 2 * tokens * tokens * features
    return pl.pallas_call(
        functools.partial(attention_kernel, tiles_t, tiles_h),
        out_shape=[tile, tile] + [grads] * 9,
        in_specs=[pl.BlockSpec(memory_space=pltpu.SMEM), whole, whole] + [anywhere] * 9,
        out_specs=[whole, whole] + [anywhere] * 9,
        scratch_shapes=[
            pltpu.VMEM((9, 2) + q.shape, bf16),
            pltpu.VMEM((9, pairs, tokens, wide), bf16),
            pltpu.VMEM((pairs, PAIR, wide), bf16),
            pltpu.VMEM((pairs, wide, PAIR), bf16),
            pltpu.VMEM((pairs, PAIR, wide), bf16),
            pltpu.VMEM((pairs, wide, PAIR), bf16),
            pltpu.VMEM((9, pairs, 1, wide), f32),
            pltpu.VMEM((pairs, 1, wide), f32),
            pltpu.VMEM((pairs, 1, wide), f32),
            pltpu.VMEM((pairs, 1, wide), f32),
            pltpu.VMEM((pairs, PAIR, wide), f32),
            pltpu.VMEM((pairs, PAIR, wide), f32),
            pltpu.VMEM((2, 2) + q.shape, bf16),
            pltpu.SemaphoreType.DMA((9,)),
            pltpu.SemaphoreType.DMA((2,)),
        ],
        compiler_params=pltpu.CompilerParams(vmem_limit_bytes=48 * 1024 * 1024),
        cost_estimate=pl.CostEstimate(flops=flops, bytes_accessed=20 * 2 * tokens * features * 2, transcendentals=0),
    )(mask, q, d, *kvs)


def local(queries, key_tokens, value_tokens, cotangent, window_mask):
    shape = queries.shape
    features = shape[-1]
    q = queries.reshape(-1, features)
    d = cotangent.reshape(-1, features)
    own = jnp.stack([key_tokens.reshape(-1, features), value_tokens.reshape(-1, features)])
    f32, bf16 = jnp.float32, jnp.bfloat16

    far_own = far(own)
    own_before = shifted(own, "tm", 1)
    own_after = shifted(own, "tm", -1)
    far_before = shifted(far_own, "tm", 1)
    far_after = shifted(far_own, "tm", -1)
    near_all = near(jnp.stack([own, own_before, own_after]))
    kvs = [own, own_before, own_after, far_own, far_before, far_after, near_all[0], near_all[1], near_all[2]]
    out, dq, *g = attention(window_mask, q, d, kvs, lax.axis_size("tm"), lax.axis_size("height"))

    far_total = (
        g[3].astype(f32) + shifted(g[4], "tm", -1).astype(f32) + shifted(g[5], "tm", 1).astype(f32)
    )
    back = near(jnp.stack(g[6:9])).astype(f32)
    before = (g[1].astype(f32) + back[1]).astype(bf16)
    after = (g[2].astype(f32) + back[2]).astype(bf16)
    from_far = far(far_total.astype(bf16)).astype(f32)
    total = (
        g[0].astype(f32)
        + back[0]
        + shifted(before, "tm", -1).astype(f32)
        + shifted(after, "tm", 1).astype(f32)
        + from_far
    )
    grads = total.astype(bf16)
    return out.reshape(shape), dq.reshape(shape), grads[0].reshape(shape), grads[1].reshape(shape)


def solution(mesh):
    spec = P("tm", "height", None, "heads")
    return jax.shard_map(
        local, mesh=mesh, in_specs=(spec, spec, spec, spec, P()), out_specs=(spec,) * 4, check_vma=False
    )
```

```python
import functools

import jax
import jax.numpy as jnp
from jax import lax
from jax.experimental import pallas as pl
from jax.experimental.pallas import tpu as pltpu
from jax.sharding import PartitionSpec as P

HEAD_DIM = 64
PAIR = 2 * HEAD_DIM
LOG2E = 1.4426950408889634
SCALE = HEAD_DIM ** -0.5
BF16 = jnp.bfloat16
F32 = jnp.float32


def pairing(size, first):
    pairs = [(i, i + 1) for i in range(first, size - 1, 2)]
    return pairs + [(b, a) for a, b in pairs]


def near(array):
    return lax.ppermute(array, "height", pairing(lax.axis_size("height"), 0))


def far(array):
    return lax.ppermute(array, "height", pairing(lax.axis_size("height"), 1))


def in_time(array, first):
    return lax.ppermute(array, "tm", pairing(lax.axis_size("tm"), first))


def in_time_middle(array, first):
    heights = lax.axis_size("height")
    pairs = [
        (a * heights + h, b * heights + h)
        for a, b in pairing(lax.axis_size("tm"), first)
        for h in range(1, heights - 1)
    ]
    return lax.ppermute(array, ("tm", "height"), pairs)


def offset(kind, index):
    even = 1 - 2 * lax.rem(index, 2)
    return jnp.where(kind == 0, 0, jnp.where(kind == 1, even, -even))


def allowed(mask_ref, slot, tiles_t, tiles_h):
    time = lax.axis_index("tm")
    height = lax.axis_index("height")
    dt = offset(lax.rem(slot, 3), time)
    dh = offset(slot // 3, height)
    inside = (
        (time + dt >= 0) & (time + dt < tiles_t) & (height + dh >= 0) & (height + dh < tiles_h)
    )
    flag = mask_ref[time, height, 3 * (dt + 1) + dh + 1]
    return inside & ((slot == 0) | (flag == 1))


def choose(index, values):
    result = jnp.int32(values[-1])
    for at, value in enumerate(values[:-1]):
        result = jnp.where(index == at, value, result)
    return result


def diagonal(x):
    tokens = x.shape[1] // 2
    return jnp.concatenate([x[:HEAD_DIM, :tokens], x[HEAD_DIM:, tokens:]], axis=0)


def put_blocks(p, x, wide_ref, tall_ref):
    tokens = x.shape[0]
    x_t = x.T
    zero_t = jnp.zeros((HEAD_DIM, tokens), x.dtype)
    wide_ref[p, :HEAD_DIM, :tokens] = x_t[:HEAD_DIM]
    wide_ref[p, :HEAD_DIM, tokens:] = zero_t
    wide_ref[p, HEAD_DIM:, :tokens] = zero_t
    wide_ref[p, HEAD_DIM:, tokens:] = x_t[HEAD_DIM:]
    low = lax.broadcasted_iota(jnp.int32, x.shape, 1) < HEAD_DIM
    zero = jnp.zeros_like(x)
    tall_ref[p, :tokens] = jnp.where(low, x, zero)
    tall_ref[p, tokens:] = jnp.where(low, zero, x)


class Phase:
    def __init__(self, slots, forward, backward, kept, given, first, last):
        self.slots, self.forward, self.backward = slots, forward, backward
        self.kept, self.given = kept, given
        self.first, self.last = first, last
        self.finish = forward > 0 and backward > 0


def phase_kernel(phase, names_in, names_out, tiles_t, tiles_h, kv_at, p_at, *refs):
    ins = dict(zip(names_in, refs))
    outs = dict(zip(names_out, refs[len(names_in):]))
    kv, p_ref, stage, kv_sem, p_sem, g_sem = refs[len(names_in) + len(names_out):]
    mask_ref = ins["mask"]
    count = len(phase.slots)
    pairs = kv.shape[-1] // PAIR

    def ok(slot):
        return allowed(mask_ref, slot, tiles_t, tiles_h)

    def load_kv(i):
        name, at = kv_at[i]
        source = ins[name] if at is None else ins[name].at[at]
        return pltpu.make_async_copy(source, kv.at[i], kv_sem.at[i])

    def load_p(i):
        name, at = p_at[i]
        return pltpu.make_async_copy(ins[name].at[at], p_ref.at[i], p_sem.at[i])

    def save_p(i):
        return pltpu.make_async_copy(p_ref.at[i], outs["p"].at[phase.kept.index(i)], p_sem.at[i])

    def save_g(i):
        return pltpu.make_async_copy(stage.at[i], outs["g"].at[i], g_sem.at[i])

    for i in range(count):
        @pl.when(ok(jnp.int32(phase.slots[i])))
        def _():
            load_kv(i).start()
            if i in phase.given:
                load_p(i).start()

    if phase.first:
        qdt, qdm = outs["qdt"], outs["qdm"]
        for p in range(pairs):
            lanes = slice(p * PAIR, (p + 1) * PAIR)
            q = (ins["q"][:, lanes].astype(F32) * SCALE).astype(BF16)
            put_blocks(p, q, qdt.at[0], qdm.at[0])
            put_blocks(p, ins["d"][:, lanes], qdt.at[1], qdm.at[1])
    else:
        qdt, qdm = ins["qdt"], ins.get("qdm")

    if phase.forward:
        stat, m_all, acc = outs["stat"], outs["m_all"], outs["acc"]
        if phase.first:
            stat[0:pairs] = jnp.full((pairs, stat.shape[1]), -1e30, F32)
            stat[pairs:] = jnp.zeros((stat.shape[0] - pairs, stat.shape[1]), F32)
            acc[...] = jnp.zeros_like(acc)
            m_all[...] = jnp.zeros_like(m_all)
        else:
            stat[...] = ins["stat"][...]
            m_all[...] = ins["m_all"][...]
            acc[...] = ins["acc"][...]

        def forward(i, carry):
            slot = choose(i, phase.slots[: phase.forward])

            @pl.when(ok(slot))
            def _():
                for j in range(phase.forward):
                    @pl.when(i == j)
                    def _():
                        load_kv(j).wait()

                for p in range(pairs):
                    lanes = slice(p * PAIR, (p + 1) * PAIR)
                    s = jnp.dot(kv[i, 0, :, lanes], qdt[0, p], preferred_element_type=F32)
                    m_old = stat[p : p + 1]
                    m_new = jnp.maximum(m_old, jnp.max(s, axis=0, keepdims=True))
                    e = jnp.exp2((s - m_new) * LOG2E)
                    alpha = jnp.exp2((m_old - m_new) * LOG2E)
                    row = slice(pairs + p, pairs + p + 1)
                    stat[row] = stat[row] * alpha + jnp.sum(e, axis=0, keepdims=True)
                    stat[p : p + 1] = m_new
                    m_all[slot, p : p + 1] = m_new
                    low = e.astype(BF16)
                    p_ref[i, p] = low
                    v_t = kv[i, 1, :, lanes].T
                    acc[p] = acc[p] * alpha + jnp.dot(v_t, low, preferred_element_type=F32)

                for j in phase.kept:
                    @pl.when(i == j)
                    def _():
                        save_p(j).start()

            return carry

        lax.fori_loop(0, phase.forward, forward, 0)
    else:
        stat, m_all = ins["stat"], ins["m_all"]

    if phase.finish:
        for p in range(pairs):
            inverse = 1.0 / stat[pairs + p : pairs + p + 1]
            stat[pairs + p : pairs + p + 1] = inverse
            out_t = diagonal(acc[p] * inverse).astype(BF16)
            outs["out"][:, p * PAIR : (p + 1) * PAIR] = out_t.T
            both = diagonal(qdt[1, p]).astype(F32) * out_t.astype(F32)
            row = slice(2 * pairs + p, 2 * pairs + p + 1)
            tokens = both.shape[1]
            stat[row, :tokens] = jnp.sum(both[:HEAD_DIM], axis=0, keepdims=True)
            stat[row, tokens:] = jnp.sum(both[HEAD_DIM:], axis=0, keepdims=True)

    if phase.backward:
        dq = outs["dq"]
        base = count - phase.backward
        if phase.finish:
            dq[...] = jnp.zeros_like(dq)
        else:
            dq[...] = ins["dq"][...]

        def backward(step, carry):
            i = base + step
            slot = choose(step, phase.slots[base:])
            good = ok(slot)

            @pl.when(jnp.logical_not(good))
            def _():
                stage[step] = jnp.zeros(stage.shape[1:], stage.dtype)

            @pl.when(good)
            def _():
                for j in range(base, count):
                    @pl.when(i == j)
                    def _():
                        if j >= phase.forward:
                            load_kv(j).wait()
                        if j in phase.given:
                            load_p(j).wait()

                for p in range(pairs):
                    lanes = slice(p * PAIR, (p + 1) * PAIR)
                    beta = jnp.exp2((m_all[slot, p : p + 1] - stat[p : p + 1]) * LOG2E)
                    beta = (beta * stat[pairs + p : pairs + p + 1]).astype(BF16)
                    w = p_ref[i, p] * beta
                    dp = jnp.dot(kv[i, 1, :, lanes], qdt[1, p], preferred_element_type=F32)
                    ds = w * (dp - stat[2 * pairs + p : 2 * pairs + p + 1]).astype(BF16)
                    dv = jnp.dot(w, qdm[1, p], preferred_element_type=F32)
                    dk = jnp.dot(ds, qdm[0, p], preferred_element_type=F32)
                    stage[step, 0, :, lanes] = dk.astype(stage.dtype)
                    stage[step, 1, :, lanes] = dv.astype(stage.dtype)
                    k_t = kv[i, 0, :, lanes].T
                    dq[p] += jnp.dot(k_t, ds, preferred_element_type=F32)

            for j in range(phase.backward):
                @pl.when(step == j)
                def _():
                    save_g(j).start()

            return carry

        lax.fori_loop(0, phase.backward, backward, 0)
        if phase.last:
            for p in range(pairs):
                dq_t = (diagonal(dq[p]) * SCALE).astype(BF16)
                outs["dq_out"][:, p * PAIR : (p + 1) * PAIR] = dq_t.T
        for j in range(phase.backward):
            save_g(j).wait()

    for j in phase.kept:
        @pl.when(ok(jnp.int32(phase.slots[j])))
        def _():
            save_p(j).wait()


def run_phase(phase, state, kvs, ps, tiles_t, tiles_h):
    tokens, features = state["q"].shape
    pairs = features // PAIR
    wide = 2 * tokens
    count = len(phase.slots)
    vmem = pl.BlockSpec(memory_space=pltpu.VMEM)
    anywhere = pl.BlockSpec(memory_space=pl.ANY)
    shapes = {
        "qdt": ((2, pairs, PAIR, wide), BF16),
        "qdm": ((2, pairs, wide, PAIR), BF16),
        "stat": ((3 * pairs, wide), F32),
        "m_all": ((9, pairs, wide), F32),
        "acc": ((pairs, PAIR, wide), F32),
        "dq": ((pairs, PAIR, wide), F32),
        "out": ((tokens, features), BF16),
        "dq_out": ((tokens, features), BF16),
        "p": ((len(phase.kept), pairs, tokens, wide), BF16),
        "g": ((phase.backward, 2, tokens, features), BF16),
    }
    names_in = ["mask"]
    names_out = []
    if phase.first:
        names_in += ["q", "d"]
        names_out += ["qdt", "qdm"]
    else:
        names_in += ["qdt", "stat", "m_all"]
    if phase.forward:
        names_out += ["stat", "m_all", "acc"]
        if not phase.first:
            names_in += ["acc"]
    if phase.finish:
        names_out += ["out"]
    if phase.backward:
        names_in += ["qdm"]
        if not phase.finish:
            names_in += ["dq"]
        names_out += ["dq", "g"]
    if phase.last:
        names_out += ["dq_out"]
    if phase.kept:
        names_out += ["p"]
    inputs = {name: state[name] for name in names_in}
    specs = [pl.BlockSpec(memory_space=pltpu.SMEM)] + [vmem] * (len(names_in) - 1)
    seen = {}

    def reference_to(array):
        if id(array) not in seen:
            seen[id(array)] = "big%d" % len(seen)
            inputs[seen[id(array)]] = array
            specs.append(anywhere)
        return seen[id(array)]

    kv_at = [(reference_to(array), at) for array, at in kvs]
    p_at = {i: (reference_to(array), at) for i, (array, at) in ps.items()}
    unit = 2 * tokens * tokens * features
    results = pl.pallas_call(
        functools.partial(
            phase_kernel, phase, list(inputs), names_out, tiles_t, tiles_h, kv_at, p_at
        ),
        out_shape=[jax.ShapeDtypeStruct(*shapes[name]) for name in names_out],
        in_specs=specs,
        out_specs=[anywhere if name in ("p", "g") else vmem for name in names_out],
        scratch_shapes=[
            pltpu.VMEM((count, 2, tokens, features), BF16),
            pltpu.VMEM((count, pairs, tokens, wide), BF16),
            pltpu.VMEM((max(phase.backward, 1), 2, tokens, features), BF16),
            pltpu.SemaphoreType.DMA((count,)),
            pltpu.SemaphoreType.DMA((count,)),
            pltpu.SemaphoreType.DMA((max(phase.backward, 1),)),
        ],
        compiler_params=pltpu.CompilerParams(vmem_limit_bytes=32 * 1024 * 1024),
        cost_estimate=pl.CostEstimate(
            flops=16 * unit * (2 * phase.forward + 4 * phase.backward),
            bytes_accessed=2 * unit // tokens * count,
            transcendentals=0,
        ),
    )(*inputs.values())
    state.update(zip(names_out, results))
    return state


def local(queries, key_tokens, value_tokens, cotangent, window_mask):
    shape = queries.shape
    features = shape[-1]
    tiles_t, tiles_h = lax.axis_size("tm"), lax.axis_size("height")
    run = functools.partial(run_phase, tiles_t=tiles_t, tiles_h=tiles_h)
    state = {
        "mask": window_mask,
        "q": queries.reshape(-1, features),
        "d": cotangent.reshape(-1, features),
    }
    own = jnp.stack([key_tokens.reshape(-1, features), value_tokens.reshape(-1, features)])

    far_own = far(own)
    near_own = near(own)
    own_even = in_time(own, 0)
    own_odd = in_time(own, 1)
    far_even = in_time_middle(far_own, 0)
    far_odd = in_time_middle(far_own, 1)
    near_times = near(jnp.stack([own_even, own_odd]))

    state = run(Phase([0, 3], 2, 0, [0, 1], [], True, False), state, [(own, None), (near_own, None)], {})
    p_first = state["p"]
    state = run(
        Phase([6, 1, 2], 3, 0, [0, 1, 2], [], False, False),
        state,
        [(far_own, None), (own_even, None), (own_odd, None)],
        {},
    )
    p_second = state["p"]
    state = run(
        Phase([4, 5, 7, 8, 6], 4, 3, [0, 1], [4], False, False),
        state,
        [(near_times, 0), (near_times, 1), (far_even, None), (far_odd, None), (far_own, None)],
        {4: (p_second, 0)},
    )
    p_third = state["p"]
    g_far = state["g"]
    hop_even = in_time_middle(g_far[0], 0).astype(F32)
    hop_odd = in_time_middle(g_far[1], 1).astype(F32)
    from_far = far((g_far[2].astype(F32) + hop_even + hop_odd).astype(BF16))

    state = run(
        Phase([3, 4, 5], 0, 3, [], [0, 1, 2], False, False),
        state,
        [(near_own, None), (near_times, 0), (near_times, 1)],
        {0: (p_first, 1), 1: (p_third, 0), 2: (p_third, 1)},
    )
    from_near = near(state["g"]).astype(F32)
    state = run(
        Phase([1, 2], 0, 2, [], [0, 1], False, False),
        state,
        [(own_even, None), (own_odd, None)],
        {0: (p_second, 1), 1: (p_second, 2)},
    )
    g_times = state["g"].astype(F32)
    from_even = in_time((g_times[0] + from_near[1]).astype(BF16), 0).astype(F32)
    from_odd = in_time((g_times[1] + from_near[2]).astype(BF16), 1).astype(F32)
    state = run(
        Phase([0], 0, 1, [], [0], False, True), state, [(own, None)], {0: (p_first, 0)}
    )
    total = state["g"][0].astype(F32) + from_near[0] + from_far.astype(F32) + from_even + from_odd
    grads = total.astype(BF16)
    return (
        state["out"].reshape(shape),
        state["dq_out"].reshape(shape),
        grads[0].reshape(shape),
        grads[1].reshape(shape),
    )


def solution(mesh):
    spec = P("tm", "height", None, "heads")
    return jax.shard_map(
        local, mesh=mesh, in_specs=(spec, spec, spec, spec, P()), out_specs=(spec,) * 4, check_vma=False
    )
```

```python
import functools

import jax
import jax.numpy as jnp
from jax import lax
from jax.experimental import pallas as pl
from jax.experimental.pallas import tpu as pltpu
from jax.sharding import PartitionSpec as P

HEAD_DIM = 64
PAIR = 2 * HEAD_DIM
LIMIT = 1e17
SHORT = 4
LONG = 200
SCALE = HEAD_DIM ** -0.5
BF16 = jnp.bfloat16
F32 = jnp.float32


def pairing(size, first):
    pairs = [(i, i + 1) for i in range(first, size - 1, 2)]
    return pairs + [(b, a) for a, b in pairs]


def near(array):
    return lax.ppermute(array, "height", pairing(lax.axis_size("height"), 0))


def far(array):
    return lax.ppermute(array, "height", pairing(lax.axis_size("height"), 1))


def in_time(array, first):
    return lax.ppermute(array, "tm", pairing(lax.axis_size("tm"), first))


def in_time_middle(array, first):
    heights = lax.axis_size("height")
    pairs = [
        (a * heights + h, b * heights + h)
        for a, b in pairing(lax.axis_size("tm"), first)
        for h in range(1, heights - 1)
    ]
    return lax.ppermute(array, ("tm", "height"), pairs)


def offset(kind, index):
    even = 1 - 2 * lax.rem(index, 2)
    return jnp.where(kind == 0, 0, jnp.where(kind == 1, even, -even))


def allowed(mask_ref, slot, tiles_t, tiles_h):
    time = lax.axis_index("tm")
    height = lax.axis_index("height")
    dt = offset(lax.rem(slot, 3), time)
    dh = offset(slot // 3, height)
    inside = (
        (time + dt >= 0) & (time + dt < tiles_t) & (height + dh >= 0) & (height + dh < tiles_h)
    )
    flag = mask_ref[time, height, 3 * (dt + 1) + dh + 1]
    return inside & ((slot == 0) | (flag == 1))


def choose(index, values):
    result = jnp.int32(values[-1])
    for at, value in enumerate(values[:-1]):
        result = jnp.where(index == at, value, result)
    return result


def diagonal(x):
    tokens = x.shape[1] // 2
    return jnp.concatenate([x[:HEAD_DIM, :tokens], x[HEAD_DIM:, tokens:]], axis=0)


def put_blocks(p, x, wide_ref):
    tokens = x.shape[0]
    x_t = x.T
    zero_t = jnp.zeros((HEAD_DIM, tokens), x.dtype)
    wide_ref[p, :HEAD_DIM, :tokens] = x_t[:HEAD_DIM]
    wide_ref[p, :HEAD_DIM, tokens:] = zero_t
    wide_ref[p, HEAD_DIM:, :tokens] = zero_t
    wide_ref[p, HEAD_DIM:, tokens:] = x_t[HEAD_DIM:]


def prepare_kernel(q_ref, d_ref, kv_ref, qdt_ref, copy_ref, sem):
    copy = pltpu.make_async_copy(kv_ref, copy_ref, sem)
    copy.start()
    for p in range(q_ref.shape[1] // PAIR):
        lanes = slice(p * PAIR, (p + 1) * PAIR)
        q = (q_ref[:, lanes].astype(F32) * SCALE).astype(BF16)
        put_blocks(p, q, qdt_ref.at[0])
        put_blocks(p, d_ref[:, lanes], qdt_ref.at[1])
    copy.wait()


def prepare(q, d, kv):
    tokens, features = q.shape
    vmem = pl.BlockSpec(memory_space=pltpu.VMEM)
    anywhere = pl.BlockSpec(memory_space=pl.ANY)
    return pl.pallas_call(
        prepare_kernel,
        out_shape=[
            jax.ShapeDtypeStruct((2, features // PAIR, PAIR, 2 * tokens), BF16),
            jax.ShapeDtypeStruct(kv.shape, kv.dtype),
        ],
        in_specs=[vmem, vmem, anywhere],
        out_specs=[vmem, anywhere],
        scratch_shapes=[pltpu.SemaphoreType.DMA(())],
        compiler_params=pltpu.CompilerParams(vmem_limit_bytes=8 * 1024 * 1024),
        cost_estimate=pl.CostEstimate(flops=2_000_000_000, bytes_accessed=4 * tokens * features, transcendentals=0),
    )(q, d, kv)


class Phase:
    def __init__(self, slots, forward, backward, kept, given, first, last):
        self.slots, self.forward, self.backward = slots, forward, backward
        self.kept, self.given = kept, given
        self.first, self.last = first, last
        self.finish = forward > 0 and backward > 0


def phase_kernel(phase, names_in, names_out, tiles_t, tiles_h, kv_at, p_at, *refs):
    ins = dict(zip(names_in, refs))
    outs = dict(zip(names_out, refs[len(names_in):]))
    kv, p_ref, stage, acc, sums, kv_sem, p_sem, g_sem = refs[len(names_in) + len(names_out):]
    mask_ref = ins["mask"]
    count = len(phase.slots)
    pairs = kv.shape[-1] // PAIR

    def ok(slot):
        return allowed(mask_ref, slot, tiles_t, tiles_h)

    def load_kv(i):
        name, at = kv_at[i]
        source = ins[name] if at is None else ins[name].at[at]
        return pltpu.make_async_copy(source, kv.at[i], kv_sem.at[i])

    def load_p(i):
        name, at = p_at[i]
        return pltpu.make_async_copy(ins[name].at[at], p_ref.at[i], p_sem.at[i])

    def save_p(i):
        return pltpu.make_async_copy(p_ref.at[i], outs["p"].at[phase.kept.index(i)], p_sem.at[i])

    def save_g(i):
        return pltpu.make_async_copy(stage.at[i], outs["g"].at[i], g_sem.at[i])

    def start_loads(i):
        @pl.when(ok(jnp.int32(phase.slots[i])))
        def _():
            load_kv(i).start()
            if i in phase.given:
                load_p(i).start()

    qdt = ins["qdt"]
    start_loads(0)

    if phase.forward:
        stat, m_all = outs["stat"], outs["m_all"]
        if phase.first:
            stat[0:pairs] = jnp.full((pairs, stat.shape[1]), -1e30, F32)
            stat[pairs:] = jnp.zeros((stat.shape[0] - pairs, stat.shape[1]), F32)
            acc[0] = jnp.zeros(acc.shape[1:], F32)
            m_all[...] = jnp.zeros_like(m_all)
        else:
            stat[...] = ins["stat"][...]
            m_all[...] = ins["m_all"][...]
            acc[0] = ins["acc"][...]

        def forward(i, side):
            slot = choose(i, phase.slots[: phase.forward])
            good = ok(slot)
            for j in range(min(phase.forward, count - 1)):
                @pl.when(i == j)
                def _():
                    start_loads(j + 1)

            def scores(p):
                lanes = slice(p * PAIR, (p + 1) * PAIR)
                return jnp.dot(kv[i, 0, :, lanes], qdt[0, p], preferred_element_type=F32)

            def attend(p, e):
                lanes = slice(p * PAIR, (p + 1) * PAIR)
                low = e.astype(BF16)
                p_ref[i, p] = low
                return jnp.dot(kv[i, 1, :, lanes].T, low, preferred_element_type=F32)

            @pl.when(good)
            def _():
                for j in range(phase.forward):
                    @pl.when(i == j)
                    def _():
                        load_kv(j).wait()

            @pl.when(good & (slot != 0))
            def _():
                for p in range(pairs):
                    shift = stat[p : p + 1]
                    e = jnp.exp(scores(p) - shift)
                    sums[p : p + 1] = jnp.sum(e, axis=0, keepdims=True)
                    m_all[slot, p : p + 1] = shift
                    acc[1 - side, p] = acc[side, p] + attend(p, e)

            fits = (slot != 0) & (jnp.max(sums[...]) < LIMIT)

            @pl.when(good & fits)
            def _():
                stat[pairs : 2 * pairs] = stat[pairs : 2 * pairs] + sums[...]

            @pl.when(good & jnp.logical_not(fits))
            def _():
                for p in range(pairs):
                    s = scores(p)
                    m_old = stat[p : p + 1]
                    m_new = jnp.maximum(m_old, jnp.max(s, axis=0, keepdims=True))
                    e = jnp.exp(s - m_new)
                    alpha = jnp.exp(m_old - m_new)
                    row = slice(pairs + p, pairs + p + 1)
                    stat[row] = stat[row] * alpha + jnp.sum(e, axis=0, keepdims=True)
                    stat[p : p + 1] = m_new
                    m_all[slot, p : p + 1] = m_new
                    acc[1 - side, p] = acc[side, p] * alpha + attend(p, e)

            @pl.when(good)
            def _():
                for j in phase.kept:
                    @pl.when(i == j)
                    def _():
                        save_p(j).start()

            return jnp.where(good, 1 - side, side)

        sums[...] = jnp.zeros_like(sums)
        side = lax.fori_loop(0, phase.forward, forward, jnp.int32(0))
        if not phase.finish:
            outs["acc"][...] = acc[side]
    else:
        stat, m_all = ins["stat"], ins["m_all"]

    if phase.finish:
        qdm = outs["qdm"]
        for p in range(pairs):
            inverse = 1.0 / stat[pairs + p : pairs + p + 1]
            stat[pairs + p : pairs + p + 1] = inverse
            out_t = diagonal(acc[side, p] * inverse).astype(BF16)
            outs["out"][:, p * PAIR : (p + 1) * PAIR] = out_t.T
            both = diagonal(qdt[1, p]).astype(F32) * out_t.astype(F32)
            row = slice(2 * pairs + p, 2 * pairs + p + 1)
            tokens = both.shape[1]
            stat[row, :tokens] = jnp.sum(both[:HEAD_DIM], axis=0, keepdims=True)
            stat[row, tokens:] = jnp.sum(both[HEAD_DIM:], axis=0, keepdims=True)
            for x in range(2):
                qdm[x, p] = (qdt[x, p].astype(F32) * inverse).astype(BF16).T
    elif phase.backward:
        qdm = ins["qdm"]

    if phase.backward:
        dq = outs["dq"]
        base = count - phase.backward
        if phase.finish:
            dq[...] = jnp.zeros_like(dq)
        else:
            dq[...] = ins["dq"][...]

        def backward(step, carry):
            i = base + step
            slot = choose(step, phase.slots[base:])
            good = ok(slot)
            for j in range(base, count - 1):
                @pl.when(i == j)
                def _():
                    start_loads(j + 1)

            @pl.when(jnp.logical_not(good))
            def _():
                stage[step] = jnp.zeros(stage.shape[1:], stage.dtype)

            @pl.when(good)
            def _():
                for j in range(base, count):
                    @pl.when(i == j)
                    def _():
                        if j >= phase.forward:
                            load_kv(j).wait()
                        if j in phase.given:
                            load_p(j).wait()

            @pl.when(good & (jnp.max(stat[0:pairs] - m_all[slot]) > 0.0))
            def _():
                for p in range(pairs):
                    gamma = jnp.exp(m_all[slot, p : p + 1] - stat[p : p + 1])
                    p_ref[i, p] = p_ref[i, p] * gamma.astype(BF16)

            @pl.when(good)
            def _():
                for p in range(pairs):
                    lanes = slice(p * PAIR, (p + 1) * PAIR)
                    w = p_ref[i, p]
                    dp = jnp.dot(kv[i, 1, :, lanes], qdt[1, p], preferred_element_type=F32)
                    ds = w * (dp - stat[2 * pairs + p : 2 * pairs + p + 1]).astype(BF16)
                    dv = jnp.dot(w, qdm[1, p], preferred_element_type=F32)
                    dk = jnp.dot(ds, qdm[0, p], preferred_element_type=F32)
                    stage[step, 0, :, lanes] = dk.astype(stage.dtype)
                    stage[step, 1, :, lanes] = dv.astype(stage.dtype)
                    k_t = kv[i, 0, :, lanes].T
                    dq[p] += jnp.dot(k_t, ds, preferred_element_type=F32)

            for j in range(phase.backward):
                @pl.when(step == j)
                def _():
                    save_g(j).start()

            return carry

        lax.fori_loop(0, phase.backward, backward, 0)
        if phase.last:
            for p in range(pairs):
                inverse = stat[pairs + p : pairs + p + 1] * SCALE
                dq_t = diagonal(dq[p] * inverse).astype(BF16)
                outs["dq_out"][:, p * PAIR : (p + 1) * PAIR] = dq_t.T
        for j in range(phase.backward):
            save_g(j).wait()

    for j in phase.kept:
        @pl.when(ok(jnp.int32(phase.slots[j])))
        def _():
            save_p(j).wait()


def run_phase(phase, state, kvs, ps, tiles_t, tiles_h, work=SHORT, after=()):
    _, pairs, _, wide = state["qdt"].shape
    tokens, features = wide // 2, pairs * PAIR
    count = len(phase.slots)
    vmem = pl.BlockSpec(memory_space=pltpu.VMEM)
    anywhere = pl.BlockSpec(memory_space=pl.ANY)
    shapes = {
        "qdt": ((2, pairs, PAIR, wide), BF16),
        "qdm": ((2, pairs, wide, PAIR), BF16),
        "stat": ((3 * pairs, wide), F32),
        "m_all": ((9, pairs, wide), F32),
        "acc": ((pairs, PAIR, wide), F32),
        "dq": ((pairs, PAIR, wide), F32),
        "out": ((tokens, features), BF16),
        "dq_out": ((tokens, features), BF16),
        "p": ((len(phase.kept), pairs, tokens, wide), BF16),
        "g": ((phase.backward, 2, tokens, features), BF16),
    }
    names_in = ["mask", "qdt"]
    names_out = []
    if not phase.first:
        names_in += ["stat", "m_all"]
    if phase.forward:
        names_out += ["stat", "m_all"]
        if not phase.first:
            names_in += ["acc"]
        if not phase.finish:
            names_out += ["acc"]
    if phase.finish:
        names_out += ["out", "qdm"]
    if phase.backward:
        if not phase.finish:
            names_in += ["dq", "qdm"]
        names_out += ["dq", "g"]
    if phase.last:
        names_out += ["dq_out"]
    if phase.kept:
        names_out += ["p"]
    inputs = {name: state[name] for name in names_in}
    specs = [pl.BlockSpec(memory_space=pltpu.SMEM)] + [vmem] * (len(names_in) - 1)
    seen = {}

    def reference_to(array):
        if id(array) not in seen:
            seen[id(array)] = "big%d" % len(seen)
            inputs[seen[id(array)]] = array
            specs.append(anywhere)
        return seen[id(array)]

    for array in after:
        reference_to(array)
    kv_at = [(reference_to(array), at) for array, at in kvs]
    p_at = {i: (reference_to(array), at) for i, (array, at) in ps.items()}
    unit = 2 * tokens * tokens * features
    results = pl.pallas_call(
        functools.partial(
            phase_kernel, phase, list(inputs), names_out, tiles_t, tiles_h, kv_at, p_at
        ),
        out_shape=[jax.ShapeDtypeStruct(*shapes[name]) for name in names_out],
        in_specs=specs,
        out_specs=[anywhere if name in ("p", "g") else vmem for name in names_out],
        scratch_shapes=[
            pltpu.VMEM((count, 2, tokens, features), BF16),
            pltpu.VMEM((count, pairs, tokens, wide), BF16),
            pltpu.VMEM((max(phase.backward, 1), 2, tokens, features), BF16),
            pltpu.VMEM((2, pairs, PAIR, wide) if phase.forward else (1, 1, 8, PAIR), F32),
            pltpu.VMEM((pairs, wide), F32),
            pltpu.SemaphoreType.DMA((count,)),
            pltpu.SemaphoreType.DMA((count,)),
            pltpu.SemaphoreType.DMA((max(phase.backward, 1),)),
        ],
        compiler_params=pltpu.CompilerParams(vmem_limit_bytes=(10 + 3 * count) * 1024 * 1024),
        cost_estimate=pl.CostEstimate(
            flops=work * unit * (phase.forward + 2 * phase.backward),
            bytes_accessed=2 * unit // tokens * count,
            transcendentals=0,
        ),
    )(*inputs.values())
    state.update(zip(names_out, results))
    return state


def local(queries, key_tokens, value_tokens, cotangent, window_mask):
    shape = queries.shape
    features = shape[-1]
    tiles_t, tiles_h = lax.axis_size("tm"), lax.axis_size("height")
    run = functools.partial(run_phase, tiles_t=tiles_t, tiles_h=tiles_h)
    own = jnp.stack([key_tokens.reshape(-1, features), value_tokens.reshape(-1, features)])
    far_own = far(own)
    near_own = near(own)
    qdt, own = prepare(queries.reshape(-1, features), cotangent.reshape(-1, features), own)
    state = {"mask": window_mask, "qdt": qdt}
    own_even = in_time(own, 0)
    own_odd = in_time(own, 1)
    far_even = in_time_middle(far_own, 0)
    far_odd = in_time_middle(far_own, 1)

    state = run(
        Phase([0, 3, 6], 3, 0, [0, 1, 2], [], True, False),
        state,
        [(own, None), (near_own, None), (far_own, None)],
        {},
        work=LONG,
    )
    p_first = state["p"]
    state["acc"], own_even, own_odd = lax.optimization_barrier((state["acc"], own_even, own_odd))
    near_times = near(jnp.stack([own_even, own_odd]))
    state = run(
        Phase([1, 2, 7, 8], 4, 0, [0, 1, 2, 3], [], False, False),
        state,
        [(own_even, None), (own_odd, None), (far_even, None), (far_odd, None)],
        {},
        work=LONG,
    )
    p_second = state["p"]
    state = run(
        Phase([4, 5, 7, 8, 6], 2, 3, [0, 1], [2, 3, 4], False, False),
        state,
        [(near_times, 0), (near_times, 1), (far_even, None), (far_odd, None), (far_own, None)],
        {2: (p_second, 2), 3: (p_second, 3), 4: (p_first, 2)},
    )
    p_third = state["p"]
    g_far = state["g"]
    hop_even = in_time_middle(g_far[0], 0)
    hop_odd = in_time_middle(g_far[1], 1)
    from_far = far((g_far[2].astype(F32) + hop_even.astype(F32) + hop_odd.astype(F32)).astype(BF16))

    state = run(
        Phase([3, 4, 5], 0, 3, [], [0, 1, 2], False, False),
        state,
        [(near_own, None), (near_times, 0), (near_times, 1)],
        {0: (p_first, 1), 1: (p_third, 0), 2: (p_third, 1)},
    )
    from_near = near(state["g"]).astype(F32)
    state = run(
        Phase([1, 2], 0, 2, [], [0, 1], False, False),
        state,
        [(own_even, None), (own_odd, None)],
        {0: (p_second, 0), 1: (p_second, 1)},
        work=LONG,
        after=(hop_even, hop_odd),
    )
    g_times = state["g"].astype(F32)
    from_even = in_time((g_times[0] + from_near[1]).astype(BF16), 0).astype(F32)
    from_odd = in_time((g_times[1] + from_near[2]).astype(BF16), 1).astype(F32)
    state = run(
        Phase([0], 0, 1, [], [0], False, True), state, [(own, None)], {0: (p_first, 0)}
    )
    total = state["g"][0].astype(F32) + from_near[0] + from_far.astype(F32) + from_even + from_odd
    grads = total.astype(BF16)
    return (
        state["out"].reshape(shape),
        state["dq_out"].reshape(shape),
        grads[0].reshape(shape),
        grads[1].reshape(shape),
    )


def solution(mesh):
    spec = P("tm", "height", None, "heads")
    return jax.shard_map(
        local, mesh=mesh, in_specs=(spec, spec, spec, spec, P()), out_specs=(spec,) * 4, check_vma=False
    )
```

```python
import functools

import jax
import jax.numpy as jnp
from jax import lax
from jax.experimental import pallas as pl
from jax.experimental.pallas import tpu as pltpu
from jax.sharding import PartitionSpec as P

HEAD_DIM = 64
PAIR = 2 * HEAD_DIM
LIMIT = 1e17
LIMIT_VMEM = 24 * 1024 * 1024
SHORT = 4
LONG = 200
SCALE = HEAD_DIM ** -0.5
BF16 = jnp.bfloat16
F32 = jnp.float32


def pairing(size, first):
    pairs = [(i, i + 1) for i in range(first, size - 1, 2)]
    return pairs + [(b, a) for a, b in pairs]


def near(array):
    return lax.ppermute(array, "height", pairing(lax.axis_size("height"), 0))


def far(array):
    return lax.ppermute(array, "height", pairing(lax.axis_size("height"), 1))


def in_time(array, first):
    return lax.ppermute(array, "tm", pairing(lax.axis_size("tm"), first))


def in_time_middle(array, first):
    heights = lax.axis_size("height")
    pairs = [
        (a * heights + h, b * heights + h)
        for a, b in pairing(lax.axis_size("tm"), first)
        for h in range(1, heights - 1)
    ]
    return lax.ppermute(array, ("tm", "height"), pairs)


def offset(kind, index):
    even = 1 - 2 * lax.rem(index, 2)
    return jnp.where(kind == 0, 0, jnp.where(kind == 1, even, -even))


def allowed(mask_ref, slot, tiles_t, tiles_h):
    time = lax.axis_index("tm")
    height = lax.axis_index("height")
    dt = offset(lax.rem(slot, 3), time)
    dh = offset(slot // 3, height)
    inside = (
        (time + dt >= 0) & (time + dt < tiles_t) & (height + dh >= 0) & (height + dh < tiles_h)
    )
    flag = mask_ref[time, height, 3 * (dt + 1) + dh + 1]
    return inside & ((slot == 0) | (flag == 1))


def choose(index, values):
    result = jnp.int32(values[-1])
    for at, value in enumerate(values[:-1]):
        result = jnp.where(index == at, value, result)
    return result


def diagonal(x):
    tokens = x.shape[1] // 2
    return jnp.concatenate([x[:HEAD_DIM, :tokens], x[HEAD_DIM:, tokens:]], axis=0)


def put_blocks(p, x, wide_ref):
    tokens = x.shape[0]
    x_t = x.T
    zero_t = jnp.zeros((HEAD_DIM, tokens), x.dtype)
    wide_ref[p, :HEAD_DIM, :tokens] = x_t[:HEAD_DIM]
    wide_ref[p, :HEAD_DIM, tokens:] = zero_t
    wide_ref[p, HEAD_DIM:, :tokens] = zero_t
    wide_ref[p, HEAD_DIM:, tokens:] = x_t[HEAD_DIM:]


def prepare_kernel(q_ref, d_ref, kv_ref, qdt_ref, copy_ref, sem):
    copy = pltpu.make_async_copy(kv_ref, copy_ref, sem)
    copy.start()
    for p in range(q_ref.shape[1] // PAIR):
        lanes = slice(p * PAIR, (p + 1) * PAIR)
        q = (q_ref[:, lanes].astype(F32) * SCALE).astype(BF16)
        put_blocks(p, q, qdt_ref.at[0])
        put_blocks(p, d_ref[:, lanes], qdt_ref.at[1])
    copy.wait()


def prepare(q, d, kv):
    tokens, features = q.shape
    vmem = pl.BlockSpec(memory_space=pltpu.VMEM)
    anywhere = pl.BlockSpec(memory_space=pl.ANY)
    return pl.pallas_call(
        prepare_kernel,
        out_shape=[
            jax.ShapeDtypeStruct((2, features // PAIR, PAIR, 2 * tokens), BF16),
            jax.ShapeDtypeStruct(kv.shape, kv.dtype),
        ],
        in_specs=[vmem, vmem, anywhere],
        out_specs=[vmem, anywhere],
        scratch_shapes=[pltpu.SemaphoreType.DMA(())],
        compiler_params=pltpu.CompilerParams(vmem_limit_bytes=8 * 1024 * 1024),
        cost_estimate=pl.CostEstimate(flops=2_000_000_000, bytes_accessed=4 * tokens * features, transcendentals=0),
    )(q, d, kv)


FLAGS = 16
RARE = 9


def gather_kernel(k_ref, v_ref, out_ref, sem):
    copies = [pltpu.make_async_copy(ref, out_ref.at[i], sem.at[i]) for i, ref in enumerate((k_ref, v_ref))]
    for copy in copies:
        copy.start()
    for copy in copies:
        copy.wait()


def gather(k, v):
    anywhere = pl.BlockSpec(memory_space=pl.ANY)
    return pl.pallas_call(
        gather_kernel,
        out_shape=jax.ShapeDtypeStruct((2,) + k.shape, k.dtype),
        in_specs=[anywhere, anywhere],
        out_specs=anywhere,
        scratch_shapes=[pltpu.SemaphoreType.DMA((2,))],
        compiler_params=pltpu.CompilerParams(vmem_limit_bytes=4 * 1024 * 1024),
    )(k, v)


def sum_kernel(terms, *refs):
    outs = refs[len(refs) - len(terms):]
    for out, parts in zip(outs, terms):
        total = None
        for operand, at in parts:
            value = (refs[operand] if at is None else refs[operand].at[at])[...].astype(F32)
            total = value if total is None else total + value
        out[...] = total.astype(out.dtype)


def sums_of(operands, terms, shape):
    vmem = pl.BlockSpec(memory_space=pltpu.VMEM)
    return pl.pallas_call(
        functools.partial(sum_kernel, terms),
        out_shape=[jax.ShapeDtypeStruct(shape, BF16)] * len(terms),
        in_specs=[vmem] * len(operands),
        out_specs=[vmem] * len(terms),
        compiler_params=pltpu.CompilerParams(vmem_limit_bytes=8 * 1024 * 1024),
        cost_estimate=pl.CostEstimate(flops=1000, bytes_accessed=1_000_000, transcendentals=0),
    )(*operands)


class Phase:
    def __init__(self, forward=(), backward=(), first=False, last=False):
        self.forward = list(forward)
        self.segments = list(backward)
        self.backward = [slot for slots, _ in backward for slot in slots]
        self.first, self.last = first, last
        self.finish = bool(forward) and bool(backward)
        self.slots = self.forward + [slot for slot in self.backward if slot not in self.forward]


def phase_kernel(phase, names_in, names_out, tiles_t, tiles_h, kv_at, *refs):
    ins = dict(zip(names_in, refs))
    outs = dict(zip(names_out, refs[len(names_in):]))
    kv, acc, sums, kv_sem = refs[len(names_in) + len(names_out):]
    count = len(phase.slots)
    pairs = kv.shape[-1] // PAIR

    if phase.forward:
        flags = outs["flags"]
        for slot in range(FLAGS):
            if not phase.first:
                flags[slot] = ins["flags"][slot]
            elif slot < 9:
                flags[slot] = allowed(ins["mask"], jnp.int32(slot), tiles_t, tiles_h).astype(jnp.int32)
            else:
                flags[slot] = 0
    else:
        flags = ins["flags"]

    def ok(slot):
        return flags[slot] != 0

    def load_kv(i):
        name, at = kv_at[i]
        source = ins[name] if at is None else ins[name].at[at]
        return pltpu.make_async_copy(source, kv.at[i], kv_sem.at[i])

    def start_load(i):
        if i < count:
            @pl.when(ok(phase.slots[i]))
            def _():
                load_kv(i).start()

    def wait_load(i):
        load_kv(i).wait()

    qdt = ins["qdt"]
    start_load(0)
    start_load(1)

    if phase.forward:
        stat, m_all, p_out = outs["stat"], outs["m_all"], outs["p"]
        if phase.first:
            stat[0:pairs] = jnp.full((pairs, stat.shape[1]), -1e30, F32)
            stat[pairs:] = jnp.zeros((stat.shape[0] - pairs, stat.shape[1]), F32)
            acc[0] = jnp.zeros(acc.shape[1:], F32)
            m_all[...] = jnp.zeros_like(m_all)
        else:
            stat[...] = ins["stat"][...]
            m_all[...] = ins["m_all"][...]
            acc[0] = ins["acc"][...]

        def forward(i, side):
            slot = choose(i, phase.forward)
            good = ok(slot)

            def scores(p):
                lanes = slice(p * PAIR, (p + 1) * PAIR)
                return jnp.dot(kv[i, 0, :, lanes], qdt[0, p], preferred_element_type=F32)

            def attend(p, e):
                lanes = slice(p * PAIR, (p + 1) * PAIR)
                low = e.astype(BF16)
                p_out[i, p] = low
                return jnp.dot(kv[i, 1, :, lanes].T, low, preferred_element_type=F32)

            for j in range(len(phase.forward)):
                @pl.when(i == j)
                def _():
                    start_load(j + 2)

                @pl.when(good & (i == j))
                def _():
                    wait_load(j)

            def exact():
                for p in range(pairs):
                    s = scores(p)
                    m_old = stat[p : p + 1]
                    m_new = jnp.maximum(m_old, jnp.max(s, axis=0, keepdims=True))
                    e = jnp.exp(s - m_new)
                    alpha = jnp.exp(m_old - m_new)
                    row = slice(pairs + p, pairs + p + 1)
                    stat[row] = stat[row] * alpha + jnp.sum(e, axis=0, keepdims=True)
                    stat[p : p + 1] = m_new
                    m_all[slot, p : p + 1] = m_new
                    acc[1 - side, p] = acc[side, p] * alpha + attend(p, e)

            @pl.when(good & (slot != 0))
            def _():
                for p in range(pairs):
                    shift = stat[p : p + 1]
                    e = jnp.exp(scores(p) - shift)
                    sums[p : p + 1] = jnp.sum(e, axis=0, keepdims=True)
                    m_all[slot, p : p + 1] = shift
                    acc[1 - side, p] = acc[side, p] + attend(p, e)

                fits = jnp.max(sums[...]) < LIMIT

                @pl.when(fits)
                def _():
                    stat[pairs : 2 * pairs] = stat[pairs : 2 * pairs] + sums[...]

                @pl.when(jnp.logical_not(fits))
                def _():
                    flags[RARE] = 1
                    exact()

            if 0 in phase.forward:
                @pl.when(slot == 0)
                def _():
                    exact()

            return jnp.where(good, 1 - side, side)

        side = lax.fori_loop(0, len(phase.forward), forward, jnp.int32(0))
        if not phase.finish:
            outs["acc"][...] = acc[side]
    else:
        stat, m_all = ins["stat"], ins["m_all"]

    if phase.finish:
        qdm = outs["qdm"]
        for p in range(pairs):
            inverse = 1.0 / stat[pairs + p : pairs + p + 1]
            stat[pairs + p : pairs + p + 1] = inverse
            out_t = diagonal(acc[side, p] * inverse).astype(BF16)
            outs["out"][:, p * PAIR : (p + 1) * PAIR] = out_t.T
            both = diagonal(qdt[1, p]).astype(F32) * out_t.astype(F32)
            row = slice(2 * pairs + p, 2 * pairs + p + 1)
            tokens = both.shape[1]
            stat[row, :tokens] = jnp.sum(both[:HEAD_DIM], axis=0, keepdims=True)
            stat[row, tokens:] = jnp.sum(both[HEAD_DIM:], axis=0, keepdims=True)
            for x in range(2):
                qdm[x, p] = (qdt[x, p].astype(F32) * inverse).astype(BF16).T
    elif phase.backward:
        qdm = ins["qdm"]

    if phase.backward:
        dq, g = outs["dq"], outs["g"]
        if phase.finish:
            dq[...] = jnp.zeros_like(dq)
        else:
            dq[...] = ins["dq"][...]
        done = 0
        for number, (slots, places) in enumerate(phase.segments):
            p_in = ins["p%d" % number]
            base = done
            done += len(slots)
            where = [phase.slots.index(slot) for slot in slots]
            loading = len(phase.forward)

            def backward(step, carry):
                slot = choose(step, slots)
                place = choose(step, places)
                i = choose(step, where)
                good = ok(slot)
                for j in range(len(slots)):
                    if where[j] >= loading:
                        @pl.when(step == j)
                        def _():
                            start_load(where[j] + 2)

                        @pl.when(good & (step == j))
                        def _():
                            wait_load(where[j])

                @pl.when(jnp.logical_not(good))
                def _():
                    g[base + step] = jnp.zeros(g.shape[1:], g.dtype)

                def terms(moved):
                    for p in range(pairs):
                        lanes = slice(p * PAIR, (p + 1) * PAIR)
                        w = p_in[place, p]
                        if moved:
                            gamma = jnp.exp(m_all[slot, p : p + 1] - stat[p : p + 1])
                            w = w * gamma.astype(BF16)
                        dp = jnp.dot(kv[i, 1, :, lanes], qdt[1, p], preferred_element_type=F32)
                        ds = w * (dp - stat[2 * pairs + p : 2 * pairs + p + 1]).astype(BF16)
                        dv = jnp.dot(w, qdm[1, p], preferred_element_type=F32)
                        dk = jnp.dot(ds, qdm[0, p], preferred_element_type=F32)
                        g[base + step, 0, :, lanes] = dk.astype(g.dtype)
                        g[base + step, 1, :, lanes] = dv.astype(g.dtype)
                        k_t = kv[i, 0, :, lanes].T
                        dq[p] += jnp.dot(k_t, ds, preferred_element_type=F32)

                moved = flags[RARE] != 0

                @pl.when(good & jnp.logical_not(moved))
                def _():
                    terms(False)

                @pl.when(good & moved)
                def _():
                    terms(True)

                return carry

            lax.fori_loop(0, len(slots), backward, 0)
        if phase.last:
            for p in range(pairs):
                inverse = stat[pairs + p : pairs + p + 1] * SCALE
                dq_t = diagonal(dq[p] * inverse).astype(BF16)
                outs["dq_out"][:, p * PAIR : (p + 1) * PAIR] = dq_t.T


def run_phase(phase, state, kvs, ps, tiles_t, tiles_h, work=SHORT, after=()):
    _, pairs, _, wide = state["qdt"].shape
    tokens, features = wide // 2, pairs * PAIR
    count = len(phase.slots)
    vmem = pl.BlockSpec(memory_space=pltpu.VMEM)
    smem = pl.BlockSpec(memory_space=pltpu.SMEM)
    anywhere = pl.BlockSpec(memory_space=pl.ANY)
    shapes = {
        "flags": ((FLAGS,), jnp.int32),
        "qdm": ((2, pairs, wide, PAIR), BF16),
        "stat": ((3 * pairs, wide), F32),
        "m_all": ((9, pairs, wide), F32),
        "acc": ((pairs, PAIR, wide), F32),
        "dq": ((pairs, PAIR, wide), F32),
        "out": ((tokens, features), BF16),
        "dq_out": ((tokens, features), BF16),
        "p": ((len(phase.forward), pairs, tokens, wide), BF16),
        "g": ((len(phase.backward), 2, tokens, features), BF16),
    }
    names_in = ["qdt"]
    names_out = []
    if phase.first:
        names_in += ["mask"]
    else:
        names_in += ["flags", "stat", "m_all"]
    if phase.forward:
        names_out += ["flags", "stat", "m_all", "p"]
        if not phase.first:
            names_in += ["acc"]
        if not phase.finish:
            names_out += ["acc"]
    if phase.finish:
        names_out += ["out", "qdm"]
    if phase.backward:
        if not phase.finish:
            names_in += ["dq", "qdm"]
        names_out += ["dq", "g"]
    if phase.last:
        names_out += ["dq_out"]
    inputs = {name: state[name] for name in names_in}
    specs = [smem if name in ("flags", "mask") else vmem for name in names_in]
    for number, array in enumerate(ps):
        inputs["p%d" % number] = array
        specs.append(vmem)
    seen = {}

    def reference_to(array):
        if id(array) not in seen:
            seen[id(array)] = "big%d" % len(seen)
            inputs[seen[id(array)]] = array
            specs.append(anywhere)
        return seen[id(array)]

    for array in after:
        reference_to(array)
    kv_at = [(reference_to(array), at) for array, at in kvs]
    unit = 2 * tokens * tokens * features
    results = pl.pallas_call(
        functools.partial(
            phase_kernel, phase, list(inputs), names_out, tiles_t, tiles_h, kv_at
        ),
        out_shape=[jax.ShapeDtypeStruct(*shapes[name]) for name in names_out],
        in_specs=specs,
        out_specs=[smem if name == "flags" else vmem for name in names_out],
        scratch_shapes=[
            pltpu.VMEM((count, 2, tokens, features), BF16),
            pltpu.VMEM((2, pairs, PAIR, wide) if phase.forward else (1, 1, 8, PAIR), F32),
            pltpu.VMEM((pairs, wide), F32),
            pltpu.SemaphoreType.DMA((count,)),
        ],
        compiler_params=pltpu.CompilerParams(vmem_limit_bytes=LIMIT_VMEM),
        cost_estimate=pl.CostEstimate(
            flops=work * unit * (len(phase.forward) + 2 * len(phase.backward)),
            bytes_accessed=2 * unit // tokens * count,
            transcendentals=0,
        ),
    )(*inputs.values())
    state.update(zip(names_out, results))
    return state


def local(queries, key_tokens, value_tokens, cotangent, window_mask):
    shape = queries.shape
    features = shape[-1]
    tiles_t, tiles_h = lax.axis_size("tm"), lax.axis_size("height")
    run = functools.partial(run_phase, tiles_t=tiles_t, tiles_h=tiles_h)
    own = gather(key_tokens.reshape(-1, features), value_tokens.reshape(-1, features))
    far_own = far(own)
    near_own = near(own)
    qdt, own = prepare(queries.reshape(-1, features), cotangent.reshape(-1, features), own)
    state = {"mask": window_mask, "qdt": qdt}
    own_even = in_time(own, 0)
    own_odd = in_time(own, 1)
    far_even = in_time_middle(far_own, 0)
    far_odd = in_time_middle(far_own, 1)

    state = run(
        Phase(forward=[0, 3, 6], first=True),
        state,
        [(own, None), (near_own, None), (far_own, None)],
        [],
        work=LONG,
    )
    p_first = state["p"]
    state["acc"], own_even, own_odd = lax.optimization_barrier((state["acc"], own_even, own_odd))
    near_times = near(jnp.stack([own_even, own_odd]))
    state = run(
        Phase(forward=[1, 2, 7, 8]),
        state,
        [(own_even, None), (own_odd, None), (far_even, None), (far_odd, None)],
        [],
        work=LONG,
    )
    p_second = state["p"]
    state = run(
        Phase(forward=[4, 5], backward=[([7, 8], [2, 3]), ([6], [2])]),
        state,
        [(near_times, 0), (near_times, 1), (far_even, None), (far_odd, None), (far_own, None)],
        [p_second, p_first],
    )
    p_third = state["p"]
    g_far = state["g"]
    hop_even = in_time_middle(g_far[0], 0)
    hop_odd = in_time_middle(g_far[1], 1)
    (to_far,) = sums_of([g_far, hop_even, hop_odd], [[(0, 2), (1, None), (2, None)]], own.shape)
    from_far = far(to_far)

    state = run(
        Phase(backward=[([3], [1]), ([4, 5], [0, 1])]),
        state,
        [(near_own, None), (near_times, 0), (near_times, 1)],
        [p_first, p_third],
    )
    from_near = near(state["g"])
    state = run(
        Phase(backward=[([1, 2], [0, 1])]),
        state,
        [(own_even, None), (own_odd, None)],
        [p_second],
        work=LONG,
        after=(hop_even, hop_odd),
    )
    to_even, to_odd = sums_of([state["g"], from_near], [[(0, 0), (1, 1)], [(0, 1), (1, 2)]], own.shape)
    from_even = in_time(to_even, 0)
    from_odd = in_time(to_odd, 1)
    state = run(
        Phase(backward=[([0], [0])], last=True), state, [(own, None)], [p_first]
    )
    key_grad, value_grad = sums_of(
        [state["g"], from_near, from_far, from_even, from_odd],
        [[(0, (0, x)), (1, (0, x))] + [(i, x) for i in (2, 3, 4)] for x in range(2)],
        own.shape[1:],
    )
    return (
        state["out"].reshape(shape),
        state["dq_out"].reshape(shape),
        key_grad.reshape(shape),
        value_grad.reshape(shape),
    )


def solution(mesh):
    spec = P("tm", "height", None, "heads")
    return jax.shard_map(
        local, mesh=mesh, in_specs=(spec, spec, spec, spec, P()), out_specs=(spec,) * 4, check_vma=False
    )
```

```python
import functools

import jax
import jax.numpy as jnp
from jax import lax
from jax.experimental import pallas as pl
from jax.experimental.pallas import tpu as pltpu
from jax.sharding import PartitionSpec as P

HEAD_DIM = 64
PAIR = 2 * HEAD_DIM
LIMIT = 1e17
LIMIT_VMEM = 24 * 1024 * 1024
COST = 1.15e9
COSTS = (50, 2, 4, 50, 1, 1, 50, 1)
SCALE = HEAD_DIM ** -0.5
BF16 = jnp.bfloat16
F32 = jnp.float32


def pairing(size, first):
    pairs = [(i, i + 1) for i in range(first, size - 1, 2)]
    return pairs + [(b, a) for a, b in pairs]


def near(array):
    return lax.ppermute(array, "height", pairing(lax.axis_size("height"), 0))


def far(array):
    return lax.ppermute(array, "height", pairing(lax.axis_size("height"), 1))


def in_time(array, first):
    return lax.ppermute(array, "tm", pairing(lax.axis_size("tm"), first))


def in_time_middle(array, first):
    heights = lax.axis_size("height")
    pairs = [
        (a * heights + h, b * heights + h)
        for a, b in pairing(lax.axis_size("tm"), first)
        for h in range(1, heights - 1)
    ]
    return lax.ppermute(array, ("tm", "height"), pairs)


def offset(kind, index):
    even = 1 - 2 * lax.rem(index, 2)
    return jnp.where(kind == 0, 0, jnp.where(kind == 1, even, -even))


def allowed(mask_ref, slot, tiles_t, tiles_h):
    time = lax.axis_index("tm")
    height = lax.axis_index("height")
    dt = offset(lax.rem(slot, 3), time)
    dh = offset(slot // 3, height)
    inside = (
        (time + dt >= 0) & (time + dt < tiles_t) & (height + dh >= 0) & (height + dh < tiles_h)
    )
    flag = mask_ref[time, height, 3 * (dt + 1) + dh + 1]
    return inside & ((slot == 0) | (flag == 1))


def choose(index, values):
    result = jnp.int32(values[-1])
    for at, value in enumerate(values[:-1]):
        result = jnp.where(index == at, value, result)
    return result


def diagonal(x):
    tokens = x.shape[1] // 2
    return jnp.concatenate([x[:HEAD_DIM, :tokens], x[HEAD_DIM:, tokens:]], axis=0)


def put_blocks(p, x, wide_ref):
    tokens = x.shape[0]
    x_t = x.T
    zero_t = jnp.zeros((HEAD_DIM, tokens), x.dtype)
    wide_ref[p, :HEAD_DIM, :tokens] = x_t[:HEAD_DIM]
    wide_ref[p, :HEAD_DIM, tokens:] = zero_t
    wide_ref[p, HEAD_DIM:, :tokens] = zero_t
    wide_ref[p, HEAD_DIM:, tokens:] = x_t[HEAD_DIM:]


def prepare_kernel(q_ref, d_ref, kv_ref, qdt_ref, copy_ref, sem):
    copy = pltpu.make_async_copy(kv_ref, copy_ref, sem)
    copy.start()
    for p in range(q_ref.shape[1] // PAIR):
        lanes = slice(p * PAIR, (p + 1) * PAIR)
        q = (q_ref[:, lanes].astype(F32) * SCALE).astype(BF16)
        put_blocks(p, q, qdt_ref.at[0])
        put_blocks(p, d_ref[:, lanes], qdt_ref.at[1])
    copy.wait()


def prepare(q, d, kv):
    tokens, features = q.shape
    vmem = pl.BlockSpec(memory_space=pltpu.VMEM)
    anywhere = pl.BlockSpec(memory_space=pl.ANY)
    return pl.pallas_call(
        prepare_kernel,
        out_shape=[
            jax.ShapeDtypeStruct((2, features // PAIR, PAIR, 2 * tokens), BF16),
            jax.ShapeDtypeStruct(kv.shape, kv.dtype),
        ],
        in_specs=[vmem, vmem, anywhere],
        out_specs=[vmem, anywhere],
        scratch_shapes=[pltpu.SemaphoreType.DMA(())],
        compiler_params=pltpu.CompilerParams(vmem_limit_bytes=8 * 1024 * 1024),
        cost_estimate=pl.CostEstimate(flops=2_000_000_000, bytes_accessed=4 * tokens * features, transcendentals=0),
    )(q, d, kv)


FLAGS = 16
RARE = 9


def sum_kernel(terms, *refs):
    outs = refs[len(refs) - len(terms):]
    for out, parts in zip(outs, terms):
        total = None
        for operand, at in parts:
            value = (refs[operand] if at is None else refs[operand].at[at])[...].astype(F32)
            total = value if total is None else total + value
        out[...] = total.astype(out.dtype)


def sums_of(operands, terms, shape):
    vmem = pl.BlockSpec(memory_space=pltpu.VMEM)
    return pl.pallas_call(
        functools.partial(sum_kernel, terms),
        out_shape=[jax.ShapeDtypeStruct(shape, BF16)] * len(terms),
        in_specs=[vmem] * len(operands),
        out_specs=[vmem] * len(terms),
        compiler_params=pltpu.CompilerParams(vmem_limit_bytes=8 * 1024 * 1024),
        cost_estimate=pl.CostEstimate(flops=1000, bytes_accessed=1_000_000, transcendentals=0),
    )(*operands)


class Phase:
    def __init__(self, forward=(), backward=(), first=False, last=False):
        self.forward = list(forward)
        self.segments = list(backward)
        self.backward = [slot for slots, _, _ in backward for slot in slots]
        self.sizes = {}
        self.bases = []
        for slots, _, name in backward:
            self.bases.append(self.sizes.get(name, 0))
            self.sizes[name] = self.bases[-1] + len(slots)
        self.first, self.last = first, last
        self.finish = bool(forward) and bool(backward)
        self.slots = self.forward + [slot for slot in self.backward if slot not in self.forward]


def phase_kernel(phase, names_in, names_out, tiles_t, tiles_h, kv_at, *refs):
    ins = dict(zip(names_in, refs))
    outs = dict(zip(names_out, refs[len(names_in):]))
    kv, acc, sums, kv_sem = refs[len(names_in) + len(names_out):]
    count = len(phase.slots)
    pairs = kv.shape[-1] // PAIR

    if phase.forward:
        flags = outs["flags"]
        for slot in range(FLAGS):
            if not phase.first:
                flags[slot] = ins["flags"][slot]
            elif slot < 9:
                flags[slot] = allowed(ins["mask"], jnp.int32(slot), tiles_t, tiles_h).astype(jnp.int32)
            else:
                flags[slot] = 0
    else:
        flags = ins["flags"]

    def ok(slot):
        return flags[slot] != 0

    def load_kv(i):
        name, at = kv_at[i]
        source = ins[name] if at is None else ins[name].at[at]
        return pltpu.make_async_copy(source, kv.at[i], kv_sem.at[i])

    def start_load(i):
        if i < count:
            @pl.when(ok(phase.slots[i]))
            def _():
                load_kv(i).start()

    def wait_load(i):
        load_kv(i).wait()

    qdt = ins["qdt"]
    start_load(0)
    start_load(1)

    if phase.forward:
        stat, m_all, p_out = outs["stat"], outs["m_all"], outs["p"]
        if phase.first:
            stat[0:pairs] = jnp.full((pairs, stat.shape[1]), -1e30, F32)
            stat[pairs:] = jnp.zeros((stat.shape[0] - pairs, stat.shape[1]), F32)
            acc[0] = jnp.zeros(acc.shape[1:], F32)
            m_all[...] = jnp.zeros_like(m_all)
        else:
            stat[...] = ins["stat"][...]
            m_all[...] = ins["m_all"][...]
            acc[0] = ins["acc"][...]

        def forward(i, side):
            slot = choose(i, phase.forward)
            good = ok(slot)

            def scores(p):
                lanes = slice(p * PAIR, (p + 1) * PAIR)
                return jnp.dot(kv[i, 0, :, lanes], qdt[0, p], preferred_element_type=F32)

            def attend(p, e):
                lanes = slice(p * PAIR, (p + 1) * PAIR)
                low = e.astype(BF16)
                p_out[i, p] = low
                return jnp.dot(kv[i, 1, :, lanes].T, low, preferred_element_type=F32)

            for j in range(len(phase.forward)):
                @pl.when(i == j)
                def _():
                    start_load(j + 2)

                @pl.when(good & (i == j))
                def _():
                    wait_load(j)

            def exact():
                for p in range(pairs):
                    s = scores(p)
                    m_old = stat[p : p + 1]
                    m_new = jnp.maximum(m_old, jnp.max(s, axis=0, keepdims=True))
                    e = jnp.exp(s - m_new)
                    alpha = jnp.exp(m_old - m_new)
                    row = slice(pairs + p, pairs + p + 1)
                    stat[row] = stat[row] * alpha + jnp.sum(e, axis=0, keepdims=True)
                    stat[p : p + 1] = m_new
                    m_all[slot, p : p + 1] = m_new
                    acc[1 - side, p] = acc[side, p] * alpha + attend(p, e)

            @pl.when(good & (slot != 0))
            def _():
                for p in range(pairs):
                    shift = stat[p : p + 1]
                    e = jnp.exp(scores(p) - shift)
                    sums[p : p + 1] = jnp.sum(e, axis=0, keepdims=True)
                    m_all[slot, p : p + 1] = shift
                    acc[1 - side, p] = acc[side, p] + attend(p, e)

                fits = jnp.max(sums[...]) < LIMIT

                @pl.when(fits)
                def _():
                    stat[pairs : 2 * pairs] = stat[pairs : 2 * pairs] + sums[...]

                @pl.when(jnp.logical_not(fits))
                def _():
                    flags[RARE] = 1
                    exact()

            if 0 in phase.forward:
                @pl.when(slot == 0)
                def _():
                    exact()

            return jnp.where(good, 1 - side, side)

        side = lax.fori_loop(0, len(phase.forward), forward, jnp.int32(0))
        if not phase.finish:
            outs["acc"][...] = acc[side]
    else:
        stat, m_all = ins["stat"], ins["m_all"]

    if phase.finish:
        qdm = outs["qdm"]
        for p in range(pairs):
            inverse = 1.0 / stat[pairs + p : pairs + p + 1]
            stat[pairs + p : pairs + p + 1] = inverse
            out_t = diagonal(acc[side, p] * inverse).astype(BF16)
            outs["out"][:, p * PAIR : (p + 1) * PAIR] = out_t.T
            both = diagonal(qdt[1, p]).astype(F32) * out_t.astype(F32)
            row = slice(2 * pairs + p, 2 * pairs + p + 1)
            tokens = both.shape[1]
            stat[row, :tokens] = jnp.sum(both[:HEAD_DIM], axis=0, keepdims=True)
            stat[row, tokens:] = jnp.sum(both[HEAD_DIM:], axis=0, keepdims=True)
            for x in range(2):
                qdm[x, p] = (qdt[x, p].astype(F32) * inverse).astype(BF16).T
    elif phase.backward:
        qdm = ins["qdm"]

    if phase.backward:
        dq = outs["dq"]
        if phase.finish:
            dq[...] = jnp.zeros_like(dq)
        else:
            dq[...] = ins["dq"][...]
        for number, (slots, places, name) in enumerate(phase.segments):
            p_in, g, base = ins["p%d" % number], outs[name], phase.bases[number]
            where = [phase.slots.index(slot) for slot in slots]
            loading = len(phase.forward)

            def backward(step, carry):
                slot = choose(step, slots)
                place = choose(step, places)
                i = choose(step, where)
                good = ok(slot)
                for j in range(len(slots)):
                    if where[j] >= loading:
                        @pl.when(step == j)
                        def _():
                            start_load(where[j] + 2)

                        @pl.when(good & (step == j))
                        def _():
                            wait_load(where[j])

                @pl.when(jnp.logical_not(good))
                def _():
                    g[base + step] = jnp.zeros(g.shape[1:], g.dtype)

                def terms(moved):
                    for p in range(pairs):
                        lanes = slice(p * PAIR, (p + 1) * PAIR)
                        w = p_in[place, p]
                        if moved:
                            gamma = jnp.exp(m_all[slot, p : p + 1] - stat[p : p + 1])
                            w = w * gamma.astype(BF16)
                        dp = jnp.dot(kv[i, 1, :, lanes], qdt[1, p], preferred_element_type=F32)
                        ds = w * (dp - stat[2 * pairs + p : 2 * pairs + p + 1]).astype(BF16)
                        dv = jnp.dot(w, qdm[1, p], preferred_element_type=F32)
                        dk = jnp.dot(ds, qdm[0, p], preferred_element_type=F32)
                        g[base + step, 0, :, lanes] = dk.astype(g.dtype)
                        g[base + step, 1, :, lanes] = dv.astype(g.dtype)
                        k_t = kv[i, 0, :, lanes].T
                        dq[p] += jnp.dot(k_t, ds, preferred_element_type=F32)

                moved = flags[RARE] != 0

                @pl.when(good & jnp.logical_not(moved))
                def _():
                    terms(False)

                @pl.when(good & moved)
                def _():
                    terms(True)

                return carry

            lax.fori_loop(0, len(slots), backward, 0)
        if phase.last:
            for p in range(pairs):
                inverse = stat[pairs + p : pairs + p + 1] * SCALE
                dq_t = diagonal(dq[p] * inverse).astype(BF16)
                outs["dq_out"][:, p * PAIR : (p + 1) * PAIR] = dq_t.T


def run_phase(tiles_t, tiles_h, phase, state, kvs, ps, cost, after=()):
    _, pairs, _, wide = state["qdt"].shape
    tokens, features = wide // 2, pairs * PAIR
    count = len(phase.slots)
    vmem = pl.BlockSpec(memory_space=pltpu.VMEM)
    smem = pl.BlockSpec(memory_space=pltpu.SMEM)
    anywhere = pl.BlockSpec(memory_space=pl.ANY)
    shapes = {
        "flags": ((FLAGS,), jnp.int32),
        "qdm": ((2, pairs, wide, PAIR), BF16),
        "stat": ((3 * pairs, wide), F32),
        "m_all": ((9, pairs, wide), F32),
        "acc": ((pairs, PAIR, wide), F32),
        "dq": ((pairs, PAIR, wide), F32),
        "out": ((tokens, features), BF16),
        "dq_out": ((tokens, features), BF16),
        "p": ((len(phase.forward), pairs, tokens, wide), BF16),
    }
    shapes.update({name: ((size, 2, tokens, features), BF16) for name, size in phase.sizes.items()})
    names_in = ["qdt"]
    names_out = []
    if phase.first:
        names_in += ["mask"]
    else:
        names_in += ["flags", "stat", "m_all"]
    if phase.forward:
        names_out += ["flags", "stat", "m_all", "p"]
        if not phase.first:
            names_in += ["acc"]
        if not phase.finish:
            names_out += ["acc"]
    if phase.finish:
        names_out += ["out", "qdm"]
    if phase.backward:
        if not phase.finish:
            names_in += ["dq", "qdm"]
        names_out += ["dq"] + list(phase.sizes)
    if phase.last:
        names_out += ["dq_out"]
    inputs = {name: state[name] for name in names_in}
    specs = [smem if name in ("flags", "mask") else vmem for name in names_in]
    for number, array in enumerate(ps):
        inputs["p%d" % number] = array
        specs.append(vmem)
    seen = {}

    def reference_to(array):
        if id(array) not in seen:
            seen[id(array)] = "big%d" % len(seen)
            inputs[seen[id(array)]] = array
            specs.append(anywhere)
        return seen[id(array)]

    for array in after:
        reference_to(array)
    kv_at = [(reference_to(array), at) for array, at in kvs]
    unit = 2 * tokens * tokens * features
    results = pl.pallas_call(
        functools.partial(
            phase_kernel, phase, list(inputs), names_out, tiles_t, tiles_h, kv_at
        ),
        out_shape=[jax.ShapeDtypeStruct(*shapes[name]) for name in names_out],
        in_specs=specs,
        out_specs=[smem if name == "flags" else vmem for name in names_out],
        scratch_shapes=[
            pltpu.VMEM((count, 2, tokens, features), BF16),
            pltpu.VMEM((2, pairs, PAIR, wide) if phase.forward else (1, 1, 8, PAIR), F32),
            pltpu.VMEM((pairs, wide), F32),
            pltpu.SemaphoreType.DMA((count,)),
        ],
        compiler_params=pltpu.CompilerParams(vmem_limit_bytes=LIMIT_VMEM),
        cost_estimate=pl.CostEstimate(
            flops=int(cost * COST),
            bytes_accessed=2 * unit // tokens * count,
            transcendentals=0,
        ),
    )(*inputs.values())
    state.update(zip(names_out, results))
    return state


def local(queries, key_tokens, value_tokens, cotangent, window_mask):
    shape = queries.shape
    features = shape[-1]
    tiles_t, tiles_h = lax.axis_size("tm"), lax.axis_size("height")
    run = functools.partial(run_phase, tiles_t, tiles_h)
    own = jnp.stack([key_tokens.reshape(-1, features), value_tokens.reshape(-1, features)])
    far_own = far(own)
    near_own = near(own)
    qdt, own = prepare(queries.reshape(-1, features), cotangent.reshape(-1, features), own)
    state = {"mask": window_mask, "qdt": qdt}
    own_even = in_time(own, 0)
    own_odd = in_time(own, 1)

    state = run(
        Phase(forward=[0, 3], first=True), state, [(own, None), (near_own, None)], [], COSTS[0]
    )
    p_first = state["p"]
    state["acc"], far_own = lax.optimization_barrier((state["acc"], far_own))
    far_even = in_time_middle(far_own, 0)
    far_odd = in_time_middle(far_own, 1)
    state = run(Phase(forward=[6]), state, [(far_own, None)], [], COSTS[1])
    p_far = state["p"]
    state["acc"], own_even, own_odd = lax.optimization_barrier((state["acc"], own_even, own_odd))
    near_times = near(jnp.stack([own_even, own_odd]))
    state = run(Phase(forward=[1, 2]), state, [(own_even, None), (own_odd, None)], [], COSTS[2])
    p_second = state["p"]
    state = run(Phase(forward=[7, 8]), state, [(far_even, None), (far_odd, None)], [], COSTS[3])
    p_third = state["p"]
    state = run(
        Phase(forward=[4, 5], backward=[([7, 8], [0, 1], "g_far")]),
        state,
        [(near_times, 0), (near_times, 1), (far_even, None), (far_odd, None)],
        [p_third],
        COSTS[4],
    )
    p_fourth = state["p"]
    g_far = state["g_far"]
    hop_even = in_time_middle(g_far[0], 0)
    hop_odd = in_time_middle(g_far[1], 1)

    state = run(
        Phase(backward=[([6], [0], "g_own_far"), ([3], [1], "g_near"), ([4, 5], [0, 1], "g_near")]),
        state,
        [(far_own, None), (near_own, None), (near_times, 0), (near_times, 1)],
        [p_far, p_first, p_fourth],
        COSTS[5],
    )
    from_near = near(state["g_near"])
    (to_far,) = sums_of(
        [state["g_own_far"], hop_even, hop_odd], [[(0, 0), (1, None), (2, None)]], own.shape
    )
    from_far = far(to_far)
    state = run(
        Phase(backward=[([1, 2], [0, 1], "g_times")]),
        state,
        [(own_even, None), (own_odd, None)],
        [p_second],
        COSTS[6],
        after=(hop_even, hop_odd),
    )
    to_even, to_odd = sums_of(
        [state["g_times"], from_near], [[(0, 0), (1, 1)], [(0, 1), (1, 2)]], own.shape
    )
    from_even = in_time(to_even, 0)
    from_odd = in_time(to_odd, 1)
    state = run(
        Phase(backward=[([0], [0], "g_own")], last=True), state, [(own, None)], [p_first], COSTS[7]
    )
    key_grad, value_grad = sums_of(
        [state["g_own"], from_near, from_far, from_even, from_odd],
        [[(0, (0, x)), (1, (0, x))] + [(i, x) for i in (2, 3, 4)] for x in range(2)],
        own.shape[1:],
    )
    return (
        state["out"].reshape(shape),
        state["dq_out"].reshape(shape),
        key_grad.reshape(shape),
        value_grad.reshape(shape),
    )


def solution(mesh):
    spec = P("tm", "height", None, "heads")
    return jax.shard_map(
        local, mesh=mesh, in_specs=(spec, spec, spec, spec, P()), out_specs=(spec,) * 4, check_vma=False
    )
```

```python
import functools

import jax
import jax.numpy as jnp
from jax import lax
from jax.experimental import pallas as pl
from jax.experimental.pallas import tpu as pltpu
from jax.sharding import PartitionSpec as P

HEAD_DIM = 64
PAIR = 2 * HEAD_DIM
LIMIT = 1e17
LIMIT_VMEM = 24 * 1024 * 1024
COST = 1.15e9
COSTS = (50, 2, 4, 50, 1, 1, 50, 1)
SCALE = HEAD_DIM ** -0.5
BF16 = jnp.bfloat16
F32 = jnp.float32


def pairing(size, first):
    pairs = [(i, i + 1) for i in range(first, size - 1, 2)]
    return pairs + [(b, a) for a, b in pairs]


def near(array):
    return lax.ppermute(array, "height", pairing(lax.axis_size("height"), 0))


def far(array):
    return lax.ppermute(array, "height", pairing(lax.axis_size("height"), 1))


def in_time(array, first):
    return lax.ppermute(array, "tm", pairing(lax.axis_size("tm"), first))


def in_time_middle(array, first):
    heights = lax.axis_size("height")
    pairs = [
        (a * heights + h, b * heights + h)
        for a, b in pairing(lax.axis_size("tm"), first)
        for h in range(1, heights - 1)
    ]
    return lax.ppermute(array, ("tm", "height"), pairs)


def offset(kind, index):
    even = 1 - 2 * lax.rem(index, 2)
    return jnp.where(kind == 0, 0, jnp.where(kind == 1, even, -even))


def allowed(mask_ref, slot, tiles_t, tiles_h):
    time = lax.axis_index("tm")
    height = lax.axis_index("height")
    dt = offset(lax.rem(slot, 3), time)
    dh = offset(slot // 3, height)
    inside = (
        (time + dt >= 0) & (time + dt < tiles_t) & (height + dh >= 0) & (height + dh < tiles_h)
    )
    flag = mask_ref[time, height, 3 * (dt + 1) + dh + 1]
    return inside & ((slot == 0) | (flag == 1))


def choose(index, values):
    result = jnp.int32(values[-1])
    for at, value in enumerate(values[:-1]):
        result = jnp.where(index == at, value, result)
    return result


def diagonal(x):
    tokens = x.shape[1] // 2
    return jnp.concatenate([x[:HEAD_DIM, :tokens], x[HEAD_DIM:, tokens:]], axis=0)


def put_blocks(p, x, wide_ref):
    tokens = x.shape[0]
    x_t = x.T
    zero_t = jnp.zeros((HEAD_DIM, tokens), x.dtype)
    wide_ref[p, :HEAD_DIM, :tokens] = x_t[:HEAD_DIM]
    wide_ref[p, :HEAD_DIM, tokens:] = zero_t
    wide_ref[p, HEAD_DIM:, :tokens] = zero_t
    wide_ref[p, HEAD_DIM:, tokens:] = x_t[HEAD_DIM:]


def prepare_kernel(q_ref, d_ref, kv_ref, qdt_ref, copy_ref, sem):
    copy = pltpu.make_async_copy(kv_ref, copy_ref, sem)
    copy.start()
    for p in range(q_ref.shape[1] // PAIR):
        lanes = slice(p * PAIR, (p + 1) * PAIR)
        q = (q_ref[:, lanes].astype(F32) * SCALE).astype(BF16)
        put_blocks(p, q, qdt_ref.at[0])
        put_blocks(p, d_ref[:, lanes], qdt_ref.at[1])
    copy.wait()


def prepare(q, d, kv):
    tokens, features = q.shape
    vmem = pl.BlockSpec(memory_space=pltpu.VMEM)
    anywhere = pl.BlockSpec(memory_space=pl.ANY)
    return pl.pallas_call(
        prepare_kernel,
        out_shape=[
            jax.ShapeDtypeStruct((2, features // PAIR, PAIR, 2 * tokens), BF16),
            jax.ShapeDtypeStruct(kv.shape, kv.dtype),
        ],
        in_specs=[vmem, vmem, anywhere],
        out_specs=[vmem, anywhere],
        scratch_shapes=[pltpu.SemaphoreType.DMA(())],
        compiler_params=pltpu.CompilerParams(vmem_limit_bytes=8 * 1024 * 1024),
        cost_estimate=pl.CostEstimate(flops=2_000_000_000, bytes_accessed=4 * tokens * features, transcendentals=0),
    )(q, d, kv)


FLAGS = 16
RARE = 9


def sum_kernel(terms, *refs):
    outs = refs[len(refs) - len(terms):]
    for out, parts in zip(outs, terms):
        total = None
        for operand, at in parts:
            value = (refs[operand] if at is None else refs[operand].at[at])[...].astype(F32)
            total = value if total is None else total + value
        out[...] = total.astype(out.dtype)


def sums_of(operands, terms, shape):
    vmem = pl.BlockSpec(memory_space=pltpu.VMEM)
    return pl.pallas_call(
        functools.partial(sum_kernel, terms),
        out_shape=[jax.ShapeDtypeStruct(shape, BF16)] * len(terms),
        in_specs=[vmem] * len(operands),
        out_specs=[vmem] * len(terms),
        compiler_params=pltpu.CompilerParams(vmem_limit_bytes=8 * 1024 * 1024),
        cost_estimate=pl.CostEstimate(flops=1000, bytes_accessed=1_000_000, transcendentals=0),
    )(*operands)


class Phase:
    def __init__(self, forward=(), backward=(), first=False, last=False):
        self.forward = list(forward)
        self.segments = list(backward)
        self.backward = [slot for slots, _, _ in backward for slot in slots]
        self.sizes = {}
        self.bases = []
        for slots, _, name in backward:
            self.bases.append(self.sizes.get(name, 0))
            self.sizes[name] = self.bases[-1] + len(slots)
        self.first, self.last = first, last
        self.finish = bool(forward) and bool(backward)
        self.slots = self.forward + [slot for slot in self.backward if slot not in self.forward]


def phase_kernel(phase, names_in, names_out, tiles_t, tiles_h, kv_at, *refs):
    ins = dict(zip(names_in, refs))
    outs = dict(zip(names_out, refs[len(names_in):]))
    kv, acc, sums, tall, todo, kv_sem = refs[len(names_in) + len(names_out):]
    count = len(phase.slots)
    pairs = kv.shape[-1] // PAIR

    if phase.forward:
        flags = outs["flags"]
        for slot in range(FLAGS):
            if not phase.first:
                flags[slot] = ins["flags"][slot]
            elif slot < 9:
                flags[slot] = allowed(ins["mask"], jnp.int32(slot), tiles_t, tiles_h).astype(jnp.int32)
            else:
                flags[slot] = 0
    else:
        flags = ins["flags"]

    def ok(slot):
        return flags[slot] != 0

    def load_kv(i):
        name, at = kv_at[i]
        source = ins[name] if at is None else ins[name].at[at]
        return pltpu.make_async_copy(source, kv.at[i], kv_sem.at[i])

    def start_load(i):
        if i < count:
            @pl.when(ok(phase.slots[i]))
            def _():
                load_kv(i).start()

    def wait_load(i):
        load_kv(i).wait()

    qdt = ins["qdt"]
    start_load(0)
    start_load(1)

    if phase.forward:
        stat, m_all, p_out = outs["stat"], outs["m_all"], outs["p"]
        if phase.first:
            stat[0:pairs] = jnp.full((pairs, stat.shape[1]), -1e30, F32)
            stat[pairs:] = jnp.zeros((stat.shape[0] - pairs, stat.shape[1]), F32)
            acc[0] = jnp.zeros(acc.shape[1:], F32)
            m_all[...] = jnp.zeros_like(m_all)
        else:
            stat[...] = ins["stat"][...]
            m_all[...] = ins["m_all"][...]
            acc[0] = ins["acc"][...]

        def forward(i, side):
            slot = choose(i, phase.forward)
            good = ok(slot)

            def scores(p):
                lanes = slice(p * PAIR, (p + 1) * PAIR)
                return jnp.dot(kv[i, 0, :, lanes], qdt[0, p], preferred_element_type=F32)

            def attend(p, e):
                lanes = slice(p * PAIR, (p + 1) * PAIR)
                low = e.astype(BF16)
                p_out[i, p] = low
                return jnp.dot(kv[i, 1, :, lanes].T, low, preferred_element_type=F32)

            for j in range(len(phase.forward)):
                @pl.when(i == j)
                def _():
                    start_load(j + 2)

                @pl.when(good & (i == j))
                def _():
                    wait_load(j)

            def raise_shift():
                for p in range(pairs):
                    m_old = stat[p : p + 1]
                    m_new = jnp.maximum(m_old, jnp.max(scores(p), axis=0, keepdims=True))
                    alpha = jnp.exp(m_old - m_new)
                    row = slice(pairs + p, pairs + p + 1)
                    stat[row] = stat[row] * alpha
                    stat[p : p + 1] = m_new
                    acc[side, p] = acc[side, p] * alpha

            def attempt(number, carry):
                @pl.when(good & (todo[0] != 0))
                def _():
                    @pl.when((slot == 0) | (number != 0))
                    def _():
                        raise_shift()

                    for p in range(pairs):
                        shift = stat[p : p + 1]
                        e = jnp.exp(scores(p) - shift)
                        sums[p : p + 1] = jnp.sum(e, axis=0, keepdims=True)
                        m_all[slot, p : p + 1] = shift
                        acc[1 - side, p] = acc[side, p] + attend(p, e)

                    fits = jnp.max(sums[...]) < LIMIT
                    todo[0] = jnp.where(fits, 0, 1)

                    @pl.when(fits)
                    def _():
                        stat[pairs : 2 * pairs] = stat[pairs : 2 * pairs] + sums[...]

                    @pl.when(jnp.logical_not(fits))
                    def _():
                        flags[RARE] = 1

                return carry

            todo[0] = 1
            lax.fori_loop(0, 2, attempt, 0)

            return jnp.where(good, 1 - side, side)

        side = lax.fori_loop(0, len(phase.forward), forward, jnp.int32(0))
        if not phase.finish:
            outs["acc"][...] = acc[side]
    else:
        stat, m_all = ins["stat"], ins["m_all"]

    if phase.finish:
        qdm = outs["qdm"]
        for p in range(pairs):
            inverse = 1.0 / stat[pairs + p : pairs + p + 1]
            stat[pairs + p : pairs + p + 1] = inverse
            out_t = diagonal(acc[side, p] * inverse).astype(BF16)
            outs["out"][:, p * PAIR : (p + 1) * PAIR] = out_t.T
            both = diagonal(qdt[1, p]).astype(F32) * out_t.astype(F32)
            row = slice(2 * pairs + p, 2 * pairs + p + 1)
            tokens = both.shape[1]
            stat[row, :tokens] = jnp.sum(both[:HEAD_DIM], axis=0, keepdims=True)
            stat[row, tokens:] = jnp.sum(both[HEAD_DIM:], axis=0, keepdims=True)
            for x in range(2):
                qdm[x, p] = (qdt[x, p].astype(F32) * inverse).astype(BF16).T
    elif phase.backward:
        qdm = ins["qdm"]

    if phase.backward:
        dq = outs["dq"]
        tall[...] = qdm[...]
        if phase.finish:
            dq[...] = jnp.zeros_like(dq)
        else:
            dq[...] = ins["dq"][...]
        for number, (slots, places, name) in enumerate(phase.segments):
            p_in, g, base = ins["p%d" % number], outs[name], phase.bases[number]
            where = [phase.slots.index(slot) for slot in slots]
            loading = len(phase.forward)

            def backward(step, carry):
                slot = choose(step, slots)
                place = choose(step, places)
                i = choose(step, where)
                good = ok(slot)
                for j in range(len(slots)):
                    if where[j] >= loading:
                        @pl.when(step == j)
                        def _():
                            start_load(where[j] + 2)

                        @pl.when(good & (step == j))
                        def _():
                            wait_load(where[j])

                @pl.when(jnp.logical_not(good))
                def _():
                    g[base + step] = jnp.zeros(g.shape[1:], g.dtype)

                @pl.when(good & (flags[RARE] != 0))
                def _():
                    for p in range(pairs):
                        gamma = jnp.exp(m_all[slot, p : p + 1] - stat[p : p + 1])
                        gamma = gamma * stat[pairs + p : pairs + p + 1]
                        for x in range(2):
                            tall[x, p] = (qdt[x, p].astype(F32) * gamma).astype(BF16).T

                @pl.when(good)
                def _():
                    for p in range(pairs):
                        lanes = slice(p * PAIR, (p + 1) * PAIR)
                        gamma = jnp.exp(m_all[slot, p : p + 1] - stat[p : p + 1])
                        w = p_in[place, p]
                        dp = jnp.dot(kv[i, 1, :, lanes], qdt[1, p], preferred_element_type=F32)
                        ds = w * (dp - stat[2 * pairs + p : 2 * pairs + p + 1]).astype(BF16)
                        dv = jnp.dot(w, tall[1, p], preferred_element_type=F32)
                        dk = jnp.dot(ds, tall[0, p], preferred_element_type=F32)
                        g[base + step, 0, :, lanes] = dk.astype(g.dtype)
                        g[base + step, 1, :, lanes] = dv.astype(g.dtype)
                        k_t = kv[i, 0, :, lanes].T
                        dq[p] += jnp.dot(k_t, ds, preferred_element_type=F32) * gamma

                return carry

            lax.fori_loop(0, len(slots), backward, 0)
        if phase.last:
            for p in range(pairs):
                inverse = stat[pairs + p : pairs + p + 1] * SCALE
                dq_t = diagonal(dq[p] * inverse).astype(BF16)
                outs["dq_out"][:, p * PAIR : (p + 1) * PAIR] = dq_t.T


def run_phase(tiles_t, tiles_h, phase, state, kvs, ps, cost, after=()):
    _, pairs, _, wide = state["qdt"].shape
    tokens, features = wide // 2, pairs * PAIR
    count = len(phase.slots)
    vmem = pl.BlockSpec(memory_space=pltpu.VMEM)
    smem = pl.BlockSpec(memory_space=pltpu.SMEM)
    anywhere = pl.BlockSpec(memory_space=pl.ANY)
    shapes = {
        "flags": ((FLAGS,), jnp.int32),
        "qdm": ((2, pairs, wide, PAIR), BF16),
        "stat": ((3 * pairs, wide), F32),
        "m_all": ((9, pairs, wide), F32),
        "acc": ((pairs, PAIR, wide), F32),
        "dq": ((pairs, PAIR, wide), F32),
        "out": ((tokens, features), BF16),
        "dq_out": ((tokens, features), BF16),
        "p": ((len(phase.forward), pairs, tokens, wide), BF16),
    }
    shapes.update({name: ((size, 2, tokens, features), BF16) for name, size in phase.sizes.items()})
    names_in = ["qdt"]
    names_out = []
    if phase.first:
        names_in += ["mask"]
    else:
        names_in += ["flags", "stat", "m_all"]
    if phase.forward:
        names_out += ["flags", "stat", "m_all", "p"]
        if not phase.first:
            names_in += ["acc"]
        if not phase.finish:
            names_out += ["acc"]
    if phase.finish:
        names_out += ["out", "qdm"]
    if phase.backward:
        if not phase.finish:
            names_in += ["dq", "qdm"]
        names_out += ["dq"] + list(phase.sizes)
    if phase.last:
        names_out += ["dq_out"]
    inputs = {name: state[name] for name in names_in}
    specs = [smem if name in ("flags", "mask") else vmem for name in names_in]
    for number, array in enumerate(ps):
        inputs["p%d" % number] = array
        specs.append(vmem)
    seen = {}

    def reference_to(array):
        if id(array) not in seen:
            seen[id(array)] = "big%d" % len(seen)
            inputs[seen[id(array)]] = array
            specs.append(anywhere)
        return seen[id(array)]

    for array in after:
        reference_to(array)
    kv_at = [(reference_to(array), at) for array, at in kvs]
    unit = 2 * tokens * tokens * features
    results = pl.pallas_call(
        functools.partial(
            phase_kernel, phase, list(inputs), names_out, tiles_t, tiles_h, kv_at
        ),
        out_shape=[jax.ShapeDtypeStruct(*shapes[name]) for name in names_out],
        in_specs=specs,
        out_specs=[smem if name == "flags" else vmem for name in names_out],
        scratch_shapes=[
            pltpu.VMEM((count, 2, tokens, features), BF16),
            pltpu.VMEM((2, pairs, PAIR, wide) if phase.forward else (1, 1, 8, PAIR), F32),
            pltpu.VMEM((pairs, wide), F32),
            pltpu.VMEM(shapes["qdm"][0] if phase.backward else (1, 1, 16, PAIR), BF16),
            pltpu.SMEM((1,), jnp.int32),
            pltpu.SemaphoreType.DMA((count,)),
        ],
        compiler_params=pltpu.CompilerParams(vmem_limit_bytes=LIMIT_VMEM),
        cost_estimate=pl.CostEstimate(
            flops=int(cost * COST),
            bytes_accessed=2 * unit // tokens * count,
            transcendentals=0,
        ),
    )(*inputs.values())
    state.update(zip(names_out, results))
    return state


def local(queries, key_tokens, value_tokens, cotangent, window_mask):
    shape = queries.shape
    features = shape[-1]
    tiles_t, tiles_h = lax.axis_size("tm"), lax.axis_size("height")
    run = functools.partial(run_phase, tiles_t, tiles_h)
    own = jnp.stack([key_tokens.reshape(-1, features), value_tokens.reshape(-1, features)])
    far_own = far(own)
    near_own = near(own)
    qdt, own = prepare(queries.reshape(-1, features), cotangent.reshape(-1, features), own)
    state = {"mask": window_mask, "qdt": qdt}
    own_even = in_time(own, 0)
    own_odd = in_time(own, 1)

    state = run(
        Phase(forward=[0, 3], first=True), state, [(own, None), (near_own, None)], [], COSTS[0]
    )
    p_first = state["p"]
    state["acc"], far_own = lax.optimization_barrier((state["acc"], far_own))
    far_even = in_time_middle(far_own, 0)
    far_odd = in_time_middle(far_own, 1)
    state = run(Phase(forward=[6]), state, [(far_own, None)], [], COSTS[1])
    p_far = state["p"]
    state["acc"], own_even, own_odd = lax.optimization_barrier((state["acc"], own_even, own_odd))
    near_times = near(jnp.stack([own_even, own_odd]))
    state = run(Phase(forward=[1, 2]), state, [(own_even, None), (own_odd, None)], [], COSTS[2])
    p_second = state["p"]
    state = run(Phase(forward=[7, 8]), state, [(far_even, None), (far_odd, None)], [], COSTS[3])
    p_third = state["p"]
    state = run(
        Phase(forward=[4, 5], backward=[([7, 8], [0, 1], "g_far")]),
        state,
        [(near_times, 0), (near_times, 1), (far_even, None), (far_odd, None)],
        [p_third],
        COSTS[4],
    )
    p_fourth = state["p"]
    g_far = state["g_far"]
    hop_even = in_time_middle(g_far[0], 0)
    hop_odd = in_time_middle(g_far[1], 1)

    state = run(
        Phase(backward=[([6], [0], "g_own_far"), ([3], [1], "g_near"), ([4, 5], [0, 1], "g_near")]),
        state,
        [(far_own, None), (near_own, None), (near_times, 0), (near_times, 1)],
        [p_far, p_first, p_fourth],
        COSTS[5],
    )
    from_near = near(state["g_near"])
    (to_far,) = sums_of(
        [state["g_own_far"], hop_even, hop_odd], [[(0, 0), (1, None), (2, None)]], own.shape
    )
    from_far = far(to_far)
    state = run(
        Phase(backward=[([1, 2], [0, 1], "g_times")]),
        state,
        [(own_even, None), (own_odd, None)],
        [p_second],
        COSTS[6],
        after=(hop_even, hop_odd),
    )
    to_even, to_odd = sums_of(
        [state["g_times"], from_near], [[(0, 0), (1, 1)], [(0, 1), (1, 2)]], own.shape
    )
    from_even = in_time(to_even, 0)
    from_odd = in_time(to_odd, 1)
    state = run(
        Phase(backward=[([0], [0], "g_own")], last=True), state, [(own, None)], [p_first], COSTS[7]
    )
    key_grad, value_grad = sums_of(
        [state["g_own"], from_near, from_far, from_even, from_odd],
        [[(0, (0, x)), (1, (0, x))] + [(i, x) for i in (2, 3, 4)] for x in range(2)],
        own.shape[1:],
    )
    return (
        state["out"].reshape(shape),
        state["dq_out"].reshape(shape),
        key_grad.reshape(shape),
        value_grad.reshape(shape),
    )


def solution(mesh):
    spec = P("tm", "height", None, "heads")
    return jax.shard_map(
        local, mesh=mesh, in_specs=(spec, spec, spec, spec, P()), out_specs=(spec,) * 4, check_vma=False
    )
```

```python
import functools

import jax
import jax.numpy as jnp
from jax import lax
from jax.experimental import pallas as pl
from jax.experimental.pallas import tpu as pltpu
from jax.sharding import PartitionSpec as P

HEAD_DIM = 64
LIMIT = 1e17
SCALE = HEAD_DIM ** -0.5
BF16 = jnp.bfloat16
F32 = jnp.float32
COST = 1.15e9
COSTS = (50, 4, 50, 1, 1)
MIB = 1024 * 1024
FLAGS = 24
RARE = 18


def pairing(size, first):
    pairs = [(i, i + 1) for i in range(first, size - 1, 2)]
    return pairs + [(b, a) for a, b in pairs]


def near(array):
    return lax.ppermute(array, "height", pairing(lax.axis_size("height"), 0))


def far(array):
    peers = lax.axis_size("height")
    return lax.ppermute(array, "height", [(i, (i + 2) % peers) for i in range(peers)])


def in_time(array, first):
    return lax.ppermute(array, "tm", pairing(lax.axis_size("tm"), first))


def offset(kind, index):
    even = 1 - 2 * lax.rem(index, 2)
    return jnp.where(kind == 0, 0, jnp.where(kind == 1, even, -even))


def near_far_tile(height):
    return jnp.where((height == 1) | (height == 2), 0, 1)


def allowed(mask_ref, unit, tiles_t):
    time = lax.axis_index("tm")
    height = lax.axis_index("height")
    slot, query = unit // 2, unit % 2
    column, place = slot // 3, slot % 3
    other = height + offset(1, height)
    query_height = height if query == 0 else other
    key_height = (height, other, jnp.where(height < 2, 2, 1))[column]
    dt = offset(place, time)
    dh = key_height - query_height
    inside = (time + dt >= 0) & (time + dt < tiles_t) & (dh >= -1) & (dh <= 1)
    if slot == 3 * query:
        return inside
    flag = mask_ref[time, query_height, jnp.clip(3 * (dt + 1) + dh + 1, 0, 8)]
    return inside & (flag == 1)


def choose(index, values):
    result = jnp.int32(values[-1])
    for at, value in enumerate(values[:-1]):
        result = jnp.where(index == at, value, result)
    return result


def call(kernel, inputs, outputs, scratch=(), mib=16, cost=1, places=None):
    vmem = pl.BlockSpec(memory_space=pltpu.VMEM)
    places = places or {}
    return pl.pallas_call(
        kernel,
        out_shape=[jax.ShapeDtypeStruct(*output[:2]) for output in outputs],
        in_specs=[pl.BlockSpec(memory_space=places[i]) if i in places else vmem for i in range(len(inputs))],
        out_specs=[pl.BlockSpec(memory_space=output[2]) if len(output) > 2 else vmem for output in outputs],
        scratch_shapes=list(scratch),
        compiler_params=pltpu.CompilerParams(vmem_limit_bytes=mib * MIB),
        cost_estimate=pl.CostEstimate(flops=int(cost * COST), bytes_accessed=1000, transcendentals=0),
    )(*inputs)


def swapped_halves(x):
    return pltpu.roll(x.astype(F32), x.shape[1] // 2, 1).astype(x.dtype)


def lane_is_low(shape):
    return lax.broadcasted_iota(jnp.int32, shape, 1) < shape[1] // 2


def split_kernel(q_ref, k_ref, v_ref, d_ref, keep_ref, send_ref):
    odd = lax.rem(lax.axis_index("height"), 2)
    low = lane_is_low(k_ref.shape)
    for row, (a_ref, b_ref) in enumerate(((k_ref, v_ref), (q_ref, d_ref))):
        a, b = a_ref[...], b_ref[...]
        if row == 1:
            a = (a.astype(F32) * SCALE).astype(BF16)
        first = jnp.where(low, a, swapped_halves(b))
        second = jnp.where(low, swapped_halves(a), b)

        @pl.when(odd == 0)
        def _():
            keep_ref[row] = first
            send_ref[row] = second

        @pl.when(odd != 0)
        def _():
            keep_ref[row] = second
            send_ref[row] = first


def merge_kernel(keep_ref, recv_ref, both_ref, far_ref):
    both_ref[0] = keep_ref[0]
    both_ref[1] = recv_ref[0]
    beside = near_far_tile(lax.axis_index("height"))

    @pl.when(beside == 0)
    def _():
        far_ref[...] = keep_ref[0]

    @pl.when(beside != 0)
    def _():
        far_ref[...] = recv_ref[0]


def join_rows_kernel(own_ref, recv_ref, out_ref, dq_ref):
    odd = lax.rem(lax.axis_index("height"), 2)
    half = own_ref.shape[0] // 2

    def join(low, high):
        for at, ref in enumerate((out_ref, dq_ref)):
            rows = slice(at * half, (at + 1) * half)
            ref[...] = jnp.concatenate([low[rows], high[rows]], axis=0).T

    @pl.when(odd == 0)
    def _():
        join(own_ref, recv_ref)

    @pl.when(odd != 0)
    def _():
        join(recv_ref, own_ref)


def join_lanes_kernel(own_ref, recv_ref, key_ref, value_ref):
    odd = lax.rem(lax.axis_index("height"), 2)

    def join(low_ref, high_ref):
        lanes_low = lane_is_low(low_ref.shape)
        low, high = low_ref[...], high_ref[...]
        key_ref[...] = jnp.where(lanes_low, low, swapped_halves(high))
        value_ref[...] = jnp.where(lanes_low, swapped_halves(low), high)

    @pl.when(odd == 0)
    def _():
        join(own_ref, recv_ref)

    @pl.when(odd != 0)
    def _():
        join(recv_ref, own_ref)


def far_sum_kernel(own_ref, even_ref, odd_ref, out_ref):
    total = own_ref[...].astype(F32) + even_ref[...].astype(F32) + odd_ref[...].astype(F32)
    out_ref[...] = total.astype(BF16)


def total_kernel(own_ref, even_ref, odd_ref, far_ref, mine_ref, partner_ref):
    beside = near_far_tile(lax.axis_index("height"))
    for tile, ref in enumerate((mine_ref, partner_ref)):
        total = own_ref[tile].astype(F32) + even_ref[tile].astype(F32) + odd_ref[tile].astype(F32)
        share = jnp.where(beside == tile, 1.0, 0.0).astype(F32)
        ref[...] = (total + far_ref[...].astype(F32) * share).astype(BF16)


class Phase:
    def __init__(self, forward=(), backward=(), targets=None, first=False, last=False):
        self.forward = list(forward)
        self.segments = list(backward)
        self.backward = [slot for slots, _ in backward for slot in slots]
        self.targets = targets or {}
        self.first, self.last = first, last
        self.finish = bool(forward) and bool(backward)
        self.slots = self.forward + [slot for slot in self.backward if slot not in self.forward]


def phase_kernel(phase, names_in, names_out, tiles_t, kv_at, *refs):
    ins = dict(zip(names_in, refs))
    outs = dict(zip(names_out, refs[len(names_in):]))
    kv, acc, sums, state_s, turned, g_acc, tall_s, kv_sem = refs[len(names_in) + len(names_out):]
    count, tokens, lanes = kv.shape
    half = lanes // 2
    heads = half // HEAD_DIM
    depth = lanes - 128
    key_lanes, value_lanes = slice(0, depth), slice(lanes - depth, lanes)
    pad = depth - half
    columns = [slice(j * tokens, (j + 1) * tokens) for j in range(heads)]
    rows = [slice(j * HEAD_DIM, (j + 1) * HEAD_DIM) for j in range(heads)]

    if phase.forward:
        flags = outs["flags"]
        for unit in range(FLAGS):
            if not phase.first:
                flags[unit] = ins["flags"][unit]
            elif unit < 18:
                flags[unit] = allowed(ins["mask"], unit, tiles_t).astype(jnp.int32)
            else:
                flags[unit] = 0
    else:
        flags = ins["flags"]

    def ok(slot):
        return (flags[2 * slot] + flags[2 * slot + 1]) != 0

    def load_kv(i):
        name, at = kv_at[i]
        source = ins[name] if at is None else ins[name].at[at]
        return pltpu.make_async_copy(source, kv.at[i], kv_sem.at[i])

    def start_load(i):
        if i < count:
            @pl.when(ok(phase.slots[i]))
            def _():
                load_kv(i).start()

    start_load(0)
    start_load(1)

    if phase.first:
        wide = outs["wide"]
        wide[...] = jnp.zeros_like(wide)
        for query, name in enumerate(("keep", "recv")):
            turned_rows = ins[name][1].T
            for j in range(heads):
                wide[0, query, rows[j], columns[j]] = turned_rows[rows[j]]
                at = slice(pad + j * HEAD_DIM, pad + (j + 1) * HEAD_DIM)
                wide[1, query, at, columns[j]] = turned_rows[half + j * HEAD_DIM : half + (j + 1) * HEAD_DIM]
    else:
        wide = ins["wide"]

    if phase.forward:
        stat, m_all, p_out = outs["stat"], outs["m_all"], outs["p"]
        if phase.first:
            stat[...] = jnp.zeros_like(stat)
            stat[:, 0:1] = jnp.full((2, 1, stat.shape[2]), -1e30, F32)
            acc[0] = jnp.zeros(acc.shape[1:], F32)
            m_all[...] = jnp.zeros_like(m_all)
        else:
            stat[...] = ins["stat"][...]
            m_all[...] = ins["m_all"][...]
            acc[0] = ins["acc"][...]
        for query in range(2):
            state_s[query] = 0
            state_s[3 + query] = 0 if phase.first else 1

        def forward(i, carry):
            slot = choose(i, phase.forward)

            for j in range(len(phase.forward)):
                @pl.when(i == j)
                def _():
                    start_load(j + 2)

                @pl.when(ok(slot) & (i == j))
                def _():
                    load_kv(j).wait()

            @pl.when(ok(slot))
            def _():
                turned[...] = kv[i, :, value_lanes].T[pad:]

            def with_query(query, carry):
                unit = 2 * slot + query
                side = state_s[query]

                def scores():
                    return jnp.dot(kv[i, :, key_lanes], wide[0, query], preferred_element_type=F32)

                def raise_shift():
                    m_old = stat[query, 0:1]
                    m_new = jnp.maximum(m_old, jnp.max(scores(), axis=0, keepdims=True))
                    alpha = jnp.exp(m_old - m_new)
                    stat[query, 0:1] = m_new
                    stat[query, 1:2] = stat[query, 1:2] * alpha
                    for j in range(heads):
                        acc[side, query, rows[j]] = acc[side, query, rows[j]] * alpha[:, columns[j]]

                def attempt(number, carry):
                    @pl.when((flags[unit] != 0) & (state_s[2] != 0))
                    def _():
                        @pl.when((state_s[3 + query] == 0) | (number != 0))
                        def _():
                            raise_shift()

                        shift = stat[query, 0:1]
                        m_all[unit] = shift
                        e = jnp.exp(scores() - shift)
                        sums[...] = jnp.sum(e, axis=0, keepdims=True)
                        low = e.astype(BF16)
                        p_out[2 * i + query] = low
                        for j in range(heads):
                            acc[1 - side, query, rows[j]] = acc[side, query, rows[j]] + jnp.dot(
                                turned[rows[j]], low[:, columns[j]], preferred_element_type=F32
                            )
                        fits = jnp.max(sums[...]) < LIMIT
                        state_s[2] = jnp.where(fits, 0, 1)

                        @pl.when(fits)
                        def _():
                            stat[query, 1:2] = stat[query, 1:2] + sums[...]
                            state_s[query] = 1 - side
                            state_s[3 + query] = 1

                        @pl.when(jnp.logical_not(fits))
                        def _():
                            flags[RARE] = 1

                    return carry

                state_s[2] = 1
                lax.fori_loop(0, 2, attempt, 0)
                return carry

            lax.fori_loop(0, 2, with_query, 0)
            return carry

        lax.fori_loop(0, len(phase.forward), forward, 0)
        if not phase.finish:
            for query in range(2):
                outs["acc"][query] = acc[state_s[query], query]
    else:
        stat, m_all = ins["stat"], ins["m_all"]

    if phase.finish:
        tall = outs["tall"]
        for query in range(2):
            inverse = 1.0 / stat[query, 1:2]
            stat[query, 1:2] = inverse
            side = state_s[query]
            for j in range(heads):
                out_t = (acc[side, query, rows[j]] * inverse[:, columns[j]]).astype(BF16)
                outs["out_t"][query, rows[j]] = out_t
                at = slice(pad + j * HEAD_DIM, pad + (j + 1) * HEAD_DIM)
                both = wide[1, query, at, columns[j]].astype(F32) * out_t.astype(F32)
                stat[query, 2:3, columns[j]] = jnp.sum(both, axis=0, keepdims=True)
            for x in range(2):
                tall[x, query] = (wide[x, query].astype(F32) * inverse).astype(BF16).T
    elif phase.backward:
        tall = ins["tall"]

    if phase.backward:
        dq = outs["dq"]
        if phase.finish:
            dq[...] = jnp.zeros_like(dq)
        else:
            dq[...] = ins["dq"][...]
        for number, (slots, places) in enumerate(phase.segments):
            p_in = outs["p"] if phase.finish else ins["p%d" % number]
            where = [phase.slots.index(slot) for slot in slots]
            loading = len(phase.forward)

            def backward(step, carry):
                slot = choose(step, slots)
                place = choose(step, places)
                i = choose(step, where)
                for j in range(len(slots)):
                    if where[j] >= loading:
                        @pl.when(step == j)
                        def _():
                            start_load(where[j] + 2)

                        @pl.when(ok(slot) & (step == j))
                        def _():
                            load_kv(where[j]).wait()

                g_acc[...] = jnp.zeros_like(g_acc)

                @pl.when(ok(slot))
                def _():
                    turned[...] = kv[i, :, key_lanes].T[:half]

                def with_query(query, carry):
                    unit = 2 * slot + query
                    good = flags[unit] != 0
                    moved = flags[RARE] != 0

                    def terms(tall_of):
                        w = p_in[2 * place + query]
                        dp = jnp.dot(kv[i, :, value_lanes], wide[1, query], preferred_element_type=F32)
                        ds = w * (dp - stat[query, 2:3]).astype(BF16)
                        g_acc[:, value_lanes] += jnp.dot(w, tall_of(1), preferred_element_type=F32)
                        g_acc[:, key_lanes] += jnp.dot(ds, tall_of(0), preferred_element_type=F32)
                        gamma = jnp.exp(m_all[unit] - stat[query, 0:1])
                        for j in range(heads):
                            dq[query, rows[j]] += gamma[:, columns[j]] * jnp.dot(
                                turned[rows[j]], ds[:, columns[j]], preferred_element_type=F32
                            )

                    @pl.when(good & jnp.logical_not(moved))
                    def _():
                        terms(lambda x: tall[x, query])

                    @pl.when(good & moved)
                    def _():
                        factor = jnp.exp(m_all[unit] - stat[query, 0:1]) * stat[query, 1:2]
                        for x in range(2):
                            tall_s[x] = (wide[x, query].astype(F32) * factor).astype(BF16).T
                        terms(lambda x: tall_s[x])

                    return carry

                lax.fori_loop(0, 2, with_query, 0)
                for j, s in enumerate(slots):
                    name, at = phase.targets[s]
                    target = outs[name] if at is None else outs[name].at[at]

                    @pl.when(step == j)
                    def _():
                        target[...] = g_acc[...].astype(BF16)

                return carry

            lax.fori_loop(0, len(slots), backward, 0)
        if phase.last:
            for query in range(2):
                result = outs["rows%d" % query]
                result[:half] = ins["out_t"][query]
                for j in range(heads):
                    at = slice(half + j * HEAD_DIM, half + (j + 1) * HEAD_DIM)
                    result[at] = (dq[query, rows[j]] * (stat[query, 1:2, columns[j]] * SCALE)).astype(BF16)


def run_phase(tiles_t, phase, state, kvs, ps, cost, after=()):
    tokens, lanes = state["keep"].shape[1:]
    half = lanes // 2
    depth = lanes - 128
    wide = half // HEAD_DIM * tokens
    count = len(phase.slots)
    smem = pltpu.SMEM
    tile = ((tokens, lanes), BF16)
    shapes = {
        "flags": ((FLAGS,), jnp.int32, smem),
        "wide": ((2, 2, depth, wide), BF16),
        "tall": ((2, 2, wide, depth), BF16),
        "stat": ((2, 3, wide), F32),
        "m_all": ((18, 1, wide), F32),
        "acc": ((2, half, tokens), F32),
        "dq": ((2, half, tokens), F32),
        "out_t": ((2, half, tokens), BF16),
        "rows0": tile,
        "rows1": tile,
        "p": ((2 * len(phase.forward), tokens, wide), BF16),
    }
    sizes = {}
    for name, at in phase.targets.values():
        sizes[name] = None if at is None else max(sizes.get(name, 0), at + 1)
    shapes.update({n: tile if size is None else ((size, tokens, lanes), BF16) for n, size in sizes.items()})
    names_in, names_out = [], []
    if phase.first:
        names_in += ["mask", "keep", "recv"]
        names_out += ["wide"]
    else:
        names_in += ["flags", "wide", "stat", "m_all"]
    if phase.forward:
        names_out += ["flags", "stat", "m_all", "p"]
        if not phase.first:
            names_in += ["acc"]
        if not phase.finish:
            names_out += ["acc"]
    if phase.finish:
        names_out += ["out_t", "tall"]
    if phase.backward:
        if not phase.finish:
            names_in += ["dq", "tall"]
        names_out += ["dq"] + list(sizes)
    if phase.last:
        names_in += ["out_t"]
        names_out += ["rows0", "rows1"]
    inputs = {name: state[name] for name in names_in}
    for number, array in enumerate(ps):
        inputs["p%d" % number] = array
    seen = {}

    def reference_to(array):
        if id(array) not in seen:
            seen[id(array)] = "big%d" % len(seen)
            inputs[seen[id(array)]] = array
        return seen[id(array)]

    for array in after:
        reference_to(array)
    kv_at = [(reference_to(array), at) for array, at in kvs]
    names = list(inputs)
    places = {i: pl.ANY for i, name in enumerate(names) if name.startswith("big")}
    places.update({i: smem for i, name in enumerate(names) if name in ("flags", "mask")})
    small = (8, 128)
    results = call(
        functools.partial(phase_kernel, phase, names, names_out, tiles_t, kv_at),
        list(inputs.values()),
        [shapes[name] for name in names_out],
        scratch=[
            pltpu.VMEM((count, tokens, lanes), BF16),
            pltpu.VMEM((2, 2, half, tokens) if phase.forward else (1, 1) + small, F32),
            pltpu.VMEM((1, wide), F32),
            pltpu.SMEM((8,), jnp.int32),
            pltpu.VMEM((half, tokens), BF16),
            pltpu.VMEM((tokens, lanes) if phase.backward else small, F32),
            pltpu.VMEM((2, wide, depth) if phase.backward else (1, 16, 128), BF16),
            pltpu.SemaphoreType.DMA((count,)),
        ],
        mib=24,
        cost=cost,
        places=places,
    )
    state.update(zip(names_out, results))
    return state


def local(queries, key_tokens, value_tokens, cotangent, window_mask):
    shape = queries.shape
    features = shape[-1]
    tokens = queries.size // features
    tile = ((tokens, features), BF16)
    two = ((2, tokens, features), BF16)
    run = functools.partial(run_phase, lax.axis_size("tm"))

    keep, send = call(
        split_kernel, [x.reshape(tokens, features) for x in (queries, key_tokens, value_tokens, cotangent)], [two, two]
    )
    recv = near(send)
    both, to_far = call(merge_kernel, [keep, recv], [two, tile])
    far_own = far(to_far)
    both_even = in_time(both, 0)
    both_odd = in_time(both, 1)
    state = {"mask": window_mask, "keep": keep, "recv": recv}
    state = run(Phase(forward=[0, 3], first=True), state, [(both, 0), (both, 1)], [], COSTS[0])
    p_own = state["p"]
    state["acc"], far_own = lax.optimization_barrier((state["acc"], far_own))
    far_even = in_time(far_own, 0)
    far_odd = in_time(far_own, 1)
    times = [(both_even, 0), (both_even, 1), (both_odd, 0), (both_odd, 1)]
    state = run(Phase(forward=[6, 1, 4, 2, 5]), state, [(far_own, None)] + times, [], COSTS[1])
    p_times = state["p"]
    state = run(
        Phase(forward=[7, 8], backward=[([7, 8], [0, 1])], targets={7: ("g_even", None), 8: ("g_odd", None)}),
        state,
        [(far_even, None), (far_odd, None)],
        [],
        COSTS[2],
    )
    hop_even = in_time(state["g_even"], 0)
    hop_odd = in_time(state["g_odd"], 1)
    state = run(
        Phase(
            backward=[([6, 1, 4, 2, 5], [0, 1, 2, 3, 4])],
            targets={6: ("g_far", None), 1: ("g_te", 0), 4: ("g_te", 1), 2: ("g_to", 0), 5: ("g_to", 1)},
        ),
        state,
        [(far_own, None)] + times,
        [p_times],
        COSTS[3],
    )
    from_even = in_time(state["g_te"], 0)
    from_odd = in_time(state["g_to"], 1)
    (to_far,) = call(far_sum_kernel, [state["g_far"], hop_even, hop_odd], [tile])
    from_far = far(to_far)
    state = run(
        Phase(backward=[([0, 3], [0, 1])], targets={0: ("g_own", 0), 3: ("g_own", 1)}, last=True),
        state,
        [(both, 0), (both, 1)],
        [p_own],
        COSTS[4],
    )
    rows_recv = near(state["rows1"])
    out, dq = call(join_rows_kernel, [state["rows0"], rows_recv], [tile, tile])
    mine, partner = call(total_kernel, [state["g_own"], from_even, from_odd, from_far], [tile, tile])
    recv_total = near(partner)
    key_grad, value_grad = call(join_lanes_kernel, [mine, recv_total], [tile, tile])
    return tuple(x.reshape(shape) for x in (out, dq, key_grad, value_grad))


def solution(mesh):
    spec = P("tm", "height", None, "heads")
    return jax.shard_map(
        local, mesh=mesh, in_specs=(spec, spec, spec, spec, P()), out_specs=(spec,) * 4, check_vma=False
    )
```

```python
import functools

import jax
import jax.numpy as jnp
from jax import lax
from jax.experimental import pallas as pl
from jax.experimental.pallas import tpu as pltpu
from jax.sharding import PartitionSpec as P

HEAD_DIM = 64
LIMIT = 1e17
SCALE = HEAD_DIM ** -0.5
BF16 = jnp.bfloat16
F32 = jnp.float32
COST = 1.15e9
COSTS = (2, 4, 50, 1, 1, 1, 4)
MIB = 1024 * 1024
FLAGS = 24
CHUNKS = 4
RARE = 18


def pairing(size, first):
    pairs = [(i, i + 1) for i in range(first, size - 1, 2)]
    return pairs + [(b, a) for a, b in pairs]


def near(array):
    return lax.ppermute(array, "height", pairing(lax.axis_size("height"), 0))


def far(array):
    peers = lax.axis_size("height")
    return lax.ppermute(array, "height", [(i, (i + 2) % peers) for i in range(peers)])


def in_time(array, first):
    return lax.ppermute(array, "tm", pairing(lax.axis_size("tm"), first))


def offset(kind, index):
    even = 1 - 2 * lax.rem(index, 2)
    return jnp.where(kind == 0, 0, jnp.where(kind == 1, even, -even))


def near_far_tile(height):
    return jnp.where((height == 1) | (height == 2), 0, 1)


def allowed(mask_ref, unit, time, height, tiles_t):
    slot, query = unit // 2, unit % 2
    column, place = slot // 3, slot % 3
    other = height + offset(1, height)
    query_height = height if query == 0 else other
    key_height = (height, other, jnp.where(height < 2, 2, 1))[column]
    dt = offset(place, time)
    dh = key_height - query_height
    inside = (time + dt >= 0) & (time + dt < tiles_t) & (dh >= -1) & (dh <= 1)
    if slot == 3 * query:
        return inside
    flag = mask_ref[time, query_height, jnp.clip(3 * (dt + 1) + dh + 1, 0, 8)]
    return inside & (flag == 1)


def choose(index, values):
    result = jnp.int32(values[-1])
    for at, value in enumerate(values[:-1]):
        result = jnp.where(index == at, value, result)
    return result


def call(kernel, inputs, outputs, scratch=(), mib=16, cost=1, places=None):
    vmem = pl.BlockSpec(memory_space=pltpu.VMEM)
    places = places or {}
    return pl.pallas_call(
        kernel,
        out_shape=[jax.ShapeDtypeStruct(*output[:2]) for output in outputs],
        in_specs=[pl.BlockSpec(memory_space=places[i]) if i in places else vmem for i in range(len(inputs))],
        out_specs=[pl.BlockSpec(memory_space=output[2]) if len(output) > 2 else vmem for output in outputs],
        scratch_shapes=list(scratch),
        compiler_params=pltpu.CompilerParams(vmem_limit_bytes=mib * MIB),
        cost_estimate=pl.CostEstimate(flops=int(cost * COST), bytes_accessed=1000, transcendentals=0),
    )(*inputs)


def swapped_halves(x):
    return pltpu.roll(x.astype(F32), x.shape[1] // 2, 1).astype(x.dtype)


def lane_is_low(shape):
    return lax.broadcasted_iota(jnp.int32, shape, 1) < shape[1] // 2


def split_kernel(kvqd_ref, keep_ref, send_ref):
    odd = lax.rem(lax.axis_index("height"), 2)
    low = lane_is_low(kvqd_ref.shape[1:])
    for row in range(2):
        a, b = kvqd_ref[2 * row], kvqd_ref[2 * row + 1]
        if row == 1:
            a = (a.astype(F32) * SCALE).astype(BF16)
        first = jnp.where(low, a, swapped_halves(b))
        second = jnp.where(low, swapped_halves(a), b)

        @pl.when(odd == 0)
        def _():
            keep_ref[row] = first
            send_ref[row] = second

        @pl.when(odd != 0)
        def _():
            keep_ref[row] = second
            send_ref[row] = first


def put_wide(query, rows, wide):
    tokens, lanes = rows.shape
    half = lanes // 2
    pad = wide.shape[2] - half
    turned = rows.T
    for x in range(2):
        wide[x, query] = jnp.zeros(wide.shape[2:], wide.dtype)
        for j in range(half // HEAD_DIM):
            at = x * pad + j * HEAD_DIM
            of = x * half + j * HEAD_DIM
            wide[x, query, at : at + HEAD_DIM, j * tokens : (j + 1) * tokens] = turned[of : of + HEAD_DIM]


def put_tall(query, tokens, wide, factor, target):
    depth, width = wide.shape[2:]
    heads = width // tokens
    half = heads * HEAD_DIM
    pad = depth - half
    for x in range(2):
        parts = [jnp.zeros((pad, tokens), BF16)] if x else []
        for j in range(heads):
            at = x * pad + j * HEAD_DIM
            columns = slice(j * tokens, (j + 1) * tokens)
            part = wide[x, query, at : at + HEAD_DIM, columns].astype(F32) * factor[:, columns]
            parts.append(part.astype(BF16))
        if not x:
            parts.append(jnp.zeros((pad, tokens), BF16))
        back = jnp.concatenate(parts, axis=0).T
        head = (lax.broadcasted_iota(jnp.int32, back.shape, 1) - x * pad) // HEAD_DIM
        for j in range(heads):
            target(x)[j * tokens : (j + 1) * tokens] = jnp.where(head == j, back, jnp.zeros_like(back))


def early_kernel(tiles_t, mask_ref, keep_ref, flags_ref, wide_ref):
    time = lax.axis_index("tm")
    height = lax.axis_index("height")
    for unit in range(FLAGS):
        flags_ref[unit] = allowed(mask_ref, unit, time, height, tiles_t).astype(jnp.int32) if unit < 18 else 0
    put_wide(0, keep_ref[1], wide_ref)


def merge_kernel(keep_ref, recv_ref, after_ref, both_ref, far_ref):
    del after_ref
    both_ref[0] = keep_ref[0]
    both_ref[1] = recv_ref[0]
    beside = near_far_tile(lax.axis_index("height"))

    @pl.when(beside == 0)
    def _():
        far_ref[...] = keep_ref[0]

    @pl.when(beside != 0)
    def _():
        far_ref[...] = recv_ref[0]


def join_rows_kernel(own_ref, recv_ref, out_ref, dq_ref):
    odd = lax.rem(lax.axis_index("height"), 2)
    half = own_ref.shape[0] // 2

    def join(low, high):
        for at, ref in enumerate((out_ref, dq_ref)):
            rows = slice(at * half, (at + 1) * half)
            ref[...] = jnp.concatenate([low[rows], high[rows]], axis=0).T

    @pl.when(odd == 0)
    def _():
        join(own_ref, recv_ref)

    @pl.when(odd != 0)
    def _():
        join(recv_ref, own_ref)


def join_lanes_kernel(own_ref, recv_ref, key_hbm, value_hbm, staged, sem):
    odd = lax.rem(lax.axis_index("height"), 2)
    rows = own_ref.shape[0] // CHUNKS
    copies = []
    for c in range(CHUNKS):
        at = slice(c * rows, (c + 1) * rows)

        def join(low_ref, high_ref):
            low, high = low_ref[at], high_ref[at]
            lanes_low = lane_is_low(low.shape)
            staged[0, at] = jnp.where(lanes_low, low, swapped_halves(high))
            staged[1, at] = jnp.where(lanes_low, swapped_halves(low), high)

        @pl.when(odd == 0)
        def _():
            join(own_ref, recv_ref)

        @pl.when(odd != 0)
        def _():
            join(recv_ref, own_ref)

        for n, target in enumerate((key_hbm, value_hbm)):
            copies.append(pltpu.make_async_copy(staged.at[n, at], target.at[at], sem.at[n, c]))
            copies[-1].start()
    for copy in copies:
        copy.wait()


def far_sum_kernel(own_ref, even_ref, odd_ref, out_ref):
    total = own_ref[...].astype(F32) + even_ref[...].astype(F32) + odd_ref[...].astype(F32)
    out_ref[...] = total.astype(BF16)


def total_kernel(own_ref, even_ref, odd_ref, far_ref, mine_ref, partner_ref):
    beside = near_far_tile(lax.axis_index("height"))
    for tile, ref in enumerate((mine_ref, partner_ref)):
        total = own_ref[tile].astype(F32) + even_ref[tile].astype(F32) + odd_ref[tile].astype(F32)
        share = jnp.where(beside == tile, 1.0, 0.0).astype(F32)
        ref[...] = (total + far_ref[...].astype(F32) * share).astype(BF16)


class Phase:
    def __init__(self, forward=(), backward=(), targets=None, first=False, last=False):
        self.forward = list(forward)
        self.segments = list(backward)
        self.backward = [slot for slots, _ in backward for slot in slots]
        self.targets = targets or {}
        self.first, self.last = first, last
        self.finish = bool(forward) and bool(backward)
        self.slots = self.forward + [slot for slot in self.backward if slot not in self.forward]


def phase_kernel(phase, names_in, names_out, kv_at, *refs):
    ins = dict(zip(names_in, refs))
    outs = dict(zip(names_out, refs[len(names_in):]))
    kv, acc, sums, state_s, turned, g_acc, tall_s, kv_sem = refs[len(names_in) + len(names_out):]
    count, tokens, lanes = kv.shape
    half = lanes // 2
    heads = half // HEAD_DIM
    depth = lanes - 128
    key_lanes, value_lanes = slice(0, depth), slice(lanes - depth, lanes)
    pad = depth - half
    columns = [slice(j * tokens, (j + 1) * tokens) for j in range(heads)]
    rows = [slice(j * HEAD_DIM, (j + 1) * HEAD_DIM) for j in range(heads)]

    if phase.forward:
        flags = outs["flags"]
        for unit in range(FLAGS):
            flags[unit] = ins["flags"][unit]
    else:
        flags = ins["flags"]

    def ok(slot):
        return (flags[2 * slot] + flags[2 * slot + 1]) != 0

    def load_kv(i):
        name, at = kv_at[i]
        source = ins[name] if at is None else ins[name].at[at]
        return pltpu.make_async_copy(source, kv.at[i], kv_sem.at[i])

    def start_load(i):
        if i < count:
            @pl.when(ok(phase.slots[i]))
            def _():
                load_kv(i).start()

    start_load(0)
    start_load(1)

    if phase.first:
        wide = outs["wide"]
        wide[:, 0:1] = ins["own_wide"][...]
        put_wide(1, ins["recv"][1], wide)
    else:
        wide = ins["wide"]

    if phase.forward:
        stat, m_all, p_out = outs["stat"], outs["m_all"], outs["p"]
        if phase.first:
            stat[...] = jnp.zeros_like(stat)
            stat[:, 0:1] = jnp.full((2, 1, stat.shape[2]), -1e30, F32)
            acc[0] = jnp.zeros(acc.shape[1:], F32)
            m_all[...] = jnp.zeros_like(m_all)
        else:
            stat[...] = ins["stat"][...]
            m_all[...] = ins["m_all"][...]
            acc[0] = ins["acc"][...]
        for query in range(2):
            state_s[query] = 0
            state_s[3 + query] = 0 if phase.first else 1

        def forward(i, carry):
            slot = choose(i, phase.forward)

            for j in range(len(phase.forward)):
                @pl.when(i == j)
                def _():
                    start_load(j + 2)

                @pl.when(ok(slot) & (i == j))
                def _():
                    load_kv(j).wait()

            @pl.when(ok(slot))
            def _():
                turned[...] = kv[i, :, value_lanes].T[pad:]

            def with_query(query, carry):
                unit = 2 * slot + query
                side = state_s[query]

                def scores():
                    return jnp.dot(kv[i, :, key_lanes], wide[0, query], preferred_element_type=F32)

                def raise_shift():
                    m_old = stat[query, 0:1]
                    m_new = jnp.maximum(m_old, jnp.max(scores(), axis=0, keepdims=True))
                    alpha = jnp.exp(m_old - m_new)
                    stat[query, 0:1] = m_new
                    stat[query, 1:2] = stat[query, 1:2] * alpha
                    for j in range(heads):
                        acc[side, query, rows[j]] = acc[side, query, rows[j]] * alpha[:, columns[j]]

                def attempt(number, carry):
                    @pl.when((flags[unit] != 0) & (state_s[2] != 0))
                    def _():
                        @pl.when((state_s[3 + query] == 0) | (number != 0))
                        def _():
                            raise_shift()

                        shift = stat[query, 0:1]
                        m_all[unit] = shift
                        e = jnp.exp(scores() - shift)
                        sums[...] = jnp.sum(e, axis=0, keepdims=True)
                        low = e.astype(BF16)
                        p_out[2 * i + query] = low
                        for j in range(heads):
                            acc[1 - side, query, rows[j]] = acc[side, query, rows[j]] + jnp.dot(
                                turned[rows[j]], low[:, columns[j]], preferred_element_type=F32
                            )
                        fits = jnp.max(sums[...]) < LIMIT
                        state_s[2] = jnp.where(fits, 0, 1)

                        @pl.when(fits)
                        def _():
                            stat[query, 1:2] = stat[query, 1:2] + sums[...]
                            state_s[query] = 1 - side
                            state_s[3 + query] = 1

                        @pl.when(jnp.logical_not(fits))
                        def _():
                            flags[RARE] = 1

                    return carry

                state_s[2] = 1
                lax.fori_loop(0, 2, attempt, 0)
                return carry

            lax.fori_loop(0, 2, with_query, 0)
            return carry

        lax.fori_loop(0, len(phase.forward), forward, 0)
        if not phase.finish:
            for query in range(2):
                outs["acc"][query] = acc[state_s[query], query]
    else:
        stat, m_all = ins["stat"], ins["m_all"]

    if phase.finish:
        tall = outs["tall"]
        for query in range(2):
            inverse = 1.0 / stat[query, 1:2]
            stat[query, 1:2] = inverse
            side = state_s[query]
            for j in range(heads):
                out_t = (acc[side, query, rows[j]] * inverse[:, columns[j]]).astype(BF16)
                outs["out_t"][query, rows[j]] = out_t
                at = slice(pad + j * HEAD_DIM, pad + (j + 1) * HEAD_DIM)
                both = wide[1, query, at, columns[j]].astype(F32) * out_t.astype(F32)
                stat[query, 2:3, columns[j]] = jnp.sum(both, axis=0, keepdims=True)
            put_tall(query, tokens, wide, inverse, lambda x: tall.at[x, query])
    elif phase.backward:
        tall = ins["tall"]

    if phase.backward:
        dq = outs["dq"]
        if phase.finish:
            dq[...] = jnp.zeros_like(dq)
        else:
            dq[...] = ins["dq"][...]
        for number, (slots, places) in enumerate(phase.segments):
            p_in = outs["p"] if phase.finish else ins["p%d" % number]
            where = [phase.slots.index(slot) for slot in slots]
            loading = len(phase.forward)

            def backward(step, carry):
                slot = choose(step, slots)
                place = choose(step, places)
                i = choose(step, where)
                for j in range(len(slots)):
                    if where[j] >= loading:
                        @pl.when(step == j)
                        def _():
                            start_load(where[j] + 2)

                        @pl.when(ok(slot) & (step == j))
                        def _():
                            load_kv(where[j]).wait()

                g_acc[...] = jnp.zeros_like(g_acc)

                @pl.when(ok(slot))
                def _():
                    turned[...] = kv[i, :, key_lanes].T[:half]

                def with_query(query, carry):
                    unit = 2 * slot + query
                    good = flags[unit] != 0
                    moved = flags[RARE] != 0

                    def terms(tall_of):
                        w = p_in[2 * place + query]
                        dp = jnp.dot(kv[i, :, value_lanes], wide[1, query], preferred_element_type=F32)
                        ds = w * (dp - stat[query, 2:3]).astype(BF16)
                        g_acc[:, value_lanes] += jnp.dot(w, tall_of(1), preferred_element_type=F32)
                        g_acc[:, key_lanes] += jnp.dot(ds, tall_of(0), preferred_element_type=F32)
                        gamma = jnp.exp(m_all[unit] - stat[query, 0:1])
                        for j in range(heads):
                            dq[query, rows[j]] += gamma[:, columns[j]] * jnp.dot(
                                turned[rows[j]], ds[:, columns[j]], preferred_element_type=F32
                            )

                    @pl.when(good & jnp.logical_not(moved))
                    def _():
                        terms(lambda x: tall[x, query])

                    @pl.when(good & moved)
                    def _():
                        factor = jnp.exp(m_all[unit] - stat[query, 0:1]) * stat[query, 1:2]
                        put_tall(query, tokens, wide, factor, lambda x: tall_s.at[x])
                        terms(lambda x: tall_s[x])

                    return carry

                lax.fori_loop(0, 2, with_query, 0)
                for j, s in enumerate(slots):
                    name, at = phase.targets[s]
                    target = outs[name] if at is None else outs[name].at[at]

                    @pl.when(step == j)
                    def _():
                        target[...] = g_acc[...].astype(BF16)

                return carry

            lax.fori_loop(0, len(slots), backward, 0)
        if phase.last:
            for query in range(2):
                result = outs["rows%d" % query]
                result[:half] = ins["out_t"][query]
                for j in range(heads):
                    at = slice(half + j * HEAD_DIM, half + (j + 1) * HEAD_DIM)
                    result[at] = (dq[query, rows[j]] * (stat[query, 1:2, columns[j]] * SCALE)).astype(BF16)


def run_phase(phase, state, kvs, ps, cost, after=()):
    tokens, lanes = state["keep"].shape[1:]
    half = lanes // 2
    depth = lanes - 128
    wide = half // HEAD_DIM * tokens
    count = len(phase.slots)
    smem = pltpu.SMEM
    tile = ((tokens, lanes), BF16)
    shapes = {
        "flags": ((FLAGS,), jnp.int32, smem),
        "wide": ((2, 2, depth, wide), BF16),
        "tall": ((2, 2, wide, depth), BF16),
        "stat": ((2, 3, wide), F32),
        "m_all": ((18, 1, wide), F32),
        "acc": ((2, half, tokens), F32),
        "dq": ((2, half, tokens), F32),
        "out_t": ((2, half, tokens), BF16),
        "rows0": tile,
        "rows1": tile,
        "p": ((2 * len(phase.forward), tokens, wide), BF16),
    }
    sizes = {}
    for name, at in phase.targets.values():
        sizes[name] = None if at is None else max(sizes.get(name, 0), at + 1)
    shapes.update({n: tile if size is None else ((size, tokens, lanes), BF16) for n, size in sizes.items()})
    names_in, names_out = [], []
    if phase.first:
        names_in += ["flags", "own_wide", "recv"]
        names_out += ["wide"]
    else:
        names_in += ["flags", "wide", "stat", "m_all"]
    if phase.forward:
        names_out += ["flags", "stat", "m_all", "p"]
        if not phase.first:
            names_in += ["acc"]
        if not phase.finish:
            names_out += ["acc"]
    if phase.finish:
        names_out += ["out_t", "tall"]
    if phase.backward:
        if not phase.finish:
            names_in += ["dq", "tall"]
        names_out += ["dq"] + list(sizes)
    if phase.last:
        names_in += ["out_t"]
        names_out += ["rows0", "rows1"]
    inputs = {name: state[name] for name in names_in}
    for number, array in enumerate(ps):
        inputs["p%d" % number] = array
    seen = {}

    def reference_to(array):
        if id(array) not in seen:
            seen[id(array)] = "big%d" % len(seen)
            inputs[seen[id(array)]] = array
        return seen[id(array)]

    for array in after:
        reference_to(array)
    kv_at = [(reference_to(array), at) for array, at in kvs]
    names = list(inputs)
    places = {i: pl.ANY for i, name in enumerate(names) if name.startswith("big")}
    places.update({i: smem for i, name in enumerate(names) if name in ("flags", "mask")})
    small = (8, 128)
    results = call(
        functools.partial(phase_kernel, phase, names, names_out, kv_at),
        list(inputs.values()),
        [shapes[name] for name in names_out],
        scratch=[
            pltpu.VMEM((count, tokens, lanes), BF16),
            pltpu.VMEM((2, 2, half, tokens) if phase.forward else (1, 1) + small, F32),
            pltpu.VMEM((1, wide), F32),
            pltpu.SMEM((8,), jnp.int32),
            pltpu.VMEM((half, tokens), BF16),
            pltpu.VMEM((tokens, lanes) if phase.backward else small, F32),
            pltpu.VMEM((2, wide, depth) if phase.backward else (1, 16, 128), BF16),
            pltpu.SemaphoreType.DMA((count,)),
        ],
        mib=24,
        cost=cost,
        places=places,
    )
    state.update(zip(names_out, results))
    return state


def local(queries, key_tokens, value_tokens, cotangent, window_mask):
    shape = queries.shape
    features = shape[-1]
    tokens = queries.size // features
    tile = ((tokens, features), BF16)
    two = ((2, tokens, features), BF16)

    keep, send = call(
        split_kernel,
        [jnp.stack([x.reshape(tokens, features) for x in (key_tokens, value_tokens, queries, cotangent)])],
        [two, two],
    )
    recv = near(send)
    depth, wide = features - 128, features // 2 // HEAD_DIM * tokens
    flags, own_wide = call(
        functools.partial(early_kernel, lax.axis_size("tm")),
        [window_mask, keep],
        [((FLAGS,), jnp.int32, pltpu.SMEM), ((2, 1, depth, wide), BF16)],
        places={0: pltpu.SMEM},
    )
    both, to_far = call(merge_kernel, [keep, recv, own_wide], [two, tile], places={2: pl.ANY})
    far_own = far(to_far)
    both_even = in_time(both, 0)
    both_odd = in_time(both, 1)
    state = {"flags": flags, "own_wide": own_wide, "keep": keep, "recv": recv}
    state = run_phase(Phase(forward=[0, 3], first=True), state, [(both, 0), (both, 1)], [], COSTS[0])
    p_own = state["p"]
    state["acc"], far_own = lax.optimization_barrier((state["acc"], far_own))
    far_even = in_time(far_own, 0)
    far_odd = in_time(far_own, 1)
    times = [(both_even, 0), (both_even, 1), (both_odd, 0), (both_odd, 1)]
    state = run_phase(Phase(forward=[6]), state, [(far_own, None)], [], COSTS[6])
    p_far = state["p"]
    state = run_phase(Phase(forward=[1, 4, 2, 5]), state, times, [], COSTS[1])
    p_times = state["p"]
    state = run_phase(
        Phase(forward=[7, 8], backward=[([7, 8], [0, 1])], targets={7: ("g_even", None), 8: ("g_odd", None)}),
        state,
        [(far_even, None), (far_odd, None)],
        [],
        COSTS[2],
    )
    hop_even = in_time(state["g_even"], 0)
    hop_odd = in_time(state["g_odd"], 1)
    state = run_phase(
        Phase(
            backward=[([1, 4, 2, 5], [0, 1, 2, 3])],
            targets={1: ("g_te", 0), 4: ("g_te", 1), 2: ("g_to", 0), 5: ("g_to", 1)},
        ),
        state,
        times,
        [p_times],
        COSTS[3],
    )
    from_even = in_time(state["g_te"], 0)
    from_odd = in_time(state["g_to"], 1)
    state = run_phase(
        Phase(backward=[([6], [0])], targets={6: ("g_far", None)}),
        state,
        [(far_own, None)],
        [p_far],
        COSTS[4],
    )
    (to_far,) = call(far_sum_kernel, [state["g_far"], hop_even, hop_odd], [tile])
    from_far = far(to_far)
    state = run_phase(
        Phase(backward=[([0, 3], [0, 1])], targets={0: ("g_own", 0), 3: ("g_own", 1)}, last=True),
        state,
        [(both, 0), (both, 1)],
        [p_own],
        COSTS[5],
    )
    rows_recv = near(state["rows1"])
    out, dq = call(join_rows_kernel, [state["rows0"], rows_recv], [tile, tile])
    mine, partner = call(total_kernel, [state["g_own"], from_even, from_odd, from_far], [tile, tile])
    recv_total = near(partner)
    key_grad, value_grad = call(
        join_lanes_kernel,
        [mine, recv_total],
        [tile + (pl.ANY,), tile + (pl.ANY,)],
        scratch=[pltpu.VMEM((2, tokens, features), BF16), pltpu.SemaphoreType.DMA((2, CHUNKS))],
    )
    return tuple(x.reshape(shape) for x in (out, dq, key_grad, value_grad))


def solution(mesh):
    spec = P("tm", "height", None, "heads")
    return jax.shard_map(
        local, mesh=mesh, in_specs=(spec, spec, spec, spec, P()), out_specs=(spec,) * 4, check_vma=False
    )
```

```python
import functools

import jax
import jax.numpy as jnp
from jax import lax
from jax.experimental import pallas as pl
from jax.experimental.pallas import tpu as pltpu
from jax.sharding import PartitionSpec as P

HEAD_DIM = 64
LIMIT = 1e17
SCALE = HEAD_DIM ** -0.5
BF16 = jnp.bfloat16
F32 = jnp.float32
COST = 1.15e9
COSTS = (4, 4, 50, 1, 1, 1, 2)
MIB = 1024 * 1024
FLAGS = 24
CHUNKS = 4
CHUNK = 256
RARE = 18


def pairing(size, first):
    pairs = [(i, i + 1) for i in range(first, size - 1, 2)]
    return pairs + [(b, a) for a, b in pairs]


def near(array):
    return lax.ppermute(array, "height", pairing(lax.axis_size("height"), 0))


def far(array):
    peers = lax.axis_size("height")
    return lax.ppermute(array, "height", [(i, (i + 2) % peers) for i in range(peers)])


def in_time(array, first):
    return lax.ppermute(array, "tm", pairing(lax.axis_size("tm"), first))


def offset(kind, index):
    even = 1 - 2 * lax.rem(index, 2)
    return jnp.where(kind == 0, 0, jnp.where(kind == 1, even, -even))


def near_far_tile(height):
    return jnp.where((height == 1) | (height == 2), 0, 1)


def allowed(mask_ref, unit, time, height, tiles_t):
    slot, query = unit // 2, unit % 2
    column, place = slot // 3, slot % 3
    other = height + offset(1, height)
    query_height = height if query == 0 else other
    key_height = (height, other, jnp.where(height < 2, 2, 1))[column]
    dt = offset(place, time)
    dh = key_height - query_height
    inside = (time + dt >= 0) & (time + dt < tiles_t) & (dh >= -1) & (dh <= 1)
    if slot == 3 * query:
        return inside
    flag = mask_ref[time, query_height, jnp.clip(3 * (dt + 1) + dh + 1, 0, 8)]
    return inside & (flag == 1)


def choose(index, values):
    result = jnp.int32(values[-1])
    for at, value in enumerate(values[:-1]):
        result = jnp.where(index == at, value, result)
    return result


def call(kernel, inputs, outputs, scratch=(), mib=16, cost=1, places=None):
    vmem = pl.BlockSpec(memory_space=pltpu.VMEM)
    places = places or {}
    return pl.pallas_call(
        kernel,
        out_shape=[jax.ShapeDtypeStruct(*output[:2]) for output in outputs],
        in_specs=[pl.BlockSpec(memory_space=places[i]) if i in places else vmem for i in range(len(inputs))],
        out_specs=[pl.BlockSpec(memory_space=output[2]) if len(output) > 2 else vmem for output in outputs],
        scratch_shapes=list(scratch),
        compiler_params=pltpu.CompilerParams(vmem_limit_bytes=mib * MIB),
        cost_estimate=pl.CostEstimate(flops=int(cost * COST), bytes_accessed=1000, transcendentals=0),
    )(*inputs)


def swapped_halves(x):
    return pltpu.roll(x.astype(F32), x.shape[1] // 2, 1).astype(x.dtype)


def lane_is_low(shape):
    return lax.broadcasted_iota(jnp.int32, shape, 1) < shape[1] // 2


def split_kernel(kvqd_ref, keep_ref, send_ref):
    odd = lax.rem(lax.axis_index("height"), 2)
    low = lane_is_low(kvqd_ref.shape[1:])
    for row in range(2):
        a, b = kvqd_ref[2 * row], kvqd_ref[2 * row + 1]
        if row == 1:
            a = (a.astype(F32) * SCALE).astype(BF16)
        first = jnp.where(low, a, swapped_halves(b))
        second = jnp.where(low, swapped_halves(a), b)

        @pl.when(odd == 0)
        def _():
            keep_ref[row] = first
            send_ref[row] = second

        @pl.when(odd != 0)
        def _():
            keep_ref[row] = second
            send_ref[row] = first


def put_wide(query, rows, wide):
    tokens, lanes = rows.shape
    half = lanes // 2
    pad = wide.shape[2] - half
    turned = rows.T
    for x in range(2):
        wide[x, query] = jnp.zeros(wide.shape[2:], wide.dtype)
        for j in range(half // HEAD_DIM):
            at = x * pad + j * HEAD_DIM
            of = x * half + j * HEAD_DIM
            wide[x, query, at : at + HEAD_DIM, j * tokens : (j + 1) * tokens] = turned[of : of + HEAD_DIM]


def put_tall(query, rows, factor, target):
    tokens, lanes = rows.shape
    half = lanes // 2
    depth = lanes - 128
    heads = half // HEAD_DIM
    padded = jnp.zeros((8 - heads, tokens), F32)
    by_head = jnp.concatenate([factor[:, j * tokens : (j + 1) * tokens] for j in range(heads)] + [padded], axis=0).T
    lane = lax.broadcasted_iota(jnp.int32, (1, lanes), 1)
    lane = jnp.where(lane >= half, lane - half, lane)
    scale = jnp.zeros(rows.shape, F32)
    for j in range(heads):
        here = (lane >= j * HEAD_DIM) & (lane < (j + 1) * HEAD_DIM)
        scale = jnp.where(here, by_head[:, j : j + 1], scale)
    scaled = rows.astype(F32) * scale
    for x, part in enumerate((slice(0, depth), slice(lanes - depth, lanes))):
        position = lax.broadcasted_iota(jnp.int32, (1, depth), 1) - x * (depth - half)
        for j in range(heads):
            here = (position >= j * HEAD_DIM) & (position < (j + 1) * HEAD_DIM)
            target(x)[j * tokens : (j + 1) * tokens] = jnp.where(here, scaled[:, part], 0.0).astype(BF16)


def early_kernel(tiles_t, mask_ref, keep_ref, flags_ref, wide_ref):
    time = lax.axis_index("tm")
    height = lax.axis_index("height")
    for unit in range(FLAGS):
        flags_ref[unit] = allowed(mask_ref, unit, time, height, tiles_t).astype(jnp.int32) if unit < 18 else 0
    put_wide(0, keep_ref[1], wide_ref)


def merge_kernel(keep_ref, recv_ref, after_ref, both_ref, far_ref, rows_ref):
    del after_ref
    rows_ref[0] = keep_ref[1]
    rows_ref[1] = recv_ref[1]
    both_ref[0] = keep_ref[0]
    both_ref[1] = recv_ref[0]
    beside = near_far_tile(lax.axis_index("height"))

    @pl.when(beside == 0)
    def _():
        far_ref[...] = keep_ref[0]

    @pl.when(beside != 0)
    def _():
        far_ref[...] = recv_ref[0]


def join_rows_kernel(own_ref, recv_ref, out_ref, dq_ref):
    odd = lax.rem(lax.axis_index("height"), 2)
    half = own_ref.shape[0] // 2

    def join(low, high):
        for at, ref in enumerate((out_ref, dq_ref)):
            rows = slice(at * half, (at + 1) * half)
            ref[...] = jnp.concatenate([low[rows], high[rows]], axis=0).T

    @pl.when(odd == 0)
    def _():
        join(own_ref, recv_ref)

    @pl.when(odd != 0)
    def _():
        join(recv_ref, own_ref)


def join_lanes_kernel(own_ref, recv_ref, key_hbm, value_hbm, staged, sem):
    odd = lax.rem(lax.axis_index("height"), 2)
    rows = own_ref.shape[0] // CHUNKS
    copies = []
    for c in range(CHUNKS):
        at = slice(c * rows, (c + 1) * rows)

        def join(low_ref, high_ref):
            low, high = low_ref[at], high_ref[at]
            lanes_low = lane_is_low(low.shape)
            staged[0, at] = jnp.where(lanes_low, low, swapped_halves(high))
            staged[1, at] = jnp.where(lanes_low, swapped_halves(low), high)

        @pl.when(odd == 0)
        def _():
            join(own_ref, recv_ref)

        @pl.when(odd != 0)
        def _():
            join(recv_ref, own_ref)

        for n, target in enumerate((key_hbm, value_hbm)):
            copies.append(pltpu.make_async_copy(staged.at[n, at], target.at[at], sem.at[n, c]))
            copies[-1].start()
    for copy in copies:
        copy.wait()


def far_sum_kernel(own_ref, even_ref, odd_ref, out_ref):
    total = own_ref[...].astype(F32) + even_ref[...].astype(F32) + odd_ref[...].astype(F32)
    out_ref[...] = total.astype(BF16)


def total_kernel(own_ref, even_ref, odd_ref, far_ref, mine_ref, partner_ref):
    beside = near_far_tile(lax.axis_index("height"))
    for tile, ref in enumerate((mine_ref, partner_ref)):
        total = own_ref[tile].astype(F32) + even_ref[tile].astype(F32) + odd_ref[tile].astype(F32)
        share = jnp.where(beside == tile, 1.0, 0.0).astype(F32)
        ref[...] = (total + far_ref[...].astype(F32) * share).astype(BF16)


class Phase:
    def __init__(self, forward=(), backward=(), targets=None, first=False, last=False):
        self.forward = list(forward)
        self.segments = list(backward)
        self.backward = [slot for slots, _ in backward for slot in slots]
        self.targets = targets or {}
        self.first, self.last = first, last
        self.finish = bool(forward) and bool(backward)
        self.slots = self.forward + [slot for slot in self.backward if slot not in self.forward]


def phase_kernel(phase, names_in, names_out, kv_at, *refs):
    ins = dict(zip(names_in, refs))
    outs = dict(zip(names_out, refs[len(names_in):]))
    kv, acc, sums, state_s, turned, g_acc, tall_s, slopes, kv_sem = refs[len(names_in) + len(names_out):]
    count, tokens, lanes = kv.shape
    half = lanes // 2
    heads = half // HEAD_DIM
    depth = lanes - 128
    key_lanes, value_lanes = slice(0, depth), slice(lanes - depth, lanes)
    pad = depth - half
    columns = [slice(j * tokens, (j + 1) * tokens) for j in range(heads)]
    rows = [slice(j * HEAD_DIM, (j + 1) * HEAD_DIM) for j in range(heads)]
    width = heads * tokens
    chunks = [slice(at, min(at + CHUNK, width)) for at in range(0, width, CHUNK)]

    if phase.forward:
        flags = outs["flags"]
        for unit in range(FLAGS):
            flags[unit] = ins["flags"][unit]
    else:
        flags = ins["flags"]

    def ok(slot):
        return (flags[2 * slot] + flags[2 * slot + 1]) != 0

    def load_kv(i):
        name, at = kv_at[i]
        source = ins[name] if at is None else ins[name].at[at]
        return pltpu.make_async_copy(source, kv.at[i], kv_sem.at[i])

    def start_load(i):
        if i < count:
            @pl.when(ok(phase.slots[i]))
            def _():
                load_kv(i).start()

    start_load(0)
    start_load(1)

    if phase.first:
        wide = outs["wide"]
        wide[:, 0:1] = ins["own_wide"][...]
        put_wide(1, ins["rows"][1], wide)
    else:
        wide = ins["wide"]

    if phase.forward:
        stat, m_all, p_out = outs["stat"], outs["m_all"], outs["p"]
        if phase.first:
            stat[...] = jnp.zeros_like(stat)
            stat[:, 0:1] = jnp.full((2, 1, stat.shape[2]), -1e30, F32)
            acc[0] = jnp.zeros(acc.shape[1:], F32)
            m_all[...] = jnp.zeros_like(m_all)
        else:
            stat[...] = ins["stat"][...]
            m_all[...] = ins["m_all"][...]
            acc[0] = ins["acc"][...]
        for query in range(2):
            state_s[query] = 0
            state_s[3 + query] = 0 if phase.first else 1

        def forward(i, carry):
            slot = choose(i, phase.forward)

            for j in range(len(phase.forward)):
                @pl.when(i == j)
                def _():
                    start_load(j + 2)

                @pl.when(ok(slot) & (i == j))
                def _():
                    load_kv(j).wait()

            @pl.when(ok(slot))
            def _():
                turned[...] = kv[i, :, value_lanes].T[pad:]

            def with_query(query, carry):
                unit = 2 * slot + query
                side = state_s[query]

                def scores(at):
                    return jnp.dot(kv[i, :, key_lanes], wide[0, query, :, at], preferred_element_type=F32)

                def raise_shift():
                    m_old = stat[query, 0:1]
                    for at in chunks:
                        sums[:, at] = jnp.max(scores(at), axis=0, keepdims=True)
                    m_new = jnp.maximum(m_old, sums[...])
                    alpha = jnp.exp(m_old - m_new)
                    stat[query, 0:1] = m_new
                    stat[query, 1:2] = stat[query, 1:2] * alpha
                    for j in range(heads):
                        acc[side, query, rows[j]] = acc[side, query, rows[j]] * alpha[:, columns[j]]

                def attempt(number, carry):
                    @pl.when((flags[unit] != 0) & (state_s[2] != 0))
                    def _():
                        @pl.when((state_s[3 + query] == 0) | (number != 0))
                        def _():
                            raise_shift()

                        m_all[unit] = stat[query, 0:1]
                        for at in chunks:
                            e = jnp.exp(scores(at) - stat[query, 0:1, at])
                            sums[:, at] = jnp.sum(e, axis=0, keepdims=True)
                            p_out[2 * i + query, :, at] = e.astype(BF16)
                        for j in range(heads):
                            acc[1 - side, query, rows[j]] = acc[side, query, rows[j]] + jnp.dot(
                                turned[rows[j]], p_out[2 * i + query, :, columns[j]], preferred_element_type=F32
                            )
                        fits = jnp.max(sums[...]) < LIMIT
                        state_s[2] = jnp.where(fits, 0, 1)

                        @pl.when(fits)
                        def _():
                            stat[query, 1:2] = stat[query, 1:2] + sums[...]
                            state_s[query] = 1 - side
                            state_s[3 + query] = 1

                        @pl.when(jnp.logical_not(fits))
                        def _():
                            flags[RARE] = 1

                    return carry

                state_s[2] = 1
                lax.fori_loop(0, 2, attempt, 0)
                return carry

            lax.fori_loop(0, 2, with_query, 0)
            return carry

        lax.fori_loop(0, len(phase.forward), forward, 0)
        if not phase.finish:
            for query in range(2):
                outs["acc"][query] = acc[state_s[query], query]
    else:
        stat, m_all = ins["stat"], ins["m_all"]

    if phase.finish:
        tall = outs["tall"]
        for query in range(2):
            inverse = 1.0 / stat[query, 1:2]
            stat[query, 1:2] = inverse
            side = state_s[query]
            for j in range(heads):
                out_t = (acc[side, query, rows[j]] * inverse[:, columns[j]]).astype(BF16)
                outs["out_t"][query, rows[j]] = out_t
                at = slice(pad + j * HEAD_DIM, pad + (j + 1) * HEAD_DIM)
                both = wide[1, query, at, columns[j]].astype(F32) * out_t.astype(F32)
                stat[query, 2:3, columns[j]] = jnp.sum(both, axis=0, keepdims=True)
            put_tall(query, ins["rows"][query], inverse, lambda x: tall.at[x, query])
    elif phase.backward:
        tall = ins["tall"]

    if phase.backward:
        dq = outs["dq"]
        if phase.finish:
            dq[...] = jnp.zeros_like(dq)
        else:
            dq[...] = ins["dq"][...]
        for number, (slots, places) in enumerate(phase.segments):
            p_in = outs["p"] if phase.finish else ins["p%d" % number]
            where = [phase.slots.index(slot) for slot in slots]
            loading = len(phase.forward)

            def backward(step, carry):
                slot = choose(step, slots)
                place = choose(step, places)
                i = choose(step, where)
                for j in range(len(slots)):
                    if where[j] >= loading:
                        @pl.when(step == j)
                        def _():
                            start_load(where[j] + 2)

                        @pl.when(ok(slot) & (step == j))
                        def _():
                            load_kv(where[j]).wait()

                g_acc[...] = jnp.zeros_like(g_acc)

                @pl.when(ok(slot))
                def _():
                    turned[...] = kv[i, :, key_lanes].T[:half]

                def with_query(query, carry):
                    unit = 2 * slot + query
                    good = flags[unit] != 0
                    moved = flags[RARE] != 0

                    def terms(tall_of):
                        for at in chunks:
                            dp = jnp.dot(kv[i, :, value_lanes], wide[1, query, :, at], preferred_element_type=F32)
                            low = (dp - stat[query, 2:3, at]).astype(BF16)
                            slopes[:, at] = p_in[2 * place + query, :, at] * low
                        w, ds = p_in[2 * place + query], slopes[...]
                        g_acc[:, value_lanes] += jnp.dot(w, tall_of(1), preferred_element_type=F32)
                        g_acc[:, key_lanes] += jnp.dot(ds, tall_of(0), preferred_element_type=F32)
                        gamma = jnp.exp(m_all[unit] - stat[query, 0:1])
                        for j in range(heads):
                            dq[query, rows[j]] += gamma[:, columns[j]] * jnp.dot(
                                turned[rows[j]], slopes[:, columns[j]], preferred_element_type=F32
                            )

                    @pl.when(good & jnp.logical_not(moved))
                    def _():
                        terms(lambda x: tall[x, query])

                    @pl.when(good & moved)
                    def _():
                        factor = jnp.exp(m_all[unit] - stat[query, 0:1]) * stat[query, 1:2]
                        put_tall(query, ins["rows"][query], factor, lambda x: tall_s.at[x])
                        terms(lambda x: tall_s[x])

                    return carry

                lax.fori_loop(0, 2, with_query, 0)
                for j, s in enumerate(slots):
                    name, at = phase.targets[s]
                    target = outs[name] if at is None else outs[name].at[at]

                    @pl.when(step == j)
                    def _():
                        target[...] = g_acc[...].astype(BF16)

                return carry

            lax.fori_loop(0, len(slots), backward, 0)
        if phase.last:
            for query in range(2):
                result = outs["rows%d" % query]
                result[:half] = ins["out_t"][query]
                for j in range(heads):
                    at = slice(half + j * HEAD_DIM, half + (j + 1) * HEAD_DIM)
                    result[at] = (dq[query, rows[j]] * (stat[query, 1:2, columns[j]] * SCALE)).astype(BF16)


def run_phase(phase, state, kvs, ps, cost, after=()):
    tokens, lanes = state["rows"].shape[1:]
    half = lanes // 2
    depth = lanes - 128
    wide = half // HEAD_DIM * tokens
    count = len(phase.slots)
    smem = pltpu.SMEM
    tile = ((tokens, lanes), BF16)
    shapes = {
        "flags": ((FLAGS,), jnp.int32, smem),
        "wide": ((2, 2, depth, wide), BF16),
        "tall": ((2, 2, wide, depth), BF16),
        "stat": ((2, 3, wide), F32),
        "m_all": ((18, 1, wide), F32),
        "acc": ((2, half, tokens), F32),
        "dq": ((2, half, tokens), F32),
        "out_t": ((2, half, tokens), BF16),
        "rows0": tile,
        "rows1": tile,
        "p": ((2 * len(phase.forward), tokens, wide), BF16),
    }
    sizes = {}
    for name, at in phase.targets.values():
        sizes[name] = None if at is None else max(sizes.get(name, 0), at + 1)
    shapes.update({n: tile if size is None else ((size, tokens, lanes), BF16) for n, size in sizes.items()})
    names_in, names_out = [], []
    if phase.first:
        names_in += ["flags", "own_wide", "rows"]
        names_out += ["wide"]
    else:
        names_in += ["flags", "wide", "stat", "m_all"]
    if phase.forward:
        names_out += ["flags", "stat", "m_all", "p"]
        if not phase.first:
            names_in += ["acc"]
        if not phase.finish:
            names_out += ["acc"]
    if phase.finish:
        names_out += ["out_t", "tall"]
    if phase.backward:
        names_in += ["rows"]
        if not phase.finish:
            names_in += ["dq", "tall"]
        names_out += ["dq"] + list(sizes)
    if phase.last:
        names_in += ["out_t"]
        names_out += ["rows0", "rows1"]
    inputs = {name: state[name] for name in names_in}
    for number, array in enumerate(ps):
        inputs["p%d" % number] = array
    seen = {}

    def reference_to(array):
        if id(array) not in seen:
            seen[id(array)] = "big%d" % len(seen)
            inputs[seen[id(array)]] = array
        return seen[id(array)]

    for array in after:
        reference_to(array)
    kv_at = [(reference_to(array), at) for array, at in kvs]
    names = list(inputs)
    places = {i: pl.ANY for i, name in enumerate(names) if name.startswith("big")}
    places.update({i: smem for i, name in enumerate(names) if name in ("flags", "mask")})
    small = (8, 128)
    results = call(
        functools.partial(phase_kernel, phase, names, names_out, kv_at),
        list(inputs.values()),
        [shapes[name] for name in names_out],
        scratch=[
            pltpu.VMEM((count, tokens, lanes), BF16),
            pltpu.VMEM((2, 2, half, tokens) if phase.forward else (1, 1) + small, F32),
            pltpu.VMEM((1, wide), F32),
            pltpu.SMEM((8,), jnp.int32),
            pltpu.VMEM((half, tokens), BF16),
            pltpu.VMEM((tokens, lanes) if phase.backward else small, F32),
            pltpu.VMEM((2, wide, depth) if phase.backward else (1, 16, 128), BF16),
            pltpu.VMEM((tokens, wide) if phase.backward else (16, 128), BF16),
            pltpu.SemaphoreType.DMA((count,)),
        ],
        mib=24,
        cost=cost,
        places=places,
    )
    state.update(zip(names_out, results))
    return state


def local(queries, key_tokens, value_tokens, cotangent, window_mask):
    shape = queries.shape
    features = shape[-1]
    tokens = queries.size // features
    tile = ((tokens, features), BF16)
    two = ((2, tokens, features), BF16)

    keep, send = call(
        split_kernel,
        [jnp.stack([x.reshape(tokens, features) for x in (key_tokens, value_tokens, queries, cotangent)])],
        [two, two],
    )
    recv = near(send)
    depth, wide = features - 128, features // 2 // HEAD_DIM * tokens
    flags, own_wide = call(
        functools.partial(early_kernel, lax.axis_size("tm")),
        [window_mask, keep],
        [((FLAGS,), jnp.int32, pltpu.SMEM), ((2, 1, depth, wide), BF16)],
        places={0: pltpu.SMEM},
    )
    both, to_far, rows = call(merge_kernel, [keep, recv, own_wide], [two, tile, two], places={2: pl.ANY})
    far_own = far(to_far)
    both_even = in_time(both, 0)
    both_odd = in_time(both, 1)
    state = {"flags": flags, "own_wide": own_wide, "rows": rows}
    state = run_phase(Phase(forward=[0, 3], first=True), state, [(both, 0), (both, 1)], [], COSTS[0])
    p_own = state["p"]
    state["acc"], far_own = lax.optimization_barrier((state["acc"], far_own))
    far_even = in_time(far_own, 0)
    far_odd = in_time(far_own, 1)
    times = [(both_even, 0), (both_even, 1), (both_odd, 0), (both_odd, 1)]
    state = run_phase(Phase(forward=[6]), state, [(far_own, None)], [], COSTS[6])
    p_far = state["p"]
    state = run_phase(Phase(forward=[1, 4, 2, 5]), state, times, [], COSTS[1])
    p_times = state["p"]
    state = run_phase(
        Phase(forward=[7, 8], backward=[([7, 8], [0, 1])], targets={7: ("g_even", None), 8: ("g_odd", None)}),
        state,
        [(far_even, None), (far_odd, None)],
        [],
        COSTS[2],
    )
    hop_even = in_time(state["g_even"], 0)
    hop_odd = in_time(state["g_odd"], 1)
    state = run_phase(
        Phase(
            backward=[([1, 4, 2, 5], [0, 1, 2, 3])],
            targets={1: ("g_te", 0), 4: ("g_te", 1), 2: ("g_to", 0), 5: ("g_to", 1)},
        ),
        state,
        times,
        [p_times],
        COSTS[3],
    )
    from_even = in_time(state["g_te"], 0)
    from_odd = in_time(state["g_to"], 1)
    state = run_phase(
        Phase(backward=[([6], [0])], targets={6: ("g_far", None)}),
        state,
        [(far_own, None)],
        [p_far],
        COSTS[4],
    )
    (to_far,) = call(far_sum_kernel, [state["g_far"], hop_even, hop_odd], [tile])
    from_far = far(to_far)
    state = run_phase(
        Phase(backward=[([0, 3], [0, 1])], targets={0: ("g_own", 0), 3: ("g_own", 1)}, last=True),
        state,
        [(both, 0), (both, 1)],
        [p_own],
        COSTS[5],
    )
    rows_recv = near(state["rows1"])
    out, dq = call(join_rows_kernel, [state["rows0"], rows_recv], [tile, tile])
    mine, partner = call(total_kernel, [state["g_own"], from_even, from_odd, from_far], [tile, tile])
    recv_total = near(partner)
    key_grad, value_grad = call(
        join_lanes_kernel,
        [mine, recv_total],
        [tile + (pl.ANY,), tile + (pl.ANY,)],
        scratch=[pltpu.VMEM((2, tokens, features), BF16), pltpu.SemaphoreType.DMA((2, CHUNKS))],
    )
    return tuple(x.reshape(shape) for x in (out, dq, key_grad, value_grad))


def solution(mesh):
    spec = P("tm", "height", None, "heads")
    return jax.shard_map(
        local, mesh=mesh, in_specs=(spec, spec, spec, spec, P()), out_specs=(spec,) * 4, check_vma=False
    )
```

```python
import functools

import jax
import jax.numpy as jnp
from jax import lax
from jax.experimental import pallas as pl
from jax.experimental.pallas import tpu as pltpu
from jax.sharding import PartitionSpec as P

HEAD_DIM = 64
LIMIT = 1e17
SCALE = HEAD_DIM ** -0.5
BF16 = jnp.bfloat16
F32 = jnp.float32
COST = 1.15e9
COSTS = (4, 4, 50, 1, 1, 1, 2)
MIB = 1024 * 1024
FLAGS = 24
CHUNKS = 4
ROWS = HEAD_DIM + 16
RARE = 18


def pairing(size, first):
    pairs = [(i, i + 1) for i in range(first, size - 1, 2)]
    return pairs + [(b, a) for a, b in pairs]


def near(array):
    return lax.ppermute(array, "height", pairing(lax.axis_size("height"), 0))


def far(array):
    peers = lax.axis_size("height")
    return lax.ppermute(array, "height", [(i, (i + 2) % peers) for i in range(peers)])


def in_time(array, first):
    return lax.ppermute(array, "tm", pairing(lax.axis_size("tm"), first))


def offset(kind, index):
    even = 1 - 2 * lax.rem(index, 2)
    return jnp.where(kind == 0, 0, jnp.where(kind == 1, even, -even))


def near_far_tile(height):
    return jnp.where((height == 1) | (height == 2), 0, 1)


def allowed(mask_ref, unit, time, height, tiles_t):
    slot, query = unit // 2, unit % 2
    column, place = slot // 3, slot % 3
    other = height + offset(1, height)
    query_height = height if query == 0 else other
    key_height = (height, other, jnp.where(height < 2, 2, 1))[column]
    dt = offset(place, time)
    dh = key_height - query_height
    inside = (time + dt >= 0) & (time + dt < tiles_t) & (dh >= -1) & (dh <= 1)
    if slot == 3 * query:
        return inside
    flag = mask_ref[time, query_height, jnp.clip(3 * (dt + 1) + dh + 1, 0, 8)]
    return inside & (flag == 1)


def choose(index, values):
    result = jnp.int32(values[-1])
    for at, value in enumerate(values[:-1]):
        result = jnp.where(index == at, value, result)
    return result


def call(kernel, inputs, outputs, scratch=(), mib=16, cost=1, places=None):
    vmem = pl.BlockSpec(memory_space=pltpu.VMEM)
    places = places or {}
    return pl.pallas_call(
        kernel,
        out_shape=[jax.ShapeDtypeStruct(*output[:2]) for output in outputs],
        in_specs=[pl.BlockSpec(memory_space=places[i]) if i in places else vmem for i in range(len(inputs))],
        out_specs=[pl.BlockSpec(memory_space=output[2]) if len(output) > 2 else vmem for output in outputs],
        scratch_shapes=list(scratch),
        compiler_params=pltpu.CompilerParams(vmem_limit_bytes=mib * MIB),
        cost_estimate=pl.CostEstimate(flops=int(cost * COST), bytes_accessed=1000, transcendentals=0),
    )(*inputs)


def swapped_halves(x):
    return pltpu.roll(x.astype(F32), x.shape[1] // 2, 1).astype(x.dtype)


def lane_is_low(shape):
    return lax.broadcasted_iota(jnp.int32, shape, 1) < shape[1] // 2


def split_kernel(kvqd_ref, keep_ref, send_ref):
    odd = lax.rem(lax.axis_index("height"), 2)
    low = lane_is_low(kvqd_ref.shape[1:])
    for row in range(2):
        a, b = kvqd_ref[2 * row], kvqd_ref[2 * row + 1]
        if row == 1:
            a = (a.astype(F32) * SCALE).astype(BF16)
        first = jnp.where(low, a, swapped_halves(b))
        second = jnp.where(low, swapped_halves(a), b)

        @pl.when(odd == 0)
        def _():
            keep_ref[row] = first
            send_ref[row] = second

        @pl.when(odd != 0)
        def _():
            keep_ref[row] = second
            send_ref[row] = first


def groups(part, heads):
    found = {}
    for j in range(heads):
        found.setdefault((part * heads + j) * HEAD_DIM // 128, []).append(j)
    return list(found.items())


def block(part, tile, of, tokens):
    return slice((tile - part) * 128, (tile - part + 1) * 128), slice(of[0] * tokens, (of[-1] + 1) * tokens)


def put_wide(query, rows, wide):
    tokens, lanes = rows.shape
    half = lanes // 2
    pad = wide.shape[2] - half
    turned = rows.T
    heads = half // HEAD_DIM
    for x in range(2):
        for tile, of in groups(x, heads):
            deep, columns = block(x, tile, of, tokens)
            wide[x, query, deep, columns] = jnp.zeros((128, len(of) * tokens), wide.dtype)
        for j in range(heads):
            at = x * pad + j * HEAD_DIM
            source = x * half + j * HEAD_DIM
            wide[x, query, at : at + HEAD_DIM, j * tokens : (j + 1) * tokens] = turned[source : source + HEAD_DIM]


def put_tall(query, rows, factor, target):
    tokens, lanes = rows.shape
    half = lanes // 2
    heads = half // HEAD_DIM
    padded = jnp.zeros((8 - heads, tokens), F32)
    by_head = jnp.concatenate([factor[:, j * tokens : (j + 1) * tokens] for j in range(heads)] + [padded], axis=0).T
    lane = lax.broadcasted_iota(jnp.int32, (1, lanes), 1)
    lane = jnp.where(lane >= half, lane - half, lane)
    scale = jnp.zeros(rows.shape, F32)
    for j in range(heads):
        here = (lane >= j * HEAD_DIM) & (lane < (j + 1) * HEAD_DIM)
        scale = jnp.where(here, by_head[:, j : j + 1], scale)
    scaled = rows.astype(F32) * scale
    position = lax.broadcasted_iota(jnp.int32, (1, 128), 1)
    for x in range(2):
        for tile, of in groups(x, heads):
            values = scaled[:, tile * 128 : (tile + 1) * 128]
            for j in of:
                start = (x * heads + j) * HEAD_DIM - tile * 128
                here = (position >= start) & (position < start + HEAD_DIM)
                deep, _ = block(x, tile, of, tokens)
                target(x)[j * tokens : (j + 1) * tokens, deep] = jnp.where(here, values, 0.0).astype(BF16)


def early_kernel(tiles_t, mask_ref, keep_ref, flags_ref, wide_ref):
    time = lax.axis_index("tm")
    height = lax.axis_index("height")
    for unit in range(FLAGS):
        flags_ref[unit] = allowed(mask_ref, unit, time, height, tiles_t).astype(jnp.int32) if unit < 18 else 0
    put_wide(0, keep_ref[1], wide_ref)


def merge_kernel(keep_ref, recv_ref, after_ref, both_ref, far_ref, rows_ref):
    del after_ref
    rows_ref[0] = keep_ref[1]
    rows_ref[1] = recv_ref[1]
    both_ref[0] = keep_ref[0]
    both_ref[1] = recv_ref[0]
    beside = near_far_tile(lax.axis_index("height"))

    @pl.when(beside == 0)
    def _():
        far_ref[...] = keep_ref[0]

    @pl.when(beside != 0)
    def _():
        far_ref[...] = recv_ref[0]


def join_rows_kernel(own_ref, recv_ref, out_ref, dq_ref):
    odd = lax.rem(lax.axis_index("height"), 2)
    half = own_ref.shape[0] // 2

    def join(low, high):
        for at, ref in enumerate((out_ref, dq_ref)):
            rows = slice(at * half, (at + 1) * half)
            ref[...] = jnp.concatenate([low[rows], high[rows]], axis=0).T

    @pl.when(odd == 0)
    def _():
        join(own_ref, recv_ref)

    @pl.when(odd != 0)
    def _():
        join(recv_ref, own_ref)


def join_lanes_kernel(own_ref, recv_ref, key_hbm, value_hbm, staged, sem):
    odd = lax.rem(lax.axis_index("height"), 2)
    rows = own_ref.shape[0] // CHUNKS
    copies = []
    for c in range(CHUNKS):
        at = slice(c * rows, (c + 1) * rows)

        def join(low_ref, high_ref):
            low, high = low_ref[at], high_ref[at]
            lanes_low = lane_is_low(low.shape)
            staged[0, at] = jnp.where(lanes_low, low, swapped_halves(high))
            staged[1, at] = jnp.where(lanes_low, swapped_halves(low), high)

        @pl.when(odd == 0)
        def _():
            join(own_ref, recv_ref)

        @pl.when(odd != 0)
        def _():
            join(recv_ref, own_ref)

        for n, target in enumerate((key_hbm, value_hbm)):
            copies.append(pltpu.make_async_copy(staged.at[n, at], target.at[at], sem.at[n, c]))
            copies[-1].start()
    for copy in copies:
        copy.wait()


def far_sum_kernel(own_ref, even_ref, odd_ref, out_ref):
    total = own_ref[...].astype(F32) + even_ref[...].astype(F32) + odd_ref[...].astype(F32)
    out_ref[...] = total.astype(BF16)


def total_kernel(own_ref, even_ref, odd_ref, far_ref, mine_ref, partner_ref):
    beside = near_far_tile(lax.axis_index("height"))
    for tile, ref in enumerate((mine_ref, partner_ref)):
        total = own_ref[tile].astype(F32) + even_ref[tile].astype(F32) + odd_ref[tile].astype(F32)
        share = jnp.where(beside == tile, 1.0, 0.0).astype(F32)
        ref[...] = (total + far_ref[...].astype(F32) * share).astype(BF16)


class Phase:
    def __init__(self, forward=(), backward=(), targets=None, first=False, last=False):
        self.forward = list(forward)
        self.segments = list(backward)
        self.backward = [slot for slots, _ in backward for slot in slots]
        self.targets = targets or {}
        self.first, self.last = first, last
        self.finish = bool(forward) and bool(backward)
        self.slots = self.forward + [slot for slot in self.backward if slot not in self.forward]


def phase_kernel(phase, names_in, names_out, kv_at, *refs):
    ins = dict(zip(names_in, refs))
    outs = dict(zip(names_out, refs[len(names_in):]))
    kv, acc, sums, state_s, turned, g_acc, tall_s, slopes, kv_sem = refs[len(names_in) + len(names_out):]
    count, tokens, lanes = kv.shape
    half = lanes // 2
    heads = half // HEAD_DIM
    depth = lanes - 128
    key_lanes, value_lanes = slice(0, depth), slice(lanes - depth, lanes)
    pad = depth - half
    columns = [slice(j * tokens, (j + 1) * tokens) for j in range(heads)]
    rows = [slice(j * HEAD_DIM, (j + 1) * HEAD_DIM) for j in range(heads)]
    with_ones = [slice(j * ROWS, (j + 1) * ROWS) for j in range(heads)]
    values_of = [slice(j * ROWS, j * ROWS + HEAD_DIM) for j in range(heads)]
    ones_of = [slice(j * ROWS + HEAD_DIM, j * ROWS + HEAD_DIM + 1) for j in range(heads)]

    if phase.forward:
        flags = outs["flags"]
        for unit in range(FLAGS):
            flags[unit] = ins["flags"][unit]
    else:
        flags = ins["flags"]

    def ok(slot):
        return (flags[2 * slot] + flags[2 * slot + 1]) != 0

    def load_kv(i):
        name, at = kv_at[i]
        source = ins[name] if at is None else ins[name].at[at]
        return pltpu.make_async_copy(source, kv.at[i], kv_sem.at[i])

    def start_load(i):
        if i < count:
            @pl.when(ok(phase.slots[i]))
            def _():
                load_kv(i).start()

    start_load(0)
    start_load(1)

    if phase.first:
        wide = outs["wide"]
        wide[:, 0:1] = ins["own_wide"][...]
        put_wide(1, ins["rows"][1], wide)
    else:
        wide = ins["wide"]

    if phase.forward:
        stat, m_out, p_out = outs["stat"], outs["m"], outs["p"]
        if phase.first:
            stat[...] = jnp.zeros_like(stat)
            stat[:, 0:1] = jnp.full((2, 1, stat.shape[2]), -1e30, F32)
            acc[0] = jnp.zeros(acc.shape[1:], F32)
        else:
            stat[...] = ins["stat"][...]
            acc[0] = ins["acc"][...]
        for j in range(heads):
            turned[j * ROWS + HEAD_DIM : (j + 1) * ROWS] = jnp.ones((ROWS - HEAD_DIM, tokens), BF16)
        for query in range(2):
            state_s[query] = 0
            state_s[3 + query] = 0 if phase.first else 1

        def forward(i, carry):
            slot = choose(i, phase.forward)

            for j in range(len(phase.forward)):
                @pl.when(i == j)
                def _():
                    start_load(j + 2)

                @pl.when(ok(slot) & (i == j))
                def _():
                    load_kv(j).wait()

            @pl.when(ok(slot))
            def _():
                back = kv[i, :, value_lanes].T[pad:]
                for j in range(heads):
                    turned[values_of[j]] = back[rows[j]]

            def with_query(query, carry):
                unit = 2 * slot + query
                side = state_s[query]

                def scores(tile, of):
                    deep, wide_columns = block(0, tile, of, tokens)
                    keys = kv[i, :, tile * 128 : (tile + 1) * 128]
                    return jnp.dot(keys, wide[0, query, deep, wide_columns], preferred_element_type=F32)

                def raise_shift():
                    m_old = stat[query, 0:1]
                    for tile, of in groups(0, heads):
                        _, at = block(0, tile, of, tokens)
                        sums[:, at] = jnp.max(scores(tile, of), axis=0, keepdims=True)
                    m_new = jnp.maximum(m_old, sums[...])
                    alpha = jnp.exp(m_old - m_new)
                    stat[query, 0:1] = m_new
                    for j in range(heads):
                        acc[side, query, with_ones[j]] = acc[side, query, with_ones[j]] * alpha[:, columns[j]]

                def attempt(number, carry):
                    @pl.when((flags[unit] != 0) & (state_s[2] != 0))
                    def _():
                        @pl.when((state_s[3 + query] == 0) | (number != 0))
                        def _():
                            raise_shift()

                        m_out[2 * i + query] = stat[query, 0:1]
                        for tile, of in groups(0, heads):
                            _, at = block(0, tile, of, tokens)
                            e = jnp.exp(scores(tile, of) - stat[query, 0:1, at])
                            p_out[2 * i + query, :, at] = e.astype(BF16)
                        for j in range(heads):
                            total = acc[side, query, with_ones[j]] + jnp.dot(
                                turned[with_ones[j]], p_out[2 * i + query, :, columns[j]], preferred_element_type=F32
                            )
                            acc[1 - side, query, with_ones[j]] = total
                            sums[:, columns[j]] = total[HEAD_DIM : HEAD_DIM + 1]
                        fits = jnp.max(sums[...]) < LIMIT
                        state_s[2] = jnp.where(fits, 0, 1)

                        @pl.when(fits)
                        def _():
                            state_s[query] = 1 - side
                            state_s[3 + query] = 1

                        @pl.when(jnp.logical_not(fits))
                        def _():
                            flags[RARE] = 1

                    return carry

                state_s[2] = 1
                lax.fori_loop(0, 2, attempt, 0)
                return carry

            lax.fori_loop(0, 2, with_query, 0)
            return carry

        lax.fori_loop(0, len(phase.forward), forward, 0)
        if not phase.finish:
            for query in range(2):
                outs["acc"][query] = acc[state_s[query], query]
    else:
        stat = ins["stat"]

    if phase.finish:
        tall = outs["tall"]
        for query in range(2):
            side = state_s[query]
            for j in range(heads):
                stat[query, 1:2, columns[j]] = 1.0 / acc[side, query, ones_of[j]]
            inverse = stat[query, 1:2]
            for j in range(heads):
                out_t = (acc[side, query, values_of[j]] * inverse[:, columns[j]]).astype(BF16)
                outs["out_t"][query, rows[j]] = out_t
                at = slice(pad + j * HEAD_DIM, pad + (j + 1) * HEAD_DIM)
                both = wide[1, query, at, columns[j]].astype(F32) * out_t.astype(F32)
                stat[query, 2:3, columns[j]] = jnp.sum(both, axis=0, keepdims=True)
            put_tall(query, ins["rows"][query], inverse, lambda x: tall.at[x, query])
    elif phase.backward:
        tall = ins["tall"]

    if phase.backward:
        dq = outs["dq"]
        if phase.finish:
            dq[...] = jnp.zeros_like(dq)
        else:
            dq[...] = ins["dq"][...]
        for number, (slots, places) in enumerate(phase.segments):
            p_in = outs["p"] if phase.finish else ins["p%d" % number]
            m_in = outs["m"] if phase.finish else ins["m%d" % number]
            where = [phase.slots.index(slot) for slot in slots]
            loading = len(phase.forward)

            def backward(step, carry):
                slot = choose(step, slots)
                place = choose(step, places)
                i = choose(step, where)
                for j in range(len(slots)):
                    if where[j] >= loading:
                        @pl.when(step == j)
                        def _():
                            start_load(where[j] + 2)

                        @pl.when(ok(slot) & (step == j))
                        def _():
                            load_kv(where[j]).wait()

                g_acc[...] = jnp.zeros_like(g_acc)

                @pl.when(ok(slot))
                def _():
                    turned[0:half] = kv[i, :, key_lanes].T[:half]

                def with_query(query, carry):
                    unit = 2 * slot + query
                    good = flags[unit] != 0
                    moved = flags[RARE] != 0

                    def terms(tall_of, gamma):
                        at_p = 2 * place + query
                        for tile, of in groups(1, heads):
                            deep, at = block(1, tile, of, tokens)
                            values = kv[i, :, tile * 128 : (tile + 1) * 128]
                            dp = jnp.dot(values, wide[1, query, deep, at], preferred_element_type=F32)
                            slopes[:, at] = p_in[at_p, :, at] * (dp - stat[query, 2:3, at]).astype(BF16)
                        for x in range(2):
                            for tile, of in groups(x, heads):
                                deep, at = block(x, tile, of, tokens)
                                left = p_in[at_p, :, at] if x else slopes[:, at]
                                g_acc[:, tile * 128 : (tile + 1) * 128] += jnp.dot(
                                    left, tall_of(x)[at, deep], preferred_element_type=F32
                                )
                        for j in range(heads):
                            term = jnp.dot(turned[rows[j]], slopes[:, columns[j]], preferred_element_type=F32)
                            dq[query, rows[j]] += term if gamma is None else term * gamma[:, columns[j]]

                    @pl.when(good & jnp.logical_not(moved))
                    def _():
                        terms(lambda x: tall.at[x, query], None)

                    @pl.when(good & moved)
                    def _():
                        gamma = jnp.exp(m_in[2 * place + query] - stat[query, 0:1])
                        factor = gamma * stat[query, 1:2]
                        put_tall(query, ins["rows"][query], factor, lambda x: tall_s.at[x])
                        terms(lambda x: tall_s.at[x], gamma)

                    return carry

                lax.fori_loop(0, 2, with_query, 0)
                for j, s in enumerate(slots):
                    name, at = phase.targets[s]
                    target = outs[name] if at is None else outs[name].at[at]

                    @pl.when(step == j)
                    def _():
                        target[...] = g_acc[...].astype(BF16)

                return carry

            lax.fori_loop(0, len(slots), backward, 0)
        if phase.last:
            for query in range(2):
                result = outs["rows%d" % query]
                result[:half] = ins["out_t"][query]
                for j in range(heads):
                    at = slice(half + j * HEAD_DIM, half + (j + 1) * HEAD_DIM)
                    result[at] = (dq[query, rows[j]] * (stat[query, 1:2, columns[j]] * SCALE)).astype(BF16)


def run_phase(phase, state, kvs, ps, cost, after=()):
    tokens, lanes = state["rows"].shape[1:]
    half = lanes // 2
    depth = lanes - 128
    wide = half // HEAD_DIM * tokens
    count = len(phase.slots)
    smem = pltpu.SMEM
    tile = ((tokens, lanes), BF16)
    shapes = {
        "flags": ((FLAGS,), jnp.int32, smem),
        "wide": ((2, 2, depth, wide), BF16),
        "tall": ((2, 2, wide, depth), BF16),
        "stat": ((2, 3, wide), F32),
        "m": ((2 * len(phase.forward), 1, wide), F32),
        "acc": ((2, half // HEAD_DIM * ROWS, tokens), F32),
        "dq": ((2, half, tokens), F32),
        "out_t": ((2, half, tokens), BF16),
        "rows0": tile,
        "rows1": tile,
        "p": ((2 * len(phase.forward), tokens, wide), BF16),
    }
    sizes = {}
    for name, at in phase.targets.values():
        sizes[name] = None if at is None else max(sizes.get(name, 0), at + 1)
    shapes.update({n: tile if size is None else ((size, tokens, lanes), BF16) for n, size in sizes.items()})
    names_in, names_out = [], []
    if phase.first:
        names_in += ["flags", "own_wide", "rows"]
        names_out += ["wide"]
    else:
        names_in += ["flags", "wide", "stat"]
    if phase.forward:
        names_out += ["flags", "stat", "m", "p"]
        if not phase.first:
            names_in += ["acc"]
        if not phase.finish:
            names_out += ["acc"]
    if phase.finish:
        names_out += ["out_t", "tall"]
    if phase.backward:
        names_in += ["rows"]
        if not phase.finish:
            names_in += ["dq", "tall"]
        names_out += ["dq"] + list(sizes)
    if phase.last:
        names_in += ["out_t"]
        names_out += ["rows0", "rows1"]
    inputs = {name: state[name] for name in names_in}
    for number, array in enumerate(ps):
        inputs["p%d" % number], inputs["m%d" % number] = array
    seen = {}

    def reference_to(array):
        if id(array) not in seen:
            seen[id(array)] = "big%d" % len(seen)
            inputs[seen[id(array)]] = array
        return seen[id(array)]

    for array in after:
        reference_to(array)
    kv_at = [(reference_to(array), at) for array, at in kvs]
    names = list(inputs)
    places = {i: pl.ANY for i, name in enumerate(names) if name.startswith("big")}
    places.update({i: smem for i, name in enumerate(names) if name in ("flags", "mask")})
    small = (8, 128)
    results = call(
        functools.partial(phase_kernel, phase, names, names_out, kv_at),
        list(inputs.values()),
        [shapes[name] for name in names_out],
        scratch=[
            pltpu.VMEM((count, tokens, lanes), BF16),
            pltpu.VMEM((2, 2, half // HEAD_DIM * ROWS, tokens) if phase.forward else (1, 1) + small, F32),
            pltpu.VMEM((1, wide), F32),
            pltpu.SMEM((8,), jnp.int32),
            pltpu.VMEM((half // HEAD_DIM * ROWS, tokens), BF16),
            pltpu.VMEM((tokens, lanes) if phase.backward else small, F32),
            pltpu.VMEM((2, wide, depth) if phase.backward else (1, 16, 128), BF16),
            pltpu.VMEM((tokens, wide) if phase.backward else (16, 128), BF16),
            pltpu.SemaphoreType.DMA((count,)),
        ],
        mib=24,
        cost=cost,
        places=places,
    )
    state.update(zip(names_out, results))
    return state


def local(queries, key_tokens, value_tokens, cotangent, window_mask):
    shape = queries.shape
    features = shape[-1]
    tokens = queries.size // features
    tile = ((tokens, features), BF16)
    two = ((2, tokens, features), BF16)

    keep, send = call(
        split_kernel,
        [jnp.stack([x.reshape(tokens, features) for x in (key_tokens, value_tokens, queries, cotangent)])],
        [two, two],
    )
    recv = near(send)
    depth, wide = features - 128, features // 2 // HEAD_DIM * tokens
    flags, own_wide = call(
        functools.partial(early_kernel, lax.axis_size("tm")),
        [window_mask, keep],
        [((FLAGS,), jnp.int32, pltpu.SMEM), ((2, 1, depth, wide), BF16)],
        places={0: pltpu.SMEM},
    )
    both, to_far, rows = call(merge_kernel, [keep, recv, own_wide], [two, tile, two], places={2: pl.ANY})
    far_own = far(to_far)
    both_even = in_time(both, 0)
    both_odd = in_time(both, 1)
    state = {"flags": flags, "own_wide": own_wide, "rows": rows}
    state = run_phase(Phase(forward=[0, 3], first=True), state, [(both, 0), (both, 1)], [], COSTS[0])
    p_own = state["p"], state["m"]
    state["acc"], far_own = lax.optimization_barrier((state["acc"], far_own))
    far_even = in_time(far_own, 0)
    far_odd = in_time(far_own, 1)
    times = [(both_even, 0), (both_even, 1), (both_odd, 0), (both_odd, 1)]
    state = run_phase(Phase(forward=[6]), state, [(far_own, None)], [], COSTS[6])
    p_far = state["p"], state["m"]
    state = run_phase(Phase(forward=[1, 4, 2, 5]), state, times, [], COSTS[1])
    p_times = state["p"], state["m"]
    state = run_phase(
        Phase(forward=[7, 8], backward=[([7, 8], [0, 1])], targets={7: ("g_even", None), 8: ("g_odd", None)}),
        state,
        [(far_even, None), (far_odd, None)],
        [],
        COSTS[2],
    )
    hop_even = in_time(state["g_even"], 0)
    hop_odd = in_time(state["g_odd"], 1)
    state = run_phase(
        Phase(
            backward=[([1, 4, 2, 5], [0, 1, 2, 3])],
            targets={1: ("g_te", 0), 4: ("g_te", 1), 2: ("g_to", 0), 5: ("g_to", 1)},
        ),
        state,
        times,
        [p_times],
        COSTS[3],
    )
    from_even = in_time(state["g_te"], 0)
    from_odd = in_time(state["g_to"], 1)
    state = run_phase(
        Phase(backward=[([6], [0])], targets={6: ("g_far", None)}),
        state,
        [(far_own, None)],
        [p_far],
        COSTS[4],
    )
    (to_far,) = call(far_sum_kernel, [state["g_far"], hop_even, hop_odd], [tile])
    from_far = far(to_far)
    state = run_phase(
        Phase(backward=[([0, 3], [0, 1])], targets={0: ("g_own", 0), 3: ("g_own", 1)}, last=True),
        state,
        [(both, 0), (both, 1)],
        [p_own],
        COSTS[5],
    )
    rows_recv = near(state["rows1"])
    out, dq = call(join_rows_kernel, [state["rows0"], rows_recv], [tile, tile])
    mine, partner = call(total_kernel, [state["g_own"], from_even, from_odd, from_far], [tile, tile])
    recv_total = near(partner)
    key_grad, value_grad = call(
        join_lanes_kernel,
        [mine, recv_total],
        [tile + (pl.ANY,), tile + (pl.ANY,)],
        scratch=[pltpu.VMEM((2, tokens, features), BF16), pltpu.SemaphoreType.DMA((2, CHUNKS))],
    )
    return tuple(x.reshape(shape) for x in (out, dq, key_grad, value_grad))


def solution(mesh):
    spec = P("tm", "height", None, "heads")
    return jax.shard_map(
        local, mesh=mesh, in_specs=(spec, spec, spec, spec, P()), out_specs=(spec,) * 4, check_vma=False
    )
```

```python
import functools

import jax
import jax.numpy as jnp
from jax import lax
from jax.experimental import pallas as pl
from jax.experimental.pallas import tpu as pltpu
from jax.sharding import PartitionSpec as P

HEAD_DIM = 64
LIMIT = 1e17
SCALE = HEAD_DIM ** -0.5
BF16 = jnp.bfloat16
F32 = jnp.float32
COST = 1.15e9
COSTS = (4, 4, 50, 1, 1, 1, 2)
MIB = 1024 * 1024
FLAGS = 18
CHUNKS = 4


def pairing(size, first):
    pairs = [(i, i + 1) for i in range(first, size - 1, 2)]
    return pairs + [(b, a) for a, b in pairs]


def near(array):
    return lax.ppermute(array, "height", pairing(lax.axis_size("height"), 0))


def far(array):
    peers = lax.axis_size("height")
    return lax.ppermute(array, "height", [(i, (i + 2) % peers) for i in range(peers)])


def in_time(array, first):
    return lax.ppermute(array, "tm", pairing(lax.axis_size("tm"), first))


def offset(kind, index):
    even = 1 - 2 * lax.rem(index, 2)
    return jnp.where(kind == 0, 0, jnp.where(kind == 1, even, -even))


def near_far_tile(height):
    return jnp.where((height == 1) | (height == 2), 0, 1)


def allowed(mask_ref, unit, time, height, tiles_t):
    slot, query = unit // 2, unit % 2
    column, place = slot // 3, slot % 3
    other = height + offset(1, height)
    query_height = height if query == 0 else other
    key_height = (height, other, jnp.where(height < 2, 2, 1))[column]
    dt = offset(place, time)
    dh = key_height - query_height
    inside = (time + dt >= 0) & (time + dt < tiles_t) & (dh >= -1) & (dh <= 1)
    if slot == 3 * query:
        return inside
    flag = mask_ref[time, query_height, jnp.clip(3 * (dt + 1) + dh + 1, 0, 8)]
    return inside & (flag == 1)


def choose(index, values):
    result = jnp.int32(values[-1])
    for at, value in enumerate(values[:-1]):
        result = jnp.where(index == at, value, result)
    return result


def call(kernel, inputs, outputs, scratch=(), mib=16, cost=1, places=None):
    vmem = pl.BlockSpec(memory_space=pltpu.VMEM)
    places = places or {}
    return pl.pallas_call(
        kernel,
        out_shape=[jax.ShapeDtypeStruct(*output[:2]) for output in outputs],
        in_specs=[pl.BlockSpec(memory_space=places[i]) if i in places else vmem for i in range(len(inputs))],
        out_specs=[pl.BlockSpec(memory_space=output[2]) if len(output) > 2 else vmem for output in outputs],
        scratch_shapes=list(scratch),
        compiler_params=pltpu.CompilerParams(vmem_limit_bytes=mib * MIB),
        cost_estimate=pl.CostEstimate(flops=int(cost * COST), bytes_accessed=1000, transcendentals=0),
    )(*inputs)


def swapped_halves(x):
    return pltpu.roll(x.astype(F32), x.shape[1] // 2, 1).astype(x.dtype)


def lane_is_low(shape):
    return lax.broadcasted_iota(jnp.int32, shape, 1) < shape[1] // 2


def split_kernel(kvqd_ref, keep_ref, send_ref):
    odd = lax.rem(lax.axis_index("height"), 2)
    low = lane_is_low(kvqd_ref.shape[1:])
    for row in range(2):
        a, b = kvqd_ref[2 * row], kvqd_ref[2 * row + 1]
        if row == 1:
            a = (a.astype(F32) * SCALE).astype(BF16)
        first = jnp.where(low, a, swapped_halves(b))
        second = jnp.where(low, swapped_halves(a), b)

        @pl.when(odd == 0)
        def _():
            keep_ref[row] = first
            send_ref[row] = second

        @pl.when(odd != 0)
        def _():
            keep_ref[row] = second
            send_ref[row] = first


def groups(part, heads):
    found = {}
    for j in range(heads):
        found.setdefault((part * heads + j) * HEAD_DIM // 128, []).append(j)
    return list(found.items())


def block(part, tile, of, tokens):
    return slice((tile - part) * 128, (tile - part + 1) * 128), slice(of[0] * tokens, (of[-1] + 1) * tokens)


def put_wide(query, rows, wide):
    tokens, lanes = rows.shape
    half = lanes // 2
    pad = wide.shape[2] - half
    turned = rows.T
    heads = half // HEAD_DIM
    for x in range(2):
        for tile, of in groups(x, heads):
            deep, columns = block(x, tile, of, tokens)
            wide[x, query, deep, columns] = jnp.zeros((128, len(of) * tokens), wide.dtype)
        for j in range(heads):
            at = x * pad + j * HEAD_DIM
            source = x * half + j * HEAD_DIM
            wide[x, query, at : at + HEAD_DIM, j * tokens : (j + 1) * tokens] = turned[source : source + HEAD_DIM]


def put_tall(query, rows, factor, target):
    tokens, lanes = rows.shape
    half = lanes // 2
    heads = half // HEAD_DIM
    padded = jnp.zeros((8 - heads, tokens), F32)
    by_head = jnp.concatenate([factor[:, j * tokens : (j + 1) * tokens] for j in range(heads)] + [padded], axis=0).T
    lane = lax.broadcasted_iota(jnp.int32, (1, lanes), 1)
    lane = jnp.where(lane >= half, lane - half, lane)
    scale = jnp.zeros(rows.shape, F32)
    for j in range(heads):
        here = (lane >= j * HEAD_DIM) & (lane < (j + 1) * HEAD_DIM)
        scale = jnp.where(here, by_head[:, j : j + 1], scale)
    scaled = rows.astype(F32) * scale
    position = lax.broadcasted_iota(jnp.int32, (1, 128), 1)
    for x in range(2):
        for tile, of in groups(x, heads):
            values = scaled[:, tile * 128 : (tile + 1) * 128]
            for j in of:
                start = (x * heads + j) * HEAD_DIM - tile * 128
                here = (position >= start) & (position < start + HEAD_DIM)
                deep, _ = block(x, tile, of, tokens)
                target(x)[j * tokens : (j + 1) * tokens, deep] = jnp.where(here, values, 0.0).astype(BF16)


def early_kernel(tiles_t, mask_ref, keep_ref, flags_ref, wide_ref):
    time = lax.axis_index("tm")
    height = lax.axis_index("height")
    for unit in range(FLAGS):
        flags_ref[unit] = allowed(mask_ref, unit, time, height, tiles_t).astype(jnp.int32)
    put_wide(0, keep_ref[1], wide_ref)


def merge_kernel(keep_ref, recv_ref, after_ref, both_ref, far_ref, rows_ref):
    del after_ref
    rows_ref[0] = keep_ref[1]
    rows_ref[1] = recv_ref[1]
    both_ref[0] = keep_ref[0]
    both_ref[1] = recv_ref[0]
    beside = near_far_tile(lax.axis_index("height"))

    @pl.when(beside == 0)
    def _():
        far_ref[...] = keep_ref[0]

    @pl.when(beside != 0)
    def _():
        far_ref[...] = recv_ref[0]


def join_rows_kernel(own_ref, recv_ref, out_ref, dq_ref):
    odd = lax.rem(lax.axis_index("height"), 2)
    half = own_ref.shape[0] // 2

    def join(low, high):
        for at, ref in enumerate((out_ref, dq_ref)):
            rows = slice(at * half, (at + 1) * half)
            ref[...] = jnp.concatenate([low[rows], high[rows]], axis=0).T

    @pl.when(odd == 0)
    def _():
        join(own_ref, recv_ref)

    @pl.when(odd != 0)
    def _():
        join(recv_ref, own_ref)


def join_lanes_kernel(own_ref, recv_ref, key_hbm, value_hbm, staged, sem):
    odd = lax.rem(lax.axis_index("height"), 2)
    rows = own_ref.shape[0] // CHUNKS
    copies = []
    for c in range(CHUNKS):
        at = slice(c * rows, (c + 1) * rows)

        def join(low_ref, high_ref):
            low, high = low_ref[at], high_ref[at]
            lanes_low = lane_is_low(low.shape)
            staged[0, at] = jnp.where(lanes_low, low, swapped_halves(high))
            staged[1, at] = jnp.where(lanes_low, swapped_halves(low), high)

        @pl.when(odd == 0)
        def _():
            join(own_ref, recv_ref)

        @pl.when(odd != 0)
        def _():
            join(recv_ref, own_ref)

        for n, target in enumerate((key_hbm, value_hbm)):
            copies.append(pltpu.make_async_copy(staged.at[n, at], target.at[at], sem.at[n, c]))
            copies[-1].start()
    for copy in copies:
        copy.wait()


def far_sum_kernel(own_ref, even_ref, odd_ref, out_ref):
    total = own_ref[...].astype(F32) + even_ref[...].astype(F32) + odd_ref[...].astype(F32)
    out_ref[...] = total.astype(BF16)


def total_kernel(own_ref, even_ref, odd_ref, far_ref, mine_ref, partner_ref):
    beside = near_far_tile(lax.axis_index("height"))
    for tile, ref in enumerate((mine_ref, partner_ref)):
        total = own_ref[tile].astype(F32) + even_ref[tile].astype(F32) + odd_ref[tile].astype(F32)
        share = jnp.where(beside == tile, 1.0, 0.0).astype(F32)
        ref[...] = (total + far_ref[...].astype(F32) * share).astype(BF16)


class Phase:
    def __init__(self, forward=(), backward=(), targets=None, first=False, last=False):
        self.forward = list(forward)
        self.segments = list(backward)
        self.backward = [slot for slots, _ in backward for slot in slots]
        self.targets = targets or {}
        self.first, self.last = first, last
        self.finish = bool(forward) and bool(backward)
        self.slots = self.forward + [slot for slot in self.backward if slot not in self.forward]


def phase_kernel(phase, names_in, names_out, kv_at, *refs):
    ins = dict(zip(names_in, refs))
    outs = dict(zip(names_out, refs[len(names_in):]))
    kv, acc_s, sums, state_s, turned, g_acc, tall_s, slopes, dq_s, p_s, m_s, kv_sem = refs[len(names_in) + len(names_out):]
    count, tokens, lanes = kv.shape
    half = lanes // 2
    heads = half // HEAD_DIM
    depth = lanes - 128
    key_lanes, value_lanes = slice(0, depth), slice(lanes - depth, lanes)
    pad = depth - half
    columns = [slice(j * tokens, (j + 1) * tokens) for j in range(heads)]
    rows = [slice(j * HEAD_DIM, (j + 1) * HEAD_DIM) for j in range(heads)]
    flags = ins["flags"]

    def ok(slot):
        return (flags[2 * slot] + flags[2 * slot + 1]) != 0

    def load_kv(i):
        name, at = kv_at[i]
        source = ins[name] if at is None else ins[name].at[at]
        return pltpu.make_async_copy(source, kv.at[i], kv_sem.at[i])

    def start_load(i):
        if i < count:
            @pl.when(ok(phase.slots[i]))
            def _():
                load_kv(i).start()

    start_load(0)
    start_load(1)

    if phase.first:
        wide = outs["wide"]
        wide[:, 0:1] = ins["own_wide"][...]
        put_wide(1, ins["rows"][1], wide)
    else:
        wide = ins["wide"]

    if phase.forward:
        stat = outs["stat"]
        acc, p_out, m_out = (acc_s, p_s, m_s) if phase.finish else (outs["acc"], outs["p"], outs["m"])

        def attempt(number, carry):
            def begin():
                if phase.first:
                    stat[...] = jnp.zeros_like(stat)
                    stat[:, 0:1] = jnp.full((2, 1, stat.shape[2]), -1e30, F32)
                    acc[...] = jnp.zeros_like(acc)
                    state_s[1] = 0
                    state_s[2] = 0
                else:
                    stat[...] = ins["stat"][...]
                    acc[...] = ins["acc"][...]

                @pl.when(number != 0)
                def _():
                    stat[:, 3:4] = jnp.ones((2, 1, stat.shape[2]), F32)

            def forward(i, carry):
                slot = choose(i, phase.forward)
                for j in range(len(phase.forward)):
                    @pl.when((i == j) & (number == 0))
                    def _():
                        start_load(j + 2)

                    @pl.when(ok(slot) & (i == j) & (number == 0))
                    def _():
                        load_kv(j).wait()

                @pl.when(ok(slot))
                def _():
                    turned[...] = kv[i, :, value_lanes].T[pad:]

                def with_query(query, carry):
                    unit = 2 * slot + query

                    def scores(tile, of):
                        deep, at = block(0, tile, of, tokens)
                        keys = kv[i, :, tile * 128 : (tile + 1) * 128]
                        return at, jnp.dot(keys, wide[0, query, deep, at], preferred_element_type=F32)

                    raised = number != 0
                    if phase.first:
                        raised = raised | (state_s[1 + query] == 0)

                    @pl.when((flags[unit] != 0) & raised)
                    def _():
                        m_old = stat[query, 0:1]
                        for tile, of in groups(0, heads):
                            at, s = scores(tile, of)
                            sums[:, at] = jnp.max(s, axis=0, keepdims=True)
                        m_new = jnp.maximum(m_old, sums[...])
                        alpha = jnp.exp(m_old - m_new)
                        stat[query, 0:1] = m_new
                        stat[query, 1:2] = stat[query, 1:2] * alpha
                        for j in range(heads):
                            acc[query, rows[j]] = acc[query, rows[j]] * alpha[:, columns[j]]
                        if phase.first:
                            state_s[1 + query] = 1

                    @pl.when(flags[unit] != 0)
                    def _():
                        m_out[2 * i + query] = stat[query, 0:1]
                        for tile, of in groups(0, heads):
                            at, s = scores(tile, of)
                            e = jnp.exp(s - stat[query, 0:1, at])
                            stat[query, 1:2, at] += jnp.sum(e, axis=0, keepdims=True)
                            p_out[2 * i + query, :, at] = e.astype(BF16)
                        for j in range(heads):
                            acc[query, rows[j]] += jnp.dot(
                                turned[rows[j]], p_out[2 * i + query, :, columns[j]], preferred_element_type=F32
                            )

                    return carry

                lax.fori_loop(0, 2, with_query, 0)
                return carry

            @pl.when(state_s[0] != 0)
            def _():
                begin()
                lax.fori_loop(0, len(phase.forward), forward, 0)
                state_s[0] = jnp.where(jnp.max(stat[:, 1:2]) < LIMIT, 0, 1)

            return carry

        state_s[0] = 1
        lax.fori_loop(0, 2, attempt, 0)
    else:
        stat = ins["stat"]

    if phase.finish:
        tall = outs["tall"]
        for query in range(2):
            inverse = 1.0 / stat[query, 1:2]
            stat[query, 1:2] = inverse
            for j in range(heads):
                out_t = (acc[query, rows[j]] * inverse[:, columns[j]]).astype(BF16)
                outs["out_t"][query, rows[j]] = out_t
                at = slice(pad + j * HEAD_DIM, pad + (j + 1) * HEAD_DIM)
                both = wide[1, query, at, columns[j]].astype(F32) * out_t.astype(F32)
                stat[query, 2:3, columns[j]] = jnp.sum(both, axis=0, keepdims=True)
            put_tall(query, ins["rows"][query], inverse, lambda x: tall.at[x, query])
    elif phase.backward:
        tall = ins["tall"]

    if phase.backward:
        dq = dq_s if phase.last else outs["dq"]
        moved = jnp.max(stat[0, 3:4, 0:128]) > 0.0
        if phase.finish:
            dq[...] = jnp.zeros_like(dq)
        else:
            dq[...] = ins["dq"][...]
        for number, (slots, places) in enumerate(phase.segments):
            p_in = p_s if phase.finish else ins["p%d" % number]
            m_in = m_s if phase.finish else ins["m%d" % number]
            where = [phase.slots.index(slot) for slot in slots]
            loading = len(phase.forward)

            def backward(step, carry):
                slot = choose(step, slots)
                place = choose(step, places)
                i = choose(step, where)
                for j in range(len(slots)):
                    if where[j] >= loading:
                        @pl.when(step == j)
                        def _():
                            start_load(where[j] + 2)

                        @pl.when(ok(slot) & (step == j))
                        def _():
                            load_kv(where[j]).wait()

                g_acc[...] = jnp.zeros_like(g_acc)

                @pl.when(ok(slot))
                def _():
                    turned[...] = kv[i, :, key_lanes].T[:half]

                def with_query(query, carry):
                    unit = 2 * slot + query
                    good = flags[unit] != 0

                    def terms(tall_of, gamma):
                        at_p = 2 * place + query
                        for tile, of in groups(1, heads):
                            deep, at = block(1, tile, of, tokens)
                            values = kv[i, :, tile * 128 : (tile + 1) * 128]
                            dp = jnp.dot(values, wide[1, query, deep, at], preferred_element_type=F32)
                            slopes[:, at] = p_in[at_p, :, at] * (dp - stat[query, 2:3, at]).astype(BF16)
                        for x in range(2):
                            for tile, of in groups(x, heads):
                                deep, at = block(x, tile, of, tokens)
                                left = p_in[at_p, :, at] if x else slopes[:, at]
                                g_acc[:, tile * 128 : (tile + 1) * 128] += jnp.dot(
                                    left, tall_of(x)[at, deep], preferred_element_type=F32
                                )
                        for j in range(heads):
                            term = jnp.dot(turned[rows[j]], slopes[:, columns[j]], preferred_element_type=F32)
                            dq[query, rows[j]] += term if gamma is None else term * gamma[:, columns[j]]

                    @pl.when(good & jnp.logical_not(moved))
                    def _():
                        terms(lambda x: tall.at[x, query], None)

                    @pl.when(good & moved)
                    def _():
                        gamma = jnp.exp(m_in[2 * place + query] - stat[query, 0:1])
                        factor = gamma * stat[query, 1:2]
                        put_tall(query, ins["rows"][query], factor, lambda x: tall_s.at[x])
                        terms(lambda x: tall_s.at[x], gamma)

                    return carry

                lax.fori_loop(0, 2, with_query, 0)
                for j, s in enumerate(slots):
                    name, at = phase.targets[s]
                    target = outs[name] if at is None else outs[name].at[at]

                    @pl.when(step == j)
                    def _():
                        target[...] = g_acc[...].astype(BF16)

                return carry

            lax.fori_loop(0, len(slots), backward, 0)
        if phase.last:
            for query in range(2):
                result = outs["rows%d" % query]
                result[:half] = ins["out_t"][query]
                for j in range(heads):
                    at = slice(half + j * HEAD_DIM, half + (j + 1) * HEAD_DIM)
                    result[at] = (dq[query, rows[j]] * (stat[query, 1:2, columns[j]] * SCALE)).astype(BF16)


def run_phase(phase, state, kvs, ps, cost, after=()):
    tokens, lanes = state["rows"].shape[1:]
    half = lanes // 2
    depth = lanes - 128
    wide = half // HEAD_DIM * tokens
    count = len(phase.slots)
    smem = pltpu.SMEM
    tile = ((tokens, lanes), BF16)
    shapes = {
        "wide": ((2, 2, depth, wide), BF16),
        "tall": ((2, 2, wide, depth), BF16),
        "stat": ((2, 4, wide), F32),
        "m": ((2 * len(phase.forward), 1, wide), F32),
        "acc": ((2, half, tokens), F32),
        "dq": ((2, half, tokens), F32),
        "out_t": ((2, half, tokens), BF16),
        "rows0": tile,
        "rows1": tile,
        "p": ((2 * len(phase.forward), tokens, wide), BF16),
    }
    sizes = {}
    for name, at in phase.targets.values():
        sizes[name] = None if at is None else max(sizes.get(name, 0), at + 1)
    shapes.update({n: tile if size is None else ((size, tokens, lanes), BF16) for n, size in sizes.items()})
    names_in, names_out = [], []
    if phase.first:
        names_in += ["flags", "own_wide", "rows"]
        names_out += ["wide"]
    else:
        names_in += ["flags", "wide", "stat"]
    if phase.forward:
        names_out += ["stat"]
        if not phase.first:
            names_in += ["acc"]
        if not phase.finish:
            names_out += ["m", "p", "acc"]
    if phase.finish:
        names_out += ["out_t", "tall"]
    if phase.backward:
        names_in += ["rows"]
        if not phase.finish:
            names_in += ["dq", "tall"]
        names_out += ([] if phase.last else ["dq"]) + list(sizes)
    if phase.last:
        names_in += ["out_t"]
        names_out += ["rows0", "rows1"]
    inputs = {name: state[name] for name in names_in}
    for number, array in enumerate(ps):
        inputs["p%d" % number], inputs["m%d" % number] = array
    seen = {}

    def reference_to(array):
        if id(array) not in seen:
            seen[id(array)] = "big%d" % len(seen)
            inputs[seen[id(array)]] = array
        return seen[id(array)]

    for array in after:
        reference_to(array)
    kv_at = [(reference_to(array), at) for array, at in kvs]
    names = list(inputs)
    places = {i: pl.ANY for i, name in enumerate(names) if name.startswith("big")}
    places.update({i: smem for i, name in enumerate(names) if name in ("flags", "mask")})
    small = (8, 128)
    results = call(
        functools.partial(phase_kernel, phase, names, names_out, kv_at),
        list(inputs.values()),
        [shapes[name] for name in names_out],
        scratch=[
            pltpu.VMEM((count, tokens, lanes), BF16),
            pltpu.VMEM(shapes["acc"][0] if phase.finish else small, F32),
            pltpu.VMEM((1, wide), F32),
            pltpu.SMEM((8,), jnp.int32),
            pltpu.VMEM((half, tokens), BF16),
            pltpu.VMEM((tokens, lanes) if phase.backward else small, F32),
            pltpu.VMEM((2, wide, depth) if phase.backward else (1, 16, 128), BF16),
            pltpu.VMEM((tokens, wide) if phase.backward else (16, 128), BF16),
            pltpu.VMEM(shapes["dq"][0] if phase.last else small, F32),
            pltpu.VMEM(shapes["p"][0] if phase.finish else (16, 128), BF16),
            pltpu.VMEM(shapes["m"][0] if phase.finish else small, F32),
            pltpu.SemaphoreType.DMA((count,)),
        ],
        mib=24,
        cost=cost,
        places=places,
    )
    state.update(zip(names_out, results))
    return state


def local(queries, key_tokens, value_tokens, cotangent, window_mask):
    shape = queries.shape
    features = shape[-1]
    tokens = queries.size // features
    tile = ((tokens, features), BF16)
    two = ((2, tokens, features), BF16)

    keep, send = call(
        split_kernel,
        [jnp.stack([x.reshape(tokens, features) for x in (key_tokens, value_tokens, queries, cotangent)])],
        [two, two],
    )
    recv = near(send)
    depth, wide = features - 128, features // 2 // HEAD_DIM * tokens
    flags, own_wide = call(
        functools.partial(early_kernel, lax.axis_size("tm")),
        [window_mask, keep],
        [((FLAGS,), jnp.int32, pltpu.SMEM), ((2, 1, depth, wide), BF16)],
        places={0: pltpu.SMEM},
    )
    both, to_far, rows = call(merge_kernel, [keep, recv, own_wide], [two, tile, two], places={2: pl.ANY})
    far_own = far(to_far)
    both_even = in_time(both, 0)
    both_odd = in_time(both, 1)
    state = {"flags": flags, "own_wide": own_wide, "rows": rows}
    state = run_phase(Phase(forward=[0, 3], first=True), state, [(both, 0), (both, 1)], [], COSTS[0])
    p_own = state["p"], state["m"]
    state["acc"], far_own = lax.optimization_barrier((state["acc"], far_own))
    far_even = in_time(far_own, 0)
    far_odd = in_time(far_own, 1)
    times = [(both_even, 0), (both_even, 1), (both_odd, 0), (both_odd, 1)]
    state = run_phase(Phase(forward=[6]), state, [(far_own, None)], [], COSTS[6])
    p_far = state["p"], state["m"]
    state = run_phase(Phase(forward=[1, 4, 2, 5]), state, times, [], COSTS[1])
    p_times = state["p"], state["m"]
    state = run_phase(
        Phase(forward=[7, 8], backward=[([7, 8], [0, 1])], targets={7: ("g_even", None), 8: ("g_odd", None)}),
        state,
        [(far_even, None), (far_odd, None)],
        [],
        COSTS[2],
    )
    hop_even = in_time(state["g_even"], 0)
    hop_odd = in_time(state["g_odd"], 1)
    state = run_phase(
        Phase(
            backward=[([1, 4, 2, 5], [0, 1, 2, 3])],
            targets={1: ("g_te", 0), 4: ("g_te", 1), 2: ("g_to", 0), 5: ("g_to", 1)},
        ),
        state,
        times,
        [p_times],
        COSTS[3],
    )
    from_even = in_time(state["g_te"], 0)
    from_odd = in_time(state["g_to"], 1)
    state = run_phase(
        Phase(backward=[([6], [0])], targets={6: ("g_far", None)}),
        state,
        [(far_own, None)],
        [p_far],
        COSTS[4],
    )
    (to_far,) = call(far_sum_kernel, [state["g_far"], hop_even, hop_odd], [tile])
    from_far = far(to_far)
    state = run_phase(
        Phase(backward=[([0, 3], [0, 1])], targets={0: ("g_own", 0), 3: ("g_own", 1)}, last=True),
        state,
        [(both, 0), (both, 1)],
        [p_own],
        COSTS[5],
    )
    rows_recv = near(state["rows1"])
    out, dq = call(join_rows_kernel, [state["rows0"], rows_recv], [tile, tile])
    mine, partner = call(total_kernel, [state["g_own"], from_even, from_odd, from_far], [tile, tile])
    recv_total = near(partner)
    key_grad, value_grad = call(
        join_lanes_kernel,
        [mine, recv_total],
        [tile + (pl.ANY,), tile + (pl.ANY,)],
        scratch=[pltpu.VMEM((2, tokens, features), BF16), pltpu.SemaphoreType.DMA((2, CHUNKS))],
    )
    return tuple(x.reshape(shape) for x in (out, dq, key_grad, value_grad))


def solution(mesh):
    spec = P("tm", "height", None, "heads")
    return jax.shard_map(
        local, mesh=mesh, in_specs=(spec, spec, spec, spec, P()), out_specs=(spec,) * 4, check_vma=False
    )
```

```python
import functools

import jax
import jax.numpy as jnp
from jax import lax
from jax.experimental import pallas as pl
from jax.experimental.pallas import tpu as pltpu
from jax.sharding import PartitionSpec as P

HEAD_DIM = 64
LIMIT = 1e17
FLOOR = 1e-17
SCALE = HEAD_DIM ** -0.5
BF16 = jnp.bfloat16
F32 = jnp.float32
COST = 1.15e9
COSTS = (2, 4, 50, 1, 1, 1, 3)
MIB = 1024 * 1024
FLAGS = 18
CHUNKS = 4


def pairing(size, first):
    pairs = [(i, i + 1) for i in range(first, size - 1, 2)]
    return pairs + [(b, a) for a, b in pairs]


def near(array):
    return lax.ppermute(array, "height", pairing(lax.axis_size("height"), 0))


def far(array):
    peers = lax.axis_size("height")
    return lax.ppermute(array, "height", [(i, (i + 2) % peers) for i in range(peers)])


def in_time(array, first):
    return lax.ppermute(array, "tm", pairing(lax.axis_size("tm"), first))


def offset(kind, index):
    even = 1 - 2 * lax.rem(index, 2)
    return jnp.where(kind == 0, 0, jnp.where(kind == 1, even, -even))


def near_far_tile(height):
    return jnp.where((height == 1) | (height == 2), 0, 1)


def allowed(mask_ref, unit, time, height, tiles_t):
    slot, query = unit // 2, unit % 2
    column, place = slot // 3, slot % 3
    other = height + offset(1, height)
    query_height = height if query == 0 else other
    key_height = (height, other, jnp.where(height < 2, 2, 1))[column]
    dt = offset(place, time)
    dh = key_height - query_height
    inside = (time + dt >= 0) & (time + dt < tiles_t) & (dh >= -1) & (dh <= 1)
    if slot == 3 * query:
        return inside
    flag = mask_ref[time, query_height, jnp.clip(3 * (dt + 1) + dh + 1, 0, 8)]
    return inside & (flag == 1)


def choose(index, values):
    result = jnp.int32(values[-1])
    for at, value in enumerate(values[:-1]):
        result = jnp.where(index == at, value, result)
    return result


def call(kernel, inputs, outputs, scratch=(), mib=16, cost=1, places=None):
    vmem = pl.BlockSpec(memory_space=pltpu.VMEM)
    places = places or {}
    return pl.pallas_call(
        kernel,
        out_shape=[jax.ShapeDtypeStruct(*output[:2]) for output in outputs],
        in_specs=[pl.BlockSpec(memory_space=places[i]) if i in places else vmem for i in range(len(inputs))],
        out_specs=[pl.BlockSpec(memory_space=output[2]) if len(output) > 2 else vmem for output in outputs],
        scratch_shapes=list(scratch),
        compiler_params=pltpu.CompilerParams(vmem_limit_bytes=mib * MIB),
        cost_estimate=pl.CostEstimate(flops=int(cost * COST), bytes_accessed=1000, transcendentals=0),
    )(*inputs)


def swapped_halves(x):
    return pltpu.roll(x.astype(F32), x.shape[1] // 2, 1).astype(x.dtype)


def lane_is_low(shape):
    return lax.broadcasted_iota(jnp.int32, shape, 1) < shape[1] // 2


def split_kernel(kvqd_ref, keep_kv_ref, keep_qd_ref, send_ref):
    odd = lax.rem(lax.axis_index("height"), 2)
    low = lane_is_low(kvqd_ref.shape[1:])
    for row in range(2):
        a, b = kvqd_ref[2 * row], kvqd_ref[2 * row + 1]
        if row == 1:
            a = (a.astype(F32) * SCALE).astype(BF16)
        first = jnp.where(low, a, swapped_halves(b))
        second = jnp.where(low, swapped_halves(a), b)

        keep_ref = (keep_kv_ref, keep_qd_ref)[row]

        @pl.when(odd == 0)
        def _():
            keep_ref[...] = first
            send_ref[row] = second

        @pl.when(odd != 0)
        def _():
            keep_ref[...] = second
            send_ref[row] = first


def groups(part, heads):
    found = {}
    for j in range(heads):
        found.setdefault((part * heads + j) * HEAD_DIM // 128, []).append(j)
    return list(found.items())


def block(part, tile, of, tokens):
    return slice((tile - part) * 128, (tile - part + 1) * 128), slice(of[0] * tokens, (of[-1] + 1) * tokens)


def put_wide(query, rows, wide):
    tokens, lanes = rows.shape
    half = lanes // 2
    pad = wide.shape[2] - half
    turned = rows.T
    heads = half // HEAD_DIM
    for x in range(2):
        for tile, of in groups(x, heads):
            deep, columns = block(x, tile, of, tokens)
            wide[x, query, deep, columns] = jnp.zeros((128, len(of) * tokens), wide.dtype)
        for j in range(heads):
            at = x * pad + j * HEAD_DIM
            source = x * half + j * HEAD_DIM
            wide[x, query, at : at + HEAD_DIM, j * tokens : (j + 1) * tokens] = turned[source : source + HEAD_DIM]


def put_tall(query, rows, factor, target):
    tokens, lanes = rows.shape
    half = lanes // 2
    heads = half // HEAD_DIM
    padded = jnp.zeros((8 - heads, tokens), F32)
    by_head = jnp.concatenate([factor[:, j * tokens : (j + 1) * tokens] for j in range(heads)] + [padded], axis=0).T
    lane = lax.broadcasted_iota(jnp.int32, (1, lanes), 1)
    lane = jnp.where(lane >= half, lane - half, lane)
    scale = jnp.zeros(rows.shape, F32)
    for j in range(heads):
        here = (lane >= j * HEAD_DIM) & (lane < (j + 1) * HEAD_DIM)
        scale = jnp.where(here, by_head[:, j : j + 1], scale)
    scaled = rows.astype(F32) * scale
    position = lax.broadcasted_iota(jnp.int32, (1, 128), 1)
    for x in range(2):
        for tile, of in groups(x, heads):
            values = scaled[:, tile * 128 : (tile + 1) * 128]
            for j in of:
                start = (x * heads + j) * HEAD_DIM - tile * 128
                here = (position >= start) & (position < start + HEAD_DIM)
                deep, _ = block(x, tile, of, tokens)
                target(x)[j * tokens : (j + 1) * tokens, deep] = jnp.where(here, values, 0.0).astype(BF16)


def early_kernel(tiles_t, mask_ref, keep_qd_ref, flags_ref, wide_ref):
    time = lax.axis_index("tm")
    height = lax.axis_index("height")
    for unit in range(FLAGS):
        flags_ref[unit] = allowed(mask_ref, unit, time, height, tiles_t).astype(jnp.int32)
    put_wide(0, keep_qd_ref[...], wide_ref)


def merge_kernel(keep_kv_ref, keep_qd_ref, recv_ref, after_ref, partner_ref, far_ref, rows_ref):
    del after_ref
    partner_ref[...] = recv_ref[0]
    rows_ref[0] = keep_qd_ref[...]
    rows_ref[1] = recv_ref[1]
    beside = near_far_tile(lax.axis_index("height"))

    @pl.when(beside == 0)
    def _():
        far_ref[...] = keep_kv_ref[...]

    @pl.when(beside != 0)
    def _():
        far_ref[...] = recv_ref[0]


def join_rows_kernel(own_ref, recv_ref, out_ref, dq_ref):
    odd = lax.rem(lax.axis_index("height"), 2)
    half = own_ref.shape[0] // 2

    def join(low, high):
        for at, ref in enumerate((out_ref, dq_ref)):
            rows = slice(at * half, (at + 1) * half)
            ref[...] = jnp.concatenate([low[rows], high[rows]], axis=0).T

    @pl.when(odd == 0)
    def _():
        join(own_ref, recv_ref)

    @pl.when(odd != 0)
    def _():
        join(recv_ref, own_ref)


def join_lanes_kernel(own_ref, recv_ref, key_hbm, value_hbm, staged, sem):
    odd = lax.rem(lax.axis_index("height"), 2)
    rows = own_ref.shape[0] // CHUNKS
    copies = []
    for c in range(CHUNKS):
        at = slice(c * rows, (c + 1) * rows)

        def join(low_ref, high_ref):
            low, high = low_ref[at], high_ref[at]
            lanes_low = lane_is_low(low.shape)
            staged[0, at] = jnp.where(lanes_low, low, swapped_halves(high))
            staged[1, at] = jnp.where(lanes_low, swapped_halves(low), high)

        @pl.when(odd == 0)
        def _():
            join(own_ref, recv_ref)

        @pl.when(odd != 0)
        def _():
            join(recv_ref, own_ref)

        for n, target in enumerate((key_hbm, value_hbm)):
            copies.append(pltpu.make_async_copy(staged.at[n, at], target.at[at], sem.at[n, c]))
            copies[-1].start()
    for copy in copies:
        copy.wait()


def far_sum_kernel(own_ref, even_ref, odd_ref, out_ref):
    total = own_ref[...].astype(F32) + even_ref[...].astype(F32) + odd_ref[...].astype(F32)
    out_ref[...] = total.astype(BF16)


def total_kernel(own_ref, even_ref, odd_ref, far_ref, mine_ref, partner_ref):
    beside = near_far_tile(lax.axis_index("height"))
    for tile, ref in enumerate((mine_ref, partner_ref)):
        total = own_ref[tile].astype(F32) + even_ref[tile].astype(F32) + odd_ref[tile].astype(F32)
        share = jnp.where(beside == tile, 1.0, 0.0).astype(F32)
        ref[...] = (total + far_ref[...].astype(F32) * share).astype(BF16)


class Phase:
    def __init__(self, forward=(), backward=(), targets=None, first=False, last=False):
        self.forward = list(forward)
        self.segments = list(backward)
        self.backward = [slot for slots, _ in backward for slot in slots]
        self.targets = targets or {}
        self.first, self.last = first, last
        self.finish = bool(forward) and bool(backward)
        self.slots = self.forward + [slot for slot in self.backward if slot not in self.forward]


def phase_kernel(phase, names_in, names_out, kv_at, *refs):
    ins = dict(zip(names_in, refs))
    outs = dict(zip(names_out, refs[len(names_in):]))
    kv, acc_s, sums, state_s, turned, g_acc, tall_s, slopes, dq_s, p_s, m_s, kv_sem = refs[len(names_in) + len(names_out):]
    count, tokens, lanes = kv.shape
    half = lanes // 2
    heads = half // HEAD_DIM
    depth = lanes - 128
    key_lanes, value_lanes = slice(0, depth), slice(lanes - depth, lanes)
    pad = depth - half
    columns = [slice(j * tokens, (j + 1) * tokens) for j in range(heads)]
    rows = [slice(j * HEAD_DIM, (j + 1) * HEAD_DIM) for j in range(heads)]
    flags = ins["flags"]

    def ok(slot):
        return (flags[2 * slot] + flags[2 * slot + 1]) != 0

    def load_kv(i):
        name, at = kv_at[i]
        source = ins[name] if at is None else ins[name].at[at]
        return pltpu.make_async_copy(source, kv.at[i], kv_sem.at[i])

    def start_load(i):
        if i < count:
            @pl.when(ok(phase.slots[i]))
            def _():
                load_kv(i).start()

    start_load(0)
    start_load(1)

    if phase.first:
        wide = outs["wide"]
        wide[:, 0:1] = ins["own_wide"][...]
        put_wide(1, ins["rows"][1], wide)
    else:
        wide = ins["wide"]

    if phase.forward:
        stat = outs["stat"]
        acc, p_out, m_out = (acc_s, p_s, m_s) if phase.finish else (outs["acc"], outs["p"], outs["m"])

        if phase.first:
            shifted = jnp.bool_(False)
        else:
            shifted = jnp.max(ins["stat"][0, 3:4, 0:128]) > 0.0

        def attempt(number, carry):
            def begin():
                if phase.first:
                    stat[...] = jnp.zeros_like(stat)
                    acc[...] = jnp.zeros_like(acc)
                else:
                    stat[...] = ins["stat"][...]
                    acc[...] = ins["acc"][...]

                @pl.when(number != 0)
                def _():
                    stat[:, 3:4] = jnp.ones((2, 1, stat.shape[2]), F32)
                    if phase.first:
                        stat[:, 0:1] = jnp.full((2, 1, stat.shape[2]), -1e30, F32)

            def forward(i, carry):
                slot = choose(i, phase.forward)
                for j in range(len(phase.forward)):
                    @pl.when((i == j) & (number == 0))
                    def _():
                        start_load(j + 2)

                    @pl.when(ok(slot) & (i == j) & (number == 0))
                    def _():
                        load_kv(j).wait()

                @pl.when(ok(slot))
                def _():
                    turned[...] = kv[i, :, value_lanes].T[pad:]

                def with_query(query, carry):
                    unit = 2 * slot + query

                    def scores(tile, of):
                        deep, at = block(0, tile, of, tokens)
                        keys = kv[i, :, tile * 128 : (tile + 1) * 128]
                        return at, jnp.dot(keys, wide[0, query, deep, at], preferred_element_type=F32)

                    exact = shifted | (number != 0)

                    def attend(weights_of):
                        for tile, of in groups(0, heads):
                            at, s = scores(tile, of)
                            e = weights_of(s, at)
                            stat[query, 1:2, at] += jnp.sum(e, axis=0, keepdims=True)
                            p_out[2 * i + query, :, at] = e.astype(BF16)
                        for j in range(heads):
                            acc[query, rows[j]] += jnp.dot(
                                turned[rows[j]], p_out[2 * i + query, :, columns[j]], preferred_element_type=F32
                            )

                    @pl.when((flags[unit] != 0) & jnp.logical_not(exact))
                    def _():
                        m_out[2 * i + query] = jnp.zeros((1, stat.shape[2]), F32)
                        attend(lambda s, at: jnp.exp(s))

                    @pl.when((flags[unit] != 0) & exact)
                    def _():
                        m_old = stat[query, 0:1]
                        for tile, of in groups(0, heads):
                            at, s = scores(tile, of)
                            sums[:, at] = jnp.max(s, axis=0, keepdims=True)
                        m_new = jnp.maximum(m_old, sums[...])
                        alpha = jnp.exp(m_old - m_new)
                        stat[query, 0:1] = m_new
                        m_out[2 * i + query] = m_new
                        stat[query, 1:2] = stat[query, 1:2] * alpha
                        for j in range(heads):
                            acc[query, rows[j]] = acc[query, rows[j]] * alpha[:, columns[j]]
                        attend(lambda s, at: jnp.exp(s - stat[query, 0:1, at]))

                    return carry

                lax.fori_loop(0, 2, with_query, 0)
                return carry

            @pl.when(state_s[0] != 0)
            def _():
                begin()
                lax.fori_loop(0, len(phase.forward), forward, 0)
                fits = jnp.max(stat[:, 1:2]) < LIMIT
                if phase.first:
                    fits = fits & (jnp.min(stat[:, 1:2]) > FLOOR)
                state_s[0] = jnp.where(fits, 0, 1)

            return carry

        state_s[0] = 1
        lax.fori_loop(0, 2, attempt, 0)
    else:
        stat = ins["stat"]

    if phase.finish:
        tall = outs["tall"]
        for query in range(2):
            inverse = 1.0 / stat[query, 1:2]
            stat[query, 1:2] = inverse
            for j in range(heads):
                out_t = (acc[query, rows[j]] * inverse[:, columns[j]]).astype(BF16)
                outs["out_t"][query, rows[j]] = out_t
                at = slice(pad + j * HEAD_DIM, pad + (j + 1) * HEAD_DIM)
                both = wide[1, query, at, columns[j]].astype(F32) * out_t.astype(F32)
                stat[query, 2:3, columns[j]] = jnp.sum(both, axis=0, keepdims=True)
            put_tall(query, ins["rows"][query], inverse, lambda x: tall.at[x, query])
    elif phase.backward:
        tall = ins["tall"]

    if phase.backward:
        dq = dq_s if phase.last else outs["dq"]
        moved = jnp.max(stat[0, 3:4, 0:128]) > 0.0
        if phase.finish:
            dq[...] = jnp.zeros_like(dq)
        else:
            dq[...] = ins["dq"][...]
        for number, (slots, places) in enumerate(phase.segments):
            p_in = p_s if phase.finish else ins["p%d" % number]
            m_in = m_s if phase.finish else ins["m%d" % number]
            where = [phase.slots.index(slot) for slot in slots]
            loading = len(phase.forward)

            def backward(step, carry):
                slot = choose(step, slots)
                place = choose(step, places)
                i = choose(step, where)
                for j in range(len(slots)):
                    if where[j] >= loading:
                        @pl.when(step == j)
                        def _():
                            start_load(where[j] + 2)

                        @pl.when(ok(slot) & (step == j))
                        def _():
                            load_kv(where[j]).wait()

                g_acc[...] = jnp.zeros_like(g_acc)

                @pl.when(ok(slot))
                def _():
                    turned[...] = kv[i, :, key_lanes].T[:half]

                def with_query(query, carry):
                    unit = 2 * slot + query
                    good = flags[unit] != 0

                    def terms(tall_of, gamma):
                        at_p = 2 * place + query
                        for tile, of in groups(1, heads):
                            deep, at = block(1, tile, of, tokens)
                            values = kv[i, :, tile * 128 : (tile + 1) * 128]
                            dp = jnp.dot(values, wide[1, query, deep, at], preferred_element_type=F32)
                            slopes[:, at] = p_in[at_p, :, at] * (dp - stat[query, 2:3, at]).astype(BF16)
                        for x in range(2):
                            for tile, of in groups(x, heads):
                                deep, at = block(x, tile, of, tokens)
                                left = p_in[at_p, :, at] if x else slopes[:, at]
                                g_acc[:, tile * 128 : (tile + 1) * 128] += jnp.dot(
                                    left, tall_of(x)[at, deep], preferred_element_type=F32
                                )
                        for j in range(heads):
                            term = jnp.dot(turned[rows[j]], slopes[:, columns[j]], preferred_element_type=F32)
                            dq[query, rows[j]] += term if gamma is None else term * gamma[:, columns[j]]

                    @pl.when(good & jnp.logical_not(moved))
                    def _():
                        terms(lambda x: tall.at[x, query], None)

                    @pl.when(good & moved)
                    def _():
                        gamma = jnp.exp(m_in[2 * place + query] - stat[query, 0:1])
                        factor = gamma * stat[query, 1:2]
                        put_tall(query, ins["rows"][query], factor, lambda x: tall_s.at[x])
                        terms(lambda x: tall_s.at[x], gamma)

                    return carry

                lax.fori_loop(0, 2, with_query, 0)
                for j, s in enumerate(slots):
                    name, at = phase.targets[s]
                    target = outs[name] if at is None else outs[name].at[at]

                    @pl.when(step == j)
                    def _():
                        target[...] = g_acc[...].astype(BF16)

                return carry

            lax.fori_loop(0, len(slots), backward, 0)
        if phase.last:
            for query in range(2):
                result = outs["rows%d" % query]
                result[:half] = ins["out_t"][query]
                for j in range(heads):
                    at = slice(half + j * HEAD_DIM, half + (j + 1) * HEAD_DIM)
                    result[at] = (dq[query, rows[j]] * (stat[query, 1:2, columns[j]] * SCALE)).astype(BF16)


def run_phase(phase, state, kvs, ps, cost, after=()):
    tokens, lanes = state["rows"].shape[1:]
    half = lanes // 2
    depth = lanes - 128
    wide = half // HEAD_DIM * tokens
    count = len(phase.slots)
    smem = pltpu.SMEM
    tile = ((tokens, lanes), BF16)
    shapes = {
        "wide": ((2, 2, depth, wide), BF16),
        "tall": ((2, 2, wide, depth), BF16),
        "stat": ((2, 4, wide), F32),
        "m": ((2 * len(phase.forward), 1, wide), F32),
        "acc": ((2, half, tokens), F32),
        "dq": ((2, half, tokens), F32),
        "out_t": ((2, half, tokens), BF16),
        "rows0": tile,
        "rows1": tile,
        "p": ((2 * len(phase.forward), tokens, wide), BF16),
    }
    sizes = {}
    for name, at in phase.targets.values():
        sizes[name] = None if at is None else max(sizes.get(name, 0), at + 1)
    shapes.update({n: tile if size is None else ((size, tokens, lanes), BF16) for n, size in sizes.items()})
    names_in, names_out = [], []
    if phase.first:
        names_in += ["flags", "own_wide", "rows"]
        names_out += ["wide"]
    else:
        names_in += ["flags", "wide", "stat"]
    if phase.forward:
        names_out += ["stat"]
        if not phase.first:
            names_in += ["acc"]
        if not phase.finish:
            names_out += ["m", "p", "acc"]
    if phase.finish:
        names_out += ["out_t", "tall"]
    if phase.backward:
        names_in += ["rows"]
        if not phase.finish:
            names_in += ["dq", "tall"]
        names_out += ([] if phase.last else ["dq"]) + list(sizes)
    if phase.last:
        names_in += ["out_t"]
        names_out += ["rows0", "rows1"]
    inputs = {name: state[name] for name in names_in}
    for number, array in enumerate(ps):
        inputs["p%d" % number], inputs["m%d" % number] = array
    seen = {}

    def reference_to(array):
        if id(array) not in seen:
            seen[id(array)] = "big%d" % len(seen)
            inputs[seen[id(array)]] = array
        return seen[id(array)]

    for array in after:
        reference_to(array)
    kv_at = [(reference_to(array), at) for array, at in kvs]
    names = list(inputs)
    places = {i: pl.ANY for i, name in enumerate(names) if name.startswith("big")}
    places.update({i: smem for i, name in enumerate(names) if name in ("flags", "mask")})
    small = (8, 128)
    results = call(
        functools.partial(phase_kernel, phase, names, names_out, kv_at),
        list(inputs.values()),
        [shapes[name] for name in names_out],
        scratch=[
            pltpu.VMEM((count, tokens, lanes), BF16),
            pltpu.VMEM(shapes["acc"][0] if phase.finish else small, F32),
            pltpu.VMEM((1, wide), F32),
            pltpu.SMEM((8,), jnp.int32),
            pltpu.VMEM((half, tokens), BF16),
            pltpu.VMEM((tokens, lanes) if phase.backward else small, F32),
            pltpu.VMEM((2, wide, depth) if phase.backward else (1, 16, 128), BF16),
            pltpu.VMEM((tokens, wide) if phase.backward else (16, 128), BF16),
            pltpu.VMEM(shapes["dq"][0] if phase.last else small, F32),
            pltpu.VMEM(shapes["p"][0] if phase.finish else (16, 128), BF16),
            pltpu.VMEM(shapes["m"][0] if phase.finish else small, F32),
            pltpu.SemaphoreType.DMA((count,)),
        ],
        mib=24,
        cost=cost,
        places=places,
    )
    state.update(zip(names_out, results))
    return state


def local(queries, key_tokens, value_tokens, cotangent, window_mask):
    shape = queries.shape
    features = shape[-1]
    tokens = queries.size // features
    tile = ((tokens, features), BF16)
    two = ((2, tokens, features), BF16)

    keep_kv, keep_qd, send = call(
        split_kernel,
        [jnp.stack([x.reshape(tokens, features) for x in (key_tokens, value_tokens, queries, cotangent)])],
        [tile, tile, two],
    )
    own_even = in_time(keep_kv, 0)
    own_odd = in_time(keep_kv, 1)
    recv = near(send)
    depth, wide = features - 128, features // 2 // HEAD_DIM * tokens
    flags, own_wide = call(
        functools.partial(early_kernel, lax.axis_size("tm")),
        [window_mask, keep_qd],
        [((FLAGS,), jnp.int32, pltpu.SMEM), ((2, 1, depth, wide), BF16)],
        places={0: pltpu.SMEM},
    )
    partner_kv, to_far, rows = call(
        merge_kernel, [keep_kv, keep_qd, recv, own_wide], [tile, tile, two], places={3: pl.ANY}
    )
    far_own = far(to_far)
    partner_even = in_time(partner_kv, 0)
    partner_odd = in_time(partner_kv, 1)
    state = {"flags": flags, "own_wide": own_wide, "rows": rows}
    state = run_phase(Phase(forward=[0, 3], first=True), state, [(keep_kv, None), (partner_kv, None)], [], COSTS[0])
    p_own = state["p"], state["m"]
    state["acc"], far_own, own_even, own_odd = lax.optimization_barrier((state["acc"], far_own, own_even, own_odd))
    far_even = in_time(far_own, 0)
    far_odd = in_time(far_own, 1)
    times = [(array, None) for array in (own_even, partner_even, own_odd, partner_odd)]
    state = run_phase(Phase(forward=[6]), state, [(far_own, None)], [], COSTS[6])
    p_far = state["p"], state["m"]
    state = run_phase(Phase(forward=[1, 4, 2, 5]), state, times, [], COSTS[1])
    p_times = state["p"], state["m"]
    state = run_phase(
        Phase(forward=[7, 8], backward=[([7, 8], [0, 1])], targets={7: ("g_even", None), 8: ("g_odd", None)}),
        state,
        [(far_even, None), (far_odd, None)],
        [],
        COSTS[2],
    )
    hop_even = in_time(state["g_even"], 0)
    hop_odd = in_time(state["g_odd"], 1)
    state = run_phase(
        Phase(
            backward=[([1, 4, 2, 5], [0, 1, 2, 3])],
            targets={1: ("g_te", 0), 4: ("g_te", 1), 2: ("g_to", 0), 5: ("g_to", 1)},
        ),
        state,
        times,
        [p_times],
        COSTS[3],
    )
    from_even = in_time(state["g_te"], 0)
    from_odd = in_time(state["g_to"], 1)
    state = run_phase(
        Phase(backward=[([6], [0])], targets={6: ("g_far", None)}),
        state,
        [(far_own, None)],
        [p_far],
        COSTS[4],
    )
    (to_far,) = call(far_sum_kernel, [state["g_far"], hop_even, hop_odd], [tile])
    from_far = far(to_far)
    state = run_phase(
        Phase(backward=[([0, 3], [0, 1])], targets={0: ("g_own", 0), 3: ("g_own", 1)}, last=True),
        state,
        [(keep_kv, None), (partner_kv, None)],
        [p_own],
        COSTS[5],
    )
    rows_recv = near(state["rows1"])
    out, dq = call(join_rows_kernel, [state["rows0"], rows_recv], [tile, tile])
    mine, partner = call(total_kernel, [state["g_own"], from_even, from_odd, from_far], [tile, tile])
    recv_total = near(partner)
    key_grad, value_grad = call(
        join_lanes_kernel,
        [mine, recv_total],
        [tile + (pl.ANY,), tile + (pl.ANY,)],
        scratch=[pltpu.VMEM((2, tokens, features), BF16), pltpu.SemaphoreType.DMA((2, CHUNKS))],
    )
    return tuple(x.reshape(shape) for x in (out, dq, key_grad, value_grad))


def solution(mesh):
    spec = P("tm", "height", None, "heads")
    return jax.shard_map(
        local, mesh=mesh, in_specs=(spec, spec, spec, spec, P()), out_specs=(spec,) * 4, check_vma=False
    )
```

```python
import functools

import jax
import jax.numpy as jnp
from jax import lax
from jax.experimental import pallas as pl
from jax.experimental.pallas import tpu as pltpu
from jax.sharding import PartitionSpec as P

HEAD_DIM = 64
LIMIT = 1e17
FLOOR = 1e-17
SCALE = HEAD_DIM ** -0.5
BF16 = jnp.bfloat16
F32 = jnp.float32
COST = 1.15e9
COSTS = (2, 4, 50, 1, 1, 1, 3)
MIB = 1024 * 1024
FLAGS = 18
CHUNKS = 4


def pairing(size, first):
    pairs = [(i, i + 1) for i in range(first, size - 1, 2)]
    return pairs + [(b, a) for a, b in pairs]


def near(array):
    return lax.ppermute(array, "height", pairing(lax.axis_size("height"), 0))


def far(array):
    peers = lax.axis_size("height")
    return lax.ppermute(array, "height", [(i, (i + 2) % peers) for i in range(peers)])


def in_time(array, first):
    return lax.ppermute(array, "tm", pairing(lax.axis_size("tm"), first))


def offset(kind, index):
    even = 1 - 2 * lax.rem(index, 2)
    return jnp.where(kind == 0, 0, jnp.where(kind == 1, even, -even))


def near_far_tile(height):
    return jnp.where((height == 1) | (height == 2), 0, 1)


def allowed(mask_ref, unit, time, height, tiles_t):
    slot, query = unit // 2, unit % 2
    column, place = slot // 3, slot % 3
    other = height + offset(1, height)
    query_height = height if query == 0 else other
    key_height = (height, other, jnp.where(height < 2, 2, 1))[column]
    dt = offset(place, time)
    dh = key_height - query_height
    inside = (time + dt >= 0) & (time + dt < tiles_t) & (dh >= -1) & (dh <= 1)
    if slot == 3 * query:
        return inside
    flag = mask_ref[time, query_height, jnp.clip(3 * (dt + 1) + dh + 1, 0, 8)]
    return inside & (flag == 1)


def choose(index, values):
    result = jnp.int32(values[-1])
    for at, value in enumerate(values[:-1]):
        result = jnp.where(index == at, value, result)
    return result


def call(kernel, inputs, outputs, scratch=(), mib=16, cost=1, places=None):
    vmem = pl.BlockSpec(memory_space=pltpu.VMEM)
    places = places or {}
    return pl.pallas_call(
        kernel,
        out_shape=[jax.ShapeDtypeStruct(*output[:2]) for output in outputs],
        in_specs=[pl.BlockSpec(memory_space=places[i]) if i in places else vmem for i in range(len(inputs))],
        out_specs=[pl.BlockSpec(memory_space=output[2]) if len(output) > 2 else vmem for output in outputs],
        scratch_shapes=list(scratch),
        compiler_params=pltpu.CompilerParams(vmem_limit_bytes=mib * MIB),
        cost_estimate=pl.CostEstimate(flops=int(cost * COST), bytes_accessed=1000, transcendentals=0),
    )(*inputs)


def swapped_halves(x):
    return pltpu.roll(x.astype(F32), x.shape[1] // 2, 1).astype(x.dtype)


def lane_is_low(shape):
    return lax.broadcasted_iota(jnp.int32, shape, 1) < shape[1] // 2


def split_kernel(kvqd_ref, keep_kv_ref, keep_qd_ref, send_ref):
    odd = lax.rem(lax.axis_index("height"), 2)
    low = lane_is_low(kvqd_ref.shape[1:])
    for row in range(2):
        a, b = kvqd_ref[2 * row], kvqd_ref[2 * row + 1]
        if row == 1:
            a = (a.astype(F32) * SCALE).astype(BF16)
        first = jnp.where(low, a, swapped_halves(b))
        second = jnp.where(low, swapped_halves(a), b)

        keep_ref = (keep_kv_ref, keep_qd_ref)[row]

        @pl.when(odd == 0)
        def _():
            keep_ref[...] = first
            send_ref[row] = second

        @pl.when(odd != 0)
        def _():
            keep_ref[...] = second
            send_ref[row] = first


def groups(part, heads):
    found = {}
    for j in range(heads):
        found.setdefault((part * heads + j) * HEAD_DIM // 128, []).append(j)
    return list(found.items())


def block(part, tile, of, tokens):
    return slice((tile - part) * 128, (tile - part + 1) * 128), slice(of[0] * tokens, (of[-1] + 1) * tokens)


def put_wide(query, rows, wide):
    tokens, lanes = rows.shape
    half = lanes // 2
    pad = wide.shape[2] - half
    turned = rows.T
    heads = half // HEAD_DIM
    for x in range(2):
        for tile, of in groups(x, heads):
            deep, columns = block(x, tile, of, tokens)
            wide[x, query, deep, columns] = jnp.zeros((128, len(of) * tokens), wide.dtype)
        for j in range(heads):
            at = x * pad + j * HEAD_DIM
            source = x * half + j * HEAD_DIM
            wide[x, query, at : at + HEAD_DIM, j * tokens : (j + 1) * tokens] = turned[source : source + HEAD_DIM]


def put_tall(query, rows, factor, target):
    tokens, lanes = rows.shape
    half = lanes // 2
    heads = half // HEAD_DIM
    padded = jnp.zeros((8 - heads, tokens), F32)
    by_head = jnp.concatenate([factor[:, j * tokens : (j + 1) * tokens] for j in range(heads)] + [padded], axis=0).T
    lane = lax.broadcasted_iota(jnp.int32, (1, lanes), 1)
    lane = jnp.where(lane >= half, lane - half, lane)
    scale = jnp.zeros(rows.shape, F32)
    for j in range(heads):
        here = (lane >= j * HEAD_DIM) & (lane < (j + 1) * HEAD_DIM)
        scale = jnp.where(here, by_head[:, j : j + 1], scale)
    scaled = rows.astype(F32) * scale
    position = lax.broadcasted_iota(jnp.int32, (1, 128), 1)
    for x in range(2):
        for tile, of in groups(x, heads):
            values = scaled[:, tile * 128 : (tile + 1) * 128]
            for j in of:
                start = (x * heads + j) * HEAD_DIM - tile * 128
                here = (position >= start) & (position < start + HEAD_DIM)
                deep, _ = block(x, tile, of, tokens)
                target(x)[j * tokens : (j + 1) * tokens, deep] = jnp.where(here, values, 0.0).astype(BF16)


def early_kernel(tiles_t, mask_ref, keep_qd_ref, flags_ref, wide_ref):
    time = lax.axis_index("tm")
    height = lax.axis_index("height")
    for unit in range(FLAGS):
        flags_ref[unit] = allowed(mask_ref, unit, time, height, tiles_t).astype(jnp.int32)
    put_wide(0, keep_qd_ref[...], wide_ref)


def merge_kernel(keep_kv_ref, keep_qd_ref, recv_ref, after_ref, partner_ref, far_ref, rows_ref):
    del after_ref
    partner_ref[...] = recv_ref[0]
    rows_ref[0] = keep_qd_ref[...]
    rows_ref[1] = recv_ref[1]
    beside = near_far_tile(lax.axis_index("height"))

    @pl.when(beside == 0)
    def _():
        far_ref[...] = keep_kv_ref[...]

    @pl.when(beside != 0)
    def _():
        far_ref[...] = recv_ref[0]


def join_rows_kernel(own_ref, recv_ref, out_ref, dq_ref):
    odd = lax.rem(lax.axis_index("height"), 2)
    half = own_ref.shape[0] // 2

    def join(low, high):
        for at, ref in enumerate((out_ref, dq_ref)):
            rows = slice(at * half, (at + 1) * half)
            ref[...] = jnp.concatenate([low[rows], high[rows]], axis=0).T

    @pl.when(odd == 0)
    def _():
        join(own_ref, recv_ref)

    @pl.when(odd != 0)
    def _():
        join(recv_ref, own_ref)


def join_lanes_kernel(own_ref, recv_ref, key_hbm, value_hbm, staged, sem):
    odd = lax.rem(lax.axis_index("height"), 2)
    rows = own_ref.shape[0] // CHUNKS
    copies = []
    for c in range(CHUNKS):
        at = slice(c * rows, (c + 1) * rows)

        def join(low_ref, high_ref):
            low, high = low_ref[at], high_ref[at]
            lanes_low = lane_is_low(low.shape)
            staged[0, at] = jnp.where(lanes_low, low, swapped_halves(high))
            staged[1, at] = jnp.where(lanes_low, swapped_halves(low), high)

        @pl.when(odd == 0)
        def _():
            join(own_ref, recv_ref)

        @pl.when(odd != 0)
        def _():
            join(recv_ref, own_ref)

        for n, target in enumerate((key_hbm, value_hbm)):
            copies.append(pltpu.make_async_copy(staged.at[n, at], target.at[at], sem.at[n, c]))
            copies[-1].start()
    for copy in copies:
        copy.wait()


def far_sum_kernel(own_ref, even_ref, odd_ref, out_ref):
    total = own_ref[...].astype(F32) + even_ref[...].astype(F32) + odd_ref[...].astype(F32)
    out_ref[...] = total.astype(BF16)


def total_kernel(own_ref, even_ref, odd_ref, far_ref, mine_ref, partner_ref):
    beside = near_far_tile(lax.axis_index("height"))
    for tile, ref in enumerate((mine_ref, partner_ref)):
        total = own_ref[tile].astype(F32) + even_ref[tile].astype(F32) + odd_ref[tile].astype(F32)
        share = jnp.where(beside == tile, 1.0, 0.0).astype(F32)
        ref[...] = (total + far_ref[...].astype(F32) * share).astype(BF16)


class Phase:
    def __init__(self, forward=(), backward=(), targets=None, first=False, last=False):
        self.forward = list(forward)
        self.segments = list(backward)
        self.backward = [slot for slots, _ in backward for slot in slots]
        self.targets = targets or {}
        self.first, self.last = first, last
        self.finish = bool(forward) and bool(backward)
        self.both = all(slot < 6 for slot in (self.forward + self.backward)[-2:])
        self.slots = self.forward + [slot for slot in self.backward if slot not in self.forward]


def phase_kernel(phase, names_in, names_out, kv_at, *refs):
    ins = dict(zip(names_in, refs))
    outs = dict(zip(names_out, refs[len(names_in):]))
    kv, acc_s, sums, state_s, turned, g_acc, tall_s, slopes, dq_s, p_s, m_s, kv_sem = refs[len(names_in) + len(names_out):]
    count, tokens, lanes = kv.shape
    half = lanes // 2
    heads = half // HEAD_DIM
    depth = lanes - 128
    key_lanes, value_lanes = slice(0, depth), slice(lanes - depth, lanes)
    pad = depth - half
    columns = [slice(j * tokens, (j + 1) * tokens) for j in range(heads)]
    rows = [slice(j * HEAD_DIM, (j + 1) * HEAD_DIM) for j in range(heads)]
    flags = ins["flags"]

    def ok(slot):
        return (flags[2 * slot] + flags[2 * slot + 1]) != 0

    def load_kv(i):
        name, at = kv_at[i]
        source = ins[name] if at is None else ins[name].at[at]
        return pltpu.make_async_copy(source, kv.at[i], kv_sem.at[i])

    def start_load(i):
        if i < count:
            @pl.when(ok(phase.slots[i]))
            def _():
                load_kv(i).start()

    start_load(0)
    start_load(1)

    if phase.first:
        wide = outs["wide"]
        wide[:, 0:1] = ins["own_wide"][...]
        put_wide(1, ins["rows"][1], wide)
    else:
        wide = ins["wide"]

    if phase.forward:
        stat = outs["stat"]
        acc, p_out, m_out = (acc_s, p_s, m_s) if phase.finish else (outs["acc"], outs["p"], outs["m"])

        if phase.first:
            shifted = jnp.bool_(False)
        else:
            shifted = jnp.max(ins["stat"][0, 3:4, 0:128]) > 0.0

        def attempt(number, carry):
            def begin():
                if phase.first:
                    stat[...] = jnp.zeros_like(stat)
                    acc[...] = jnp.zeros_like(acc)
                else:
                    stat[...] = ins["stat"][...]
                    acc[...] = ins["acc"][...]

                @pl.when(number != 0)
                def _():
                    stat[:, 3:4] = jnp.ones((2, 1, stat.shape[2]), F32)
                    if phase.first:
                        stat[:, 0:1] = jnp.full((2, 1, stat.shape[2]), -1e30, F32)

            def forward(i, carry):
                slot = choose(i, phase.forward)
                for j in range(len(phase.forward)):
                    @pl.when((i == j) & (number == 0))
                    def _():
                        start_load(j + 2)

                    @pl.when(ok(slot) & (i == j) & (number == 0))
                    def _():
                        load_kv(j).wait()

                @pl.when(ok(slot))
                def _():
                    turned[...] = kv[i, :, value_lanes].T[pad:]

                exact = shifted | (number != 0)

                def scores(query, tile, of):
                    deep, at = block(0, tile, of, tokens)
                    keys = kv[i, :, tile * 128 : (tile + 1) * 128]
                    return at, jnp.dot(keys, wide[0, query, deep, at], preferred_element_type=F32)

                def attend(query, weights_of):
                    for tile, of in groups(0, heads):
                        at, s = scores(query, tile, of)
                        e = weights_of(s, at)
                        stat[query, 1:2, at] += jnp.sum(e, axis=0, keepdims=True)
                        p_out[2 * i + query, :, at] = e.astype(BF16)
                    for j in range(heads):
                        acc[query, rows[j]] += jnp.dot(
                            turned[rows[j]], p_out[2 * i + query, :, columns[j]], preferred_element_type=F32
                        )

                def plain(query):
                    m_out[2 * i + query] = jnp.zeros((1, stat.shape[2]), F32)
                    attend(query, lambda s, at: jnp.exp(s))

                two = (flags[2 * slot] != 0) & (flags[2 * slot + 1] != 0) & jnp.logical_not(exact)
                if phase.both:
                    @pl.when(two)
                    def _():
                        plain(0)
                        plain(1)
                else:
                    two = jnp.bool_(False)

                def with_query(query, carry):
                    unit = 2 * slot + query

                    @pl.when((flags[unit] != 0) & jnp.logical_not(exact | two))
                    def _():
                        plain(query)

                    @pl.when((flags[unit] != 0) & exact)
                    def _():
                        m_old = stat[query, 0:1]
                        for tile, of in groups(0, heads):
                            at, s = scores(query, tile, of)
                            sums[:, at] = jnp.max(s, axis=0, keepdims=True)
                        m_new = jnp.maximum(m_old, sums[...])
                        alpha = jnp.exp(m_old - m_new)
                        stat[query, 0:1] = m_new
                        m_out[2 * i + query] = m_new
                        stat[query, 1:2] = stat[query, 1:2] * alpha
                        for j in range(heads):
                            acc[query, rows[j]] = acc[query, rows[j]] * alpha[:, columns[j]]
                        attend(query, lambda s, at: jnp.exp(s - stat[query, 0:1, at]))

                    return carry

                lax.fori_loop(0, 2, with_query, 0)
                return carry

            @pl.when(state_s[0] != 0)
            def _():
                begin()
                lax.fori_loop(0, len(phase.forward), forward, 0)
                fits = jnp.max(stat[:, 1:2]) < LIMIT
                if phase.first:
                    fits = fits & (jnp.min(stat[:, 1:2]) > FLOOR)
                state_s[0] = jnp.where(fits, 0, 1)

            return carry

        state_s[0] = 1
        lax.fori_loop(0, 2, attempt, 0)
    else:
        stat = ins["stat"]

    if phase.finish:
        tall = outs["tall"]
        for query in range(2):
            inverse = 1.0 / stat[query, 1:2]
            stat[query, 1:2] = inverse
            for j in range(heads):
                out_t = (acc[query, rows[j]] * inverse[:, columns[j]]).astype(BF16)
                outs["out_t"][query, rows[j]] = out_t
                at = slice(pad + j * HEAD_DIM, pad + (j + 1) * HEAD_DIM)
                both = wide[1, query, at, columns[j]].astype(F32) * out_t.astype(F32)
                stat[query, 2:3, columns[j]] = jnp.sum(both, axis=0, keepdims=True)
            put_tall(query, ins["rows"][query], inverse, lambda x: tall.at[x, query])
    elif phase.backward:
        tall = ins["tall"]

    if phase.backward:
        dq = dq_s if phase.last else outs["dq"]
        moved = jnp.max(stat[0, 3:4, 0:128]) > 0.0
        if phase.finish:
            dq[...] = jnp.zeros_like(dq)
        else:
            dq[...] = ins["dq"][...]
        for number, (slots, places) in enumerate(phase.segments):
            p_in = p_s if phase.finish else ins["p%d" % number]
            m_in = m_s if phase.finish else ins["m%d" % number]
            where = [phase.slots.index(slot) for slot in slots]
            loading = len(phase.forward)

            def backward(step, carry):
                slot = choose(step, slots)
                place = choose(step, places)
                i = choose(step, where)
                for j in range(len(slots)):
                    if where[j] >= loading:
                        @pl.when(step == j)
                        def _():
                            start_load(where[j] + 2)

                        @pl.when(ok(slot) & (step == j))
                        def _():
                            load_kv(where[j]).wait()

                g_acc[...] = jnp.zeros_like(g_acc)

                @pl.when(ok(slot))
                def _():
                    turned[...] = kv[i, :, key_lanes].T[:half]

                def terms(query, tall_of, gamma):
                    at_p = 2 * place + query
                    for tile, of in groups(1, heads):
                        deep, at = block(1, tile, of, tokens)
                        values = kv[i, :, tile * 128 : (tile + 1) * 128]
                        dp = jnp.dot(values, wide[1, query, deep, at], preferred_element_type=F32)
                        slopes[:, at] = p_in[at_p, :, at] * (dp - stat[query, 2:3, at]).astype(BF16)
                    for x in range(2):
                        for tile, of in groups(x, heads):
                            deep, at = block(x, tile, of, tokens)
                            left = p_in[at_p, :, at] if x else slopes[:, at]
                            g_acc[:, tile * 128 : (tile + 1) * 128] += jnp.dot(
                                left, tall_of(x)[at, deep], preferred_element_type=F32
                            )
                    for j in range(heads):
                        term = jnp.dot(turned[rows[j]], slopes[:, columns[j]], preferred_element_type=F32)
                        dq[query, rows[j]] += term if gamma is None else term * gamma[:, columns[j]]

                def plain(query):
                    terms(query, lambda x: tall.at[x, query], None)

                two = (flags[2 * slot] != 0) & (flags[2 * slot + 1] != 0) & jnp.logical_not(moved)
                if phase.both:
                    @pl.when(two)
                    def _():
                        plain(0)
                        plain(1)
                else:
                    two = jnp.bool_(False)

                def with_query(query, carry):
                    unit = 2 * slot + query
                    good = flags[unit] != 0

                    @pl.when(good & jnp.logical_not(moved | two))
                    def _():
                        plain(query)

                    @pl.when(good & moved)
                    def _():
                        gamma = jnp.exp(m_in[2 * place + query] - stat[query, 0:1])
                        factor = gamma * stat[query, 1:2]
                        put_tall(query, ins["rows"][query], factor, lambda x: tall_s.at[x])
                        terms(query, lambda x: tall_s.at[x], gamma)

                    return carry

                lax.fori_loop(0, 2, with_query, 0)
                for j, s in enumerate(slots):
                    name, at = phase.targets[s]
                    target = outs[name] if at is None else outs[name].at[at]

                    @pl.when(step == j)
                    def _():
                        target[...] = g_acc[...].astype(BF16)

                return carry

            lax.fori_loop(0, len(slots), backward, 0)
        if phase.last:
            for query in range(2):
                result = outs["rows%d" % query]
                result[:half] = ins["out_t"][query]
                for j in range(heads):
                    at = slice(half + j * HEAD_DIM, half + (j + 1) * HEAD_DIM)
                    result[at] = (dq[query, rows[j]] * (stat[query, 1:2, columns[j]] * SCALE)).astype(BF16)


def run_phase(phase, state, kvs, ps, cost, after=()):
    tokens, lanes = state["rows"].shape[1:]
    half = lanes // 2
    depth = lanes - 128
    wide = half // HEAD_DIM * tokens
    count = len(phase.slots)
    smem = pltpu.SMEM
    tile = ((tokens, lanes), BF16)
    shapes = {
        "wide": ((2, 2, depth, wide), BF16),
        "tall": ((2, 2, wide, depth), BF16),
        "stat": ((2, 4, wide), F32),
        "m": ((2 * len(phase.forward), 1, wide), F32),
        "acc": ((2, half, tokens), F32),
        "dq": ((2, half, tokens), F32),
        "out_t": ((2, half, tokens), BF16),
        "rows0": tile,
        "rows1": tile,
        "p": ((2 * len(phase.forward), tokens, wide), BF16),
    }
    sizes = {}
    for name, at in phase.targets.values():
        sizes[name] = None if at is None else max(sizes.get(name, 0), at + 1)
    shapes.update({n: tile if size is None else ((size, tokens, lanes), BF16) for n, size in sizes.items()})
    names_in, names_out = [], []
    if phase.first:
        names_in += ["flags", "own_wide", "rows"]
        names_out += ["wide"]
    else:
        names_in += ["flags", "wide", "stat"]
    if phase.forward:
        names_out += ["stat"]
        if not phase.first:
            names_in += ["acc"]
        if not phase.finish:
            names_out += ["m", "p", "acc"]
    if phase.finish:
        names_out += ["out_t", "tall"]
    if phase.backward:
        names_in += ["rows"]
        if not phase.finish:
            names_in += ["dq", "tall"]
        names_out += ([] if phase.last else ["dq"]) + list(sizes)
    if phase.last:
        names_in += ["out_t"]
        names_out += ["rows0", "rows1"]
    inputs = {name: state[name] for name in names_in}
    for number, array in enumerate(ps):
        inputs["p%d" % number], inputs["m%d" % number] = array
    seen = {}

    def reference_to(array):
        if id(array) not in seen:
            seen[id(array)] = "big%d" % len(seen)
            inputs[seen[id(array)]] = array
        return seen[id(array)]

    for array in after:
        reference_to(array)
    kv_at = [(reference_to(array), at) for array, at in kvs]
    names = list(inputs)
    places = {i: pl.ANY for i, name in enumerate(names) if name.startswith("big")}
    places.update({i: smem for i, name in enumerate(names) if name in ("flags", "mask")})
    small = (8, 128)
    results = call(
        functools.partial(phase_kernel, phase, names, names_out, kv_at),
        list(inputs.values()),
        [shapes[name] for name in names_out],
        scratch=[
            pltpu.VMEM((count, tokens, lanes), BF16),
            pltpu.VMEM(shapes["acc"][0] if phase.finish else small, F32),
            pltpu.VMEM((1, wide), F32),
            pltpu.SMEM((8,), jnp.int32),
            pltpu.VMEM((half, tokens), BF16),
            pltpu.VMEM((tokens, lanes) if phase.backward else small, F32),
            pltpu.VMEM((2, wide, depth) if phase.backward else (1, 16, 128), BF16),
            pltpu.VMEM((tokens, wide) if phase.backward else (16, 128), BF16),
            pltpu.VMEM(shapes["dq"][0] if phase.last else small, F32),
            pltpu.VMEM(shapes["p"][0] if phase.finish else (16, 128), BF16),
            pltpu.VMEM(shapes["m"][0] if phase.finish else small, F32),
            pltpu.SemaphoreType.DMA((count,)),
        ],
        mib=24,
        cost=cost,
        places=places,
    )
    state.update(zip(names_out, results))
    return state


def local(queries, key_tokens, value_tokens, cotangent, window_mask):
    shape = queries.shape
    features = shape[-1]
    tokens = queries.size // features
    tile = ((tokens, features), BF16)
    two = ((2, tokens, features), BF16)

    keep_kv, keep_qd, send = call(
        split_kernel,
        [jnp.stack([x.reshape(tokens, features) for x in (key_tokens, value_tokens, queries, cotangent)])],
        [tile, tile, two],
    )
    own_even = in_time(keep_kv, 0)
    own_odd = in_time(keep_kv, 1)
    recv = near(send)
    depth, wide = features - 128, features // 2 // HEAD_DIM * tokens
    flags, own_wide = call(
        functools.partial(early_kernel, lax.axis_size("tm")),
        [window_mask, keep_qd],
        [((FLAGS,), jnp.int32, pltpu.SMEM), ((2, 1, depth, wide), BF16)],
        places={0: pltpu.SMEM},
    )
    partner_kv, to_far, rows = call(
        merge_kernel, [keep_kv, keep_qd, recv, own_wide], [tile, tile, two], places={3: pl.ANY}
    )
    far_own = far(to_far)
    partner_even = in_time(partner_kv, 0)
    partner_odd = in_time(partner_kv, 1)
    state = {"flags": flags, "own_wide": own_wide, "rows": rows}
    state = run_phase(Phase(forward=[0, 3], first=True), state, [(keep_kv, None), (partner_kv, None)], [], COSTS[0])
    p_own = state["p"], state["m"]
    state["acc"], far_own, own_even, own_odd = lax.optimization_barrier((state["acc"], far_own, own_even, own_odd))
    far_even = in_time(far_own, 0)
    far_odd = in_time(far_own, 1)
    times = [(array, None) for array in (own_even, partner_even, own_odd, partner_odd)]
    state = run_phase(Phase(forward=[6, 1, 4, 2, 5]), state, [(far_own, None)] + times, [], COSTS[1])
    p_times = state["p"], state["m"]
    state = run_phase(
        Phase(forward=[7, 8], backward=[([7, 8], [0, 1])], targets={7: ("g_even", None), 8: ("g_odd", None)}),
        state,
        [(far_even, None), (far_odd, None)],
        [],
        COSTS[2],
    )
    hop_even = in_time(state["g_even"], 0)
    hop_odd = in_time(state["g_odd"], 1)
    state = run_phase(
        Phase(
            backward=[([1, 4, 2, 5], [1, 2, 3, 4])],
            targets={1: ("g_te", 0), 4: ("g_te", 1), 2: ("g_to", 0), 5: ("g_to", 1)},
        ),
        state,
        times,
        [p_times],
        COSTS[3],
    )
    from_even = in_time(state["g_te"], 0)
    from_odd = in_time(state["g_to"], 1)
    state = run_phase(
        Phase(backward=[([6], [0])], targets={6: ("g_far", None)}),
        state,
        [(far_own, None)],
        [p_times],
        COSTS[4],
    )
    (to_far,) = call(far_sum_kernel, [state["g_far"], hop_even, hop_odd], [tile])
    from_far = far(to_far)
    state = run_phase(
        Phase(backward=[([0, 3], [0, 1])], targets={0: ("g_own", 0), 3: ("g_own", 1)}, last=True),
        state,
        [(keep_kv, None), (partner_kv, None)],
        [p_own],
        COSTS[5],
    )
    rows_recv = near(state["rows1"])
    out, dq = call(join_rows_kernel, [state["rows0"], rows_recv], [tile, tile])
    mine, partner = call(total_kernel, [state["g_own"], from_even, from_odd, from_far], [tile, tile])
    recv_total = near(partner)
    key_grad, value_grad = call(
        join_lanes_kernel,
        [mine, recv_total],
        [tile + (pl.ANY,), tile + (pl.ANY,)],
        scratch=[pltpu.VMEM((2, tokens, features), BF16), pltpu.SemaphoreType.DMA((2, CHUNKS))],
    )
    return tuple(x.reshape(shape) for x in (out, dq, key_grad, value_grad))


def solution(mesh):
    spec = P("tm", "height", None, "heads")
    return jax.shard_map(
        local, mesh=mesh, in_specs=(spec, spec, spec, spec, P()), out_specs=(spec,) * 4, check_vma=False
    )
```

```python
import functools

import jax
import jax.numpy as jnp
from jax import lax
from jax.experimental import pallas as pl
from jax.experimental.pallas import tpu as pltpu
from jax.sharding import PartitionSpec as P

HEAD_DIM = 64
LIMIT = 1e17
FLOOR = 1e-17
SCALE = HEAD_DIM ** -0.5
BF16 = jnp.bfloat16
F32 = jnp.float32
COST = 1.15e9
COSTS = (2, 4, 50, 1, 1, 1, 3)
MIB = 1024 * 1024
FLAGS = 18
CHUNKS = 4


def pairing(size, first):
    pairs = [(i, i + 1) for i in range(first, size - 1, 2)]
    return pairs + [(b, a) for a, b in pairs]


def near(array):
    return lax.ppermute(array, "height", pairing(lax.axis_size("height"), 0))


def far(array):
    peers = lax.axis_size("height")
    return lax.ppermute(array, "height", [(i, (i + 2) % peers) for i in range(peers)])


def in_time(array, first):
    return lax.ppermute(array, "tm", pairing(lax.axis_size("tm"), first))


def offset(kind, index):
    even = 1 - 2 * lax.rem(index, 2)
    return jnp.where(kind == 0, 0, jnp.where(kind == 1, even, -even))


def near_far_tile(height):
    return jnp.where((height == 1) | (height == 2), 0, 1)


def allowed(mask_ref, unit, time, height, tiles_t):
    slot, query = unit // 2, unit % 2
    column, place = slot // 3, slot % 3
    other = height + offset(1, height)
    query_height = height if query == 0 else other
    key_height = (height, other, jnp.where(height < 2, 2, 1))[column]
    dt = offset(place, time)
    dh = key_height - query_height
    inside = (time + dt >= 0) & (time + dt < tiles_t) & (dh >= -1) & (dh <= 1)
    if slot == 3 * query:
        return inside
    flag = mask_ref[time, query_height, jnp.clip(3 * (dt + 1) + dh + 1, 0, 8)]
    return inside & (flag == 1)


def choose(index, values):
    result = jnp.int32(values[-1])
    for at, value in enumerate(values[:-1]):
        result = jnp.where(index == at, value, result)
    return result


def call(kernel, inputs, outputs, scratch=(), mib=16, cost=1, places=None):
    vmem = pl.BlockSpec(memory_space=pltpu.VMEM)
    places = places or {}
    return pl.pallas_call(
        kernel,
        out_shape=[jax.ShapeDtypeStruct(*output[:2]) for output in outputs],
        in_specs=[pl.BlockSpec(memory_space=places[i]) if i in places else vmem for i in range(len(inputs))],
        out_specs=[pl.BlockSpec(memory_space=output[2]) if len(output) > 2 else vmem for output in outputs],
        scratch_shapes=list(scratch),
        compiler_params=pltpu.CompilerParams(vmem_limit_bytes=mib * MIB),
        cost_estimate=pl.CostEstimate(flops=int(cost * COST), bytes_accessed=1000, transcendentals=0),
    )(*inputs)


def swapped_halves(x):
    return pltpu.roll(x.astype(F32), x.shape[1] // 2, 1).astype(x.dtype)


def lane_is_low(shape):
    return lax.broadcasted_iota(jnp.int32, shape, 1) < shape[1] // 2


def split_kernel(kvqd_ref, keep_kv_ref, keep_qd_ref, send_ref):
    odd = lax.rem(lax.axis_index("height"), 2)
    low = lane_is_low(kvqd_ref.shape[1:])
    for row in range(2):
        a, b = kvqd_ref[2 * row], kvqd_ref[2 * row + 1]
        if row == 1:
            a = (a.astype(F32) * SCALE).astype(BF16)
        first = jnp.where(low, a, swapped_halves(b))
        second = jnp.where(low, swapped_halves(a), b)

        keep_ref = (keep_kv_ref, keep_qd_ref)[row]

        @pl.when(odd == 0)
        def _():
            keep_ref[...] = first
            send_ref[row] = second

        @pl.when(odd != 0)
        def _():
            keep_ref[...] = second
            send_ref[row] = first


def groups(part, heads):
    found = {}
    for j in range(heads):
        found.setdefault((part * heads + j) * HEAD_DIM // 128, []).append(j)
    return list(found.items())


def block(part, tile, of, tokens):
    return slice((tile - part) * 128, (tile - part + 1) * 128), slice(of[0] * tokens, (of[-1] + 1) * tokens)


def put_wide(query, rows, wide):
    tokens, lanes = rows.shape
    half = lanes // 2
    pad = wide.shape[2] - half
    turned = rows.T
    heads = half // HEAD_DIM
    for x in range(2):
        for tile, of in groups(x, heads):
            deep, columns = block(x, tile, of, tokens)
            wide[x, query, deep, columns] = jnp.zeros((128, len(of) * tokens), wide.dtype)
        for j in range(heads):
            at = x * pad + j * HEAD_DIM
            source = x * half + j * HEAD_DIM
            wide[x, query, at : at + HEAD_DIM, j * tokens : (j + 1) * tokens] = turned[source : source + HEAD_DIM]


def put_tall(query, rows, factor, target):
    tokens, lanes = rows.shape
    half = lanes // 2
    heads = half // HEAD_DIM
    padded = jnp.zeros((8 - heads, tokens), F32)
    by_head = jnp.concatenate([factor[:, j * tokens : (j + 1) * tokens] for j in range(heads)] + [padded], axis=0).T
    lane = lax.broadcasted_iota(jnp.int32, (1, lanes), 1)
    lane = jnp.where(lane >= half, lane - half, lane)
    scale = jnp.zeros(rows.shape, F32)
    for j in range(heads):
        here = (lane >= j * HEAD_DIM) & (lane < (j + 1) * HEAD_DIM)
        scale = jnp.where(here, by_head[:, j : j + 1], scale)
    scaled = rows.astype(F32) * scale
    position = lax.broadcasted_iota(jnp.int32, (1, 128), 1)
    for x in range(2):
        for tile, of in groups(x, heads):
            values = scaled[:, tile * 128 : (tile + 1) * 128]
            for j in of:
                start = (x * heads + j) * HEAD_DIM - tile * 128
                here = (position >= start) & (position < start + HEAD_DIM)
                deep, _ = block(x, tile, of, tokens)
                target(x)[j * tokens : (j + 1) * tokens, deep] = jnp.where(here, values, 0.0).astype(BF16)


def early_kernel(tiles_t, mask_ref, keep_qd_ref, flags_ref, wide_ref):
    time = lax.axis_index("tm")
    height = lax.axis_index("height")
    for unit in range(FLAGS):
        flags_ref[unit] = allowed(mask_ref, unit, time, height, tiles_t).astype(jnp.int32)
    put_wide(0, keep_qd_ref[...], wide_ref)


def merge_kernel(keep_kv_ref, keep_qd_ref, recv_ref, after_ref, partner_ref, far_ref, rows_ref):
    del after_ref
    partner_ref[...] = recv_ref[0]
    rows_ref[0] = keep_qd_ref[...]
    rows_ref[1] = recv_ref[1]
    beside = near_far_tile(lax.axis_index("height"))

    @pl.when(beside == 0)
    def _():
        far_ref[...] = keep_kv_ref[...]

    @pl.when(beside != 0)
    def _():
        far_ref[...] = recv_ref[0]


def join_kernel(rows_ref, mine_ref, recv_ref, key_hbm, value_hbm, out_hbm, dq_hbm, staged, sem):
    odd = lax.rem(lax.axis_index("height"), 2) != 0
    size = mine_ref.shape[0]
    half = size // 2
    rows = size // CHUNKS
    copies = []

    def send(n, target, at, c):
        copies.append(pltpu.make_async_copy(staged.at[n, at], target.at[at], sem.at[n, c]))
        copies[-1].start()

    for c in range(CHUNKS):
        at = slice(c * rows, (c + 1) * rows)
        mine, theirs = mine_ref[at].astype(F32), recv_ref[1, at].astype(F32)
        low, high = jnp.where(odd, theirs, mine), jnp.where(odd, mine, theirs)
        lanes_low = lane_is_low(mine.shape)
        staged[0, at] = jnp.where(lanes_low, low, pltpu.roll(high, half, 1)).astype(BF16)
        staged[1, at] = jnp.where(lanes_low, pltpu.roll(low, half, 1), high).astype(BF16)
        send(0, key_hbm, at, c)
        send(1, value_hbm, at, c)
    for n, target in enumerate((out_hbm, dq_hbm)):
        part = slice(n * half, (n + 1) * half)
        mine, theirs = rows_ref[part], recv_ref[0, part]
        low, high = jnp.where(odd, theirs, mine), jnp.where(odd, mine, theirs)
        staged[2 + n] = jnp.concatenate([low, high], axis=0).T
        send(2 + n, target, slice(0, size), 0)
    for copy in copies:
        copy.wait()


def far_sum_kernel(own_ref, even_ref, odd_ref, out_ref):
    total = own_ref[...].astype(F32) + even_ref[...].astype(F32) + odd_ref[...].astype(F32)
    out_ref[...] = total.astype(BF16)


def total_kernel(
    mine_ref, mine_even_ref, mine_odd_ref, theirs_ref, theirs_even_ref, theirs_odd_ref, far_ref, rows_ref,
    total_ref, share_ref,
):
    beside = near_far_tile(lax.axis_index("height"))
    far_terms = far_ref[...].astype(F32)
    total = mine_ref[...].astype(F32) + mine_even_ref[...].astype(F32) + mine_odd_ref[...].astype(F32)
    total_ref[...] = (total + far_terms * jnp.where(beside == 0, 1.0, 0.0).astype(F32)).astype(BF16)
    total = theirs_ref[...].astype(F32) + theirs_even_ref[...].astype(F32) + theirs_odd_ref[...].astype(F32)
    share_ref[0] = rows_ref[...]
    share_ref[1] = (total + far_terms * jnp.where(beside == 1, 1.0, 0.0).astype(F32)).astype(BF16)


class Phase:
    def __init__(self, forward=(), backward=(), targets=None, first=False, last=False, both=None):
        self.forward = list(forward)
        self.segments = list(backward)
        self.backward = [slot for slots, _ in backward for slot in slots]
        self.targets = targets or {}
        self.first, self.last = first, last
        self.finish = bool(forward) and bool(backward)
        self.both = all(slot < 6 for slot in (self.forward + self.backward)[-2:]) if both is None else both
        self.slots = self.forward + [slot for slot in self.backward if slot not in self.forward]


def phase_kernel(phase, names_in, names_out, kv_at, *refs):
    ins = dict(zip(names_in, refs))
    outs = dict(zip(names_out, refs[len(names_in):]))
    kv, acc_s, sums, state_s, turned, g_acc, tall_s, slopes, dq_s, p_s, m_s, kv_sem = refs[len(names_in) + len(names_out):]
    count, tokens, lanes = kv.shape
    half = lanes // 2
    heads = half // HEAD_DIM
    depth = lanes - 128
    key_lanes, value_lanes = slice(0, depth), slice(lanes - depth, lanes)
    pad = depth - half
    columns = [slice(j * tokens, (j + 1) * tokens) for j in range(heads)]
    rows = [slice(j * HEAD_DIM, (j + 1) * HEAD_DIM) for j in range(heads)]
    flags = ins["flags"]

    def ok(slot):
        return (flags[2 * slot] + flags[2 * slot + 1]) != 0

    def load_kv(i):
        name, at = kv_at[i]
        source = ins[name] if at is None else ins[name].at[at]
        return pltpu.make_async_copy(source, kv.at[i], kv_sem.at[i])

    def start_load(i):
        if i < count:
            @pl.when(ok(phase.slots[i]))
            def _():
                load_kv(i).start()

    start_load(0)
    start_load(1)

    if phase.first:
        wide = outs["wide"]
        wide[:, 0:1] = ins["own_wide"][...]
        put_wide(1, ins["rows"][1], wide)
    else:
        wide = ins["wide"]

    if phase.forward:
        stat = outs["stat"]
        acc, p_out, m_out = (acc_s, p_s, m_s) if phase.finish else (outs["acc"], outs["p"], outs["m"])

        if phase.first:
            shifted = jnp.bool_(False)
        else:
            shifted = jnp.max(ins["stat"][0, 3:4, 0:128]) > 0.0

        def attempt(number, carry):
            def begin():
                if phase.first:
                    stat[...] = jnp.zeros_like(stat)
                    acc[...] = jnp.zeros_like(acc)
                else:
                    stat[...] = ins["stat"][...]
                    acc[...] = ins["acc"][...]

                @pl.when(number != 0)
                def _():
                    stat[:, 3:4] = jnp.ones((2, 1, stat.shape[2]), F32)
                    if phase.first:
                        stat[:, 0:1] = jnp.full((2, 1, stat.shape[2]), -1e30, F32)

            def forward(i, carry):
                slot = choose(i, phase.forward)
                for j in range(len(phase.forward)):
                    @pl.when((i == j) & (number == 0))
                    def _():
                        start_load(j + 2)

                    @pl.when(ok(slot) & (i == j) & (number == 0))
                    def _():
                        load_kv(j).wait()

                @pl.when(ok(slot))
                def _():
                    turned[...] = kv[i, :, value_lanes].T[pad:]

                exact = shifted | (number != 0)

                def scores(query, tile, of):
                    deep, at = block(0, tile, of, tokens)
                    keys = kv[i, :, tile * 128 : (tile + 1) * 128]
                    return at, jnp.dot(keys, wide[0, query, deep, at], preferred_element_type=F32)

                def attend(query, weights_of):
                    for tile, of in groups(0, heads):
                        at, s = scores(query, tile, of)
                        e = weights_of(s, at)
                        stat[query, 1:2, at] += jnp.sum(e, axis=0, keepdims=True)
                        p_out[2 * i + query, :, at] = e.astype(BF16)
                    for j in range(heads):
                        acc[query, rows[j]] += jnp.dot(
                            turned[rows[j]], p_out[2 * i + query, :, columns[j]], preferred_element_type=F32
                        )

                def plain(query):
                    m_out[2 * i + query] = jnp.zeros((1, stat.shape[2]), F32)
                    attend(query, lambda s, at: jnp.exp(s))

                two = (flags[2 * slot] != 0) & (flags[2 * slot + 1] != 0) & jnp.logical_not(exact)
                if phase.both:
                    @pl.when(two)
                    def _():
                        plain(0)
                        plain(1)
                else:
                    two = jnp.bool_(False)

                def with_query(query, carry):
                    unit = 2 * slot + query

                    @pl.when((flags[unit] != 0) & jnp.logical_not(exact | two))
                    def _():
                        plain(query)

                    @pl.when((flags[unit] != 0) & exact)
                    def _():
                        m_old = stat[query, 0:1]
                        for tile, of in groups(0, heads):
                            at, s = scores(query, tile, of)
                            sums[:, at] = jnp.max(s, axis=0, keepdims=True)
                        m_new = jnp.maximum(m_old, sums[...])
                        alpha = jnp.exp(m_old - m_new)
                        stat[query, 0:1] = m_new
                        m_out[2 * i + query] = m_new
                        stat[query, 1:2] = stat[query, 1:2] * alpha
                        for j in range(heads):
                            acc[query, rows[j]] = acc[query, rows[j]] * alpha[:, columns[j]]
                        attend(query, lambda s, at: jnp.exp(s - stat[query, 0:1, at]))

                    return carry

                lax.fori_loop(0, 2, with_query, 0)
                return carry

            @pl.when(state_s[0] != 0)
            def _():
                begin()
                lax.fori_loop(0, len(phase.forward), forward, 0)
                fits = jnp.max(stat[:, 1:2]) < LIMIT
                if phase.first:
                    fits = fits & (jnp.min(stat[:, 1:2]) > FLOOR)
                state_s[0] = jnp.where(fits, 0, 1)

            return carry

        state_s[0] = 1
        lax.fori_loop(0, 2, attempt, 0)
    else:
        stat = ins["stat"]

    if phase.finish:
        tall = outs["tall"]
        for query in range(2):
            inverse = 1.0 / stat[query, 1:2]
            stat[query, 1:2] = inverse
            for j in range(heads):
                out_t = (acc[query, rows[j]] * inverse[:, columns[j]]).astype(BF16)
                outs["out_t"][query, rows[j]] = out_t
                at = slice(pad + j * HEAD_DIM, pad + (j + 1) * HEAD_DIM)
                both = wide[1, query, at, columns[j]].astype(F32) * out_t.astype(F32)
                stat[query, 2:3, columns[j]] = jnp.sum(both, axis=0, keepdims=True)
            put_tall(query, ins["rows"][query], inverse, lambda x: tall.at[x, query])
    elif phase.backward:
        tall = ins["tall"]

    if phase.backward:
        dq = dq_s if phase.last else outs["dq"]
        moved = jnp.max(stat[0, 3:4, 0:128]) > 0.0
        if phase.finish:
            dq[...] = jnp.zeros_like(dq)
        else:
            dq[...] = ins["dq"][...]
        for number, (slots, places) in enumerate(phase.segments):
            p_in = p_s if phase.finish else ins["p%d" % number]
            m_in = m_s if phase.finish else ins["m%d" % number]
            where = [phase.slots.index(slot) for slot in slots]
            loading = len(phase.forward)

            def backward(step, carry):
                slot = choose(step, slots)
                place = choose(step, places)
                i = choose(step, where)
                for j in range(len(slots)):
                    if where[j] >= loading:
                        @pl.when(step == j)
                        def _():
                            start_load(where[j] + 2)

                        @pl.when(ok(slot) & (step == j))
                        def _():
                            load_kv(where[j]).wait()

                g_acc[...] = jnp.zeros_like(g_acc)

                @pl.when(ok(slot))
                def _():
                    turned[...] = kv[i, :, key_lanes].T[:half]

                def terms(query, tall_of, gamma):
                    at_p = 2 * place + query
                    for tile, of in groups(1, heads):
                        deep, at = block(1, tile, of, tokens)
                        values = kv[i, :, tile * 128 : (tile + 1) * 128]
                        dp = jnp.dot(values, wide[1, query, deep, at], preferred_element_type=F32)
                        slopes[:, at] = p_in[at_p, :, at] * (dp - stat[query, 2:3, at]).astype(BF16)
                    for x in range(2):
                        for tile, of in groups(x, heads):
                            deep, at = block(x, tile, of, tokens)
                            left = p_in[at_p, :, at] if x else slopes[:, at]
                            g_acc[:, tile * 128 : (tile + 1) * 128] += jnp.dot(
                                left, tall_of(x)[at, deep], preferred_element_type=F32
                            )
                    for j in range(heads):
                        term = jnp.dot(turned[rows[j]], slopes[:, columns[j]], preferred_element_type=F32)
                        dq[query, rows[j]] += term if gamma is None else term * gamma[:, columns[j]]

                def plain(query):
                    terms(query, lambda x: tall.at[x, query], None)

                two = (flags[2 * slot] != 0) & (flags[2 * slot + 1] != 0) & jnp.logical_not(moved)
                if phase.both and max(slots) < 6:
                    @pl.when(two)
                    def _():
                        plain(0)
                        plain(1)
                else:
                    two = jnp.bool_(False)

                def with_query(query, carry):
                    unit = 2 * slot + query
                    good = flags[unit] != 0

                    @pl.when(good & jnp.logical_not(moved | two))
                    def _():
                        plain(query)

                    @pl.when(good & moved)
                    def _():
                        gamma = jnp.exp(m_in[2 * place + query] - stat[query, 0:1])
                        factor = gamma * stat[query, 1:2]
                        put_tall(query, ins["rows"][query], factor, lambda x: tall_s.at[x])
                        terms(query, lambda x: tall_s.at[x], gamma)

                    return carry

                lax.fori_loop(0, 2, with_query, 0)
                for j, s in enumerate(slots):
                    name, at = phase.targets[s]
                    target = outs[name] if at is None else outs[name].at[at]

                    @pl.when(step == j)
                    def _():
                        target[...] = g_acc[...].astype(BF16)

                return carry

            lax.fori_loop(0, len(slots), backward, 0)
        if phase.last:
            for query in range(2):
                result = outs["rows%d" % query]
                result[:half] = ins["out_t"][query]
                for j in range(heads):
                    at = slice(half + j * HEAD_DIM, half + (j + 1) * HEAD_DIM)
                    result[at] = (dq[query, rows[j]] * (stat[query, 1:2, columns[j]] * SCALE)).astype(BF16)


def run_phase(phase, state, kvs, ps, cost, after=()):
    tokens, lanes = state["rows"].shape[1:]
    half = lanes // 2
    depth = lanes - 128
    wide = half // HEAD_DIM * tokens
    count = len(phase.slots)
    smem = pltpu.SMEM
    tile = ((tokens, lanes), BF16)
    shapes = {
        "wide": ((2, 2, depth, wide), BF16),
        "tall": ((2, 2, wide, depth), BF16),
        "stat": ((2, 4, wide), F32),
        "m": ((2 * len(phase.forward), 1, wide), F32),
        "acc": ((2, half, tokens), F32),
        "dq": ((2, half, tokens), F32),
        "out_t": ((2, half, tokens), BF16),
        "rows0": tile,
        "rows1": tile,
        "p": ((2 * len(phase.forward), tokens, wide), BF16),
    }
    sizes = {}
    for name, at in phase.targets.values():
        sizes[name] = None if at is None else max(sizes.get(name, 0), at + 1)
    shapes.update({n: tile if size is None else ((size, tokens, lanes), BF16) for n, size in sizes.items()})
    names_in, names_out = [], []
    if phase.first:
        names_in += ["flags", "own_wide", "rows"]
        names_out += ["wide"]
    else:
        names_in += ["flags", "wide", "stat"]
    if phase.forward:
        names_out += ["stat"]
        if not phase.first:
            names_in += ["acc"]
        if not phase.finish:
            names_out += ["m", "p", "acc"]
    if phase.finish:
        names_out += ["out_t", "tall"]
    if phase.backward:
        names_in += ["rows"]
        if not phase.finish:
            names_in += ["dq", "tall"]
        names_out += ([] if phase.last else ["dq"]) + list(sizes)
    if phase.last:
        names_in += ["out_t"]
        names_out += ["rows0", "rows1"]
    inputs = {name: state[name] for name in names_in}
    for number, array in enumerate(ps):
        inputs["p%d" % number], inputs["m%d" % number] = array
    seen = {}

    def reference_to(array):
        if id(array) not in seen:
            seen[id(array)] = "big%d" % len(seen)
            inputs[seen[id(array)]] = array
        return seen[id(array)]

    for array in after:
        reference_to(array)
    kv_at = [(reference_to(array), at) for array, at in kvs]
    names = list(inputs)
    places = {i: pl.ANY for i, name in enumerate(names) if name.startswith("big")}
    places.update({i: smem for i, name in enumerate(names) if name in ("flags", "mask")})
    small = (8, 128)
    results = call(
        functools.partial(phase_kernel, phase, names, names_out, kv_at),
        list(inputs.values()),
        [shapes[name] for name in names_out],
        scratch=[
            pltpu.VMEM((count, tokens, lanes), BF16),
            pltpu.VMEM(shapes["acc"][0] if phase.finish else small, F32),
            pltpu.VMEM((1, wide), F32),
            pltpu.SMEM((8,), jnp.int32),
            pltpu.VMEM((half, tokens), BF16),
            pltpu.VMEM((tokens, lanes) if phase.backward else small, F32),
            pltpu.VMEM((2, wide, depth) if phase.backward else (1, 16, 128), BF16),
            pltpu.VMEM((tokens, wide) if phase.backward else (16, 128), BF16),
            pltpu.VMEM(shapes["dq"][0] if phase.last else small, F32),
            pltpu.VMEM(shapes["p"][0] if phase.finish else (16, 128), BF16),
            pltpu.VMEM(shapes["m"][0] if phase.finish else small, F32),
            pltpu.SemaphoreType.DMA((count,)),
        ],
        mib=24,
        cost=cost,
        places=places,
    )
    state.update(zip(names_out, results))
    return state


def local(queries, key_tokens, value_tokens, cotangent, window_mask):
    shape = queries.shape
    features = shape[-1]
    tokens = queries.size // features
    tile = ((tokens, features), BF16)
    two = ((2, tokens, features), BF16)

    keep_kv, keep_qd, send = call(
        split_kernel,
        [jnp.stack([x.reshape(tokens, features) for x in (key_tokens, value_tokens, queries, cotangent)])],
        [tile, tile, two],
    )
    own_even = in_time(keep_kv, 0)
    own_odd = in_time(keep_kv, 1)
    recv = near(send)
    depth, wide = features - 128, features // 2 // HEAD_DIM * tokens
    flags, own_wide = call(
        functools.partial(early_kernel, lax.axis_size("tm")),
        [window_mask, keep_qd],
        [((FLAGS,), jnp.int32, pltpu.SMEM), ((2, 1, depth, wide), BF16)],
        places={0: pltpu.SMEM},
    )
    partner_kv, to_far, rows = call(
        merge_kernel, [keep_kv, keep_qd, recv, own_wide], [tile, tile, two], places={3: pl.ANY}
    )
    far_own = far(to_far)
    partner_even = in_time(partner_kv, 0)
    partner_odd = in_time(partner_kv, 1)
    state = {"flags": flags, "own_wide": own_wide, "rows": rows}
    state = run_phase(Phase(forward=[0, 3], first=True), state, [(keep_kv, None), (partner_kv, None)], [], COSTS[0])
    p_own = state["p"], state["m"]
    state["acc"], far_own, own_even, own_odd = lax.optimization_barrier((state["acc"], far_own, own_even, own_odd))
    far_even = in_time(far_own, 0)
    far_odd = in_time(far_own, 1)
    state = run_phase(
        Phase(forward=[6, 1, 2]), state, [(far_own, None), (own_even, None), (own_odd, None)], [], COSTS[6]
    )
    p_first = state["p"], state["m"]
    state = run_phase(Phase(forward=[4, 5]), state, [(partner_even, None), (partner_odd, None)], [], COSTS[1])
    p_second = state["p"], state["m"]
    state = run_phase(
        Phase(forward=[7, 8], backward=[([7, 8], [0, 1])], targets={7: ("g_even", None), 8: ("g_odd", None)}),
        state,
        [(far_even, None), (far_odd, None)],
        [],
        COSTS[2],
    )
    hop_even = in_time(state["g_even"], 0)
    hop_odd = in_time(state["g_odd"], 1)
    state = run_phase(
        Phase(backward=[([1, 2], [1, 2])], targets={1: ("g_even", None), 2: ("g_odd", None)}),
        state,
        [(own_even, None), (own_odd, None)],
        [p_first],
        COSTS[3],
    )
    mine_even = in_time(state["g_even"], 0)
    mine_odd = in_time(state["g_odd"], 1)
    state = run_phase(
        Phase(
            backward=[([4, 5], [0, 1]), ([6], [0])],
            targets={4: ("g_even", None), 5: ("g_odd", None), 6: ("g_far", None)},
            both=True,
        ),
        state,
        [(partner_even, None), (partner_odd, None), (far_own, None)],
        [p_second, p_first],
        COSTS[4],
    )
    theirs_even = in_time(state["g_even"], 0)
    theirs_odd = in_time(state["g_odd"], 1)
    (to_far,) = call(far_sum_kernel, [state["g_far"], hop_even, hop_odd], [tile])
    from_far = far(to_far)
    state = run_phase(
        Phase(backward=[([0, 3], [0, 1])], targets={0: ("g_mine", None), 3: ("g_theirs", None)}, last=True),
        state,
        [(keep_kv, None), (partner_kv, None)],
        [p_own],
        COSTS[5],
        after=(mine_even, mine_odd),
    )
    mine, share = call(
        total_kernel,
        [state["g_mine"], mine_even, mine_odd, state["g_theirs"], theirs_even, theirs_odd, from_far, state["rows1"]],
        [tile, two],
    )
    recv_share = near(share)
    key_grad, value_grad, out, dq = call(
        join_kernel,
        [state["rows0"], mine, recv_share],
        [tile + (pl.ANY,)] * 4,
        scratch=[pltpu.VMEM((4, tokens, features), BF16), pltpu.SemaphoreType.DMA((4, CHUNKS))],
    )
    return tuple(x.reshape(shape) for x in (out, dq, key_grad, value_grad))


def solution(mesh):
    spec = P("tm", "height", None, "heads")
    return jax.shard_map(
        local, mesh=mesh, in_specs=(spec, spec, spec, spec, P()), out_specs=(spec,) * 4, check_vma=False
    )
```

```python
import functools

import jax
import jax.numpy as jnp
from jax import lax
from jax.experimental import pallas as pl
from jax.experimental.pallas import tpu as pltpu
from jax.sharding import PartitionSpec as P

HEAD_DIM = 64
LIMIT = 1e17
FLOOR = 1e-17
SCALE = HEAD_DIM ** -0.5
BF16 = jnp.bfloat16
F32 = jnp.float32
COST = 1.15e9
COSTS = (2, 4, 50, 1, 1, 1, 3)
MIB = 1024 * 1024
FLAGS = 18
CHUNKS = 4


def pairing(size, first):
    pairs = [(i, i + 1) for i in range(first, size - 1, 2)]
    return pairs + [(b, a) for a, b in pairs]


def near(array):
    return lax.ppermute(array, "height", pairing(lax.axis_size("height"), 0))


def far(array):
    peers = lax.axis_size("height")
    return lax.ppermute(array, "height", [(i, (i + 2) % peers) for i in range(peers)])


def in_time(array, first):
    return lax.ppermute(array, "tm", pairing(lax.axis_size("tm"), first))


def offset(kind, index):
    even = 1 - 2 * lax.rem(index, 2)
    return jnp.where(kind == 0, 0, jnp.where(kind == 1, even, -even))


def near_far_tile(height):
    return jnp.where((height == 1) | (height == 2), 0, 1)


def allowed(mask_ref, unit, time, height, tiles_t):
    slot, query = unit // 2, unit % 2
    column, place = slot // 3, slot % 3
    other = height + offset(1, height)
    query_height = height if query == 0 else other
    key_height = (height, other, jnp.where(height < 2, 2, 1))[column]
    dt = offset(place, time)
    dh = key_height - query_height
    inside = (time + dt >= 0) & (time + dt < tiles_t) & (dh >= -1) & (dh <= 1)
    if slot == 3 * query:
        return inside
    flag = mask_ref[time, query_height, jnp.clip(3 * (dt + 1) + dh + 1, 0, 8)]
    return inside & (flag == 1)


def choose(index, values):
    result = jnp.int32(values[-1])
    for at, value in enumerate(values[:-1]):
        result = jnp.where(index == at, value, result)
    return result


def call(kernel, inputs, outputs, scratch=(), mib=16, cost=1, places=None):
    vmem = pl.BlockSpec(memory_space=pltpu.VMEM)
    places = places or {}
    return pl.pallas_call(
        kernel,
        out_shape=[jax.ShapeDtypeStruct(*output[:2]) for output in outputs],
        in_specs=[pl.BlockSpec(memory_space=places[i]) if i in places else vmem for i in range(len(inputs))],
        out_specs=[pl.BlockSpec(memory_space=output[2]) if len(output) > 2 else vmem for output in outputs],
        scratch_shapes=list(scratch),
        compiler_params=pltpu.CompilerParams(vmem_limit_bytes=mib * MIB),
        cost_estimate=pl.CostEstimate(flops=int(cost * COST), bytes_accessed=1000, transcendentals=0),
    )(*inputs)


def swapped_halves(x):
    return pltpu.roll(x.astype(F32), x.shape[1] // 2, 1).astype(x.dtype)


def lane_is_low(shape):
    return lax.broadcasted_iota(jnp.int32, shape, 1) < shape[1] // 2


def split_kernel(kvqd_ref, keep_kv_ref, keep_qd_ref, send_ref):
    odd = lax.rem(lax.axis_index("height"), 2)
    low = lane_is_low(kvqd_ref.shape[1:])
    for row in range(2):
        a, b = kvqd_ref[2 * row], kvqd_ref[2 * row + 1]
        if row == 1:
            a = (a.astype(F32) * SCALE).astype(BF16)
        first = jnp.where(low, a, swapped_halves(b))
        second = jnp.where(low, swapped_halves(a), b)

        keep_ref = (keep_kv_ref, keep_qd_ref)[row]

        @pl.when(odd == 0)
        def _():
            keep_ref[...] = first
            send_ref[row] = second

        @pl.when(odd != 0)
        def _():
            keep_ref[...] = second
            send_ref[row] = first


def groups(part, heads):
    found = {}
    for j in range(heads):
        found.setdefault((part * heads + j) * HEAD_DIM // 128, []).append(j)
    return list(found.items())


def block(part, tile, of, tokens):
    return slice((tile - part) * 128, (tile - part + 1) * 128), slice(of[0] * tokens, (of[-1] + 1) * tokens)


def put_wide(query, rows, wide):
    tokens, lanes = rows.shape
    half = lanes // 2
    pad = wide.shape[2] - half
    turned = rows.T
    heads = half // HEAD_DIM
    for x in range(2):
        for tile, of in groups(x, heads):
            deep, columns = block(x, tile, of, tokens)
            wide[x, query, deep, columns] = jnp.zeros((128, len(of) * tokens), wide.dtype)
        for j in range(heads):
            at = x * pad + j * HEAD_DIM
            source = x * half + j * HEAD_DIM
            wide[x, query, at : at + HEAD_DIM, j * tokens : (j + 1) * tokens] = turned[source : source + HEAD_DIM]


def put_tall(query, rows, factor, target):
    tokens, lanes = rows.shape
    half = lanes // 2
    heads = half // HEAD_DIM
    padded = jnp.zeros((8 - heads, tokens), F32)
    by_head = jnp.concatenate([factor[:, j * tokens : (j + 1) * tokens] for j in range(heads)] + [padded], axis=0).T
    lane = lax.broadcasted_iota(jnp.int32, (1, lanes), 1)
    lane = jnp.where(lane >= half, lane - half, lane)
    scale = jnp.zeros(rows.shape, F32)
    for j in range(heads):
        here = (lane >= j * HEAD_DIM) & (lane < (j + 1) * HEAD_DIM)
        scale = jnp.where(here, by_head[:, j : j + 1], scale)
    scaled = rows.astype(F32) * scale
    position = lax.broadcasted_iota(jnp.int32, (1, 128), 1)
    for x in range(2):
        for tile, of in groups(x, heads):
            values = scaled[:, tile * 128 : (tile + 1) * 128]
            for j in of:
                start = (x * heads + j) * HEAD_DIM - tile * 128
                here = (position >= start) & (position < start + HEAD_DIM)
                deep, _ = block(x, tile, of, tokens)
                target(x)[j * tokens : (j + 1) * tokens, deep] = jnp.where(here, values, 0.0).astype(BF16)


def early_kernel(tiles_t, mask_ref, keep_qd_ref, flags_ref, wide_ref):
    time = lax.axis_index("tm")
    height = lax.axis_index("height")
    for unit in range(FLAGS):
        flags_ref[unit] = allowed(mask_ref, unit, time, height, tiles_t).astype(jnp.int32)
    put_wide(0, keep_qd_ref[...], wide_ref)


def merge_kernel(keep_kv_ref, keep_qd_ref, recv_ref, partner_ref, far_ref, rows_ref):
    partner_ref[...] = recv_ref[0]
    rows_ref[0] = keep_qd_ref[...]
    rows_ref[1] = recv_ref[1]
    beside = near_far_tile(lax.axis_index("height"))

    @pl.when(beside == 0)
    def _():
        far_ref[...] = keep_kv_ref[...]

    @pl.when(beside != 0)
    def _():
        far_ref[...] = recv_ref[0]


def join_rows_kernel(own_ref, recv_ref, out_ref, dq_ref):
    odd = lax.rem(lax.axis_index("height"), 2)
    half = own_ref.shape[0] // 2

    def join(low, high):
        for at, ref in enumerate((out_ref, dq_ref)):
            rows = slice(at * half, (at + 1) * half)
            ref[...] = jnp.concatenate([low[rows], high[rows]], axis=0).T

    @pl.when(odd == 0)
    def _():
        join(own_ref, recv_ref)

    @pl.when(odd != 0)
    def _():
        join(recv_ref, own_ref)


def join_lanes_kernel(own_ref, recv_ref, key_hbm, value_hbm, staged, sem):
    odd = lax.rem(lax.axis_index("height"), 2)
    rows = own_ref.shape[0] // CHUNKS
    copies = []
    for c in range(CHUNKS):
        at = slice(c * rows, (c + 1) * rows)

        def join(low_ref, high_ref):
            low, high = low_ref[at], high_ref[at]
            lanes_low = lane_is_low(low.shape)
            staged[0, at] = jnp.where(lanes_low, low, swapped_halves(high))
            staged[1, at] = jnp.where(lanes_low, swapped_halves(low), high)

        @pl.when(odd == 0)
        def _():
            join(own_ref, recv_ref)

        @pl.when(odd != 0)
        def _():
            join(recv_ref, own_ref)

        for n, target in enumerate((key_hbm, value_hbm)):
            copies.append(pltpu.make_async_copy(staged.at[n, at], target.at[at], sem.at[n, c]))
            copies[-1].start()
    for copy in copies:
        copy.wait()


def far_sum_kernel(own_ref, even_ref, odd_ref, out_ref):
    total = own_ref[...].astype(F32) + even_ref[...].astype(F32) + odd_ref[...].astype(F32)
    out_ref[...] = total.astype(BF16)


def total_kernel(own_ref, even_ref, odd_ref, far_ref, mine_ref, partner_ref):
    beside = near_far_tile(lax.axis_index("height"))
    for tile, ref in enumerate((mine_ref, partner_ref)):
        total = own_ref[tile].astype(F32) + even_ref[tile].astype(F32) + odd_ref[tile].astype(F32)
        share = jnp.where(beside == tile, 1.0, 0.0).astype(F32)
        ref[...] = (total + far_ref[...].astype(F32) * share).astype(BF16)


class Phase:
    def __init__(self, forward=(), backward=(), targets=None, first=False, last=False):
        self.forward = list(forward)
        self.segments = list(backward)
        self.backward = [slot for slots, _ in backward for slot in slots]
        self.targets = targets or {}
        self.first, self.last = first, last
        self.finish = bool(forward) and bool(backward)
        self.both = all(slot < 6 for slot in (self.forward + self.backward)[-2:])
        self.slots = self.forward + [slot for slot in self.backward if slot not in self.forward]


def phase_kernel(phase, names_in, names_out, kv_at, *refs):
    ins = dict(zip(names_in, refs))
    outs = dict(zip(names_out, refs[len(names_in):]))
    kv, acc_s, sums, state_s, turned, g_acc, tall_s, slopes, dq_s, p_s, m_s, kv_sem = refs[len(names_in) + len(names_out):]
    count, tokens, lanes = kv.shape
    half = lanes // 2
    heads = half // HEAD_DIM
    depth = lanes - 128
    key_lanes, value_lanes = slice(0, depth), slice(lanes - depth, lanes)
    pad = depth - half
    columns = [slice(j * tokens, (j + 1) * tokens) for j in range(heads)]
    rows = [slice(j * HEAD_DIM, (j + 1) * HEAD_DIM) for j in range(heads)]
    flags = ins["flags"]

    def ok(slot):
        return (flags[2 * slot] + flags[2 * slot + 1]) != 0

    def load_kv(i):
        name, at = kv_at[i]
        source = ins[name] if at is None else ins[name].at[at]
        return pltpu.make_async_copy(source, kv.at[i], kv_sem.at[i])

    def start_load(i):
        if i < count:
            @pl.when(ok(phase.slots[i]))
            def _():
                load_kv(i).start()

    start_load(0)
    start_load(1)

    if phase.first:
        wide = outs["wide"]
        wide[:, 0:1] = ins["own_wide"][...]
        put_wide(1, ins["rows"][1], wide)
    else:
        wide = ins["wide"]

    if phase.forward:
        stat = outs["stat"]
        acc, p_out, m_out = (acc_s, p_s, m_s) if phase.finish else (outs["acc"], outs["p"], outs["m"])

        if phase.first:
            shifted = jnp.bool_(False)
        else:
            shifted = jnp.max(ins["stat"][0, 3:4, 0:128]) > 0.0

        def attempt(number, carry):
            def begin():
                if phase.first:
                    stat[...] = jnp.zeros_like(stat)
                    acc[...] = jnp.zeros_like(acc)
                else:
                    stat[...] = ins["stat"][...]
                    acc[...] = ins["acc"][...]

                @pl.when(number != 0)
                def _():
                    stat[:, 3:4] = jnp.ones((2, 1, stat.shape[2]), F32)
                    if phase.first:
                        stat[:, 0:1] = jnp.full((2, 1, stat.shape[2]), -1e30, F32)

            def forward(i, carry):
                slot = choose(i, phase.forward)
                for j in range(len(phase.forward)):
                    @pl.when((i == j) & (number == 0))
                    def _():
                        start_load(j + 2)

                    @pl.when(ok(slot) & (i == j) & (number == 0))
                    def _():
                        load_kv(j).wait()

                @pl.when(ok(slot))
                def _():
                    turned[...] = kv[i, :, value_lanes].T[pad:]

                exact = shifted | (number != 0)

                def scores(query, tile, of):
                    deep, at = block(0, tile, of, tokens)
                    keys = kv[i, :, tile * 128 : (tile + 1) * 128]
                    return at, jnp.dot(keys, wide[0, query, deep, at], preferred_element_type=F32)

                def attend(query, weights_of):
                    for tile, of in groups(0, heads):
                        at, s = scores(query, tile, of)
                        e = weights_of(s, at)
                        stat[query, 1:2, at] += jnp.sum(e, axis=0, keepdims=True)
                        p_out[2 * i + query, :, at] = e.astype(BF16)
                    for j in range(heads):
                        acc[query, rows[j]] += jnp.dot(
                            turned[rows[j]], p_out[2 * i + query, :, columns[j]], preferred_element_type=F32
                        )

                def plain(query):
                    m_out[2 * i + query] = jnp.zeros((1, stat.shape[2]), F32)
                    attend(query, lambda s, at: jnp.exp(s))

                two = (flags[2 * slot] != 0) & (flags[2 * slot + 1] != 0) & jnp.logical_not(exact)
                if phase.both:
                    @pl.when(two)
                    def _():
                        plain(0)
                        plain(1)
                else:
                    two = jnp.bool_(False)

                def with_query(query, carry):
                    unit = 2 * slot + query

                    @pl.when((flags[unit] != 0) & jnp.logical_not(exact | two))
                    def _():
                        plain(query)

                    @pl.when((flags[unit] != 0) & exact)
                    def _():
                        m_old = stat[query, 0:1]
                        for tile, of in groups(0, heads):
                            at, s = scores(query, tile, of)
                            sums[:, at] = jnp.max(s, axis=0, keepdims=True)
                        m_new = jnp.maximum(m_old, sums[...])
                        alpha = jnp.exp(m_old - m_new)
                        stat[query, 0:1] = m_new
                        m_out[2 * i + query] = m_new
                        stat[query, 1:2] = stat[query, 1:2] * alpha
                        for j in range(heads):
                            acc[query, rows[j]] = acc[query, rows[j]] * alpha[:, columns[j]]
                        attend(query, lambda s, at: jnp.exp(s - stat[query, 0:1, at]))

                    return carry

                lax.fori_loop(0, 2, with_query, 0)
                return carry

            @pl.when(state_s[0] != 0)
            def _():
                begin()
                lax.fori_loop(0, len(phase.forward), forward, 0)
                fits = jnp.max(stat[:, 1:2]) < LIMIT
                if phase.first:
                    fits = fits & (jnp.min(stat[:, 1:2]) > FLOOR)
                state_s[0] = jnp.where(fits, 0, 1)

            return carry

        state_s[0] = 1
        lax.fori_loop(0, 2, attempt, 0)
    else:
        stat = ins["stat"]

    if phase.finish:
        tall = outs["tall"]
        for query in range(2):
            inverse = 1.0 / stat[query, 1:2]
            stat[query, 1:2] = inverse
            for j in range(heads):
                out_t = (acc[query, rows[j]] * inverse[:, columns[j]]).astype(BF16)
                outs["out_t"][query, rows[j]] = out_t
                at = slice(pad + j * HEAD_DIM, pad + (j + 1) * HEAD_DIM)
                both = wide[1, query, at, columns[j]].astype(F32) * out_t.astype(F32)
                stat[query, 2:3, columns[j]] = jnp.sum(both, axis=0, keepdims=True)
            put_tall(query, ins["rows"][query], inverse, lambda x: tall.at[x, query])
    elif phase.backward:
        tall = ins["tall"]

    if phase.backward:
        dq = dq_s if phase.last else outs["dq"]
        moved = jnp.max(stat[0, 3:4, 0:128]) > 0.0
        if phase.finish:
            dq[...] = jnp.zeros_like(dq)
        else:
            dq[...] = ins["dq"][...]
        for number, (slots, places) in enumerate(phase.segments):
            p_in = p_s if phase.finish else ins["p%d" % number]
            m_in = m_s if phase.finish else ins["m%d" % number]
            where = [phase.slots.index(slot) for slot in slots]
            loading = len(phase.forward)

            def backward(step, carry):
                slot = choose(step, slots)
                place = choose(step, places)
                i = choose(step, where)
                for j in range(len(slots)):
                    if where[j] >= loading:
                        @pl.when(step == j)
                        def _():
                            start_load(where[j] + 2)

                        @pl.when(ok(slot) & (step == j))
                        def _():
                            load_kv(where[j]).wait()

                g_acc[...] = jnp.zeros_like(g_acc)

                @pl.when(ok(slot))
                def _():
                    turned[...] = kv[i, :, key_lanes].T[:half]

                def terms(query, tall_of, gamma):
                    at_p = 2 * place + query
                    for tile, of in groups(1, heads):
                        deep, at = block(1, tile, of, tokens)
                        values = kv[i, :, tile * 128 : (tile + 1) * 128]
                        dp = jnp.dot(values, wide[1, query, deep, at], preferred_element_type=F32)
                        slopes[:, at] = p_in[at_p, :, at] * (dp - stat[query, 2:3, at]).astype(BF16)
                    for x in range(2):
                        for tile, of in groups(x, heads):
                            deep, at = block(x, tile, of, tokens)
                            left = p_in[at_p, :, at] if x else slopes[:, at]
                            g_acc[:, tile * 128 : (tile + 1) * 128] += jnp.dot(
                                left, tall_of(x)[at, deep], preferred_element_type=F32
                            )
                    for j in range(heads):
                        term = jnp.dot(turned[rows[j]], slopes[:, columns[j]], preferred_element_type=F32)
                        dq[query, rows[j]] += term if gamma is None else term * gamma[:, columns[j]]

                def plain(query):
                    terms(query, lambda x: tall.at[x, query], None)

                two = (flags[2 * slot] != 0) & (flags[2 * slot + 1] != 0) & jnp.logical_not(moved)
                if phase.both:
                    @pl.when(two)
                    def _():
                        plain(0)
                        plain(1)
                else:
                    two = jnp.bool_(False)

                def with_query(query, carry):
                    unit = 2 * slot + query
                    good = flags[unit] != 0

                    @pl.when(good & jnp.logical_not(moved | two))
                    def _():
                        plain(query)

                    @pl.when(good & moved)
                    def _():
                        gamma = jnp.exp(m_in[2 * place + query] - stat[query, 0:1])
                        factor = gamma * stat[query, 1:2]
                        put_tall(query, ins["rows"][query], factor, lambda x: tall_s.at[x])
                        terms(query, lambda x: tall_s.at[x], gamma)

                    return carry

                lax.fori_loop(0, 2, with_query, 0)
                for j, s in enumerate(slots):
                    name, at = phase.targets[s]
                    target = outs[name] if at is None else outs[name].at[at]

                    @pl.when(step == j)
                    def _():
                        target[...] = g_acc[...].astype(BF16)

                return carry

            lax.fori_loop(0, len(slots), backward, 0)
        if phase.last:
            for query in range(2):
                result = outs["rows%d" % query]
                result[:half] = ins["out_t"][query]
                for j in range(heads):
                    at = slice(half + j * HEAD_DIM, half + (j + 1) * HEAD_DIM)
                    result[at] = (dq[query, rows[j]] * (stat[query, 1:2, columns[j]] * SCALE)).astype(BF16)


def run_phase(phase, state, kvs, ps, cost, after=()):
    tokens, lanes = state["rows"].shape[1:]
    half = lanes // 2
    depth = lanes - 128
    wide = half // HEAD_DIM * tokens
    count = len(phase.slots)
    smem = pltpu.SMEM
    tile = ((tokens, lanes), BF16)
    shapes = {
        "wide": ((2, 2, depth, wide), BF16),
        "tall": ((2, 2, wide, depth), BF16),
        "stat": ((2, 4, wide), F32),
        "m": ((2 * len(phase.forward), 1, wide), F32),
        "acc": ((2, half, tokens), F32),
        "dq": ((2, half, tokens), F32),
        "out_t": ((2, half, tokens), BF16),
        "rows0": tile,
        "rows1": tile,
        "p": ((2 * len(phase.forward), tokens, wide), BF16),
    }
    sizes = {}
    for name, at in phase.targets.values():
        sizes[name] = None if at is None else max(sizes.get(name, 0), at + 1)
    shapes.update({n: tile if size is None else ((size, tokens, lanes), BF16) for n, size in sizes.items()})
    names_in, names_out = [], []
    if phase.first:
        names_in += ["flags", "own_wide", "rows"]
        names_out += ["wide"]
    else:
        names_in += ["flags", "wide", "stat"]
    if phase.forward:
        names_out += ["stat"]
        if not phase.first:
            names_in += ["acc"]
        if not phase.finish:
            names_out += ["m", "p", "acc"]
    if phase.finish:
        names_out += ["out_t", "tall"]
    if phase.backward:
        names_in += ["rows"]
        if not phase.finish:
            names_in += ["dq", "tall"]
        names_out += ([] if phase.last else ["dq"]) + list(sizes)
    if phase.last:
        names_in += ["out_t"]
        names_out += ["rows0", "rows1"]
    inputs = {name: state[name] for name in names_in}
    for number, array in enumerate(ps):
        inputs["p%d" % number], inputs["m%d" % number] = array
    seen = {}

    def reference_to(array):
        if id(array) not in seen:
            seen[id(array)] = "big%d" % len(seen)
            inputs[seen[id(array)]] = array
        return seen[id(array)]

    for array in after:
        reference_to(array)
    kv_at = [(reference_to(array), at) for array, at in kvs]
    names = list(inputs)
    places = {i: pl.ANY for i, name in enumerate(names) if name.startswith("big")}
    places.update({i: smem for i, name in enumerate(names) if name in ("flags", "mask")})
    small = (8, 128)
    results = call(
        functools.partial(phase_kernel, phase, names, names_out, kv_at),
        list(inputs.values()),
        [shapes[name] for name in names_out],
        scratch=[
            pltpu.VMEM((count, tokens, lanes), BF16),
            pltpu.VMEM(shapes["acc"][0] if phase.finish else small, F32),
            pltpu.VMEM((1, wide), F32),
            pltpu.SMEM((8,), jnp.int32),
            pltpu.VMEM((half, tokens), BF16),
            pltpu.VMEM((tokens, lanes) if phase.backward else small, F32),
            pltpu.VMEM((2, wide, depth) if phase.backward else (1, 16, 128), BF16),
            pltpu.VMEM((tokens, wide) if phase.backward else (16, 128), BF16),
            pltpu.VMEM(shapes["dq"][0] if phase.last else small, F32),
            pltpu.VMEM(shapes["p"][0] if phase.finish else (16, 128), BF16),
            pltpu.VMEM(shapes["m"][0] if phase.finish else small, F32),
            pltpu.SemaphoreType.DMA((count,)),
        ],
        mib=24,
        cost=cost,
        places=places,
    )
    state.update(zip(names_out, results))
    return state


def local(queries, key_tokens, value_tokens, cotangent, window_mask):
    shape = queries.shape
    features = shape[-1]
    tokens = queries.size // features
    tile = ((tokens, features), BF16)
    two = ((2, tokens, features), BF16)

    keep_kv, keep_qd, send = call(
        split_kernel,
        [jnp.stack([x.reshape(tokens, features) for x in (key_tokens, value_tokens, queries, cotangent)])],
        [tile, tile, two],
    )
    own_even = in_time(keep_kv, 0)
    own_odd = in_time(keep_kv, 1)
    recv = near(send)
    depth, wide = features - 128, features // 2 // HEAD_DIM * tokens
    flags, own_wide = call(
        functools.partial(early_kernel, lax.axis_size("tm")),
        [window_mask, keep_qd],
        [((FLAGS,), jnp.int32, pltpu.SMEM), ((2, 1, depth, wide), BF16)],
        places={0: pltpu.SMEM},
    )
    partner_kv, to_far, rows = call(
        merge_kernel, [keep_kv, keep_qd, recv], [tile, tile, two]
    )
    far_own = far(to_far)
    partner_even = in_time(partner_kv, 0)
    partner_odd = in_time(partner_kv, 1)
    state = {"flags": flags, "own_wide": own_wide, "rows": rows}
    state = run_phase(Phase(forward=[0, 3], first=True), state, [(keep_kv, None), (partner_kv, None)], [], COSTS[0])
    p_own = state["p"], state["m"]
    state["acc"], far_own, own_even, own_odd = lax.optimization_barrier((state["acc"], far_own, own_even, own_odd))
    far_even = in_time(far_own, 0)
    far_odd = in_time(far_own, 1)
    state = run_phase(
        Phase(forward=[6, 1, 2]), state, [(far_own, None), (own_even, None), (own_odd, None)], [], COSTS[6]
    )
    p_first = state["p"], state["m"]
    state = run_phase(Phase(forward=[4, 5]), state, [(partner_even, None), (partner_odd, None)], [], COSTS[1])
    p_second = state["p"], state["m"]
    state = run_phase(
        Phase(forward=[7, 8], backward=[([7, 8], [0, 1])], targets={7: ("g_even", None), 8: ("g_odd", None)}),
        state,
        [(far_even, None), (far_odd, None)],
        [],
        COSTS[2],
    )
    hop_even = in_time(state["g_even"], 0)
    hop_odd = in_time(state["g_odd"], 1)
    state = run_phase(
        Phase(
            backward=[([1, 2], [1, 2]), ([4, 5], [0, 1])],
            targets={1: ("g_te", 0), 4: ("g_te", 1), 2: ("g_to", 0), 5: ("g_to", 1)},
        ),
        state,
        [(array, None) for array in (own_even, own_odd, partner_even, partner_odd)],
        [p_first, p_second],
        COSTS[3],
    )
    from_even = in_time(state["g_te"], 0)
    from_odd = in_time(state["g_to"], 1)
    state = run_phase(
        Phase(backward=[([6], [0])], targets={6: ("g_far", None)}),
        state,
        [(far_own, None)],
        [p_first],
        COSTS[4],
    )
    (to_far,) = call(far_sum_kernel, [state["g_far"], hop_even, hop_odd], [tile])
    from_far = far(to_far)
    state = run_phase(
        Phase(backward=[([0, 3], [0, 1])], targets={0: ("g_own", 0), 3: ("g_own", 1)}, last=True),
        state,
        [(keep_kv, None), (partner_kv, None)],
        [p_own],
        COSTS[5],
    )
    rows_recv = near(state["rows1"])
    out, dq = call(join_rows_kernel, [state["rows0"], rows_recv], [tile, tile])
    mine, partner = call(total_kernel, [state["g_own"], from_even, from_odd, from_far], [tile, tile])
    recv_total = near(partner)
    key_grad, value_grad = call(
        join_lanes_kernel,
        [mine, recv_total],
        [tile + (pl.ANY,), tile + (pl.ANY,)],
        scratch=[pltpu.VMEM((2, tokens, features), BF16), pltpu.SemaphoreType.DMA((2, CHUNKS))],
    )
    return tuple(x.reshape(shape) for x in (out, dq, key_grad, value_grad))


def solution(mesh):
    spec = P("tm", "height", None, "heads")
    return jax.shard_map(
        local, mesh=mesh, in_specs=(spec, spec, spec, spec, P()), out_specs=(spec,) * 4, check_vma=False
    )
```

```python
import functools

import jax
import jax.numpy as jnp
from jax import lax
from jax.experimental import pallas as pl
from jax.experimental.pallas import tpu as pltpu
from jax.sharding import PartitionSpec as P

HEAD_DIM = 64
LIMIT = 1e17
FLOOR = 1e-17
SCALE = HEAD_DIM ** -0.5
BF16 = jnp.bfloat16
F32 = jnp.float32
COST = 1.15e9
COSTS = (2, 4, 50, 1, 1, 1, 3)
MIB = 1024 * 1024
FLAGS = 18
CHUNKS = 4


def pairing(size, first):
    pairs = [(i, i + 1) for i in range(first, size - 1, 2)]
    return pairs + [(b, a) for a, b in pairs]


def near(array):
    return lax.ppermute(array, "height", pairing(lax.axis_size("height"), 0))


def far(array):
    peers = lax.axis_size("height")
    return lax.ppermute(array, "height", [(i, (i + 2) % peers) for i in range(peers)])


def in_time(array, first):
    return lax.ppermute(array, "tm", pairing(lax.axis_size("tm"), first))


def offset(kind, index):
    even = 1 - 2 * lax.rem(index, 2)
    return jnp.where(kind == 0, 0, jnp.where(kind == 1, even, -even))


def near_far_tile(height):
    return jnp.where((height == 1) | (height == 2), 0, 1)


def allowed(mask_ref, unit, time, height, tiles_t):
    slot, query = unit // 2, unit % 2
    column, place = slot // 3, slot % 3
    other = height + offset(1, height)
    query_height = height if query == 0 else other
    key_height = (height, other, jnp.where(height < 2, 2, 1))[column]
    dt = offset(place, time)
    dh = key_height - query_height
    inside = (time + dt >= 0) & (time + dt < tiles_t) & (dh >= -1) & (dh <= 1)
    if slot == 3 * query:
        return inside
    flag = mask_ref[time, query_height, jnp.clip(3 * (dt + 1) + dh + 1, 0, 8)]
    return inside & (flag == 1)


def choose(index, values):
    result = jnp.int32(values[-1])
    for at, value in enumerate(values[:-1]):
        result = jnp.where(index == at, value, result)
    return result


def call(kernel, inputs, outputs, scratch=(), mib=16, cost=1, places=None):
    vmem = pl.BlockSpec(memory_space=pltpu.VMEM)
    places = places or {}
    return pl.pallas_call(
        kernel,
        out_shape=[jax.ShapeDtypeStruct(*output[:2]) for output in outputs],
        in_specs=[pl.BlockSpec(memory_space=places[i]) if i in places else vmem for i in range(len(inputs))],
        out_specs=[pl.BlockSpec(memory_space=output[2]) if len(output) > 2 else vmem for output in outputs],
        scratch_shapes=list(scratch),
        compiler_params=pltpu.CompilerParams(vmem_limit_bytes=mib * MIB),
        cost_estimate=pl.CostEstimate(flops=int(cost * COST), bytes_accessed=1000, transcendentals=0),
    )(*inputs)


def swapped_halves(x):
    return pltpu.roll(x.astype(F32), x.shape[1] // 2, 1).astype(x.dtype)


def lane_is_low(shape):
    return lax.broadcasted_iota(jnp.int32, shape, 1) < shape[1] // 2


def split_kernel(kvqd_ref, keep_kv_ref, keep_qd_ref, send_ref):
    odd = lax.rem(lax.axis_index("height"), 2)
    low = lane_is_low(kvqd_ref.shape[1:])
    for row in range(2):
        a, b = kvqd_ref[2 * row], kvqd_ref[2 * row + 1]
        if row == 1:
            a = (a.astype(F32) * SCALE).astype(BF16)
        first = jnp.where(low, a, swapped_halves(b))
        second = jnp.where(low, swapped_halves(a), b)

        keep_ref = (keep_kv_ref, keep_qd_ref)[row]

        @pl.when(odd == 0)
        def _():
            keep_ref[...] = first
            send_ref[row] = second

        @pl.when(odd != 0)
        def _():
            keep_ref[...] = second
            send_ref[row] = first


def groups(part, heads):
    found = {}
    for j in range(heads):
        found.setdefault((part * heads + j) * HEAD_DIM // 128, []).append(j)
    return list(found.items())


def block(part, tile, of, tokens):
    return slice((tile - part) * 128, (tile - part + 1) * 128), slice(of[0] * tokens, (of[-1] + 1) * tokens)


def put_wide(query, rows, wide):
    tokens, lanes = rows.shape
    half = lanes // 2
    pad = wide.shape[2] - half
    turned = rows.T
    heads = half // HEAD_DIM
    for x in range(2):
        for tile, of in groups(x, heads):
            deep, columns = block(x, tile, of, tokens)
            wide[x, query, deep, columns] = jnp.zeros((128, len(of) * tokens), wide.dtype)
        for j in range(heads):
            at = x * pad + j * HEAD_DIM
            source = x * half + j * HEAD_DIM
            wide[x, query, at : at + HEAD_DIM, j * tokens : (j + 1) * tokens] = turned[source : source + HEAD_DIM]


def put_tall(query, rows, factor, target):
    tokens, lanes = rows.shape
    half = lanes // 2
    heads = half // HEAD_DIM
    padded = jnp.zeros((8 - heads, tokens), F32)
    by_head = jnp.concatenate([factor[:, j * tokens : (j + 1) * tokens] for j in range(heads)] + [padded], axis=0).T
    lane = lax.broadcasted_iota(jnp.int32, (1, lanes), 1)
    lane = jnp.where(lane >= half, lane - half, lane)
    scale = jnp.zeros(rows.shape, F32)
    for j in range(heads):
        here = (lane >= j * HEAD_DIM) & (lane < (j + 1) * HEAD_DIM)
        scale = jnp.where(here, by_head[:, j : j + 1], scale)
    scaled = rows.astype(F32) * scale
    position = lax.broadcasted_iota(jnp.int32, (1, 128), 1)
    for x in range(2):
        for tile, of in groups(x, heads):
            values = scaled[:, tile * 128 : (tile + 1) * 128]
            for j in of:
                start = (x * heads + j) * HEAD_DIM - tile * 128
                here = (position >= start) & (position < start + HEAD_DIM)
                deep, _ = block(x, tile, of, tokens)
                target(x)[j * tokens : (j + 1) * tokens, deep] = jnp.where(here, values, 0.0).astype(BF16)


def early_kernel(tiles_t, mask_ref, keep_qd_ref, flags_ref, wide_ref):
    time = lax.axis_index("tm")
    height = lax.axis_index("height")
    for unit in range(FLAGS):
        flags_ref[unit] = allowed(mask_ref, unit, time, height, tiles_t).astype(jnp.int32)
    put_wide(0, keep_qd_ref[...], wide_ref)


def merge_kernel(keep_kv_ref, keep_qd_ref, recv_ref, partner_ref, far_ref, rows_ref):
    partner_ref[...] = recv_ref[0]
    rows_ref[0] = keep_qd_ref[...]
    rows_ref[1] = recv_ref[1]
    beside = near_far_tile(lax.axis_index("height"))

    @pl.when(beside == 0)
    def _():
        far_ref[...] = keep_kv_ref[...]

    @pl.when(beside != 0)
    def _():
        far_ref[...] = recv_ref[0]


def join_rows_kernel(own_ref, recv_ref, out_ref, dq_ref):
    odd = lax.rem(lax.axis_index("height"), 2)
    half = own_ref.shape[0] // 2

    def join(low, high):
        for at, ref in enumerate((out_ref, dq_ref)):
            rows = slice(at * half, (at + 1) * half)
            ref[...] = jnp.concatenate([low[rows], high[rows]], axis=0).T

    @pl.when(odd == 0)
    def _():
        join(own_ref, recv_ref)

    @pl.when(odd != 0)
    def _():
        join(recv_ref, own_ref)


def join_lanes_kernel(own_ref, recv_ref, key_hbm, value_hbm, staged, sem):
    odd = lax.rem(lax.axis_index("height"), 2)
    rows = own_ref.shape[0] // CHUNKS
    copies = []
    for c in range(CHUNKS):
        at = slice(c * rows, (c + 1) * rows)

        def join(low_ref, high_ref):
            low, high = low_ref[at], high_ref[at]
            lanes_low = lane_is_low(low.shape)
            staged[0, at] = jnp.where(lanes_low, low, swapped_halves(high))
            staged[1, at] = jnp.where(lanes_low, swapped_halves(low), high)

        @pl.when(odd == 0)
        def _():
            join(own_ref, recv_ref)

        @pl.when(odd != 0)
        def _():
            join(recv_ref, own_ref)

        for n, target in enumerate((key_hbm, value_hbm)):
            copies.append(pltpu.make_async_copy(staged.at[n, at], target.at[at], sem.at[n, c]))
            copies[-1].start()
    for copy in copies:
        copy.wait()


def far_sum_kernel(own_ref, even_ref, odd_ref, out_ref):
    total = own_ref[...].astype(F32) + even_ref[...].astype(F32) + odd_ref[...].astype(F32)
    out_ref[...] = total.astype(BF16)


def total_kernel(own_ref, even_ref, odd_ref, far_ref, mine_ref, partner_ref):
    beside = near_far_tile(lax.axis_index("height"))
    for tile, ref in enumerate((mine_ref, partner_ref)):
        total = own_ref[tile].astype(F32) + even_ref[tile].astype(F32) + odd_ref[tile].astype(F32)
        share = jnp.where(beside == tile, 1.0, 0.0).astype(F32)
        ref[...] = (total + far_ref[...].astype(F32) * share).astype(BF16)


class Phase:
    def __init__(self, forward=(), backward=(), targets=None, first=False, last=False, defer=False, catch=()):
        self.forward = list(forward)
        self.segments = list(backward)
        self.backward = [slot for slots, _ in backward for slot in slots]
        self.targets = targets or {}
        self.first, self.last = first, last
        self.finish = bool(forward) and bool(backward)
        self.both = all(slot < 6 for slot in (self.forward + self.backward)[-2:])
        self.defer, self.catch = defer, list(catch)
        self.slots = self.forward + [slot for slot in self.backward if slot not in self.forward] + self.catch


def phase_kernel(phase, names_in, names_out, kv_at, *refs):
    ins = dict(zip(names_in, refs))
    outs = dict(zip(names_out, refs[len(names_in):]))
    kv, acc_s, sums, state_s, turned, g_acc, tall_s, slopes, dq_s, p_s, m_s, kv_sem = refs[len(names_in) + len(names_out):]
    count, tokens, lanes = kv.shape
    half = lanes // 2
    heads = half // HEAD_DIM
    depth = lanes - 128
    key_lanes, value_lanes = slice(0, depth), slice(lanes - depth, lanes)
    pad = depth - half
    columns = [slice(j * tokens, (j + 1) * tokens) for j in range(heads)]
    rows = [slice(j * HEAD_DIM, (j + 1) * HEAD_DIM) for j in range(heads)]
    flags = ins["flags"]

    def ok(slot):
        return (flags[2 * slot] + flags[2 * slot + 1]) != 0

    def load_kv(i):
        name, at = kv_at[i]
        source = ins[name] if at is None else ins[name].at[at]
        return pltpu.make_async_copy(source, kv.at[i], kv_sem.at[i])

    def start_load(i):
        if i < count:
            @pl.when(ok(phase.slots[i]))
            def _():
                load_kv(i).start()

    start_load(0)
    start_load(1)

    if phase.first:
        wide = outs["wide"]
        wide[:, 0:1] = ins["own_wide"][...]
        put_wide(1, ins["rows"][1], wide)
    else:
        wide = ins["wide"]

    if phase.forward:
        stat = outs["stat"]
        acc, p_out, m_out = (acc_s, p_s, m_s) if phase.finish else (outs["acc"], outs["p"], outs["m"])

        if phase.first:
            shifted = jnp.bool_(False)
        else:
            shifted = jnp.max(ins["stat"][0, 3:4, 0:128]) > 0.0

        def attempt(number, carry):
            def begin():
                if phase.first:
                    stat[...] = jnp.zeros_like(stat)
                    acc[...] = jnp.zeros_like(acc)
                else:
                    stat[...] = ins["stat"][...]
                    acc[...] = ins["acc"][...]

                @pl.when(number != 0)
                def _():
                    stat[:, 3:4] = jnp.ones((2, 1, stat.shape[2]), F32)
                    if phase.first:
                        stat[:, 0:1] = jnp.full((2, 1, stat.shape[2]), -1e30, F32)

            def forward(i, carry):
                slot = choose(i, phase.forward)
                for j in range(len(phase.forward)):
                    @pl.when((i == j) & (number == 0))
                    def _():
                        start_load(j + 2)

                    @pl.when(ok(slot) & (i == j) & (number == 0))
                    def _():
                        load_kv(j).wait()

                @pl.when(ok(slot))
                def _():
                    turned[...] = kv[i, :, value_lanes].T[pad:]

                exact = shifted | (number != 0)

                def scores(query, tile, of):
                    deep, at = block(0, tile, of, tokens)
                    keys = kv[i, :, tile * 128 : (tile + 1) * 128]
                    return at, jnp.dot(keys, wide[0, query, deep, at], preferred_element_type=F32)

                def attend(query, weights_of):
                    for tile, of in groups(0, heads):
                        at, s = scores(query, tile, of)
                        e = weights_of(s, at)
                        stat[query, 1:2, at] += jnp.sum(e, axis=0, keepdims=True)
                        p_out[2 * i + query, :, at] = e.astype(BF16)
                    for j in range(heads):
                        acc[query, rows[j]] += jnp.dot(
                            turned[rows[j]], p_out[2 * i + query, :, columns[j]], preferred_element_type=F32
                        )

                def plain(query):
                    m_out[2 * i + query] = jnp.zeros((1, stat.shape[2]), F32)
                    attend(query, lambda s, at: jnp.exp(s))

                two = (flags[2 * slot] != 0) & (flags[2 * slot + 1] != 0) & jnp.logical_not(exact)
                if phase.both:
                    @pl.when(two)
                    def _():
                        plain(0)
                        plain(1)
                else:
                    two = jnp.bool_(False)

                def with_query(query, carry):
                    unit = 2 * slot + query

                    @pl.when((flags[unit] != 0) & jnp.logical_not(exact | two))
                    def _():
                        plain(query)

                    @pl.when((flags[unit] != 0) & exact)
                    def _():
                        m_old = stat[query, 0:1]
                        for tile, of in groups(0, heads):
                            at, s = scores(query, tile, of)
                            sums[:, at] = jnp.max(s, axis=0, keepdims=True)
                        m_new = jnp.maximum(m_old, sums[...])
                        alpha = jnp.exp(m_old - m_new)
                        stat[query, 0:1] = m_new
                        m_out[2 * i + query] = m_new
                        stat[query, 1:2] = stat[query, 1:2] * alpha
                        for j in range(heads):
                            acc[query, rows[j]] = acc[query, rows[j]] * alpha[:, columns[j]]
                        attend(query, lambda s, at: jnp.exp(s - stat[query, 0:1, at]))

                    return carry

                lax.fori_loop(0, 2, with_query, 0)
                return carry

            @pl.when(state_s[0] != 0)
            def _():
                begin()
                lax.fori_loop(0, len(phase.forward), forward, 0)
                fits = jnp.max(stat[:, 1:2]) < LIMIT
                if phase.first:
                    fits = fits & (jnp.min(stat[:, 1:2]) > FLOOR)
                state_s[0] = jnp.where(fits, 0, 1)

            return carry

        state_s[0] = 1
        lax.fori_loop(0, 2, attempt, 0)
    else:
        stat = ins["stat"]

    if phase.finish:
        tall = outs["tall"]
        for query in range(2):
            inverse = 1.0 / stat[query, 1:2]
            stat[query, 1:2] = inverse
            for j in range(heads):
                out_t = (acc[query, rows[j]] * inverse[:, columns[j]]).astype(BF16)
                outs["out_t"][query, rows[j]] = out_t
                at = slice(pad + j * HEAD_DIM, pad + (j + 1) * HEAD_DIM)
                both = wide[1, query, at, columns[j]].astype(F32) * out_t.astype(F32)
                stat[query, 2:3, columns[j]] = jnp.sum(both, axis=0, keepdims=True)
            put_tall(query, ins["rows"][query], inverse, lambda x: tall.at[x, query])
    elif phase.backward:
        tall = ins["tall"]

    if phase.backward:
        dq = None if phase.defer else dq_s if phase.last else outs["dq"]
        moved = jnp.max(stat[0, 3:4, 0:128]) > 0.0
        if phase.finish:
            dq[...] = jnp.zeros_like(dq)
        elif not phase.defer:
            dq[...] = ins["dq"][...]
        done = 0
        for number, (slots, places) in enumerate(phase.segments):
            p_in = p_s if phase.finish else ins["p%d" % number]
            m_in = m_s if phase.finish else ins["m%d" % number]
            where = [phase.slots.index(slot) for slot in slots]
            base = done
            done += len(slots)
            loading = len(phase.forward)

            def backward(step, carry):
                slot = choose(step, slots)
                place = choose(step, places)
                i = choose(step, where)
                for j in range(len(slots)):
                    if where[j] >= loading:
                        @pl.when(step == j)
                        def _():
                            start_load(where[j] + 2)

                        @pl.when(ok(slot) & (step == j))
                        def _():
                            load_kv(where[j]).wait()

                g_acc[...] = jnp.zeros_like(g_acc)

                if not phase.defer:
                    @pl.when(ok(slot))
                    def _():
                        turned[...] = kv[i, :, key_lanes].T[:half]

                def terms(query, tall_of, gamma):
                    at_p = 2 * place + query
                    slopes_of = outs["ds"].at[2 * (base + step) + query] if phase.defer else slopes
                    for tile, of in groups(1, heads):
                        deep, at = block(1, tile, of, tokens)
                        values = kv[i, :, tile * 128 : (tile + 1) * 128]
                        dp = jnp.dot(values, wide[1, query, deep, at], preferred_element_type=F32)
                        slopes_of[:, at] = p_in[at_p, :, at] * (dp - stat[query, 2:3, at]).astype(BF16)
                    for x in range(2):
                        for tile, of in groups(x, heads):
                            deep, at = block(x, tile, of, tokens)
                            left = p_in[at_p, :, at] if x else slopes_of[:, at]
                            g_acc[:, tile * 128 : (tile + 1) * 128] += jnp.dot(
                                left, tall_of(x)[at, deep], preferred_element_type=F32
                            )
                    if phase.defer:
                        if gamma is not None:
                            slopes_of[...] = slopes_of[...] * gamma.astype(BF16)
                        return
                    for j in range(heads):
                        term = jnp.dot(turned[rows[j]], slopes[:, columns[j]], preferred_element_type=F32)
                        dq[query, rows[j]] += term if gamma is None else term * gamma[:, columns[j]]

                def plain(query):
                    terms(query, lambda x: tall.at[x, query], None)

                two = (flags[2 * slot] != 0) & (flags[2 * slot + 1] != 0) & jnp.logical_not(moved)
                if phase.both:
                    @pl.when(two)
                    def _():
                        plain(0)
                        plain(1)
                else:
                    two = jnp.bool_(False)

                def with_query(query, carry):
                    unit = 2 * slot + query
                    good = flags[unit] != 0

                    @pl.when(good & jnp.logical_not(moved | two))
                    def _():
                        plain(query)

                    @pl.when(good & moved)
                    def _():
                        gamma = jnp.exp(m_in[2 * place + query] - stat[query, 0:1])
                        factor = gamma * stat[query, 1:2]
                        put_tall(query, ins["rows"][query], factor, lambda x: tall_s.at[x])
                        terms(query, lambda x: tall_s.at[x], gamma)

                    return carry

                lax.fori_loop(0, 2, with_query, 0)
                for j, s in enumerate(slots):
                    name, at = phase.targets[s]
                    target = outs[name] if at is None else outs[name].at[at]

                    @pl.when(step == j)
                    def _():
                        target[...] = g_acc[...].astype(BF16)

                return carry

            lax.fori_loop(0, len(slots), backward, 0)
        if phase.catch:
            first = len(phase.slots) - len(phase.catch)

            def caught(step, carry):
                slot = choose(step, phase.catch)
                i = first + step
                for j in range(len(phase.catch)):
                    @pl.when(step == j)
                    def _():
                        start_load(first + j + 2)

                    @pl.when(ok(slot) & (step == j))
                    def _():
                        load_kv(first + j).wait()

                @pl.when(ok(slot))
                def _():
                    turned[...] = kv[i, :, key_lanes].T[:half]

                def with_query(query, carry):
                    @pl.when(flags[2 * slot + query] != 0)
                    def _():
                        for j in range(heads):
                            dq[query, rows[j]] += jnp.dot(
                                turned[rows[j]], ins["ds"][2 * step + query, :, columns[j]], preferred_element_type=F32
                            )

                    return carry

                lax.fori_loop(0, 2, with_query, 0)
                return carry

            lax.fori_loop(0, len(phase.catch), caught, 0)
        if phase.last:
            for query in range(2):
                result = outs["rows%d" % query]
                result[:half] = ins["out_t"][query]
                for j in range(heads):
                    at = slice(half + j * HEAD_DIM, half + (j + 1) * HEAD_DIM)
                    result[at] = (dq[query, rows[j]] * (stat[query, 1:2, columns[j]] * SCALE)).astype(BF16)


def run_phase(phase, state, kvs, ps, cost, after=()):
    tokens, lanes = state["rows"].shape[1:]
    half = lanes // 2
    depth = lanes - 128
    wide = half // HEAD_DIM * tokens
    count = len(phase.slots)
    smem = pltpu.SMEM
    tile = ((tokens, lanes), BF16)
    shapes = {
        "wide": ((2, 2, depth, wide), BF16),
        "tall": ((2, 2, wide, depth), BF16),
        "stat": ((2, 4, wide), F32),
        "m": ((2 * len(phase.forward), 1, wide), F32),
        "acc": ((2, half, tokens), F32),
        "dq": ((2, half, tokens), F32),
        "ds": ((2 * len(phase.backward), tokens, wide), BF16),
        "out_t": ((2, half, tokens), BF16),
        "rows0": tile,
        "rows1": tile,
        "p": ((2 * len(phase.forward), tokens, wide), BF16),
    }
    sizes = {}
    for name, at in phase.targets.values():
        sizes[name] = None if at is None else max(sizes.get(name, 0), at + 1)
    shapes.update({n: tile if size is None else ((size, tokens, lanes), BF16) for n, size in sizes.items()})
    names_in, names_out = [], []
    if phase.first:
        names_in += ["flags", "own_wide", "rows"]
        names_out += ["wide"]
    else:
        names_in += ["flags", "wide", "stat"]
    if phase.forward:
        names_out += ["stat"]
        if not phase.first:
            names_in += ["acc"]
        if not phase.finish:
            names_out += ["m", "p", "acc"]
    if phase.finish:
        names_out += ["out_t", "tall"]
    if phase.backward:
        names_in += ["rows"]
        if not phase.finish:
            names_in += ["tall"] if phase.defer else ["dq", "tall"]
        names_out += (["ds"] if phase.defer else [] if phase.last else ["dq"]) + list(sizes)
        if phase.catch:
            names_in += ["ds"]
    if phase.last:
        names_in += ["out_t"]
        names_out += ["rows0", "rows1"]
    inputs = {name: state[name] for name in names_in}
    for number, array in enumerate(ps):
        inputs["p%d" % number], inputs["m%d" % number] = array
    seen = {}

    def reference_to(array):
        if id(array) not in seen:
            seen[id(array)] = "big%d" % len(seen)
            inputs[seen[id(array)]] = array
        return seen[id(array)]

    for array in after:
        reference_to(array)
    kv_at = [(reference_to(array), at) for array, at in kvs]
    names = list(inputs)
    places = {i: pl.ANY for i, name in enumerate(names) if name.startswith("big")}
    places.update({i: smem for i, name in enumerate(names) if name in ("flags", "mask")})
    small = (8, 128)
    results = call(
        functools.partial(phase_kernel, phase, names, names_out, kv_at),
        list(inputs.values()),
        [shapes[name] for name in names_out],
        scratch=[
            pltpu.VMEM((count, tokens, lanes), BF16),
            pltpu.VMEM(shapes["acc"][0] if phase.finish else small, F32),
            pltpu.VMEM((1, wide), F32),
            pltpu.SMEM((8,), jnp.int32),
            pltpu.VMEM((half, tokens), BF16),
            pltpu.VMEM((tokens, lanes) if phase.backward else small, F32),
            pltpu.VMEM((2, wide, depth) if phase.backward else (1, 16, 128), BF16),
            pltpu.VMEM((tokens, wide) if phase.backward else (16, 128), BF16),
            pltpu.VMEM(shapes["dq"][0] if phase.last else small, F32),
            pltpu.VMEM(shapes["p"][0] if phase.finish else (16, 128), BF16),
            pltpu.VMEM(shapes["m"][0] if phase.finish else small, F32),
            pltpu.SemaphoreType.DMA((count,)),
        ],
        mib=24 if phase.finish else 16,
        cost=cost,
        places=places,
    )
    state.update(zip(names_out, results))
    return state


def local(queries, key_tokens, value_tokens, cotangent, window_mask):
    shape = queries.shape
    features = shape[-1]
    tokens = queries.size // features
    tile = ((tokens, features), BF16)
    two = ((2, tokens, features), BF16)

    keep_kv, keep_qd, send = call(
        split_kernel,
        [jnp.stack([x.reshape(tokens, features) for x in (key_tokens, value_tokens, queries, cotangent)])],
        [tile, tile, two],
    )
    own_even = in_time(keep_kv, 0)
    own_odd = in_time(keep_kv, 1)
    recv = near(send)
    depth, wide = features - 128, features // 2 // HEAD_DIM * tokens
    flags, own_wide = call(
        functools.partial(early_kernel, lax.axis_size("tm")),
        [window_mask, keep_qd],
        [((FLAGS,), jnp.int32, pltpu.SMEM), ((2, 1, depth, wide), BF16)],
        places={0: pltpu.SMEM},
    )
    partner_kv, to_far, rows = call(
        merge_kernel, [keep_kv, keep_qd, recv], [tile, tile, two]
    )
    far_own = far(to_far)
    partner_even = in_time(partner_kv, 0)
    partner_odd = in_time(partner_kv, 1)
    state = {"flags": flags, "own_wide": own_wide, "rows": rows}
    state = run_phase(Phase(forward=[0, 3], first=True), state, [(keep_kv, None), (partner_kv, None)], [], COSTS[0])
    p_own = state["p"], state["m"]
    state["acc"], far_own, own_even, own_odd = lax.optimization_barrier((state["acc"], far_own, own_even, own_odd))
    far_even = in_time(far_own, 0)
    far_odd = in_time(far_own, 1)
    state = run_phase(
        Phase(forward=[6, 1, 2]), state, [(far_own, None), (own_even, None), (own_odd, None)], [], COSTS[6]
    )
    p_first = state["p"], state["m"]
    state = run_phase(Phase(forward=[4, 5]), state, [(partner_even, None), (partner_odd, None)], [], COSTS[1])
    p_second = state["p"], state["m"]
    state = run_phase(
        Phase(forward=[7, 8], backward=[([7, 8], [0, 1])], targets={7: ("g_even", None), 8: ("g_odd", None)}),
        state,
        [(far_even, None), (far_odd, None)],
        [],
        COSTS[2],
    )
    hop_even = in_time(state["g_even"], 0)
    hop_odd = in_time(state["g_odd"], 1)
    state = run_phase(
        Phase(
            backward=[([1, 2], [1, 2]), ([4, 5], [0, 1])],
            targets={1: ("g_te", 0), 4: ("g_te", 1), 2: ("g_to", 0), 5: ("g_to", 1)},
            defer=True,
        ),
        state,
        [(array, None) for array in (own_even, own_odd, partner_even, partner_odd)],
        [p_first, p_second],
        COSTS[3],
    )
    from_even = in_time(state["g_te"], 0)
    from_odd = in_time(state["g_to"], 1)
    state = run_phase(
        Phase(backward=[([6], [0])], targets={6: ("g_far", None)}),
        state,
        [(far_own, None)],
        [p_first],
        COSTS[4],
    )
    (to_far,) = call(far_sum_kernel, [state["g_far"], hop_even, hop_odd], [tile])
    from_far = far(to_far)
    state = run_phase(
        Phase(
            backward=[([0, 3], [0, 1])],
            targets={0: ("g_own", 0), 3: ("g_own", 1)},
            last=True,
            catch=[1, 2, 4, 5],
        ),
        state,
        [(array, None) for array in (keep_kv, partner_kv, own_even, own_odd, partner_even, partner_odd)],
        [p_own],
        COSTS[5],
    )
    rows_recv = near(state["rows1"])
    out, dq = call(join_rows_kernel, [state["rows0"], rows_recv], [tile, tile])
    mine, partner = call(total_kernel, [state["g_own"], from_even, from_odd, from_far], [tile, tile])
    recv_total = near(partner)
    key_grad, value_grad = call(
        join_lanes_kernel,
        [mine, recv_total],
        [tile + (pl.ANY,), tile + (pl.ANY,)],
        scratch=[pltpu.VMEM((2, tokens, features), BF16), pltpu.SemaphoreType.DMA((2, CHUNKS))],
    )
    return tuple(x.reshape(shape) for x in (out, dq, key_grad, value_grad))


def solution(mesh):
    spec = P("tm", "height", None, "heads")
    return jax.shard_map(
        local, mesh=mesh, in_specs=(spec, spec, spec, spec, P()), out_specs=(spec,) * 4, check_vma=False
    )
```

```python
import functools

import jax
import jax.numpy as jnp
from jax import lax
from jax.experimental import pallas as pl
from jax.experimental.pallas import tpu as pltpu
from jax.sharding import PartitionSpec as P

HEAD_DIM = 64
LIMIT = 1e17
FLOOR = 1e-17
SCALE = HEAD_DIM ** -0.5
BF16 = jnp.bfloat16
F32 = jnp.float32
COST = 1.15e9
COSTS = (2, 4, 50, 1, 1, 1, 3)
MIB = 1024 * 1024
FLAGS = 18
CHUNKS = 4


def pairing(size, first):
    pairs = [(i, i + 1) for i in range(first, size - 1, 2)]
    return pairs + [(b, a) for a, b in pairs]


def near(array):
    return lax.ppermute(array, "height", pairing(lax.axis_size("height"), 0))


def far(array):
    peers = lax.axis_size("height")
    return lax.ppermute(array, "height", [(i, (i + 2) % peers) for i in range(peers)])


def in_time(array, first):
    return lax.ppermute(array, "tm", pairing(lax.axis_size("tm"), first))


def offset(kind, index):
    even = 1 - 2 * lax.rem(index, 2)
    return jnp.where(kind == 0, 0, jnp.where(kind == 1, even, -even))


def near_far_tile(height):
    return jnp.where((height == 1) | (height == 2), 0, 1)


def allowed(mask_ref, unit, time, height, tiles_t):
    slot, query = unit // 2, unit % 2
    column, place = slot // 3, slot % 3
    other = height + offset(1, height)
    query_height = height if query == 0 else other
    key_height = (height, other, jnp.where(height < 2, 2, 1))[column]
    dt = offset(place, time)
    dh = key_height - query_height
    inside = (time + dt >= 0) & (time + dt < tiles_t) & (dh >= -1) & (dh <= 1)
    if slot == 3 * query:
        return inside
    flag = mask_ref[time, query_height, jnp.clip(3 * (dt + 1) + dh + 1, 0, 8)]
    return inside & (flag == 1)


def choose(index, values):
    result = jnp.int32(values[-1])
    for at, value in enumerate(values[:-1]):
        result = jnp.where(index == at, value, result)
    return result


def call(kernel, inputs, outputs, scratch=(), mib=16, cost=1, places=None):
    vmem = pl.BlockSpec(memory_space=pltpu.VMEM)
    places = places or {}
    return pl.pallas_call(
        kernel,
        out_shape=[jax.ShapeDtypeStruct(*output[:2]) for output in outputs],
        in_specs=[pl.BlockSpec(memory_space=places[i]) if i in places else vmem for i in range(len(inputs))],
        out_specs=[pl.BlockSpec(memory_space=output[2]) if len(output) > 2 else vmem for output in outputs],
        scratch_shapes=list(scratch),
        compiler_params=pltpu.CompilerParams(vmem_limit_bytes=mib * MIB),
        cost_estimate=pl.CostEstimate(flops=int(cost * COST), bytes_accessed=1000, transcendentals=0),
    )(*inputs)


def swapped_halves(x):
    return pltpu.roll(x.astype(F32), x.shape[1] // 2, 1).astype(x.dtype)


def lane_is_low(shape):
    return lax.broadcasted_iota(jnp.int32, shape, 1) < shape[1] // 2


def split_kernel(kvqd_ref, keep_kv_ref, keep_qd_ref, send_ref):
    odd = lax.rem(lax.axis_index("height"), 2)
    low = lane_is_low(kvqd_ref.shape[1:])
    for row in range(2):
        a, b = kvqd_ref[2 * row], kvqd_ref[2 * row + 1]
        if row == 1:
            a = (a.astype(F32) * SCALE).astype(BF16)
        first = jnp.where(low, a, swapped_halves(b))
        second = jnp.where(low, swapped_halves(a), b)

        keep_ref = (keep_kv_ref, keep_qd_ref)[row]

        @pl.when(odd == 0)
        def _():
            keep_ref[...] = first
            send_ref[row] = second

        @pl.when(odd != 0)
        def _():
            keep_ref[...] = second
            send_ref[row] = first


def groups(part, heads):
    found = {}
    for j in range(heads):
        found.setdefault((part * heads + j) * HEAD_DIM // 128, []).append(j)
    return list(found.items())


def block(part, tile, of, tokens):
    return slice((tile - part) * 128, (tile - part + 1) * 128), slice(of[0] * tokens, (of[-1] + 1) * tokens)


def put_wide(query, rows, wide):
    tokens, lanes = rows.shape
    half = lanes // 2
    pad = wide.shape[2] - half
    turned = rows.T
    heads = half // HEAD_DIM
    for x in range(2):
        for tile, of in groups(x, heads):
            deep, columns = block(x, tile, of, tokens)
            wide[x, query, deep, columns] = jnp.zeros((128, len(of) * tokens), wide.dtype)
        for j in range(heads):
            at = x * pad + j * HEAD_DIM
            source = x * half + j * HEAD_DIM
            wide[x, query, at : at + HEAD_DIM, j * tokens : (j + 1) * tokens] = turned[source : source + HEAD_DIM]


def put_tall(query, rows, factor, target):
    tokens, lanes = rows.shape
    half = lanes // 2
    heads = half // HEAD_DIM
    padded = jnp.zeros((8 - heads, tokens), F32)
    by_head = jnp.concatenate([factor[:, j * tokens : (j + 1) * tokens] for j in range(heads)] + [padded], axis=0).T
    lane = lax.broadcasted_iota(jnp.int32, (1, lanes), 1)
    lane = jnp.where(lane >= half, lane - half, lane)
    scale = jnp.zeros(rows.shape, F32)
    for j in range(heads):
        here = (lane >= j * HEAD_DIM) & (lane < (j + 1) * HEAD_DIM)
        scale = jnp.where(here, by_head[:, j : j + 1], scale)
    scaled = rows.astype(F32) * scale
    position = lax.broadcasted_iota(jnp.int32, (1, 128), 1)
    for x in range(2):
        for tile, of in groups(x, heads):
            values = scaled[:, tile * 128 : (tile + 1) * 128]
            for j in of:
                start = (x * heads + j) * HEAD_DIM - tile * 128
                here = (position >= start) & (position < start + HEAD_DIM)
                deep, _ = block(x, tile, of, tokens)
                target(x)[j * tokens : (j + 1) * tokens, deep] = jnp.where(here, values, 0.0).astype(BF16)


def early_kernel(tiles_t, mask_ref, keep_qd_ref, flags_ref, wide_ref):
    time = lax.axis_index("tm")
    height = lax.axis_index("height")
    for unit in range(FLAGS):
        flags_ref[unit] = allowed(mask_ref, unit, time, height, tiles_t).astype(jnp.int32)
    put_wide(0, keep_qd_ref[...], wide_ref)


def merge_kernel(keep_kv_ref, keep_qd_ref, recv_ref, partner_ref, far_ref, rows_ref):
    partner_ref[...] = recv_ref[0]
    rows_ref[0] = keep_qd_ref[...]
    rows_ref[1] = recv_ref[1]
    beside = near_far_tile(lax.axis_index("height"))

    @pl.when(beside == 0)
    def _():
        far_ref[...] = keep_kv_ref[...]

    @pl.when(beside != 0)
    def _():
        far_ref[...] = recv_ref[0]


def join_rows_kernel(own_ref, recv_ref, out_ref, dq_ref):
    odd = lax.rem(lax.axis_index("height"), 2)
    half = own_ref.shape[0] // 2

    def join(low, high):
        for at, ref in enumerate((out_ref, dq_ref)):
            rows = slice(at * half, (at + 1) * half)
            ref[...] = jnp.concatenate([low[rows], high[rows]], axis=0).T

    @pl.when(odd == 0)
    def _():
        join(own_ref, recv_ref)

    @pl.when(odd != 0)
    def _():
        join(recv_ref, own_ref)


def join_lanes_kernel(own_ref, recv_ref, key_hbm, value_hbm, staged, sem):
    odd = lax.rem(lax.axis_index("height"), 2)
    rows = own_ref.shape[0] // CHUNKS
    copies = []
    for c in range(CHUNKS):
        at = slice(c * rows, (c + 1) * rows)

        def join(low_ref, high_ref):
            low, high = low_ref[at], high_ref[at]
            lanes_low = lane_is_low(low.shape)
            staged[0, at] = jnp.where(lanes_low, low, swapped_halves(high))
            staged[1, at] = jnp.where(lanes_low, swapped_halves(low), high)

        @pl.when(odd == 0)
        def _():
            join(own_ref, recv_ref)

        @pl.when(odd != 0)
        def _():
            join(recv_ref, own_ref)

        for n, target in enumerate((key_hbm, value_hbm)):
            copies.append(pltpu.make_async_copy(staged.at[n, at], target.at[at], sem.at[n, c]))
            copies[-1].start()
    for copy in copies:
        copy.wait()


def far_sum_kernel(own_ref, even_ref, odd_ref, out_ref):
    total = own_ref[...].astype(F32) + even_ref[...].astype(F32) + odd_ref[...].astype(F32)
    out_ref[...] = total.astype(BF16)


def total_kernel(own_ref, even_ref, odd_ref, far_ref, mine_ref, partner_ref):
    beside = near_far_tile(lax.axis_index("height"))
    for tile, ref in enumerate((mine_ref, partner_ref)):
        total = own_ref[tile].astype(F32) + even_ref[tile].astype(F32) + odd_ref[tile].astype(F32)
        share = jnp.where(beside == tile, 1.0, 0.0).astype(F32)
        ref[...] = (total + far_ref[...].astype(F32) * share).astype(BF16)


class Phase:
    def __init__(self, forward=(), backward=(), targets=None, first=False, last=False, defer=False, catch=()):
        self.forward = list(forward)
        self.segments = list(backward)
        self.backward = [slot for slots, _ in backward for slot in slots]
        self.targets = targets or {}
        self.first, self.last = first, last
        self.finish = bool(forward) and bool(backward)
        self.both = all(slot < 6 for slot in (self.forward + self.backward)[-2:])
        self.defer, self.catch = defer, list(catch)
        self.slots = self.forward + [slot for slot in self.backward if slot not in self.forward] + self.catch


def phase_kernel(phase, names_in, names_out, kv_at, *refs):
    ins = dict(zip(names_in, refs))
    outs = dict(zip(names_out, refs[len(names_in):]))
    kv, acc_s, sums, state_s, turned, g_acc, tall_s, slopes, dq_s, p_s, m_s, kv_sem = refs[len(names_in) + len(names_out):]
    count, tokens, lanes = kv.shape
    half = lanes // 2
    heads = half // HEAD_DIM
    depth = lanes - 128
    key_lanes, value_lanes = slice(0, depth), slice(lanes - depth, lanes)
    pad = depth - half
    columns = [slice(j * tokens, (j + 1) * tokens) for j in range(heads)]
    rows = [slice(j * HEAD_DIM, (j + 1) * HEAD_DIM) for j in range(heads)]
    flags = ins["flags"]

    def ok(slot):
        return (flags[2 * slot] + flags[2 * slot + 1]) != 0

    def load_kv(i):
        name, at = kv_at[i]
        source = ins[name] if at is None else ins[name].at[at]
        return pltpu.make_async_copy(source, kv.at[i], kv_sem.at[i])

    def start_load(i):
        if i < count:
            @pl.when(ok(phase.slots[i]))
            def _():
                load_kv(i).start()

    start_load(0)
    start_load(1)

    if phase.first:
        wide = outs["wide"]
        wide[:, 0:1] = ins["own_wide"][...]
        put_wide(1, ins["rows"][1], wide)
    else:
        wide = ins["wide"]

    if phase.forward:
        stat = outs["stat"]
        acc, p_out, m_out = (acc_s, p_s, m_s) if phase.finish else (outs["acc"], outs["p"], outs["m"])

        if phase.first:
            shifted = jnp.bool_(False)
        else:
            shifted = jnp.max(ins["stat"][0, 3:4, 0:128]) > 0.0

        def attempt(number, carry):
            def begin():
                if phase.first:
                    stat[...] = jnp.zeros_like(stat)
                    acc[...] = jnp.zeros_like(acc)
                else:
                    stat[...] = ins["stat"][...]
                    acc[...] = ins["acc"][...]

                @pl.when(number != 0)
                def _():
                    stat[:, 3:4] = jnp.ones((2, 1, stat.shape[2]), F32)
                    if phase.first:
                        stat[:, 0:1] = jnp.full((2, 1, stat.shape[2]), -1e30, F32)

            def forward(i, carry):
                slot = choose(i, phase.forward)
                for j in range(len(phase.forward)):
                    @pl.when((i == j) & (number == 0))
                    def _():
                        start_load(j + 2)

                    @pl.when(ok(slot) & (i == j) & (number == 0))
                    def _():
                        load_kv(j).wait()

                @pl.when(ok(slot))
                def _():
                    turned[...] = kv[i, :, value_lanes].T[pad:]

                exact = shifted | (number != 0)

                def scores(query, tile, of):
                    deep, at = block(0, tile, of, tokens)
                    keys = kv[i, :, tile * 128 : (tile + 1) * 128]
                    return at, jnp.dot(keys, wide[0, query, deep, at], preferred_element_type=F32)

                def attend(query, weights_of):
                    for tile, of in groups(0, heads):
                        at, s = scores(query, tile, of)
                        e = weights_of(s, at)
                        stat[query, 1:2, at] += jnp.sum(e, axis=0, keepdims=True)
                        p_out[2 * i + query, :, at] = e.astype(BF16)
                    for j in range(heads):
                        acc[query, rows[j]] += jnp.dot(
                            turned[rows[j]], p_out[2 * i + query, :, columns[j]], preferred_element_type=F32
                        )

                def plain(query):
                    m_out[2 * i + query] = jnp.zeros((1, stat.shape[2]), F32)
                    attend(query, lambda s, at: jnp.exp(s))

                two = (flags[2 * slot] != 0) & (flags[2 * slot + 1] != 0) & jnp.logical_not(exact)
                if phase.both:
                    @pl.when(two)
                    def _():
                        plain(0)
                        plain(1)
                else:
                    two = jnp.bool_(False)

                def with_query(query, carry):
                    unit = 2 * slot + query

                    @pl.when((flags[unit] != 0) & jnp.logical_not(exact | two))
                    def _():
                        plain(query)

                    @pl.when((flags[unit] != 0) & exact)
                    def _():
                        m_old = stat[query, 0:1]
                        for tile, of in groups(0, heads):
                            at, s = scores(query, tile, of)
                            sums[:, at] = jnp.max(s, axis=0, keepdims=True)
                        m_new = jnp.maximum(m_old, sums[...])
                        alpha = jnp.exp(m_old - m_new)
                        stat[query, 0:1] = m_new
                        m_out[2 * i + query] = m_new
                        stat[query, 1:2] = stat[query, 1:2] * alpha
                        for j in range(heads):
                            acc[query, rows[j]] = acc[query, rows[j]] * alpha[:, columns[j]]
                        attend(query, lambda s, at: jnp.exp(s - stat[query, 0:1, at]))

                    return carry

                lax.fori_loop(0, 2, with_query, 0)
                return carry

            @pl.when(state_s[0] != 0)
            def _():
                begin()
                lax.fori_loop(0, len(phase.forward), forward, 0)
                fits = jnp.max(stat[:, 1:2]) < LIMIT
                if phase.first:
                    fits = fits & (jnp.min(stat[:, 1:2]) > FLOOR)
                state_s[0] = jnp.where(fits, 0, 1)

            return carry

        state_s[0] = 1
        lax.fori_loop(0, 2, attempt, 0)
    else:
        stat = ins["stat"]

    if phase.finish:
        tall = outs["tall"]
        for query in range(2):
            inverse = 1.0 / stat[query, 1:2]
            stat[query, 1:2] = inverse
            for j in range(heads):
                out_t = (acc[query, rows[j]] * inverse[:, columns[j]]).astype(BF16)
                outs["out_t"][query, rows[j]] = out_t
                at = slice(pad + j * HEAD_DIM, pad + (j + 1) * HEAD_DIM)
                both = wide[1, query, at, columns[j]].astype(F32) * out_t.astype(F32)
                stat[query, 2:3, columns[j]] = jnp.sum(both, axis=0, keepdims=True)
            put_tall(query, ins["rows"][query], inverse, lambda x: tall.at[x, query])
    elif phase.backward:
        tall = ins["tall"]

    if phase.backward:
        dq = None if phase.defer else dq_s if phase.last else outs["dq"]
        moved = jnp.max(stat[0, 3:4, 0:128]) > 0.0
        if phase.finish:
            dq[...] = jnp.zeros_like(dq)
        elif not phase.defer:
            dq[...] = ins["dq"][...]
        done = 0
        for number, (slots, places) in enumerate(phase.segments):
            p_in = p_s if phase.finish else ins["p%d" % number]
            m_in = m_s if phase.finish else ins["m%d" % number]
            where = [phase.slots.index(slot) for slot in slots]
            base = done
            done += len(slots)
            loading = len(phase.forward)

            def backward(step, carry):
                slot = choose(step, slots)
                place = choose(step, places)
                i = choose(step, where)
                for j in range(len(slots)):
                    if where[j] >= loading:
                        @pl.when(step == j)
                        def _():
                            start_load(where[j] + 2)

                        @pl.when(ok(slot) & (step == j))
                        def _():
                            load_kv(where[j]).wait()

                g_acc[...] = jnp.zeros_like(g_acc)

                if not phase.defer:
                    @pl.when(ok(slot))
                    def _():
                        turned[...] = kv[i, :, key_lanes].T[:half]

                def terms(query, tall_of, gamma):
                    at_p = 2 * place + query
                    slopes_of = outs["ds"].at[2 * (base + step) + query] if phase.defer else slopes
                    for tile, of in groups(1, heads):
                        deep, at = block(1, tile, of, tokens)
                        values = kv[i, :, tile * 128 : (tile + 1) * 128]
                        dp = jnp.dot(values, wide[1, query, deep, at], preferred_element_type=F32)
                        slopes_of[:, at] = p_in[at_p, :, at] * (dp - stat[query, 2:3, at]).astype(BF16)
                    for x in range(2):
                        for tile, of in groups(x, heads):
                            deep, at = block(x, tile, of, tokens)
                            left = p_in[at_p, :, at] if x else slopes_of[:, at]
                            g_acc[:, tile * 128 : (tile + 1) * 128] += jnp.dot(
                                left, tall_of(x)[at, deep], preferred_element_type=F32
                            )
                    if phase.defer:
                        if gamma is not None:
                            slopes_of[...] = slopes_of[...] * gamma.astype(BF16)
                        return
                    for j in range(heads):
                        term = jnp.dot(turned[rows[j]], slopes[:, columns[j]], preferred_element_type=F32)
                        dq[query, rows[j]] += term if gamma is None else term * gamma[:, columns[j]]

                def plain(query):
                    terms(query, lambda x: tall.at[x, query], None)

                two = (flags[2 * slot] != 0) & (flags[2 * slot + 1] != 0) & jnp.logical_not(moved)
                if phase.both:
                    @pl.when(two)
                    def _():
                        plain(0)
                        plain(1)
                else:
                    two = jnp.bool_(False)

                def with_query(query, carry):
                    unit = 2 * slot + query
                    good = flags[unit] != 0

                    @pl.when(good & jnp.logical_not(moved | two))
                    def _():
                        plain(query)

                    @pl.when(good & moved)
                    def _():
                        gamma = jnp.exp(m_in[2 * place + query] - stat[query, 0:1])
                        factor = gamma * stat[query, 1:2]
                        put_tall(query, ins["rows"][query], factor, lambda x: tall_s.at[x])
                        terms(query, lambda x: tall_s.at[x], gamma)

                    return carry

                lax.fori_loop(0, 2, with_query, 0)
                for j, s in enumerate(slots):
                    name, at = phase.targets[s]
                    target = outs[name] if at is None else outs[name].at[at]

                    @pl.when(step == j)
                    def _():
                        target[...] = g_acc[...].astype(BF16)

                return carry

            lax.fori_loop(0, len(slots), backward, 0)
        if phase.catch:
            first = len(phase.slots) - len(phase.catch)

            def caught(step, carry):
                slot = choose(step, phase.catch)
                i = first + step
                for j in range(len(phase.catch)):
                    @pl.when(step == j)
                    def _():
                        start_load(first + j + 2)

                    @pl.when(ok(slot) & (step == j))
                    def _():
                        load_kv(first + j).wait()

                @pl.when(ok(slot))
                def _():
                    turned[...] = kv[i, :, key_lanes].T[:half]

                def with_query(query, carry):
                    @pl.when(flags[2 * slot + query] != 0)
                    def _():
                        for j in range(heads):
                            dq[query, rows[j]] += jnp.dot(
                                turned[rows[j]], ins["ds"][2 * step + query, :, columns[j]], preferred_element_type=F32
                            )

                    return carry

                lax.fori_loop(0, 2, with_query, 0)
                return carry

            lax.fori_loop(0, len(phase.catch), caught, 0)
        if phase.last:
            for query in range(2):
                result = outs["rows%d" % query]
                result[:half] = ins["out_t"][query]
                for j in range(heads):
                    at = slice(half + j * HEAD_DIM, half + (j + 1) * HEAD_DIM)
                    result[at] = (dq[query, rows[j]] * (stat[query, 1:2, columns[j]] * SCALE)).astype(BF16)


def run_phase(phase, state, kvs, ps, cost, after=()):
    tokens, lanes = state["rows"].shape[1:]
    half = lanes // 2
    depth = lanes - 128
    wide = half // HEAD_DIM * tokens
    count = len(phase.slots)
    smem = pltpu.SMEM
    tile = ((tokens, lanes), BF16)
    shapes = {
        "wide": ((2, 2, depth, wide), BF16),
        "tall": ((2, 2, wide, depth), BF16),
        "stat": ((2, 4, wide), F32),
        "m": ((2 * len(phase.forward), 1, wide), F32),
        "acc": ((2, half, tokens), F32),
        "dq": ((2, half, tokens), F32),
        "ds": ((2 * len(phase.backward), tokens, wide), BF16),
        "out_t": ((2, half, tokens), BF16),
        "rows0": tile,
        "rows1": tile,
        "p": ((2 * len(phase.forward), tokens, wide), BF16),
    }
    sizes = {}
    for name, at in phase.targets.values():
        sizes[name] = None if at is None else max(sizes.get(name, 0), at + 1)
    shapes.update({n: tile if size is None else ((size, tokens, lanes), BF16) for n, size in sizes.items()})
    names_in, names_out = [], []
    if phase.first:
        names_in += ["flags", "own_wide", "rows"]
        names_out += ["wide"]
    else:
        names_in += ["flags", "wide", "stat"]
    if phase.forward:
        names_out += ["stat"]
        if not phase.first:
            names_in += ["acc"]
        if not phase.finish:
            names_out += ["m", "p", "acc"]
    if phase.finish:
        names_out += ["out_t", "tall"]
    if phase.backward:
        names_in += ["rows"]
        if not phase.finish:
            names_in += ["tall"] if phase.defer else ["dq", "tall"]
        names_out += (["ds"] if phase.defer else [] if phase.last else ["dq"]) + list(sizes)
        if phase.catch:
            names_in += ["ds"]
    if phase.last:
        names_in += ["out_t"]
        names_out += ["rows0", "rows1"]
    inputs = {name: state[name] for name in names_in}
    for number, array in enumerate(ps):
        inputs["p%d" % number], inputs["m%d" % number] = array
    seen = {}

    def reference_to(array):
        if id(array) not in seen:
            seen[id(array)] = "big%d" % len(seen)
            inputs[seen[id(array)]] = array
        return seen[id(array)]

    for array in after:
        reference_to(array)
    kv_at = [(reference_to(array), at) for array, at in kvs]
    names = list(inputs)
    places = {i: pl.ANY for i, name in enumerate(names) if name.startswith("big")}
    places.update({i: smem for i, name in enumerate(names) if name in ("flags", "mask")})
    small = (8, 128)
    results = call(
        functools.partial(phase_kernel, phase, names, names_out, kv_at),
        list(inputs.values()),
        [shapes[name] for name in names_out],
        scratch=[
            pltpu.VMEM((count, tokens, lanes), BF16),
            pltpu.VMEM(shapes["acc"][0] if phase.finish else small, F32),
            pltpu.VMEM((1, wide), F32),
            pltpu.SMEM((8,), jnp.int32),
            pltpu.VMEM((half, tokens), BF16),
            pltpu.VMEM((tokens, lanes) if phase.backward else small, F32),
            pltpu.VMEM((2, wide, depth) if phase.backward else (1, 16, 128), BF16),
            pltpu.VMEM((tokens, wide) if phase.backward else (16, 128), BF16),
            pltpu.VMEM(shapes["dq"][0] if phase.last else small, F32),
            pltpu.VMEM(shapes["p"][0] if phase.finish else (16, 128), BF16),
            pltpu.VMEM(shapes["m"][0] if phase.finish else small, F32),
            pltpu.SemaphoreType.DMA((count,)),
        ],
        mib=24 if phase.finish else 16,
        cost=cost,
        places=places,
    )
    state.update(zip(names_out, results))
    return state


def local(queries, key_tokens, value_tokens, cotangent, window_mask):
    shape = queries.shape
    features = shape[-1]
    tokens = queries.size // features
    tile = ((tokens, features), BF16)
    two = ((2, tokens, features), BF16)

    keep_kv, keep_qd, send = call(
        split_kernel,
        [jnp.stack([x.reshape(tokens, features) for x in (key_tokens, value_tokens, queries, cotangent)])],
        [tile, tile, two],
    )
    own_even = in_time(keep_kv, 0)
    own_odd = in_time(keep_kv, 1)
    recv = near(send)
    depth, wide = features - 128, features // 2 // HEAD_DIM * tokens
    flags, own_wide = call(
        functools.partial(early_kernel, lax.axis_size("tm")),
        [window_mask, keep_qd],
        [((FLAGS,), jnp.int32, pltpu.SMEM), ((2, 1, depth, wide), BF16)],
        places={0: pltpu.SMEM},
    )
    partner_kv, to_far, rows = call(
        merge_kernel, [keep_kv, keep_qd, recv], [tile, tile, two]
    )
    far_own = far(to_far)
    partner_even = in_time(partner_kv, 0)
    partner_odd = in_time(partner_kv, 1)
    state = {"flags": flags, "own_wide": own_wide, "rows": rows}
    state = run_phase(Phase(forward=[0, 3], first=True), state, [(keep_kv, None), (partner_kv, None)], [], COSTS[0])
    p_own = state["p"], state["m"]
    state["acc"], far_own, own_odd, own_even = lax.optimization_barrier((state["acc"], far_own, own_odd, own_even))
    far_even = in_time(far_own, 0)
    far_odd = in_time(far_own, 1)
    state = run_phase(
        Phase(forward=[6, 2, 1]), state, [(far_own, None), (own_odd, None), (own_even, None)], [], COSTS[6]
    )
    p_first = state["p"], state["m"]
    state = run_phase(Phase(forward=[5, 4]), state, [(partner_odd, None), (partner_even, None)], [], COSTS[1])
    p_second = state["p"], state["m"]
    state = run_phase(
        Phase(forward=[8, 7], backward=[([8, 7], [0, 1])], targets={7: ("g_even", None), 8: ("g_odd", None)}),
        state,
        [(far_odd, None), (far_even, None)],
        [],
        COSTS[2],
    )
    hop_even = in_time(state["g_even"], 0)
    hop_odd = in_time(state["g_odd"], 1)
    state = run_phase(
        Phase(
            backward=[([2, 1], [1, 2]), ([5, 4], [0, 1])],
            targets={1: ("g_te", 0), 4: ("g_te", 1), 2: ("g_to", 0), 5: ("g_to", 1)},
            defer=True,
        ),
        state,
        [(array, None) for array in (own_odd, own_even, partner_odd, partner_even)],
        [p_first, p_second],
        COSTS[3],
    )
    from_even = in_time(state["g_te"], 0)
    from_odd = in_time(state["g_to"], 1)
    state = run_phase(
        Phase(backward=[([6], [0])], targets={6: ("g_far", None)}),
        state,
        [(far_own, None)],
        [p_first],
        COSTS[4],
    )
    (to_far,) = call(far_sum_kernel, [state["g_far"], hop_even, hop_odd], [tile])
    from_far = far(to_far)
    state = run_phase(
        Phase(
            backward=[([0, 3], [0, 1])],
            targets={0: ("g_own", 0), 3: ("g_own", 1)},
            last=True,
            catch=[2, 1, 5, 4],
        ),
        state,
        [(array, None) for array in (keep_kv, partner_kv, own_odd, own_even, partner_odd, partner_even)],
        [p_own],
        COSTS[5],
    )
    rows_recv = near(state["rows1"])
    out, dq = call(join_rows_kernel, [state["rows0"], rows_recv], [tile, tile])
    mine, partner = call(total_kernel, [state["g_own"], from_even, from_odd, from_far], [tile, tile])
    recv_total = near(partner)
    key_grad, value_grad = call(
        join_lanes_kernel,
        [mine, recv_total],
        [tile + (pl.ANY,), tile + (pl.ANY,)],
        scratch=[pltpu.VMEM((2, tokens, features), BF16), pltpu.SemaphoreType.DMA((2, CHUNKS))],
    )
    return tuple(x.reshape(shape) for x in (out, dq, key_grad, value_grad))


def solution(mesh):
    spec = P("tm", "height", None, "heads")
    return jax.shard_map(
        local, mesh=mesh, in_specs=(spec, spec, spec, spec, P()), out_specs=(spec,) * 4, check_vma=False
    )
```

```python
import functools

import jax
import jax.numpy as jnp
from jax import lax
from jax.experimental import pallas as pl
from jax.experimental.pallas import tpu as pltpu
from jax.sharding import PartitionSpec as P

HEAD_DIM = 64
LIMIT = 1e17
FLOOR = 1e-17
SCALE = HEAD_DIM ** -0.5
BF16 = jnp.bfloat16
F32 = jnp.float32
COST = 1.15e9
COSTS = (2, 4, 50, 1, 1, 1, 3)
MIB = 1024 * 1024
FLAGS = 18
CHUNKS = 4


def pairing(size, first):
    pairs = [(i, i + 1) for i in range(first, size - 1, 2)]
    return pairs + [(b, a) for a, b in pairs]


def near(array):
    return lax.ppermute(array, "height", pairing(lax.axis_size("height"), 0))


def far(array):
    peers = lax.axis_size("height")
    return lax.ppermute(array, "height", [(i, (i + 2) % peers) for i in range(peers)])


def in_time(array, first):
    return lax.ppermute(array, "tm", pairing(lax.axis_size("tm"), first))


def offset(kind, index):
    even = 1 - 2 * lax.rem(index, 2)
    return jnp.where(kind == 0, 0, jnp.where(kind == 1, even, -even))


def near_far_tile(height):
    return jnp.where((height == 1) | (height == 2), 0, 1)


def allowed(mask_ref, unit, time, height, tiles_t):
    slot, query = unit // 2, unit % 2
    column, place = slot // 3, slot % 3
    other = height + offset(1, height)
    query_height = height if query == 0 else other
    key_height = (height, other, jnp.where(height < 2, 2, 1))[column]
    dt = offset(place, time)
    dh = key_height - query_height
    inside = (time + dt >= 0) & (time + dt < tiles_t) & (dh >= -1) & (dh <= 1)
    if slot == 3 * query:
        return inside
    flag = mask_ref[time, query_height, jnp.clip(3 * (dt + 1) + dh + 1, 0, 8)]
    return inside & (flag == 1)


def choose(index, values):
    result = jnp.int32(values[-1])
    for at, value in enumerate(values[:-1]):
        result = jnp.where(index == at, value, result)
    return result


def call(kernel, inputs, outputs, scratch=(), mib=16, cost=1, places=None):
    vmem = pl.BlockSpec(memory_space=pltpu.VMEM)
    places = places or {}
    return pl.pallas_call(
        kernel,
        out_shape=[jax.ShapeDtypeStruct(*output[:2]) for output in outputs],
        in_specs=[pl.BlockSpec(memory_space=places[i]) if i in places else vmem for i in range(len(inputs))],
        out_specs=[pl.BlockSpec(memory_space=output[2]) if len(output) > 2 else vmem for output in outputs],
        scratch_shapes=list(scratch),
        compiler_params=pltpu.CompilerParams(vmem_limit_bytes=mib * MIB),
        cost_estimate=pl.CostEstimate(flops=int(cost * COST), bytes_accessed=1000, transcendentals=0),
    )(*inputs)


def swapped_halves(x):
    return pltpu.roll(x.astype(F32), x.shape[1] // 2, 1).astype(x.dtype)


def lane_is_low(shape):
    return lax.broadcasted_iota(jnp.int32, shape, 1) < shape[1] // 2


def split_kernel(kvqd_ref, keep_kv_ref, keep_qd_ref, send_ref):
    odd = lax.rem(lax.axis_index("height"), 2)
    low = lane_is_low(kvqd_ref.shape[1:])
    for row in range(2):
        a, b = kvqd_ref[2 * row], kvqd_ref[2 * row + 1]
        if row == 1:
            a = (a.astype(F32) * SCALE).astype(BF16)
        first = jnp.where(low, a, swapped_halves(b))
        second = jnp.where(low, swapped_halves(a), b)

        keep_ref = (keep_kv_ref, keep_qd_ref)[row]

        @pl.when(odd == 0)
        def _():
            keep_ref[...] = first
            send_ref[row] = second

        @pl.when(odd != 0)
        def _():
            keep_ref[...] = second
            send_ref[row] = first


def groups(part, heads):
    found = {}
    for j in range(heads):
        found.setdefault((part * heads + j) * HEAD_DIM // 128, []).append(j)
    return list(found.items())


def block(part, tile, of, tokens):
    return slice((tile - part) * 128, (tile - part + 1) * 128), slice(of[0] * tokens, (of[-1] + 1) * tokens)


def put_wide(query, rows, wide):
    tokens, lanes = rows.shape
    half = lanes // 2
    pad = wide.shape[2] - half
    turned = rows.T
    heads = half // HEAD_DIM
    for x in range(2):
        for tile, of in groups(x, heads):
            deep, columns = block(x, tile, of, tokens)
            wide[x, query, deep, columns] = jnp.zeros((128, len(of) * tokens), wide.dtype)
        for j in range(heads):
            at = x * pad + j * HEAD_DIM
            source = x * half + j * HEAD_DIM
            wide[x, query, at : at + HEAD_DIM, j * tokens : (j + 1) * tokens] = turned[source : source + HEAD_DIM]


def put_tall(query, rows, factor, target):
    tokens, lanes = rows.shape
    half = lanes // 2
    heads = half // HEAD_DIM
    padded = jnp.zeros((8 - heads, tokens), F32)
    by_head = jnp.concatenate([factor[:, j * tokens : (j + 1) * tokens] for j in range(heads)] + [padded], axis=0).T
    lane = lax.broadcasted_iota(jnp.int32, (1, lanes), 1)
    lane = jnp.where(lane >= half, lane - half, lane)
    scale = jnp.zeros(rows.shape, F32)
    for j in range(heads):
        here = (lane >= j * HEAD_DIM) & (lane < (j + 1) * HEAD_DIM)
        scale = jnp.where(here, by_head[:, j : j + 1], scale)
    scaled = (rows.astype(F32) * scale).astype(BF16)
    position = lax.broadcasted_iota(jnp.int32, (1, 128), 1)
    for x in range(2):
        for tile, of in groups(x, heads):
            values = scaled[:, tile * 128 : (tile + 1) * 128]
            for j in of:
                start = (x * heads + j) * HEAD_DIM - tile * 128
                here = (position >= start) & (position < start + HEAD_DIM)
                deep, _ = block(x, tile, of, tokens)
                target(x)[j * tokens : (j + 1) * tokens, deep] = jnp.where(here, values, jnp.zeros_like(values))


def early_kernel(tiles_t, mask_ref, keep_qd_ref, flags_ref, wide_ref):
    time = lax.axis_index("tm")
    height = lax.axis_index("height")
    for unit in range(FLAGS):
        flags_ref[unit] = allowed(mask_ref, unit, time, height, tiles_t).astype(jnp.int32)
    put_wide(0, keep_qd_ref[...], wide_ref)


def merge_kernel(keep_kv_ref, keep_qd_ref, recv_ref, partner_ref, far_ref, rows_ref):
    partner_ref[...] = recv_ref[0]
    rows_ref[0] = keep_qd_ref[...]
    rows_ref[1] = recv_ref[1]
    beside = near_far_tile(lax.axis_index("height"))

    @pl.when(beside == 0)
    def _():
        far_ref[...] = keep_kv_ref[...]

    @pl.when(beside != 0)
    def _():
        far_ref[...] = recv_ref[0]


def join_rows_kernel(own_ref, recv_ref, out_ref, dq_ref):
    odd = lax.rem(lax.axis_index("height"), 2)
    half = own_ref.shape[0] // 2

    def join(low, high):
        for at, ref in enumerate((out_ref, dq_ref)):
            rows = slice(at * half, (at + 1) * half)
            ref[...] = jnp.concatenate([low[rows], high[rows]], axis=0).T

    @pl.when(odd == 0)
    def _():
        join(own_ref, recv_ref)

    @pl.when(odd != 0)
    def _():
        join(recv_ref, own_ref)


def join_lanes_kernel(own_ref, recv_ref, key_hbm, value_hbm, staged, sem):
    odd = lax.rem(lax.axis_index("height"), 2)
    rows = own_ref.shape[0] // CHUNKS
    copies = []
    for c in range(CHUNKS):
        at = slice(c * rows, (c + 1) * rows)

        def join(low_ref, high_ref):
            low, high = low_ref[at], high_ref[at]
            lanes_low = lane_is_low(low.shape)
            staged[0, at] = jnp.where(lanes_low, low, swapped_halves(high))
            staged[1, at] = jnp.where(lanes_low, swapped_halves(low), high)

        @pl.when(odd == 0)
        def _():
            join(own_ref, recv_ref)

        @pl.when(odd != 0)
        def _():
            join(recv_ref, own_ref)

        for n, target in enumerate((key_hbm, value_hbm)):
            copies.append(pltpu.make_async_copy(staged.at[n, at], target.at[at], sem.at[n, c]))
            copies[-1].start()
    for copy in copies:
        copy.wait()


def far_sum_kernel(own_ref, even_ref, odd_ref, out_ref):
    total = own_ref[...].astype(F32) + even_ref[...].astype(F32) + odd_ref[...].astype(F32)
    out_ref[...] = total.astype(BF16)


def total_kernel(own_ref, even_ref, odd_ref, far_ref, mine_ref, partner_ref):
    beside = near_far_tile(lax.axis_index("height"))
    for tile, ref in enumerate((mine_ref, partner_ref)):
        total = own_ref[tile].astype(F32) + even_ref[tile].astype(F32) + odd_ref[tile].astype(F32)
        share = jnp.where(beside == tile, 1.0, 0.0).astype(F32)
        ref[...] = (total + far_ref[...].astype(F32) * share).astype(BF16)


class Phase:
    def __init__(self, forward=(), backward=(), targets=None, first=False, last=False):
        self.forward = list(forward)
        self.segments = list(backward)
        self.backward = [slot for slots, _ in backward for slot in slots]
        self.targets = targets or {}
        self.first, self.last = first, last
        self.finish = bool(forward) and bool(backward)
        self.both = all(slot < 6 for slot in (self.forward + self.backward)[-2:])
        self.slots = self.forward + [slot for slot in self.backward if slot not in self.forward]


def phase_kernel(phase, names_in, names_out, kv_at, *refs):
    ins = dict(zip(names_in, refs))
    outs = dict(zip(names_out, refs[len(names_in):]))
    kv, acc_s, sums, state_s, turned, g_acc, tall_s, slopes, dq_s, p_s, m_s, kv_sem = refs[len(names_in) + len(names_out):]
    count, tokens, lanes = kv.shape
    half = lanes // 2
    heads = half // HEAD_DIM
    depth = lanes - 128
    key_lanes, value_lanes = slice(0, depth), slice(lanes - depth, lanes)
    pad = depth - half
    columns = [slice(j * tokens, (j + 1) * tokens) for j in range(heads)]
    rows = [slice(j * HEAD_DIM, (j + 1) * HEAD_DIM) for j in range(heads)]
    flags = ins["flags"]

    def ok(slot):
        return (flags[2 * slot] + flags[2 * slot + 1]) != 0

    def load_kv(i):
        name, at = kv_at[i]
        source = ins[name] if at is None else ins[name].at[at]
        return pltpu.make_async_copy(source, kv.at[i], kv_sem.at[i])

    def start_load(i):
        if i < count:
            @pl.when(ok(phase.slots[i]))
            def _():
                load_kv(i).start()

    start_load(0)
    start_load(1)

    if phase.first:
        wide = outs["wide"]
        wide[:, 0:1] = ins["own_wide"][...]
        put_wide(1, ins["rows"][1], wide)
    else:
        wide = ins["wide"]

    if phase.forward:
        stat = outs["stat"]
        acc, p_out, m_out = (acc_s, p_s, m_s) if phase.finish else (outs["acc"], outs["p"], outs["m"])

        if phase.first:
            shifted = jnp.bool_(False)
        else:
            shifted = jnp.max(ins["stat"][0, 3:4, 0:128]) > 0.0

        def attempt(number, carry):
            def begin():
                if phase.first:
                    stat[...] = jnp.zeros_like(stat)
                    acc[...] = jnp.zeros_like(acc)
                else:
                    stat[...] = ins["stat"][...]
                    acc[...] = ins["acc"][...]

                @pl.when(number != 0)
                def _():
                    stat[:, 3:4] = jnp.ones((2, 1, stat.shape[2]), F32)
                    if phase.first:
                        stat[:, 0:1] = jnp.full((2, 1, stat.shape[2]), -1e30, F32)

            def forward(i, carry):
                slot = choose(i, phase.forward)
                for j in range(len(phase.forward)):
                    @pl.when((i == j) & (number == 0))
                    def _():
                        start_load(j + 2)

                    @pl.when(ok(slot) & (i == j) & (number == 0))
                    def _():
                        load_kv(j).wait()

                @pl.when(ok(slot))
                def _():
                    turned[...] = kv[i, :, value_lanes].T[pad:]

                exact = shifted | (number != 0)

                def scores(query, tile, of):
                    deep, at = block(0, tile, of, tokens)
                    keys = kv[i, :, tile * 128 : (tile + 1) * 128]
                    return at, jnp.dot(keys, wide[0, query, deep, at], preferred_element_type=F32)

                def attend(query, weights_of):
                    for tile, of in groups(0, heads):
                        at, s = scores(query, tile, of)
                        e = weights_of(s, at)
                        stat[query, 1:2, at] += jnp.sum(e, axis=0, keepdims=True)
                        p_out[2 * i + query, :, at] = e.astype(BF16)
                    for j in range(heads):
                        acc[query, rows[j]] += jnp.dot(
                            turned[rows[j]], p_out[2 * i + query, :, columns[j]], preferred_element_type=F32
                        )

                def plain(query):
                    m_out[2 * i + query] = jnp.zeros((1, stat.shape[2]), F32)
                    attend(query, lambda s, at: jnp.exp(s))

                two = (flags[2 * slot] != 0) & (flags[2 * slot + 1] != 0) & jnp.logical_not(exact)
                if phase.both:
                    @pl.when(two)
                    def _():
                        plain(0)
                        plain(1)
                else:
                    two = jnp.bool_(False)

                def with_query(query, carry):
                    unit = 2 * slot + query

                    @pl.when((flags[unit] != 0) & jnp.logical_not(exact | two))
                    def _():
                        plain(query)

                    @pl.when((flags[unit] != 0) & exact)
                    def _():
                        m_old = stat[query, 0:1]
                        for tile, of in groups(0, heads):
                            at, s = scores(query, tile, of)
                            sums[:, at] = jnp.max(s, axis=0, keepdims=True)
                        m_new = jnp.maximum(m_old, sums[...])
                        alpha = jnp.exp(m_old - m_new)
                        stat[query, 0:1] = m_new
                        m_out[2 * i + query] = m_new
                        stat[query, 1:2] = stat[query, 1:2] * alpha
                        for j in range(heads):
                            acc[query, rows[j]] = acc[query, rows[j]] * alpha[:, columns[j]]
                        attend(query, lambda s, at: jnp.exp(s - stat[query, 0:1, at]))

                    return carry

                lax.fori_loop(0, 2, with_query, 0)
                return carry

            @pl.when(state_s[0] != 0)
            def _():
                begin()
                lax.fori_loop(0, len(phase.forward), forward, 0)
                fits = jnp.max(stat[:, 1:2]) < LIMIT
                if phase.first:
                    fits = fits & (jnp.min(stat[:, 1:2]) > FLOOR)
                state_s[0] = jnp.where(fits, 0, 1)

            return carry

        state_s[0] = 1
        lax.fori_loop(0, 2, attempt, 0)
    else:
        stat = ins["stat"]

    if phase.finish:
        tall = outs["tall"]
        for query in range(2):
            inverse = 1.0 / stat[query, 1:2]
            stat[query, 1:2] = inverse
            for j in range(heads):
                out_t = (acc[query, rows[j]] * inverse[:, columns[j]]).astype(BF16)
                outs["out_t"][query, rows[j]] = out_t
                at = slice(pad + j * HEAD_DIM, pad + (j + 1) * HEAD_DIM)
                both = wide[1, query, at, columns[j]].astype(F32) * out_t.astype(F32)
                stat[query, 2:3, columns[j]] = jnp.sum(both, axis=0, keepdims=True)
            put_tall(query, ins["rows"][query], inverse, lambda x: tall.at[x, query])
    elif phase.backward:
        tall = ins["tall"]

    if phase.backward:
        dq = dq_s if phase.last else outs["dq"]
        moved = jnp.max(stat[0, 3:4, 0:128]) > 0.0
        if phase.finish:
            dq[...] = jnp.zeros_like(dq)
        else:
            dq[...] = ins["dq"][...]
        for number, (slots, places) in enumerate(phase.segments):
            p_in = p_s if phase.finish else ins["p%d" % number]
            m_in = m_s if phase.finish else ins["m%d" % number]
            where = [phase.slots.index(slot) for slot in slots]
            loading = len(phase.forward)

            def backward(step, carry):
                slot = choose(step, slots)
                place = choose(step, places)
                i = choose(step, where)
                for j in range(len(slots)):
                    if where[j] >= loading:
                        @pl.when(step == j)
                        def _():
                            start_load(where[j] + 2)

                        @pl.when(ok(slot) & (step == j))
                        def _():
                            load_kv(where[j]).wait()

                g_acc[...] = jnp.zeros_like(g_acc)

                @pl.when(ok(slot))
                def _():
                    turned[...] = kv[i, :, key_lanes].T[:half]

                def terms(query, tall_of, gamma):
                    at_p = 2 * place + query
                    for tile, of in groups(1, heads):
                        deep, at = block(1, tile, of, tokens)
                        values = kv[i, :, tile * 128 : (tile + 1) * 128]
                        dp = jnp.dot(values, wide[1, query, deep, at], preferred_element_type=F32)
                        slopes[:, at] = p_in[at_p, :, at] * (dp - stat[query, 2:3, at]).astype(BF16)
                    for x in range(2):
                        for tile, of in groups(x, heads):
                            deep, at = block(x, tile, of, tokens)
                            left = p_in[at_p, :, at] if x else slopes[:, at]
                            g_acc[:, tile * 128 : (tile + 1) * 128] += jnp.dot(
                                left, tall_of(x)[at, deep], preferred_element_type=F32
                            )
                    for j in range(heads):
                        term = jnp.dot(turned[rows[j]], slopes[:, columns[j]], preferred_element_type=F32)
                        dq[query, rows[j]] += term if gamma is None else term * gamma[:, columns[j]]

                def plain(query):
                    terms(query, lambda x: tall.at[x, query], None)

                two = (flags[2 * slot] != 0) & (flags[2 * slot + 1] != 0) & jnp.logical_not(moved)
                if phase.both:
                    @pl.when(two)
                    def _():
                        plain(0)
                        plain(1)
                else:
                    two = jnp.bool_(False)

                def with_query(query, carry):
                    unit = 2 * slot + query
                    good = flags[unit] != 0

                    @pl.when(good & jnp.logical_not(moved | two))
                    def _():
                        plain(query)

                    @pl.when(good & moved)
                    def _():
                        gamma = jnp.exp(m_in[2 * place + query] - stat[query, 0:1])
                        factor = gamma * stat[query, 1:2]
                        put_tall(query, ins["rows"][query], factor, lambda x: tall_s.at[x])
                        terms(query, lambda x: tall_s.at[x], gamma)

                    return carry

                lax.fori_loop(0, 2, with_query, 0)
                for j, s in enumerate(slots):
                    name, at = phase.targets[s]
                    target = outs[name] if at is None else outs[name].at[at]

                    @pl.when(step == j)
                    def _():
                        target[...] = g_acc[...].astype(BF16)

                return carry

            lax.fori_loop(0, len(slots), backward, 0)
        if phase.last:
            for query in range(2):
                result = outs["rows%d" % query]
                result[:half] = ins["out_t"][query]
                for j in range(heads):
                    at = slice(half + j * HEAD_DIM, half + (j + 1) * HEAD_DIM)
                    result[at] = (dq[query, rows[j]] * (stat[query, 1:2, columns[j]] * SCALE)).astype(BF16)


def run_phase(phase, state, kvs, ps, cost, after=()):
    tokens, lanes = state["rows"].shape[1:]
    half = lanes // 2
    depth = lanes - 128
    wide = half // HEAD_DIM * tokens
    count = len(phase.slots)
    smem = pltpu.SMEM
    tile = ((tokens, lanes), BF16)
    shapes = {
        "wide": ((2, 2, depth, wide), BF16),
        "tall": ((2, 2, wide, depth), BF16),
        "stat": ((2, 4, wide), F32),
        "m": ((2 * len(phase.forward), 1, wide), F32),
        "acc": ((2, half, tokens), F32),
        "dq": ((2, half, tokens), F32),
        "out_t": ((2, half, tokens), BF16),
        "rows0": tile,
        "rows1": tile,
        "p": ((2 * len(phase.forward), tokens, wide), BF16),
    }
    sizes = {}
    for name, at in phase.targets.values():
        sizes[name] = None if at is None else max(sizes.get(name, 0), at + 1)
    shapes.update({n: tile if size is None else ((size, tokens, lanes), BF16) for n, size in sizes.items()})
    names_in, names_out = [], []
    if phase.first:
        names_in += ["flags", "own_wide", "rows"]
        names_out += ["wide"]
    else:
        names_in += ["flags", "wide", "stat"]
    if phase.forward:
        names_out += ["stat"]
        if not phase.first:
            names_in += ["acc"]
        if not phase.finish:
            names_out += ["m", "p", "acc"]
    if phase.finish:
        names_out += ["out_t", "tall"]
    if phase.backward:
        names_in += ["rows"]
        if not phase.finish:
            names_in += ["dq", "tall"]
        names_out += ([] if phase.last else ["dq"]) + list(sizes)
    if phase.last:
        names_in += ["out_t"]
        names_out += ["rows0", "rows1"]
    inputs = {name: state[name] for name in names_in}
    for number, array in enumerate(ps):
        inputs["p%d" % number], inputs["m%d" % number] = array
    seen = {}

    def reference_to(array):
        if id(array) not in seen:
            seen[id(array)] = "big%d" % len(seen)
            inputs[seen[id(array)]] = array
        return seen[id(array)]

    for array in after:
        reference_to(array)
    kv_at = [(reference_to(array), at) for array, at in kvs]
    names = list(inputs)
    places = {i: pl.ANY for i, name in enumerate(names) if name.startswith("big")}
    places.update({i: smem for i, name in enumerate(names) if name in ("flags", "mask")})
    small = (8, 128)
    results = call(
        functools.partial(phase_kernel, phase, names, names_out, kv_at),
        list(inputs.values()),
        [shapes[name] for name in names_out],
        scratch=[
            pltpu.VMEM((count, tokens, lanes), BF16),
            pltpu.VMEM(shapes["acc"][0] if phase.finish else small, F32),
            pltpu.VMEM((1, wide), F32),
            pltpu.SMEM((8,), jnp.int32),
            pltpu.VMEM((half, tokens), BF16),
            pltpu.VMEM((tokens, lanes) if phase.backward else small, F32),
            pltpu.VMEM((2, wide, depth) if phase.backward else (1, 16, 128), BF16),
            pltpu.VMEM((tokens, wide) if phase.backward else (16, 128), BF16),
            pltpu.VMEM(shapes["dq"][0] if phase.last else small, F32),
            pltpu.VMEM(shapes["p"][0] if phase.finish else (16, 128), BF16),
            pltpu.VMEM(shapes["m"][0] if phase.finish else small, F32),
            pltpu.SemaphoreType.DMA((count,)),
        ],
        mib=24,
        cost=cost,
        places=places,
    )
    state.update(zip(names_out, results))
    return state


def local(queries, key_tokens, value_tokens, cotangent, window_mask):
    shape = queries.shape
    features = shape[-1]
    tokens = queries.size // features
    tile = ((tokens, features), BF16)
    two = ((2, tokens, features), BF16)

    keep_kv, keep_qd, send = call(
        split_kernel,
        [jnp.stack([x.reshape(tokens, features) for x in (key_tokens, value_tokens, queries, cotangent)])],
        [tile, tile, two],
    )
    own_even = in_time(keep_kv, 0)
    own_odd = in_time(keep_kv, 1)
    recv = near(send)
    depth, wide = features - 128, features // 2 // HEAD_DIM * tokens
    flags, own_wide = call(
        functools.partial(early_kernel, lax.axis_size("tm")),
        [window_mask, keep_qd],
        [((FLAGS,), jnp.int32, pltpu.SMEM), ((2, 1, depth, wide), BF16)],
        places={0: pltpu.SMEM},
    )
    partner_kv, to_far, rows = call(
        merge_kernel, [keep_kv, keep_qd, recv], [tile, tile, two]
    )
    far_own = far(to_far)
    partner_even = in_time(partner_kv, 0)
    partner_odd = in_time(partner_kv, 1)
    state = {"flags": flags, "own_wide": own_wide, "rows": rows}
    state = run_phase(Phase(forward=[0, 3], first=True), state, [(keep_kv, None), (partner_kv, None)], [], COSTS[0])
    p_own = state["p"], state["m"]
    state["acc"], far_own, own_even, own_odd = lax.optimization_barrier((state["acc"], far_own, own_even, own_odd))
    far_even = in_time(far_own, 0)
    far_odd = in_time(far_own, 1)
    state = run_phase(
        Phase(forward=[6, 1, 2]), state, [(far_own, None), (own_even, None), (own_odd, None)], [], COSTS[6]
    )
    p_first = state["p"], state["m"]
    state = run_phase(Phase(forward=[4, 5]), state, [(partner_even, None), (partner_odd, None)], [], COSTS[1])
    p_second = state["p"], state["m"]
    state = run_phase(
        Phase(forward=[7, 8], backward=[([7, 8], [0, 1])], targets={7: ("g_even", None), 8: ("g_odd", None)}),
        state,
        [(far_even, None), (far_odd, None)],
        [],
        COSTS[2],
    )
    hop_even = in_time(state["g_even"], 0)
    hop_odd = in_time(state["g_odd"], 1)
    state = run_phase(
        Phase(
            backward=[([1, 2], [1, 2]), ([4, 5], [0, 1])],
            targets={1: ("g_te", 0), 4: ("g_te", 1), 2: ("g_to", 0), 5: ("g_to", 1)},
        ),
        state,
        [(array, None) for array in (own_even, own_odd, partner_even, partner_odd)],
        [p_first, p_second],
        COSTS[3],
    )
    from_even = in_time(state["g_te"], 0)
    from_odd = in_time(state["g_to"], 1)
    state = run_phase(
        Phase(backward=[([6], [0])], targets={6: ("g_far", None)}),
        state,
        [(far_own, None)],
        [p_first],
        COSTS[4],
    )
    (to_far,) = call(far_sum_kernel, [state["g_far"], hop_even, hop_odd], [tile])
    from_far = far(to_far)
    state = run_phase(
        Phase(backward=[([0, 3], [0, 1])], targets={0: ("g_own", 0), 3: ("g_own", 1)}, last=True),
        state,
        [(keep_kv, None), (partner_kv, None)],
        [p_own],
        COSTS[5],
    )
    rows_recv = near(state["rows1"])
    out, dq = call(join_rows_kernel, [state["rows0"], rows_recv], [tile, tile])
    mine, partner = call(total_kernel, [state["g_own"], from_even, from_odd, from_far], [tile, tile])
    recv_total = near(partner)
    key_grad, value_grad = call(
        join_lanes_kernel,
        [mine, recv_total],
        [tile + (pl.ANY,), tile + (pl.ANY,)],
        scratch=[pltpu.VMEM((2, tokens, features), BF16), pltpu.SemaphoreType.DMA((2, CHUNKS))],
    )
    return tuple(x.reshape(shape) for x in (out, dq, key_grad, value_grad))


def solution(mesh):
    spec = P("tm", "height", None, "heads")
    return jax.shard_map(
        local, mesh=mesh, in_specs=(spec, spec, spec, spec, P()), out_specs=(spec,) * 4, check_vma=False
    )
```
